32 devices in a mesh: dp: 4 (over z), fsdp: 8 (over y, x, core).
Axes of the slice: x: 2, y: 2, z: 4, core: 2. Of those that a mesh axis runs over, the one named last changes fastest.
Arguments:
- pixels: float32 [24576, 768], P(('dp', 'fsdp')), may hold values from 0 to 2
- masked: int32 [24576], P(('dp', 'fsdp')), may hold values from 0 to 1, as said below
- valid: int32 [24576], P(('dp', 'fsdp')), may hold values from 0 to 1, as said below
- scene_ids: int32 [24576], P(('dp', 'fsdp')), may hold values from 0 to 63, as said below
- gsd_index: int32 [64], P(('dp', 'fsdp')), may hold values from 0 to 7
- coords: int32 [24576, 2], P(('dp', 'fsdp')), may hold values from 0 to 31
- embed: float32 [768, 1024], P('fsdp'), may hold values from -0.21875 to 0.21875
- wide_enc: float32 [1024, 8704], P('fsdp'), may hold values from -0.1875 to 0.1875
- enc_down: float32 [4096, 1024], P('fsdp'), may hold values from -0.09375 to 0.09375
- wide_dec: float32 [512, 5056], P('fsdp'), may hold values from -0.25 to 0.25
- dec_down: float32 [2048, 512], P('fsdp'), may hold values from -0.125 to 0.125
- vectors: float32 [5120], replicated, may hold values from 0.5 to 1.5
- embed_mom: float32 [768, 1024], P('fsdp'), may hold values from -0.01171875 to 0.01171875
- wide_enc_mom: float32 [1024, 8704], P('fsdp'), may hold values from -0.01171875 to 0.01171875
- enc_down_mom: float32 [4096, 1024], P('fsdp'), may hold values from -0.01171875 to 0.01171875
- wide_dec_mom: float32 [512, 5056], P('fsdp'), may hold values from -0.01171875 to 0.01171875
- dec_down_mom: float32 [2048, 512], P('fsdp'), may hold values from -0.01171875 to 0.01171875
- vector_mom: float32 [5120], replicated, may hold values from -0.0390625 to 0.0390625
- embed_avg: float32 [768, 1024], P('fsdp'), may hold values from -0.21875 to 0.21875
- wide_enc_avg: float32 [1024, 8704], P('fsdp'), may hold values from -0.1875 to 0.1875
- enc_down_avg: float32 [4096, 1024], P('fsdp'), may hold values from -0.09375 to 0.09375
- wide_dec_avg: float32 [512, 5056], P('fsdp'), may hold values from -0.25 to 0.25
- dec_down_avg: float32 [2048, 512], P('fsdp'), may hold values from -0.125 to 0.125
- vector_avg: float32 [5120], replicated, may hold values from 0.5 to 1.5
Outputs:
- embed_mom_new: float32 [768, 1024], P('fsdp')
- embed_new: float32 [768, 1024], P('fsdp')
- embed_avg_new: float32 [768, 1024], P('fsdp')
- embed_copy: bfloat16 [768, 1024], P('fsdp')
- wide_enc_mom_new: float32 [1024, 8704], P('fsdp')
- wide_enc_new: float32 [1024, 8704], P('fsdp')
- wide_enc_avg_new: float32 [1024, 8704], P('fsdp')
- wide_enc_copy: bfloat16 [1024, 8704], P('fsdp')
- enc_down_mom_new: float32 [4096, 1024], P('fsdp')
- enc_down_new: float32 [4096, 1024], P('fsdp')
- enc_down_avg_new: float32 [4096, 1024], P('fsdp')
- enc_down_copy: bfloat16 [4096, 1024], P('fsdp')
- wide_dec_mom_new: float32 [512, 5056], P('fsdp')
- wide_dec_new: float32 [512, 5056], P('fsdp')
- wide_dec_avg_new: float32 [512, 5056], P('fsdp')
- wide_dec_copy: bfloat16 [512, 5056], P('fsdp')
- dec_down_mom_new: float32 [2048, 512], P('fsdp')
- dec_down_new: float32 [2048, 512], P('fsdp')
- dec_down_avg_new: float32 [2048, 512], P('fsdp')
- dec_down_copy: bfloat16 [2048, 512], P('fsdp')
- vector_mom_new: float32 [5120], replicated
- vectors_new: float32 [5120], replicated
- vector_avg_new: float32 [5120], replicated
- loss_sum: float32 [], replicated
- count: float32 [], replicated
The draws below stay inside these ranges and needn't reach their ends.
Inputs may be any that keep to these rules, and one draw needn't show every extreme that they name: In each block the valid slots are its first 4 k, k from 1 to 192; the last block holds 768 valid slots. Invalid slots are masked; in each block exactly a quarter of the valid slots are unmasked, at most 192. `scene_ids`: block b holds scene 2 b in its first slots and scene 2 b + 1 from a split on, possibly none.
All inputs are finite; a program needn't handle non-finite values.
Results may differ from the reference program's by a relative error of at most 0.0044.
The reference program's roundings to bfloat16 on the way count: a program that leaves them out, or rounds other values in their place, can miss the bound.
Values may be sent and summed in bfloat16 or wider, within the bound.
A program may use at most 320 MiB of HBM per device.

```python
from functools import partial
import jax
import jax.numpy as jnp
from jax import lax

D = 1024
HEADS = 16
FF = 4096
DD = 512
DHEADS = 16
DFF = 2048
PATCH = 16
BANDS = 3
TOK_DEV = 768
PD = 768
LOWD = 192
VIS = 192
BLOCKS = 32
TOKENS = 24576
SCENES = 64
N_DP = 4
N_FSDP = 8


def layout(key):
    blocks = N_DP * N_FSDP
    number = jnp.arange(blocks, dtype=jnp.int32)
    along = number % N_FSDP
    across = number // N_FSDP
    top = N_FSDP - 1 + N_DP - 1
    ramp = VIS // 3 + (VIS - VIS // 3) * (along + across) // top
    jitter = jax.random.randint(jax.random.fold_in(key, 11), (blocks,), 0, VIS // 6 + 1)
    seen = jnp.clip(jnp.where(along + across == top, VIS, ramp - jitter), 1, VIS)
    filled = 4 * seen
    slot = jnp.arange(TOK_DEV, dtype=jnp.int32)
    inside = slot[None, :] < filled[:, None]
    keys = jax.vmap(lambda k: jax.random.permutation(k, TOK_DEV))(jax.random.split(jax.random.fold_in(key, 12), blocks))
    score = jnp.where(inside, keys.astype(jnp.int32), TOK_DEV + slot[None, :])
    rank = jnp.argsort(jnp.argsort(score, axis=1), axis=1)
    masked = 1 - (rank < seen[:, None]).astype(jnp.int32)
    split = jax.random.randint(jax.random.fold_in(key, 13), (blocks,), 1, TOK_DEV)
    whole = jax.random.randint(jax.random.fold_in(key, 14), (blocks,), 0, 2)
    split = jnp.where(whole == 1, TOK_DEV, split)
    scene = 2 * number[:, None] + (slot[None, :] >= split[:, None]).astype(jnp.int32)
    return (inside.astype(jnp.int32).reshape(-1), masked.reshape(-1), scene.reshape(-1))


def draw_valid(key, part):
    return layout(key)[0]


def draw_masked(key, part):
    return layout(key)[1]


def draw_scene_ids(key, part):
    return layout(key)[2]


def place_ends(array, rng, low, high):
    dims = array.shape
    index_at = [jax.random.randint(jax.random.fold_in(rng, axis), (), 0, dims[axis]) for axis in range(len(dims))]
    array = array.at[tuple(index_at)].set(low)
    longest = dims.index(max(dims))
    index_at[longest] = (index_at[longest] + 1) % dims[longest]
    return array.at[tuple(index_at)].set(high)


def block_levels(rng, dims, shards, least, top_value):
    level, own = 1.0, jax.random.fold_in(rng, 6)
    for dim, blocks in shards:
        heights = jnp.exp(jax.random.uniform(jax.random.fold_in(own, dim), (blocks,), jnp.float32, least / len(shards), top_value / len(shards)))
        level = level * jnp.repeat(heights, dims[dim] // blocks).reshape([-1 if axis == dim else 1 for axis in range(len(dims))])
    return level


def gaussian(own_key, shape, scale, bound, cuts=(), kind=jnp.bfloat16):
    factor_of = block_levels(own_key, shape, cuts, -0.22, 0.18) if cuts else 1.0
    array = jax.random.normal(own_key, shape, jnp.float32) * scale * factor_of
    return jnp.minimum(jnp.maximum(array, -bound), bound).astype(kind)


def setup_inputs(seed: int = 0) -> dict:
    splits = jax.random.split(jax.random.key(seed), 25)
    return {
        "pixels": jnp.clip(2.0 * jax.random.uniform(splits[0], (TOKENS, PD), jnp.float32) ** block_levels(splits[0], (TOKENS, PD), ((0, 32),), -0.2, 0.2), 0.0, 2.0),
        "masked": draw_masked(jax.random.fold_in(splits[24], 71), 0),
        "valid": draw_valid(jax.random.fold_in(splits[24], 71), 0),
        "scene_ids": draw_scene_ids(jax.random.fold_in(splits[24], 71), 0),
        "gsd_index": place_ends(jax.random.randint(splits[4], (SCENES,), 0, 8), jax.random.fold_in(splits[4], 1), 0, 7).astype(jnp.int32),
        "coords": place_ends(jax.random.randint(splits[5], (TOKENS, 2), 0, 32), jax.random.fold_in(splits[5], 1), 0, 31).astype(jnp.int32),
        "embed": gaussian(splits[6], (PD, D), PD ** -0.5, 0.21875, ((0, 8),), jnp.float32),
        "wide_enc": gaussian(splits[7], (D, 4 * D + FF + DD), D ** -0.5, 0.1875, ((0, 8),), jnp.float32),
        "enc_down": gaussian(splits[8], (FF, D), FF ** -0.5, 0.09375, ((0, 8),), jnp.float32),
        "wide_dec": gaussian(splits[9], (DD, 4 * DD + DFF + PD + LOWD), DD ** -0.5, 0.25, ((0, 8),), jnp.float32),
        "dec_down": gaussian(splits[10], (DFF, DD), DFF ** -0.5, 0.125, ((0, 8),), jnp.float32),
        "vectors": jnp.clip(1.0 + 0.1 * jax.random.normal(splits[11], (3 * D + 4 * DD,), jnp.float32), 0.5, 1.5),
        "embed_mom": gaussian(splits[12], (PD, D), (9 / (PD * TOKENS) ** 0.5), 0.01171875, ((0, 8),), jnp.float32),
        "wide_enc_mom": gaussian(splits[13], (D, 4 * D + FF + DD), (9 / (PD * TOKENS) ** 0.5), 0.01171875, ((0, 8),), jnp.float32),
        "enc_down_mom": gaussian(splits[14], (FF, D), (9 / (PD * TOKENS) ** 0.5), 0.01171875, ((0, 8),), jnp.float32),
        "wide_dec_mom": gaussian(splits[15], (DD, 4 * DD + DFF + PD + LOWD), (9 / (PD * TOKENS) ** 0.5), 0.01171875, ((0, 8),), jnp.float32),
        "dec_down_mom": gaussian(splits[16], (DFF, DD), (9 / (PD * TOKENS) ** 0.5), 0.01171875, ((0, 8),), jnp.float32),
        "vector_mom": gaussian(splits[17], (3 * D + 4 * DD,), (30 / (PD * TOKENS) ** 0.5), 0.0390625, (), jnp.float32),
        "embed_avg": gaussian(splits[18], (PD, D), PD ** -0.5, 0.21875, ((0, 8),), jnp.float32),
        "wide_enc_avg": gaussian(splits[19], (D, 4 * D + FF + DD), D ** -0.5, 0.1875, ((0, 8),), jnp.float32),
        "enc_down_avg": gaussian(splits[20], (FF, D), FF ** -0.5, 0.09375, ((0, 8),), jnp.float32),
        "wide_dec_avg": gaussian(splits[21], (DD, 4 * DD + DFF + PD + LOWD), DD ** -0.5, 0.25, ((0, 8),), jnp.float32),
        "dec_down_avg": gaussian(splits[22], (DFF, DD), DFF ** -0.5, 0.125, ((0, 8),), jnp.float32),
        "vector_avg": jnp.clip(1.0 + 0.1 * jax.random.normal(splits[23], (3 * D + 4 * DD,), jnp.float32), 0.5, 1.5),
    }


@jax.custom_vjp
def low(v):
    return lax.optimization_barrier(v.astype(jnp.bfloat16)).astype(jnp.float32)

@jax.custom_vjp
def low_back(v):
    return v

def low_keep(v):
    return (low(v), None)

def low_pass(kept, grad):
    return (grad,)

def back_keep(v):
    return (v, None)

def back_low(kept, grad):
    return (low(grad),)
low.defvjp(low_keep, low_pass)
low_back.defvjp(back_keep, back_low)
HIGH = lax.Precision.HIGHEST
EPS = 1e-06
MOMENTUM = 0.9
DECAY = 0.0001
AVERAGE = 0.9
STEP_UNIT = 0.003

def matmul(left, right):
    return jnp.dot(left, right, precision=HIGH, preferred_element_type=jnp.float32)

def layer_norm(h, gain):
    mean = lax.optimization_barrier(jnp.mean(h, -1, keepdims=True))
    cent = h - mean
    var = lax.optimization_barrier(jnp.mean(cent * cent, -1, keepdims=True))
    return cent * lax.rsqrt(var + EPS) * gain

def positions(coord, scale, width):
    quarter = width // 4
    omega = 10000.0 ** (-jnp.arange(quarter, dtype=jnp.float32) / quarter)
    angle_x = coord[:, 0:1].astype(jnp.float32) * scale[:, None] * omega[None, :]
    angle_y = coord[:, 1:2].astype(jnp.float32) * scale[:, None] * omega[None, :]
    return jnp.concatenate([jnp.sin(angle_x), jnp.cos(angle_x), jnp.sin(angle_y), jnp.cos(angle_y)], -1)

def attend(qkv, allow, heads):
    rows, width = (qkv.shape[0], qkv.shape[1] // 3)
    size = width // heads
    query = qkv[:, :width].reshape(rows, heads, size)
    keys = qkv[:, width:2 * width].reshape(rows, heads, size)
    values = qkv[:, 2 * width:].reshape(rows, heads, size)
    scores = jnp.einsum('qhe,khe->hqk', query, keys, precision=HIGH) * size ** (-0.5)
    scores = low_back(scores)
    scores = jnp.where(allow[None], scores, -1e+30)
    scores = scores - lax.optimization_barrier(jnp.max(scores, -1, keepdims=True))
    probs = jnp.exp(scores)
    probs = probs / lax.optimization_barrier(jnp.sum(probs, -1, keepdims=True))
    mixed = jnp.einsum('hqk,khe->qhe', low(probs), values, precision=HIGH).reshape(rows, width)
    return low_back(low(mixed))

def block(h, wqkv, wout, wup, wdown, gain_one, gain_two, allow, heads):
    normed_a = low(layer_norm(h, gain_one))
    qkv = low_back(low(matmul(normed_a, wqkv)))
    h = h + low_back(matmul(attend(qkv, allow, heads), wout))
    normed_b = low(layer_norm(h, gain_two))
    hidden = low_back(matmul(normed_b, wup))
    return h + low_back(matmul(low(jax.nn.gelu(hidden, approximate=False)), wdown))

def row_loss(pred, normed):
    rows = normed.shape[0]
    coarse = lax.optimization_barrier(jnp.mean(normed.reshape(rows, BANDS, PATCH // 2, 2, PATCH // 2, 2), axis=(3, 5)))
    upper = jnp.repeat(jnp.repeat(coarse, 2, axis=2), 2, axis=3).reshape(rows, PD)
    err_high = pred[:, :PD] - (normed - upper)
    err_low = pred[:, PD:] - coarse.reshape(rows, LOWD)
    return lax.optimization_barrier(jnp.mean(jnp.sqrt(err_high * err_high + 1.0) - 1.0, -1)) + lax.optimization_barrier(jnp.mean(err_low * err_low, -1))

def sample_loss(params, normed, flags, valid, scene, coord, scale):
    embed, wide_enc, enc_down, wide_dec, dec_down, vectors = params
    embed, wide_enc, enc_down, wide_dec, dec_down = [low(w) for w in (embed, wide_enc, enc_down, wide_dec, dec_down)]
    index = jnp.arange(TOK_DEV, dtype=jnp.int32)
    seen_rows = (valid > 0) & (flags == 0)
    order = jnp.argsort(jnp.where(seen_rows, index, index + TOK_DEV))[:VIS].astype(jnp.int32)
    kept = jnp.arange(VIS, dtype=jnp.int32) < jnp.sum(seen_rows.astype(jnp.int32))
    inputs = low(normed)[order]
    h = low_back(matmul(inputs, embed)) + positions(coord[order], scale[order], D)
    scene_seen = scene[order]
    allow = kept[None, :] & (scene_seen[:, None] == scene_seen[None, :]) | jnp.eye(VIS, dtype=bool)
    h = block(h, wide_enc[:, :3 * D], wide_enc[:, 3 * D:4 * D], wide_enc[:, 4 * D:4 * D + FF], enc_down, vectors[:D], vectors[D:2 * D], allow, HEADS)
    encoded = low(layer_norm(h, vectors[2 * D:3 * D]))
    seen_out = low_back(matmul(encoded, wide_enc[:, 4 * D + FF:]))
    token = vectors[3 * D + 3 * DD:]
    keptf = kept.astype(jnp.float32)[:, None]
    y = token + positions(coord, scale, DD) + jnp.zeros((TOK_DEV, DD), jnp.float32).at[order].add((seen_out - token) * keptf)
    allow = (valid[None, :] > 0) & (scene[:, None] == scene[None, :]) | jnp.eye(TOK_DEV, dtype=bool)
    base = 3 * D
    y = block(y, wide_dec[:, :3 * DD], wide_dec[:, 3 * DD:4 * DD], wide_dec[:, 4 * DD:4 * DD + DFF], dec_down, vectors[base:base + DD], vectors[base + DD:base + 2 * DD], allow, DHEADS)
    decoded = low(layer_norm(y, vectors[base + 2 * DD:base + 3 * DD]))
    pred = low_back(matmul(decoded, wide_dec[:, 4 * DD + DFF:]))
    return jnp.sum(flags * row_loss(pred, normed))

def reference(pixels, masked, valid, scene_ids, gsd_index, coords, embed, wide_enc, enc_down, wide_dec, dec_down, vectors, embed_mom, wide_enc_mom, enc_down_mom, wide_dec_mom, dec_down_mom, vector_mom, embed_avg, wide_enc_avg, enc_down_avg, wide_dec_avg, dec_down_avg, vector_avg):
    rows_ok = valid.astype(jnp.float32)
    flags = rows_ok * masked.astype(jnp.float32)
    count = jnp.sum(flags)
    n_pix = jnp.sum(rows_ok) * (PATCH * PATCH)
    bands = pixels.reshape(TOKENS, BANDS, PATCH * PATCH)
    mean = lax.optimization_barrier(jnp.sum(bands * rows_ok[:, None, None], axis=(0, 2))) / n_pix
    cent = bands - mean[None, :, None]
    var = lax.optimization_barrier(jnp.sum(cent * cent * rows_ok[:, None, None], axis=(0, 2))) / n_pix
    normed = (cent * lax.rsqrt(var + EPS)[None, :, None]).reshape(BLOCKS, TOK_DEV, PD)
    scale = jnp.exp2(0.5 * gsd_index[scene_ids].astype(jnp.float32) - 1.0)
    data = (normed, flags.reshape(BLOCKS, TOK_DEV), valid.reshape(BLOCKS, TOK_DEV), scene_ids.reshape(BLOCKS, TOK_DEV), coords.reshape(BLOCKS, TOK_DEV, 2), scale.reshape(BLOCKS, TOK_DEV))
    params = (embed, wide_enc, enc_down, wide_dec, dec_down, vectors)

    def total(weights):
        step = jax.checkpoint(partial(sample_loss, weights))
        return jnp.sum(lax.map(lambda item: step(*item), data))
    loss_sum, pull = jax.vjp(total, params)
    grads = pull(1.0 / count)[0]
    rate = STEP_UNIT * (PD * TOKENS) ** 0.5
    moms = (embed_mom, wide_enc_mom, enc_down_mom, wide_dec_mom, dec_down_mom, vector_mom)
    avgs = (embed_avg, wide_enc_avg, enc_down_avg, wide_dec_avg, dec_down_avg, vector_avg)
    outs = []
    for number in range(6):
        weight = params[number]
        grad = grads[number] + DECAY * weight
        buf = MOMENTUM * moms[number] + grad
        new = weight - rate * (grad + MOMENTUM * buf)
        outs += [buf, new, AVERAGE * avgs[number] + (1.0 - AVERAGE) * new]
        if number < 5:
            outs.append(new.astype(jnp.bfloat16))
    return (outs[0], outs[1], outs[2], outs[3], outs[4], outs[5], outs[6], outs[7], outs[8], outs[9], outs[10], outs[11], outs[12], outs[13], outs[14], outs[15], outs[16], outs[17], outs[18], outs[19], outs[20], outs[21], outs[22], loss_sum, count)
```

```python
from functools import partial

import jax
import jax.numpy as jnp
from jax import lax
from jax.experimental import pallas as pl
from jax.experimental.pallas import tpu as pltpu
from jax.sharding import PartitionSpec as P

D = 1024
HEADS = 16
FF = 4096
DD = 512
DHEADS = 16
DFF = 2048
PATCH = 16
BANDS = 3
TOK_DEV = 768
PD = 768
LOWD = 192
VIS = 192
HID = TOK_DEV - VIS

EPS = 1e-06
MOMENTUM = 0.9
DECAY = 0.0001
AVERAGE = 0.9
STEP_UNIT = 0.003
NEGATIVE = -1e30
LANES = 128
BF = jnp.bfloat16
F32 = jnp.float32


def matmul(left, right):
    return jnp.dot(left, right, preferred_element_type=jnp.float32)


def left_t(left, right):
    return lax.dot_general(
        left, right, (((0,), (0,)), ((), ())), preferred_element_type=jnp.float32
    )


def right_t(left, right):
    return lax.dot_general(
        left, right, (((1,), (1,)), ((), ())), preferred_element_type=jnp.float32
    )


def layer_norm(h, gain):
    mean = jnp.mean(h, -1, keepdims=True)
    cent = h - mean
    var = jnp.mean(cent * cent, -1, keepdims=True)
    return cent * lax.rsqrt(var + EPS) * gain


def norm_back(h, gain, grad):
    result, pull = jax.vjp(layer_norm, h, gain)
    return pull(grad)


def positions(coord, scale, width):
    quarter = width // 4
    omega = 10000.0 ** (-jnp.arange(quarter, dtype=jnp.float32) / quarter)
    angle_x = coord[:, 0:1] * scale[:, None] * omega[None, :]
    angle_y = coord[:, 1:2] * scale[:, None] * omega[None, :]
    return jnp.concatenate(
        [jnp.sin(angle_x), jnp.cos(angle_x), jnp.sin(angle_y), jnp.cos(angle_y)], -1
    )


def row_loss(pred, normed):
    rows = normed.shape[0]
    coarse = jnp.mean(normed.reshape(rows, BANDS, PATCH // 2, 2, PATCH // 2, 2), axis=(3, 5))
    upper = jnp.repeat(jnp.repeat(coarse, 2, axis=2), 2, axis=3).reshape(rows, PD)
    err_high = pred[:, :PD] - (normed - upper)
    err_low = pred[:, PD:] - coarse.reshape(rows, LOWD)
    return jnp.mean(jnp.sqrt(err_high * err_high + 1.0) - 1.0, -1) + jnp.mean(err_low * err_low, -1)


def attend_kernel(size, qt_ref, k_ref, vt_ref, bias_ref, ot_ref, lse_ref):
    per = LANES // size
    row_head = lax.broadcasted_iota(jnp.int32, qt_ref.shape, 0) // size
    factor = size ** (-0.5)
    for j in range(per):
        query = jnp.where(row_head == j, qt_ref[...].astype(F32), 0.0).astype(BF)
        scores = matmul(k_ref[...], query) * factor + bias_ref[...]
        top = jnp.max(scores, 0, keepdims=True)
        probs = jnp.exp(scores - top)
        total = jnp.sum(probs, 0, keepdims=True)
        probs = (probs * (1.0 / total)).astype(BF)
        rows = slice(j * size, (j + 1) * size)
        ot_ref[rows, :] = matmul(vt_ref[rows, :], probs).astype(BF)
        lse_ref[0, j : j + 1, :] = top + jnp.log(total)


def attend(qt, keys, vt, bias, size):
    width, queries = qt.shape
    rows = keys.shape[0]
    groups, per = width // LANES, LANES // size
    return pl.pallas_call(
        partial(attend_kernel, size),
        grid=(groups,),
        out_shape=(
            jax.ShapeDtypeStruct((width, queries), BF),
            jax.ShapeDtypeStruct((groups, per, queries), F32),
        ),
        in_specs=[
            pl.BlockSpec((LANES, queries), lambda g: (g, 0)),
            pl.BlockSpec((rows, LANES), lambda g: (0, g)),
            pl.BlockSpec((LANES, rows), lambda g: (g, 0)),
            pl.BlockSpec((rows, queries), lambda g: (0, 0)),
        ],
        out_specs=(
            pl.BlockSpec((LANES, queries), lambda g: (g, 0)),
            pl.BlockSpec((1, per, queries), lambda g: (g, 0, 0)),
        ),
        compiler_params=pltpu.CompilerParams(vmem_limit_bytes=40 * 2**20),
        cost_estimate=pl.CostEstimate(
            flops=4 * rows * queries * width * per,
            bytes_accessed=4 * rows * queries,
            transcendentals=rows * queries * width // size,
        ),
    )(qt, keys, vt, bias)


def attend_back_kernel(
    size,
    qt_ref,
    q_ref,
    k_ref,
    kt_ref,
    v_ref,
    do_ref,
    dot_ref,
    bias_ref,
    lse_ref,
    dqt_ref,
    dk_ref,
    dv_ref,
):
    per = LANES // size
    row_head = lax.broadcasted_iota(jnp.int32, qt_ref.shape, 0) // size
    lane_head = lax.broadcasted_iota(jnp.int32, dk_ref.shape, 1) // size
    factor = size ** (-0.5)
    dkeys = jnp.zeros(dk_ref.shape, F32)
    dvalues = jnp.zeros(dv_ref.shape, F32)
    for j in range(per):
        query = jnp.where(row_head == j, qt_ref[...].astype(F32), 0.0).astype(BF)
        dout = jnp.where(row_head == j, dot_ref[...].astype(F32), 0.0).astype(BF)
        scores = matmul(k_ref[...], query) * factor + bias_ref[...]
        probs = jnp.exp(scores - lse_ref[0, j : j + 1, :])
        dvalues = jnp.where(lane_head == j, matmul(probs.astype(BF), do_ref[...]), dvalues)
        dprobs = matmul(v_ref[...], dout)
        delta = jnp.sum(dprobs * probs, 0, keepdims=True)
        dscores = (probs * (dprobs - delta)).astype(BF)
        dkeys = jnp.where(lane_head == j, matmul(dscores, q_ref[...]), dkeys)
        rows = slice(j * size, (j + 1) * size)
        dqt_ref[rows, :] = (matmul(kt_ref[rows, :], dscores) * factor).astype(BF)
    dk_ref[...] = (dkeys * factor).astype(BF)
    dv_ref[...] = dvalues.astype(BF)


def attend_back(query, keys, values, dmixed, bias, lse, size):
    queries, width = query.shape
    rows = keys.shape[0]
    groups, per = width // LANES, LANES // size
    tall = lambda n: pl.BlockSpec((n, LANES), lambda g: (0, g))
    flat = lambda n: pl.BlockSpec((LANES, n), lambda g: (g, 0))
    return pl.pallas_call(
        partial(attend_back_kernel, size),
        grid=(groups,),
        out_shape=(
            jax.ShapeDtypeStruct((width, queries), BF),
            jax.ShapeDtypeStruct((rows, width), BF),
            jax.ShapeDtypeStruct((rows, width), BF),
        ),
        in_specs=[
            flat(queries),
            tall(queries),
            tall(rows),
            flat(rows),
            tall(rows),
            tall(queries),
            flat(queries),
            pl.BlockSpec((rows, queries), lambda g: (0, 0)),
            pl.BlockSpec((1, per, queries), lambda g: (g, 0, 0)),
        ],
        out_specs=(flat(queries), tall(rows), tall(rows)),
        compiler_params=pltpu.CompilerParams(vmem_limit_bytes=48 * 2**20),
        cost_estimate=pl.CostEstimate(
            flops=10 * rows * queries * width * per,
            bytes_accessed=4 * rows * queries,
            transcendentals=rows * queries * width // size,
        ),
    )(query.T, query, keys, keys.T, values, dmixed, dmixed.T, bias, lse)


def block_forward(h, weights, gains, bias, heads, skip):
    wqkv, wout, wup, wdown = weights
    width = h.shape[1]
    normed_a = layer_norm(h, gains[0]).astype(BF)
    query = matmul(normed_a[skip:], wqkv[:, :width]).astype(BF)
    keys = matmul(normed_a, wqkv[:, width : 2 * width]).astype(BF)
    values = matmul(normed_a, wqkv[:, 2 * width :]).astype(BF)
    mixed_t, lse = attend(query.T, keys, values.T, bias, width // heads)
    middle = h[skip:] + left_t(mixed_t, wout)
    normed_b = layer_norm(middle, gains[1]).astype(BF)
    before = matmul(normed_b, wup)
    hidden = jax.nn.gelu(before, approximate=False).astype(BF)
    end = middle + matmul(hidden, wdown)
    return end, (h, normed_a, query, keys, values, mixed_t, lse, middle, normed_b, before, hidden)


def block_backward(saved, grad, weights, gains, bias, heads, skip):
    wqkv, wout, wup, wdown = weights
    h, normed_a, query, keys, values, mixed_t, lse, middle, normed_b, before, hidden = saved
    width = h.shape[1]
    dbranch = grad.astype(BF)
    after, gelu_pull = jax.vjp(partial(jax.nn.gelu, approximate=False), before)
    dbefore = gelu_pull(right_t(dbranch, wdown))[0].astype(BF)
    dmiddle, dgain_two = norm_back(middle, gains[1], right_t(dbefore, wup))
    dmiddle = dmiddle + grad
    dattn = dmiddle.astype(BF)
    dmixed = right_t(dattn, wout).astype(BF)
    dqt, dkeys, dvalues = attend_back(query, keys, values, dmixed, bias, lse, width // heads)
    dquery = dqt.T
    if skip:
        dquery = jnp.pad(dquery, ((skip, 0), (0, 0)))
        dmiddle = jnp.pad(dmiddle, ((skip, 0), (0, 0)))
    dqkv = jnp.concatenate([dquery, dkeys, dvalues], 1)
    dh, dgain_one = norm_back(h, gains[0], right_t(dqkv, wqkv))
    wgrads = (
        left_t(normed_a, dqkv),
        matmul(mixed_t, dattn),
        left_t(normed_b, dbefore),
        left_t(hidden, dbranch),
    )
    return (dh + dmiddle, wgrads, (dgain_one, dgain_two))


def reduce_rows(grad):
    return lax.psum_scatter(grad.astype(BF), "fsdp", scatter_dimension=0, tiled=True)


def enc_split(wide, down):
    return (
        (wide[:, : 3 * D], wide[:, 3 * D : 4 * D], wide[:, 4 * D : 4 * D + FF], down),
        wide[:, 4 * D + FF :],
    )


def dec_split(wide, down):
    return (
        (wide[:, : 3 * DD], wide[:, 3 * DD : 4 * DD], wide[:, 4 * DD : 4 * DD + DFF], down),
        wide[:, 4 * DD + DFF :],
    )


def advance(weight, mom, avg, grad, rate):
    grad = grad + DECAY * weight
    buf = MOMENTUM * mom + grad
    new = weight - rate * (grad + MOMENTUM * buf)
    return (buf, new, AVERAGE * avg + (1.0 - AVERAGE) * new)


def arrange(valid, masked, scene_ids):
    slots = valid.shape[0]
    live = valid > 0
    kinds = jnp.stack([live & (masked == 0), live & (masked > 0), ~live], 1)
    index = jnp.arange(slots, dtype=jnp.int32)
    ranks = matmul((index[None, :] < index[:, None]).astype(BF), kinds.astype(BF)).astype(jnp.int32)
    n_seen, n_hid = [jnp.sum(kinds[:, i].astype(jnp.int32)) for i in range(2)]
    empty = ranks[:, 2]
    to_empty = jnp.where(empty < VIS - n_seen, n_seen + empty, n_seen + n_hid + empty)
    place = jnp.where(
        kinds[:, 0], ranks[:, 0], jnp.where(kinds[:, 1], VIS + ranks[:, 1], to_empty)
    )
    return (place[None, :] == index[:, None]).astype(BF), n_seen, n_hid


def exact_pick(pick, array):
    high = lax.reduce_precision(array, 8, 7)
    rest = array - high
    mid = lax.reduce_precision(rest, 8, 7)
    low = rest - mid
    return (
        matmul(pick, high.astype(BF)) + matmul(pick, mid.astype(BF)) + matmul(pick, low.astype(BF))
    )


def body(
    pixels,
    masked,
    valid,
    scene_ids,
    gsd_index,
    coords,
    embed,
    wide_enc,
    enc_down,
    wide_dec,
    dec_down,
    vectors,
    embed_mom,
    wide_enc_mom,
    enc_down_mom,
    wide_dec_mom,
    dec_down_mom,
    vector_mom,
    embed_avg,
    wide_enc_avg,
    enc_down_avg,
    wide_dec_avg,
    dec_down_avg,
    vector_avg,
):
    slots = pixels.shape[0]
    w_embed, w_enc, w_enc_down, w_dec, w_dec_down = [
        lax.all_gather(w.astype(BF), "fsdp", axis=0, tiled=True)
        for w in (embed, wide_enc, enc_down, wide_dec, dec_down)
    ]
    enc_weights, w_link = enc_split(w_enc, w_enc_down)
    dec_weights, w_head = dec_split(w_dec, w_dec_down)
    rows_ok = valid.astype(jnp.float32)
    flags = rows_ok * masked.astype(jnp.float32)
    bands = pixels.reshape(slots, BANDS, PATCH * PATCH)
    weighted = bands * rows_ok[:, None, None]
    band_sum = jnp.sum(weighted, axis=(0, 2))
    counts = jnp.stack([jnp.sum(rows_ok), jnp.sum(flags)])
    band_sq = jnp.sum(weighted * bands, axis=(0, 2))
    stats = lax.psum(jnp.concatenate([band_sum, band_sq, counts]), ("dp", "fsdp"))
    band_sum, band_sq, counts = stats[:3], stats[3:6], stats[6:]
    n_pix = counts[0] * (PATCH * PATCH)
    mean = band_sum / n_pix
    var = band_sq / n_pix - mean * mean
    count = counts[1]

    pick, n_seen, n_hid = arrange(valid, masked, scene_ids)
    picked_pixels = exact_pick(pick, pixels)
    small = matmul(
        pick, jnp.concatenate([(scene_ids % 2)[:, None], coords], 1).astype(BF)
    )
    odd, coord = small[:, 0], small[:, 1:]
    cent = picked_pixels.reshape(slots, BANDS, PATCH * PATCH) - mean[None, :, None]
    normed = (cent * lax.rsqrt(var + EPS)[None, :, None]).reshape(slots, PD)
    level = jnp.where(odd == 0, gsd_index[0], gsd_index[1]).astype(jnp.float32)
    scale = jnp.exp2(0.5 * level - 1.0)
    index = jnp.arange(slots, dtype=jnp.int32)
    kept = index[:VIS] < n_seen
    hidden_ok = index[:HID] < n_hid
    live = jnp.concatenate([kept, hidden_ok])
    keptf = kept.astype(jnp.float32)[:, None]
    allow = live[:, None] & (odd[:, None] == odd[None, :]) | (index[:, None] == index[None, :])
    bias = jnp.where(allow, 0.0, NEGATIVE)
    bias_enc, bias_dec = bias[:VIS, :VIS], bias[:, VIS:]

    gains_enc = (vectors[:D], vectors[D : 2 * D])
    gain_enc_out = vectors[2 * D : 3 * D]
    base = 3 * D
    gains_dec = (vectors[base : base + DD], vectors[base + DD : base + 2 * DD])
    gain_dec_out = vectors[base + 2 * DD : base + 3 * DD]
    token = vectors[base + 3 * DD :]

    inputs = normed[:VIS].astype(BF)
    h_start = matmul(inputs, w_embed) + positions(coord[:VIS], scale[:VIS], D)
    h_end, enc_saved = block_forward(h_start, enc_weights, gains_enc, bias_enc, HEADS, 0)
    encoded = layer_norm(h_end, gain_enc_out).astype(BF)
    seen_out = matmul(encoded, w_link)
    y_start = positions(coord, scale, DD) + jnp.concatenate(
        [jnp.where(kept[:, None], seen_out, token), jnp.broadcast_to(token, (HID, DD))]
    )
    y_end, dec_saved = block_forward(y_start, dec_weights, gains_dec, bias_dec, DHEADS, VIS)
    decoded = layer_norm(y_end, gain_dec_out).astype(BF)
    pred = matmul(decoded, w_head)
    flag = hidden_ok.astype(jnp.float32)
    losses, loss_pull = jax.vjp(lambda values: row_loss(values, normed[VIS:]), pred)
    local_loss = jnp.sum(flag * losses)
    dpred = loss_pull(flag / count)[0].astype(BF)
    head_grad = left_t(decoded, dpred)
    dy_end, dgain_dec_out = norm_back(y_end, gain_dec_out, right_t(dpred, w_head))
    dy_start, dec_grads, dgains_dec = block_backward(
        dec_saved, dy_end, dec_weights, gains_dec, bias_dec, DHEADS, VIS
    )
    picked = dy_start[:VIS] * keptf
    dtoken = jnp.sum(dy_start, 0) - jnp.sum(picked, 0)
    dseen = picked.astype(BF)
    link_grad = left_t(encoded, dseen)
    dh_end, dgain_enc_out = norm_back(h_end, gain_enc_out, right_t(dseen, w_link))
    dh_start, enc_grads, dgains_enc = block_backward(
        enc_saved, dh_end, enc_weights, gains_enc, bias_enc, HEADS, 0
    )
    embed_grad = left_t(inputs, dh_start.astype(BF))

    dec_parts = [
        reduce_rows(jnp.concatenate([dec_grads[0], dec_grads[1], dec_grads[2], head_grad], 1)),
        reduce_rows(dec_grads[3]),
    ]
    enc_parts = [
        reduce_rows(embed_grad),
        reduce_rows(jnp.concatenate([enc_grads[0], enc_grads[1], enc_grads[2], link_grad], 1)),
        reduce_rows(enc_grads[3]),
    ]
    dec_parts = lax.psum(tuple(dec_parts), "dp")
    enc_parts = lax.psum(tuple(enc_parts), "dp")
    shard_grads = [g.astype(F32) for g in (*enc_parts, *dec_parts)]
    vector_grad = jnp.concatenate(
        [
            dgains_enc[0],
            dgains_enc[1],
            dgain_enc_out,
            dgains_dec[0],
            dgains_dec[1],
            dgain_dec_out,
            dtoken,
        ]
    )
    vector_grad, loss_sum = lax.psum((vector_grad, local_loss), ("dp", "fsdp"))
    rate = STEP_UNIT * (PD * TOK_DEV * lax.axis_size("dp") * lax.axis_size("fsdp")) ** 0.5
    weights = (embed, wide_enc, enc_down, wide_dec, dec_down)
    moms = (embed_mom, wide_enc_mom, enc_down_mom, wide_dec_mom, dec_down_mom)
    avgs = (embed_avg, wide_enc_avg, enc_down_avg, wide_dec_avg, dec_down_avg)
    outs = []
    for number in range(5):
        buf, new, avg = advance(
            weights[number], moms[number], avgs[number], shard_grads[number], rate
        )
        outs += [buf, new, avg, new.astype(jnp.bfloat16)]
    return (*outs, *advance(vectors, vector_mom, vector_avg, vector_grad, rate), loss_sum, count)


def solution(mesh):
    both, rows = P(("dp", "fsdp")), P("fsdp", None)
    placed = (P(("dp", "fsdp"), None), both, both, both, both, P(("dp", "fsdp"), None))
    states = (rows,) * 5 + (P(),)
    return jax.shard_map(
        body,
        mesh=mesh,
        in_specs=placed + states * 3,
        out_specs=(rows,) * 20 + (P(),) * 5,
        check_vma=False,
    )
```

```python
from functools import partial

import jax
import jax.numpy as jnp
from jax import lax
from jax.experimental import pallas as pl
from jax.experimental.pallas import tpu as pltpu
from jax.sharding import PartitionSpec as P

D = 1024
HEADS = 16
FF = 4096
DD = 512
DHEADS = 16
DFF = 2048
PATCH = 16
BANDS = 3
TOK_DEV = 768
PD = 768
LOWD = 192
VIS = 192
HID = TOK_DEV - VIS

EPS = 1e-06
MOMENTUM = 0.9
DECAY = 0.0001
AVERAGE = 0.9
STEP_UNIT = 0.003
NEGATIVE = -1e30
LANES = 128
BF = jnp.bfloat16
F32 = jnp.float32


def matmul(left, right):
    return jnp.dot(left, right, preferred_element_type=jnp.float32)


def left_t(left, right):
    return lax.dot_general(
        left, right, (((0,), (0,)), ((), ())), preferred_element_type=jnp.float32
    )


def right_t(left, right):
    return lax.dot_general(
        left, right, (((1,), (1,)), ((), ())), preferred_element_type=jnp.float32
    )


def layer_norm(h, gain):
    mean = jnp.mean(h, -1, keepdims=True)
    cent = h - mean
    var = jnp.mean(cent * cent, -1, keepdims=True)
    return cent * lax.rsqrt(var + EPS) * gain


def norm_back(h, gain, grad):
    result, pull = jax.vjp(layer_norm, h, gain)
    return pull(grad)


def positions(coord, scale, width):
    quarter = width // 4
    omega = 10000.0 ** (-jnp.arange(quarter, dtype=jnp.float32) / quarter)
    angle_x = coord[:, 0:1] * scale[:, None] * omega[None, :]
    angle_y = coord[:, 1:2] * scale[:, None] * omega[None, :]
    return jnp.concatenate(
        [jnp.sin(angle_x), jnp.cos(angle_x), jnp.sin(angle_y), jnp.cos(angle_y)], -1
    )


def row_loss(pred, normed):
    rows = normed.shape[0]
    coarse = jnp.mean(normed.reshape(rows, BANDS, PATCH // 2, 2, PATCH // 2, 2), axis=(3, 5))
    upper = jnp.repeat(jnp.repeat(coarse, 2, axis=2), 2, axis=3).reshape(rows, PD)
    err_high = pred[:, :PD] - (normed - upper)
    err_low = pred[:, PD:] - coarse.reshape(rows, LOWD)
    return jnp.mean(jnp.sqrt(err_high * err_high + 1.0) - 1.0, -1) + jnp.mean(err_low * err_low, -1)


def attend_kernel(size, qt_ref, k_ref, vt_ref, bias_ref, ot_ref, lse_ref):
    per = LANES // size
    row_head = lax.broadcasted_iota(jnp.int32, qt_ref.shape, 0) // size
    factor = size ** (-0.5)
    for j in range(per):
        query = jnp.where(row_head == j, qt_ref[...].astype(F32), 0.0).astype(BF)
        scores = matmul(k_ref[...], query) * factor + bias_ref[...]
        top = jnp.max(scores, 0, keepdims=True)
        probs = jnp.exp(scores - top)
        total = jnp.sum(probs, 0, keepdims=True)
        probs = (probs * (1.0 / total)).astype(BF)
        rows = slice(j * size, (j + 1) * size)
        ot_ref[rows, :] = matmul(vt_ref[rows, :], probs).astype(BF)
        lse_ref[0, j : j + 1, :] = top + jnp.log(total)


def attend(qt, keys, vt, bias, size):
    width, queries = qt.shape
    rows = keys.shape[0]
    groups, per = width // LANES, LANES // size
    return pl.pallas_call(
        partial(attend_kernel, size),
        grid=(groups,),
        out_shape=(
            jax.ShapeDtypeStruct((width, queries), BF),
            jax.ShapeDtypeStruct((groups, per, queries), F32),
        ),
        in_specs=[
            pl.BlockSpec((LANES, queries), lambda g: (g, 0)),
            pl.BlockSpec((rows, LANES), lambda g: (0, g)),
            pl.BlockSpec((LANES, rows), lambda g: (g, 0)),
            pl.BlockSpec((rows, queries), lambda g: (0, 0)),
        ],
        out_specs=(
            pl.BlockSpec((LANES, queries), lambda g: (g, 0)),
            pl.BlockSpec((1, per, queries), lambda g: (g, 0, 0)),
        ),
        compiler_params=pltpu.CompilerParams(vmem_limit_bytes=40 * 2**20),
        cost_estimate=pl.CostEstimate(
            flops=4 * rows * queries * width * per,
            bytes_accessed=4 * rows * queries,
            transcendentals=rows * queries * width // size,
        ),
    )(qt, keys, vt, bias)


def attend_back_kernel(
    size,
    qt_ref,
    q_ref,
    k_ref,
    kt_ref,
    v_ref,
    do_ref,
    dot_ref,
    bias_ref,
    lse_ref,
    dqt_ref,
    dk_ref,
    dv_ref,
):
    per = LANES // size
    row_head = lax.broadcasted_iota(jnp.int32, qt_ref.shape, 0) // size
    lane_head = lax.broadcasted_iota(jnp.int32, dk_ref.shape, 1) // size
    factor = size ** (-0.5)
    dkeys = jnp.zeros(dk_ref.shape, F32)
    dvalues = jnp.zeros(dv_ref.shape, F32)
    for j in range(per):
        query = jnp.where(row_head == j, qt_ref[...].astype(F32), 0.0).astype(BF)
        dout = jnp.where(row_head == j, dot_ref[...].astype(F32), 0.0).astype(BF)
        scores = matmul(k_ref[...], query) * factor + bias_ref[...]
        probs = jnp.exp(scores - lse_ref[0, j : j + 1, :])
        dvalues = jnp.where(lane_head == j, matmul(probs.astype(BF), do_ref[...]), dvalues)
        dprobs = matmul(v_ref[...], dout)
        delta = jnp.sum(dprobs * probs, 0, keepdims=True)
        dscores = (probs * (dprobs - delta)).astype(BF)
        dkeys = jnp.where(lane_head == j, matmul(dscores, q_ref[...]), dkeys)
        rows = slice(j * size, (j + 1) * size)
        dqt_ref[rows, :] = (matmul(kt_ref[rows, :], dscores) * factor).astype(BF)
    dk_ref[...] = (dkeys * factor).astype(BF)
    dv_ref[...] = dvalues.astype(BF)


def attend_back(query, keys, values, dmixed, bias, lse, size):
    queries, width = query.shape
    rows = keys.shape[0]
    groups, per = width // LANES, LANES // size
    tall = lambda n: pl.BlockSpec((n, LANES), lambda g: (0, g))
    flat = lambda n: pl.BlockSpec((LANES, n), lambda g: (g, 0))
    return pl.pallas_call(
        partial(attend_back_kernel, size),
        grid=(groups,),
        out_shape=(
            jax.ShapeDtypeStruct((width, queries), BF),
            jax.ShapeDtypeStruct((rows, width), BF),
            jax.ShapeDtypeStruct((rows, width), BF),
        ),
        in_specs=[
            flat(queries),
            tall(queries),
            tall(rows),
            flat(rows),
            tall(rows),
            tall(queries),
            flat(queries),
            pl.BlockSpec((rows, queries), lambda g: (0, 0)),
            pl.BlockSpec((1, per, queries), lambda g: (g, 0, 0)),
        ],
        out_specs=(flat(queries), tall(rows), tall(rows)),
        compiler_params=pltpu.CompilerParams(vmem_limit_bytes=48 * 2**20),
        cost_estimate=pl.CostEstimate(
            flops=10 * rows * queries * width * per,
            bytes_accessed=4 * rows * queries,
            transcendentals=rows * queries * width // size,
        ),
    )(query.T, query, keys, keys.T, values, dmixed, dmixed.T, bias, lse)


MESH = pl.DeviceIdType.MESH
UNIT = 1024
HALF = UNIT // 2
ROWS = 128


def put(source, target, send, recv, device):
    return pltpu.make_async_remote_copy(
        src_ref=source,
        dst_ref=target,
        send_sem=send,
        recv_sem=recv,
        device_id=device,
        device_id_type=MESH,
    )


def sum_kernel(units, vec_ref, *refs):
    n_left = max(u[0] for u in units) + 1
    n_right = max(u[2] for u in units) + 1
    lefts, rights = refs[:n_left], refs[n_left : n_left + n_right]
    out_ref, vec_out = refs[n_left + n_right : n_left + n_right + 2]
    (
        xo,
        xp,
        yo,
        yp,
        a_out,
        a_in,
        b_out,
        b_in,
        sums,
        z_out,
        z_one,
        z_two,
        v_in,
        v_out,
        load_sem,
        swap_send,
        swap_recv,
        a_send,
        a_recv,
        b_send,
        b_recv,
        z_send,
        z_recv,
        v_send,
        v_recv,
    ) = refs[n_left + n_right + 2 :]
    count = len(units)
    z, f = lax.axis_index("dp"), lax.axis_index("fsdp")
    core, place = f % 2, f // 2
    x, y = place % 2, place // 2
    partner = (z, f + 1 - 2 * core)
    x_side = (z, f + 2 - 4 * x)
    y_side = (z, f + 4 - 8 * y)
    at_x, at_y, at_far = place + 1 - 2 * x, place + 2 - 4 * y, 3 - place
    low = z < 2
    outer = (z == 0) | (z == 3)
    inner = (z == 1) | (z == 2)
    inward = (jnp.where(low, 1, 2), f)
    across = (3 - z, f)
    outward = (jnp.where(low, 0, 3), f)

    barrier = pltpu.get_barrier_semaphore()
    for device in (partner, x_side, y_side):
        pl.semaphore_signal(barrier, inc=1, device_id=device, device_id_type=MESH)

    @pl.when(outer)
    def _():
        pl.semaphore_signal(barrier, inc=1, device_id=inward, device_id_type=MESH)
        pl.semaphore_wait(barrier, 4)

    @pl.when(inner)
    def _():
        pl.semaphore_signal(barrier, inc=1, device_id=across, device_id_type=MESH)
        pl.semaphore_signal(barrier, inc=1, device_id=outward, device_id_type=MESH)
        pl.semaphore_wait(barrier, 5)

    for number, (left, sub, right, column) in enumerate(units):
        rows, cols = pl.ds(sub * ROWS, ROWS), pl.ds(column, UNIT)
        whole = pl.ds(0, rights[right].shape[0])
        put(
            lefts[left].at[:, 1 - core, rows],
            xp.at[number],
            swap_send.at[number, 0],
            swap_recv.at[number, 0],
            partner,
        ).start()
        put(
            rights[right].at[whole, cols],
            yp.at[number],
            swap_send.at[number, 1],
            swap_recv.at[number, 1],
            partner,
        ).start()
        pltpu.make_async_copy(
            lefts[left].at[:, core, rows], xo.at[number], load_sem.at[number, 0]
        ).start()
        pltpu.make_async_copy(
            rights[right].at[whole, cols], yo.at[number], load_sem.at[number, 1]
        ).start()

    first, second = pl.ds(0, HALF), pl.ds(HALF, HALF)

    def swap(u, side, source, target):
        return put(source, target, swap_send.at[u, side], swap_recv.at[u, side], partner)

    def part(u, owner, columns):
        return matmul(xo[u, owner], yo[u, :, columns]) + matmul(xp[u, owner], yp[u, :, columns])

    def copy_a(u, side):
        slot = u % a_out.shape[0]
        return put(
            a_out.at[slot, side],
            a_in.at[u, side],
            a_send.at[slot, side],
            a_recv.at[u, side],
            (x_side, y_side)[side],
        )

    def copy_b(u, side):
        slot = u % b_out.shape[0]
        return put(
            b_out.at[slot, side],
            b_in.at[u, side],
            b_send.at[slot, side],
            b_recv.at[u, side],
            (y_side, x_side)[side],
        )

    def copy_in(u):
        return put(z_out.at[u], z_one.at[u], z_send.at[u, 0], z_recv.at[u, 0], inward)

    def copy_across(u):
        return put(z_out.at[u], z_two.at[u], z_send.at[u, 0], z_recv.at[u, 1], across)

    def copy_out(u):
        return put(out_ref.at[u], z_one.at[u], z_send.at[u, 1], z_recv.at[u, 0], outward)

    def copy_v(step, device):
        return put(v_out.at[step], v_in.at[step], v_send.at[step], v_recv.at[step], device)

    def step(i, _):
        def stage(lag, also=None):
            u = i - lag
            ok = (u >= 0) & (u < count)
            if also is not None:
                ok = ok & also
            return u, pl.when(ok)

        u0, when = stage(0)

        @when
        def _():
            u = u0
            pltpu.make_async_copy(xo.at[u], xo.at[u], load_sem.at[u, 0]).wait()
            pltpu.make_async_copy(yo.at[u], yo.at[u], load_sem.at[u, 1]).wait()
            swap(u, 0, xo.at[u], xp.at[u]).wait()
            swap(u, 1, yo.at[u], yp.at[u]).wait()

            @pl.when(u >= a_out.shape[0])
            def _():
                for side in range(2):
                    copy_a(u - a_out.shape[0], side).wait_send()

            slot = u % a_out.shape[0]
            a_out[slot, 0, 0] = part(u, at_x, first).astype(BF)
            a_out[slot, 0, 1] = part(u, at_far, first).astype(BF)
            copy_a(u, 0).start()
            a_out[slot, 1, 0] = part(u, at_y, second).astype(BF)
            a_out[slot, 1, 1] = part(u, at_far, second).astype(BF)
            copy_a(u, 1).start()

        u1, when = stage(1)

        @when
        def _():
            u = u1
            slot = u % b_out.shape[0]

            @pl.when(u >= b_out.shape[0])
            def _():
                for side in range(2):
                    copy_b(u - b_out.shape[0], side).wait_send()

            copy_a(u, 0).wait_recv()
            b_out[slot, 0] = (part(u, at_y, first) + a_in[u, 0, 1].astype(F32)).astype(BF)
            copy_b(u, 0).start()
            copy_a(u, 1).wait_recv()
            b_out[slot, 1] = (part(u, at_x, second) + a_in[u, 1, 1].astype(F32)).astype(BF)
            copy_b(u, 1).start()

        u2, when = stage(2)

        @when
        def _():
            u = u2
            copy_b(u, 0).wait_recv()
            copy_b(u, 1).wait_recv()
            for side, columns in enumerate((first, second)):
                total = part(u, place, columns) + a_in[u, side, 0].astype(F32)
                sums[u % 2, :, columns] = total + b_in[u, side].astype(F32)

            @pl.when(outer)
            def _():
                z_out[u] = sums[u % 2].astype(BF)
                copy_in(u).start()

        u3, when = stage(3, inner)

        @when
        def _():
            u = u3
            copy_in(u).wait_recv()
            z_out[u] = (sums[u % 2] + z_one[u].astype(F32)).astype(BF)
            copy_across(u).start()

        u4, when = stage(4, inner)

        @when
        def _():
            u = u4
            copy_across(u).wait_recv()
            out_ref[u] = (z_out[u].astype(F32) + z_two[u].astype(F32)).astype(BF)
            copy_out(u).start()

        u5, when = stage(6, outer)

        @when
        def _():
            u = u5
            copy_out(u).wait_recv()
            out_ref[u] = z_one[u]

        for number, device in enumerate((partner, x_side, y_side)):

            @pl.when(i == number)
            def _():
                if number == 0:
                    v_out[0] = vec_ref[...]
                else:
                    copy_v(number - 1, (partner, x_side, y_side)[number - 1]).wait_recv()
                    v_out[number] = v_out[number - 1] + v_in[number - 1]
                copy_v(number, device).start()

        @pl.when(i == 3)
        def _():
            copy_v(2, y_side).wait_recv()
            v_out[3] = v_out[2] + v_in[2]

            @pl.when(outer)
            def _():
                copy_v(3, inward).start()

        @pl.when((i == 4) & inner)
        def _():
            copy_v(3, inward).wait_recv()
            v_out[4] = v_out[3] + v_in[3]
            copy_v(4, across).start()

        @pl.when((i == 5) & inner)
        def _():
            copy_v(4, across).wait_recv()
            v_out[5] = v_out[4] + v_in[4]
            copy_v(5, outward).start()
            vec_out[...] = v_out[5]

        @pl.when((i == 7) & outer)
        def _():
            copy_v(5, outward).wait_recv()
            vec_out[...] = v_in[5]

        return 0

    lax.fori_loop(0, count + 6, step, 0)

    for u in range(count - a_out.shape[0], count):
        for side in range(2):
            copy_a(u, side).wait_send()
    for u in range(count - b_out.shape[0], count):
        for side in range(2):
            copy_b(u, side).wait_send()
    for number, device in enumerate((partner, x_side, y_side)):
        copy_v(number, device).wait_send()

    @pl.when(outer)
    def _():
        copy_v(3, inward).wait_send()

        def drain(u, _):
            copy_in(u).wait_send()
            return 0

        lax.fori_loop(0, count, drain, 0)

    @pl.when(inner)
    def _():
        copy_v(4, across).wait_send()
        copy_v(5, outward).wait_send()

        def drain(u, _):
            copy_across(u).wait_send()
            copy_out(u).wait_send()
            return 0

        lax.fori_loop(0, count, drain, 0)


def sum_products(units, lefts, rights, vec):
    count, depth = len(units), rights[0].shape[0]
    lefts = [a.reshape(4, 2, a.shape[0] // 8, depth) for a in lefts]
    slots = 3
    dma = pltpu.SemaphoreType.DMA
    return pl.pallas_call(
        partial(sum_kernel, units),
        out_shape=(
            jax.ShapeDtypeStruct((count, ROWS, UNIT), BF),
            jax.ShapeDtypeStruct(vec.shape, F32),
        ),
        in_specs=[pl.BlockSpec(memory_space=pltpu.VMEM)]
        + [pl.BlockSpec(memory_space=pl.ANY)] * (len(lefts) + len(rights)),
        out_specs=(
            pl.BlockSpec(memory_space=pltpu.VMEM),
            pl.BlockSpec(memory_space=pltpu.VMEM),
        ),
        scratch_shapes=[
            pltpu.VMEM((count, 4, ROWS, depth), BF),
            pltpu.VMEM((count, 4, ROWS, depth), BF),
            pltpu.VMEM((count, depth, UNIT), BF),
            pltpu.VMEM((count, depth, UNIT), BF),
            pltpu.VMEM((slots, 2, 2, ROWS, HALF), BF),
            pltpu.VMEM((count, 2, 2, ROWS, HALF), BF),
            pltpu.VMEM((slots, 2, ROWS, HALF), BF),
            pltpu.VMEM((count, 2, ROWS, HALF), BF),
            pltpu.VMEM((2, ROWS, UNIT), F32),
            pltpu.VMEM((count, ROWS, UNIT), BF),
            pltpu.VMEM((count, ROWS, UNIT), BF),
            pltpu.VMEM((count, ROWS, UNIT), BF),
            pltpu.VMEM((6, *vec.shape), F32),
            pltpu.VMEM((6, *vec.shape), F32),
            dma((count, 2)),
            dma((count, 2)),
            dma((count, 2)),
            dma((slots, 2)),
            dma((count, 2)),
            dma((slots, 2)),
            dma((count, 2)),
            dma((count, 2)),
            dma((count, 2)),
            dma((6,)),
            dma((6,)),
        ],
        compiler_params=pltpu.CompilerParams(
            collective_id=0, has_side_effects=True, vmem_limit_bytes=58 * 2**20
        ),
        cost_estimate=pl.CostEstimate(
            flops=8 * 2 * count * ROWS * UNIT * depth,
            bytes_accessed=300 * 2**20,
            transcendentals=0,
        ),
    )(vec, *lefts, *rights)


def block_forward(h, weights, gains, bias, heads, skip):
    wqkv, wout, wup, wdown = weights
    width = h.shape[1]
    normed_a = layer_norm(h, gains[0]).astype(BF)
    query = matmul(normed_a[skip:], wqkv[:, :width]).astype(BF)
    keys = matmul(normed_a, wqkv[:, width : 2 * width]).astype(BF)
    values = matmul(normed_a, wqkv[:, 2 * width :]).astype(BF)
    mixed_t, lse = attend(query.T, keys, values.T, bias, width // heads)
    middle = h[skip:] + left_t(mixed_t, wout)
    normed_b = layer_norm(middle, gains[1]).astype(BF)
    before = matmul(normed_b, wup)
    hidden = jax.nn.gelu(before, approximate=False).astype(BF)
    end = middle + matmul(hidden, wdown)
    return end, (h, normed_a, query, keys, values, mixed_t, lse, middle, normed_b, before, hidden)


def block_backward(saved, grad, weights, gains, bias, heads, skip):
    wqkv, wout, wup, wdown = weights
    h, normed_a, query, keys, values, mixed_t, lse, middle, normed_b, before, hidden = saved
    width = h.shape[1]
    dbranch = grad.astype(BF)
    after, gelu_pull = jax.vjp(partial(jax.nn.gelu, approximate=False), before)
    dbefore = gelu_pull(right_t(dbranch, wdown))[0].astype(BF)
    dmiddle, dgain_two = norm_back(middle, gains[1], right_t(dbefore, wup))
    dmiddle = dmiddle + grad
    dattn = dmiddle.astype(BF)
    dmixed = right_t(dattn, wout).astype(BF)
    dqt, dkeys, dvalues = attend_back(query, keys, values, dmixed, bias, lse, width // heads)
    dquery = dqt.T
    if skip:
        dquery = jnp.pad(dquery, ((skip, 0), (0, 0)))
        dmiddle = jnp.pad(dmiddle, ((skip, 0), (0, 0)))
    dqkv = jnp.concatenate([dquery, dkeys, dvalues], 1)
    dh, dgain_one = norm_back(h, gains[0], right_t(dqkv, wqkv))
    factors = ((normed_a.T, dqkv), (mixed_t, dattn), (normed_b.T, dbefore), (hidden.T, dbranch))
    return (dh + dmiddle, factors, (dgain_one, dgain_two))


def reduce_rows(grad):
    return lax.psum_scatter(grad.astype(BF), "fsdp", scatter_dimension=0, tiled=True)


def sum_encoder(factors, encoded, dseen, inputs, dh_low, vector_grad, local_loss):
    lefts = [pair[0] for pair in factors] + [encoded.T]
    owners = lax.axis_size("fsdp")
    first = inputs.T.reshape(owners, PD // owners, VIS)
    lefts.append(jnp.pad(first, ((0, 0), (0, ROWS - PD // owners), (0, 0))).reshape(-1, VIS))
    rights = [pair[1] for pair in factors] + [jnp.pad(dseen, ((0, 0), (0, UNIT - DD))), dh_low]
    units = [(2, 0, 2, UNIT * n) for n in range(FF // UNIT)]
    units += [(3, n, 3, 0) for n in range(FF // owners // ROWS)]
    units += [(0, 0, 0, UNIT * n) for n in range(3 * D // UNIT)]
    units += [(1, 0, 1, 0), (4, 0, 4, 0), (5, 0, 5, 0)]
    length = vector_grad.shape[0]
    rows = -(-(length + 1) // (8 * LANES)) * 8
    vec = jnp.concatenate(
        [vector_grad, local_loss[None], jnp.zeros((rows * LANES - length - 1,), F32)]
    )
    grads, vec = sum_products(tuple(units), lefts, rights, vec.reshape(rows, LANES))
    vec = vec.reshape(-1)
    up, down, qkv = grads[:4], grads[4:8], grads[8:11]
    wide = jnp.concatenate([*qkv, grads[11], *up, grads[12][:, :DD]], 1)
    parts = (grads[13][: PD // owners], wide, down.reshape(-1, D))
    return parts, vec[:length], vec[length]


def enc_split(wide, down):
    return (
        (wide[:, : 3 * D], wide[:, 3 * D : 4 * D], wide[:, 4 * D : 4 * D + FF], down),
        wide[:, 4 * D + FF :],
    )


def dec_split(wide, down):
    return (
        (wide[:, : 3 * DD], wide[:, 3 * DD : 4 * DD], wide[:, 4 * DD : 4 * DD + DFF], down),
        wide[:, 4 * DD + DFF :],
    )


def advance(weight, mom, avg, grad, rate):
    grad = grad + DECAY * weight
    buf = MOMENTUM * mom + grad
    new = weight - rate * (grad + MOMENTUM * buf)
    return (buf, new, AVERAGE * avg + (1.0 - AVERAGE) * new)


def arrange(valid, masked, scene_ids):
    slots = valid.shape[0]
    live = valid > 0
    kinds = jnp.stack([live & (masked == 0), live & (masked > 0), ~live], 1)
    index = jnp.arange(slots, dtype=jnp.int32)
    ranks = matmul((index[None, :] < index[:, None]).astype(BF), kinds.astype(BF)).astype(jnp.int32)
    n_seen, n_hid = [jnp.sum(kinds[:, i].astype(jnp.int32)) for i in range(2)]
    empty = ranks[:, 2]
    to_empty = jnp.where(empty < VIS - n_seen, n_seen + empty, n_seen + n_hid + empty)
    place = jnp.where(
        kinds[:, 0], ranks[:, 0], jnp.where(kinds[:, 1], VIS + ranks[:, 1], to_empty)
    )
    return (place[None, :] == index[:, None]).astype(BF), n_seen, n_hid


def exact_pick(pick, array):
    high = lax.reduce_precision(array, 8, 7)
    rest = array - high
    mid = lax.reduce_precision(rest, 8, 7)
    low = rest - mid
    return (
        matmul(pick, high.astype(BF)) + matmul(pick, mid.astype(BF)) + matmul(pick, low.astype(BF))
    )


def body(
    pixels,
    masked,
    valid,
    scene_ids,
    gsd_index,
    coords,
    embed,
    wide_enc,
    enc_down,
    wide_dec,
    dec_down,
    vectors,
    embed_mom,
    wide_enc_mom,
    enc_down_mom,
    wide_dec_mom,
    dec_down_mom,
    vector_mom,
    embed_avg,
    wide_enc_avg,
    enc_down_avg,
    wide_dec_avg,
    dec_down_avg,
    vector_avg,
):
    slots = pixels.shape[0]
    w_embed, w_enc, w_enc_down, w_dec, w_dec_down = [
        lax.all_gather(w.astype(BF), "fsdp", axis=0, tiled=True)
        for w in (embed, wide_enc, enc_down, wide_dec, dec_down)
    ]
    enc_weights, w_link = enc_split(w_enc, w_enc_down)
    dec_weights, w_head = dec_split(w_dec, w_dec_down)
    rows_ok = valid.astype(jnp.float32)
    flags = rows_ok * masked.astype(jnp.float32)
    bands = pixels.reshape(slots, BANDS, PATCH * PATCH)
    weighted = bands * rows_ok[:, None, None]
    band_sum = jnp.sum(weighted, axis=(0, 2))
    counts = jnp.stack([jnp.sum(rows_ok), jnp.sum(flags)])
    band_sq = jnp.sum(weighted * bands, axis=(0, 2))
    stats = lax.psum(jnp.concatenate([band_sum, band_sq, counts]), ("dp", "fsdp"))
    band_sum, band_sq, counts = stats[:3], stats[3:6], stats[6:]
    n_pix = counts[0] * (PATCH * PATCH)
    mean = band_sum / n_pix
    var = band_sq / n_pix - mean * mean
    count = counts[1]

    pick, n_seen, n_hid = arrange(valid, masked, scene_ids)
    picked_pixels = exact_pick(pick, pixels)
    small = matmul(
        pick, jnp.concatenate([(scene_ids % 2)[:, None], coords], 1).astype(BF)
    )
    odd, coord = small[:, 0], small[:, 1:]
    cent = picked_pixels.reshape(slots, BANDS, PATCH * PATCH) - mean[None, :, None]
    normed = (cent * lax.rsqrt(var + EPS)[None, :, None]).reshape(slots, PD)
    level = jnp.where(odd == 0, gsd_index[0], gsd_index[1]).astype(jnp.float32)
    scale = jnp.exp2(0.5 * level - 1.0)
    index = jnp.arange(slots, dtype=jnp.int32)
    kept = index[:VIS] < n_seen
    hidden_ok = index[:HID] < n_hid
    live = jnp.concatenate([kept, hidden_ok])
    keptf = kept.astype(jnp.float32)[:, None]
    allow = live[:, None] & (odd[:, None] == odd[None, :]) | (index[:, None] == index[None, :])
    bias = jnp.where(allow, 0.0, NEGATIVE)
    bias_enc, bias_dec = bias[:VIS, :VIS], bias[:, VIS:]

    gains_enc = (vectors[:D], vectors[D : 2 * D])
    gain_enc_out = vectors[2 * D : 3 * D]
    base = 3 * D
    gains_dec = (vectors[base : base + DD], vectors[base + DD : base + 2 * DD])
    gain_dec_out = vectors[base + 2 * DD : base + 3 * DD]
    token = vectors[base + 3 * DD :]

    inputs = normed[:VIS].astype(BF)
    h_start = matmul(inputs, w_embed) + positions(coord[:VIS], scale[:VIS], D)
    h_end, enc_saved = block_forward(h_start, enc_weights, gains_enc, bias_enc, HEADS, 0)
    encoded = layer_norm(h_end, gain_enc_out).astype(BF)
    seen_out = matmul(encoded, w_link)
    y_start = positions(coord, scale, DD) + jnp.concatenate(
        [jnp.where(kept[:, None], seen_out, token), jnp.broadcast_to(token, (HID, DD))]
    )
    y_end, dec_saved = block_forward(y_start, dec_weights, gains_dec, bias_dec, DHEADS, VIS)
    decoded = layer_norm(y_end, gain_dec_out).astype(BF)
    pred = matmul(decoded, w_head)
    flag = hidden_ok.astype(jnp.float32)
    losses, loss_pull = jax.vjp(lambda values: row_loss(values, normed[VIS:]), pred)
    local_loss = jnp.sum(flag * losses)
    dpred = loss_pull(flag / count)[0].astype(BF)
    dy_end, dgain_dec_out = norm_back(y_end, gain_dec_out, right_t(dpred, w_head))
    dy_start, dec_factors, dgains_dec = block_backward(
        dec_saved, dy_end, dec_weights, gains_dec, bias_dec, DHEADS, VIS
    )
    dec_grads = [matmul(*pair).astype(BF) for pair in dec_factors]
    head_grad = left_t(decoded, dpred).astype(BF)
    wide_dec_grad = jnp.concatenate([dec_grads[0], dec_grads[1], dec_grads[2], head_grad], 1)
    dec_parts = (wide_dec_grad, dec_grads[3])
    dy_start, dec_parts = lax.optimization_barrier((dy_start, dec_parts))
    dec_parts = lax.psum(tuple(reduce_rows(g) for g in dec_parts), "dp")
    picked = dy_start[:VIS] * keptf
    dtoken = jnp.sum(dy_start, 0) - jnp.sum(picked, 0)
    dseen = picked.astype(BF)
    dh_end, dgain_enc_out = norm_back(h_end, gain_enc_out, right_t(dseen, w_link))
    dh_start, enc_factors, dgains_enc = block_backward(
        enc_saved, dh_end, enc_weights, gains_enc, bias_enc, HEADS, 0
    )
    dh_low = dh_start.astype(BF)
    vector_grad = jnp.concatenate(
        [
            dgains_enc[0],
            dgains_enc[1],
            dgain_enc_out,
            dgains_dec[0],
            dgains_dec[1],
            dgain_dec_out,
            dtoken,
        ]
    )
    if (lax.axis_size("dp"), lax.axis_size("fsdp")) == (4, 8):
        enc_parts, vector_grad, loss_sum = sum_encoder(
            enc_factors, encoded, dseen, inputs, dh_low, vector_grad, local_loss
        )
    else:
        enc_grads = [matmul(*pair).astype(BF) for pair in enc_factors]
        link_grad = left_t(encoded, dseen).astype(BF)
        enc_parts = lax.psum(
            (
                reduce_rows(left_t(inputs, dh_low)),
                reduce_rows(
                    jnp.concatenate([enc_grads[0], enc_grads[1], enc_grads[2], link_grad], 1)
                ),
                reduce_rows(enc_grads[3]),
            ),
            "dp",
        )
        vector_grad, loss_sum = lax.psum((vector_grad, local_loss), ("dp", "fsdp"))
    shard_grads = [g.astype(F32) for g in (*enc_parts, *dec_parts)]
    rate = STEP_UNIT * (PD * TOK_DEV * lax.axis_size("dp") * lax.axis_size("fsdp")) ** 0.5
    weights = (embed, wide_enc, enc_down, wide_dec, dec_down)
    moms = (embed_mom, wide_enc_mom, enc_down_mom, wide_dec_mom, dec_down_mom)
    avgs = (embed_avg, wide_enc_avg, enc_down_avg, wide_dec_avg, dec_down_avg)
    outs = []
    for number in range(5):
        buf, new, avg = advance(
            weights[number], moms[number], avgs[number], shard_grads[number], rate
        )
        outs += [buf, new, avg, new.astype(jnp.bfloat16)]
    return (*outs, *advance(vectors, vector_mom, vector_avg, vector_grad, rate), loss_sum, count)


def solution(mesh):
    both, rows = P(("dp", "fsdp")), P("fsdp", None)
    placed = (P(("dp", "fsdp"), None), both, both, both, both, P(("dp", "fsdp"), None))
    states = (rows,) * 5 + (P(),)
    return jax.shard_map(
        body,
        mesh=mesh,
        in_specs=placed + states * 3,
        out_specs=(rows,) * 20 + (P(),) * 5,
        check_vma=False,
    )
```

```python
from functools import partial

import jax
import jax.numpy as jnp
from jax import lax
from jax.experimental import pallas as pl
from jax.experimental.pallas import tpu as pltpu
from jax.sharding import PartitionSpec as P

D = 1024
HEADS = 16
FF = 4096
DD = 512
DHEADS = 16
DFF = 2048
PATCH = 16
BANDS = 3
TOK_DEV = 768
PD = 768
LOWD = 192
VIS = 192
HID = TOK_DEV - VIS

EPS = 1e-06
MOMENTUM = 0.9
DECAY = 0.0001
AVERAGE = 0.9
STEP_UNIT = 0.003
NEGATIVE = -1e30
LANES = 128
BF = jnp.bfloat16
F32 = jnp.float32


def matmul(left, right):
    return jnp.dot(left, right, preferred_element_type=jnp.float32)


def left_t(left, right):
    return lax.dot_general(
        left, right, (((0,), (0,)), ((), ())), preferred_element_type=jnp.float32
    )


def right_t(left, right):
    return lax.dot_general(
        left, right, (((1,), (1,)), ((), ())), preferred_element_type=jnp.float32
    )


def layer_norm(h, gain):
    mean = jnp.mean(h, -1, keepdims=True)
    cent = h - mean
    var = jnp.mean(cent * cent, -1, keepdims=True)
    return cent * lax.rsqrt(var + EPS) * gain


def norm_back(h, gain, grad):
    result, pull = jax.vjp(layer_norm, h, gain)
    return pull(grad)


def positions(coord, scale, width):
    quarter = width // 4
    omega = 10000.0 ** (-jnp.arange(quarter, dtype=jnp.float32) / quarter)
    angle_x = coord[:, 0:1] * scale[:, None] * omega[None, :]
    angle_y = coord[:, 1:2] * scale[:, None] * omega[None, :]
    return jnp.concatenate(
        [jnp.sin(angle_x), jnp.cos(angle_x), jnp.sin(angle_y), jnp.cos(angle_y)], -1
    )


def row_loss(pred, normed):
    rows = normed.shape[0]
    coarse = jnp.mean(normed.reshape(rows, BANDS, PATCH // 2, 2, PATCH // 2, 2), axis=(3, 5))
    upper = jnp.repeat(jnp.repeat(coarse, 2, axis=2), 2, axis=3).reshape(rows, PD)
    err_high = pred[:, :PD] - (normed - upper)
    err_low = pred[:, PD:] - coarse.reshape(rows, LOWD)
    return jnp.mean(jnp.sqrt(err_high * err_high + 1.0) - 1.0, -1) + jnp.mean(err_low * err_low, -1)


def attend_kernel(size, qt_ref, k_ref, vt_ref, bias_ref, ot_ref, lse_ref):
    per = LANES // size
    row_head = lax.broadcasted_iota(jnp.int32, qt_ref.shape, 0) // size
    factor = size ** (-0.5)
    for j in range(per):
        query = jnp.where(row_head == j, qt_ref[...].astype(F32), 0.0).astype(BF)
        scores = matmul(k_ref[...], query) * factor + bias_ref[...]
        top = jnp.max(scores, 0, keepdims=True)
        probs = jnp.exp(scores - top)
        total = jnp.sum(probs, 0, keepdims=True)
        probs = (probs * (1.0 / total)).astype(BF)
        rows = slice(j * size, (j + 1) * size)
        ot_ref[rows, :] = matmul(vt_ref[rows, :], probs).astype(BF)
        lse_ref[0, j : j + 1, :] = top + jnp.log(total)


def attend(qt, keys, vt, bias, size):
    width, queries = qt.shape
    rows = keys.shape[0]
    groups, per = width // LANES, LANES // size
    return pl.pallas_call(
        partial(attend_kernel, size),
        grid=(groups,),
        out_shape=(
            jax.ShapeDtypeStruct((width, queries), BF),
            jax.ShapeDtypeStruct((groups, per, queries), F32),
        ),
        in_specs=[
            pl.BlockSpec((LANES, queries), lambda g: (g, 0)),
            pl.BlockSpec((rows, LANES), lambda g: (0, g)),
            pl.BlockSpec((LANES, rows), lambda g: (g, 0)),
            pl.BlockSpec((rows, queries), lambda g: (0, 0)),
        ],
        out_specs=(
            pl.BlockSpec((LANES, queries), lambda g: (g, 0)),
            pl.BlockSpec((1, per, queries), lambda g: (g, 0, 0)),
        ),
        compiler_params=pltpu.CompilerParams(vmem_limit_bytes=40 * 2**20),
        cost_estimate=pl.CostEstimate(
            flops=4 * rows * queries * width * per,
            bytes_accessed=4 * rows * queries,
            transcendentals=rows * queries * width // size,
        ),
    )(qt, keys, vt, bias)


def attend_back_kernel(
    size,
    qt_ref,
    q_ref,
    k_ref,
    kt_ref,
    v_ref,
    do_ref,
    dot_ref,
    bias_ref,
    lse_ref,
    dqt_ref,
    dk_ref,
    dv_ref,
):
    per = LANES // size
    row_head = lax.broadcasted_iota(jnp.int32, qt_ref.shape, 0) // size
    lane_head = lax.broadcasted_iota(jnp.int32, dk_ref.shape, 1) // size
    factor = size ** (-0.5)
    dkeys = jnp.zeros(dk_ref.shape, F32)
    dvalues = jnp.zeros(dv_ref.shape, F32)
    for j in range(per):
        query = jnp.where(row_head == j, qt_ref[...].astype(F32), 0.0).astype(BF)
        dout = jnp.where(row_head == j, dot_ref[...].astype(F32), 0.0).astype(BF)
        scores = matmul(k_ref[...], query) * factor + bias_ref[...]
        probs = jnp.exp(scores - lse_ref[0, j : j + 1, :])
        dvalues = jnp.where(lane_head == j, matmul(probs.astype(BF), do_ref[...]), dvalues)
        dprobs = matmul(v_ref[...], dout)
        delta = jnp.sum(dprobs * probs, 0, keepdims=True)
        dscores = (probs * (dprobs - delta)).astype(BF)
        dkeys = jnp.where(lane_head == j, matmul(dscores, q_ref[...]), dkeys)
        rows = slice(j * size, (j + 1) * size)
        dqt_ref[rows, :] = (matmul(kt_ref[rows, :], dscores) * factor).astype(BF)
    dk_ref[...] = (dkeys * factor).astype(BF)
    dv_ref[...] = dvalues.astype(BF)


def attend_back(query, keys, values, dmixed, bias, lse, size):
    queries, width = query.shape
    rows = keys.shape[0]
    groups, per = width // LANES, LANES // size
    tall = lambda n: pl.BlockSpec((n, LANES), lambda g: (0, g))
    flat = lambda n: pl.BlockSpec((LANES, n), lambda g: (g, 0))
    return pl.pallas_call(
        partial(attend_back_kernel, size),
        grid=(groups,),
        out_shape=(
            jax.ShapeDtypeStruct((width, queries), BF),
            jax.ShapeDtypeStruct((rows, width), BF),
            jax.ShapeDtypeStruct((rows, width), BF),
        ),
        in_specs=[
            flat(queries),
            tall(queries),
            tall(rows),
            flat(rows),
            tall(rows),
            tall(queries),
            flat(queries),
            pl.BlockSpec((rows, queries), lambda g: (0, 0)),
            pl.BlockSpec((1, per, queries), lambda g: (g, 0, 0)),
        ],
        out_specs=(flat(queries), tall(rows), tall(rows)),
        compiler_params=pltpu.CompilerParams(vmem_limit_bytes=48 * 2**20),
        cost_estimate=pl.CostEstimate(
            flops=10 * rows * queries * width * per,
            bytes_accessed=4 * rows * queries,
            transcendentals=rows * queries * width // size,
        ),
    )(query.T, query, keys, keys.T, values, dmixed, dmixed.T, bias, lse)


MESH = pl.DeviceIdType.MESH
UNIT = 512
HALF = UNIT // 2
ROWS = 128
HALF_ROWS = ROWS // 2
LAGS = (2, 4, 6, 8, 11)


def put(source, target, send, recv, device):
    return pltpu.make_async_remote_copy(
        src_ref=source,
        dst_ref=target,
        send_sem=send,
        recv_sem=recv,
        device_id=device,
        device_id_type=MESH,
    )


def sum_kernel(blocks, units, spots, vec_ref, dec_ref, *refs):
    n_left = max(b[0] for b in blocks) + 1
    n_right = max(u[1] for u in units) + 1
    lefts, rights = refs[:n_left], refs[n_left : n_left + n_right]
    outs = refs[n_left + n_right : n_left + n_right + 3]
    dec_out, vec_out = refs[n_left + n_right + 3 : n_left + n_right + 5]
    (
        xo,
        xp,
        yo,
        yp,
        a_out,
        a_in,
        b_out,
        b_in,
        sums,
        z_out,
        z_one,
        z_two,
        v_in,
        v_out,
        left_sem,
        right_sem,
        a_send,
        a_recv,
        b_send,
        b_recv,
        z_send,
        z_recv,
        v_send,
        v_recv,
        store_sem,
    ) = refs[n_left + n_right + 5 :]
    count = len(units)
    extra = z_one.shape[0] - count
    z, f = lax.axis_index("dp"), lax.axis_index("fsdp")
    core, place = f % 2, f // 2
    x, y = place % 2, place // 2
    partner = (z, f + 1 - 2 * core)
    x_side = (z, f + 2 - 4 * x)
    y_side = (z, f + 4 - 8 * y)
    at_x, at_y, at_far = place + 1 - 2 * x, place + 2 - 4 * y, 3 - place
    low = z < 2
    outer = (z == 0) | (z == 3)
    inner = (z == 1) | (z == 2)
    inward = (jnp.where(low, 1, 2), f)
    across = (3 - z, f)
    outward = (jnp.where(low, 0, 3), f)

    barrier = pltpu.get_barrier_semaphore()
    for device in (partner, x_side, y_side):
        pl.semaphore_signal(barrier, inc=1, device_id=device, device_id_type=MESH)

    @pl.when(outer)
    def _():
        pl.semaphore_signal(barrier, inc=1, device_id=inward, device_id_type=MESH)
        pl.semaphore_wait(barrier, 4)

    @pl.when(inner)
    def _():
        pl.semaphore_signal(barrier, inc=1, device_id=across, device_id_type=MESH)
        pl.semaphore_signal(barrier, inc=1, device_id=outward, device_id_type=MESH)
        pl.semaphore_wait(barrier, 5)

    def swap_left(source, b):
        return put(source, xp.at[b], left_sem.at[b, 1], left_sem.at[b, 2], partner)

    def swap_right(source, u):
        return put(source, yp.at[u], right_sem.at[u, 1], right_sem.at[u, 2], partner)

    for number, (block, right, column) in enumerate(units):
        if number == 0 or block != units[number - 1][0]:
            left, sub = blocks[block]
            rows = pl.ds(sub * ROWS, ROWS)
            swap_left(lefts[left].at[:, 1 - core, rows], block).start()
            pltpu.make_async_copy(
                lefts[left].at[:, core, rows], xo.at[block], left_sem.at[block, 0]
            ).start()
        piece = rights[right].at[:, pl.ds(column, UNIT)]
        swap_right(piece, number).start()
        pltpu.make_async_copy(piece, yo.at[number], right_sem.at[number, 0]).start()

    starts = [n for n in range(1, count) if units[n][0] != units[n - 1][0]]

    def block_of(u):
        return sum([jnp.where(u >= n, 1, 0) for n in starts], jnp.int32(0))

    first, second = pl.ds(0, HALF), pl.ds(HALF, HALF)

    def part(u, owner, columns):
        b = block_of(u)
        return matmul(xo[b, owner], yo[u, :, columns]) + matmul(xp[b, owner], yp[u, :, columns])

    def copy_a(u, side):
        slot = u % a_out.shape[0]
        return put(
            a_out.at[slot, side],
            a_in.at[u, side],
            a_send.at[slot, side],
            a_recv.at[u, side],
            (x_side, y_side)[side],
        )

    def copy_b(u, side):
        slot = u % b_out.shape[0]
        return put(
            b_out.at[slot, side],
            b_in.at[u, side],
            b_send.at[slot, side],
            b_recv.at[u, side],
            (y_side, x_side)[side],
        )

    def copy_in(u):
        return put(z_out.at[u], z_one.at[u], z_send.at[u, 0], z_recv.at[u, 0], inward)

    def copy_across(u):
        return put(z_out.at[u], z_two.at[u], z_send.at[u, 0], z_recv.at[u, 1], across)

    def copy_out(u):
        return put(z_one.at[u], z_one.at[u], z_send.at[u, 1], z_recv.at[u, 0], outward)

    def copy_v(step, device):
        return put(v_out.at[step], v_in.at[step], v_send.at[step], v_recv.at[step], device)

    def ready(n):
        halves = [
            dec_ref[:, pl.ds(pl.multiple_of((2 * n + part) * UNIT, UNIT), UNIT)] for part in range(2)
        ]
        return jnp.concatenate(halves, 0).astype(F32)

    def send_in(u, value):
        z_out[u] = value.astype(BF)
        copy_in(u).start()

    def add_in(u, value):
        copy_in(u).wait_recv()
        z_out[u] = (value + z_one[u].astype(F32)).astype(BF)
        copy_across(u).start()

    def add_across(u):
        copy_across(u).wait_recv()
        z_one[u] = (z_out[u].astype(F32) + z_two[u].astype(F32)).astype(BF)
        copy_out(u).start()

    def take(u):
        copy_out(u).wait_recv()

    def step(i, _):
        def stage(lag, also=None):
            u = i - lag
            ok = (u >= 0) & (u < count)
            if also is not None:
                ok = ok & also
            return u, pl.when(ok)

        u0, when = stage(0)

        @when
        def _():
            u = u0
            b = block_of(u)

            @pl.when((u == 0) | (b != block_of(u - 1)))
            def _():
                pltpu.make_async_copy(xo.at[b], xo.at[b], left_sem.at[b, 0]).wait()
                swap_left(xo.at[b], b).wait()

            pltpu.make_async_copy(yo.at[u], yo.at[u], right_sem.at[u, 0]).wait()
            swap_right(yo.at[u], u).wait()

            @pl.when(u >= a_out.shape[0])
            def _():
                for side in range(2):
                    copy_a(u - a_out.shape[0], side).wait_send()

            slot = u % a_out.shape[0]
            a_out[slot, 0, 0] = part(u, at_x, first).astype(BF)
            a_out[slot, 0, 1] = part(u, at_far, first).astype(BF)
            copy_a(u, 0).start()
            a_out[slot, 1, 0] = part(u, at_y, second).astype(BF)
            a_out[slot, 1, 1] = part(u, at_far, second).astype(BF)
            copy_a(u, 1).start()

        u1, when = stage(LAGS[0])

        @when
        def _():
            u = u1
            slot = u % b_out.shape[0]

            @pl.when(u >= b_out.shape[0])
            def _():
                for side in range(2):
                    copy_b(u - b_out.shape[0], side).wait_send()

            copy_a(u, 0).wait_recv()
            b_out[slot, 0] = (part(u, at_y, first) + a_in[u, 0, 1].astype(F32)).astype(BF)
            copy_b(u, 0).start()
            copy_a(u, 1).wait_recv()
            b_out[slot, 1] = (part(u, at_x, second) + a_in[u, 1, 1].astype(F32)).astype(BF)
            copy_b(u, 1).start()

        u2, when = stage(LAGS[1])

        @when
        def _():
            u = u2
            copy_b(u, 0).wait_recv()
            copy_b(u, 1).wait_recv()
            for side, columns in enumerate((first, second)):
                total = part(u, place, columns) + a_in[u, side, 0].astype(F32)
                sums[u % 4, :, columns] = total + b_in[u, side].astype(F32)

            @pl.when(outer)
            def _():
                send_in(u + extra, sums[u % 4])

        u3, when = stage(LAGS[2], inner)

        @when
        def _():
            add_in(u3 + extra, sums[u3 % 4])

        u4, when = stage(LAGS[3], inner)

        @when
        def _():
            add_across(u4 + extra)

        u5, when = stage(LAGS[4], outer)

        @when
        def _():
            take(u5 + extra)

        @pl.when((i < extra) & outer)
        def _():
            send_in(i, ready(i))

        one, two, three = [lag - LAGS[1] for lag in LAGS[2:]]

        @pl.when((i >= one) & (i < extra + one) & inner)
        def _():
            add_in(i - one, ready(i - one))

        @pl.when((i >= two) & (i < extra + two) & inner)
        def _():
            add_across(i - two)

        @pl.when((i >= three) & (i < extra + three) & outer)
        def _():
            take(i - three)

        for number, device in enumerate((partner, x_side, y_side)):

            @pl.when(i == number)
            def _():
                if number == 0:
                    v_out[0] = vec_ref[...]
                else:
                    copy_v(number - 1, (partner, x_side, y_side)[number - 1]).wait_recv()
                    v_out[number] = v_out[number - 1] + v_in[number - 1]
                copy_v(number, device).start()

        @pl.when(i == 3)
        def _():
            copy_v(2, y_side).wait_recv()
            v_out[3] = v_out[2] + v_in[2]

            @pl.when(outer)
            def _():
                copy_v(3, inward).start()

        @pl.when((i == 4) & inner)
        def _():
            copy_v(3, inward).wait_recv()
            v_out[4] = v_out[3] + v_in[3]
            copy_v(4, across).start()

        @pl.when((i == 5) & inner)
        def _():
            copy_v(4, across).wait_recv()
            v_out[5] = v_out[4] + v_in[4]
            copy_v(5, outward).start()
            vec_out[...] = v_out[5]

        @pl.when((i == 7) & outer)
        def _():
            copy_v(5, outward).wait_recv()
            vec_out[...] = v_in[5]

        return 0

    lax.fori_loop(0, count + LAGS[4], step, 0)

    stores = []
    for number, (out, row, rows, column, columns) in enumerate(spots):
        stores.append(
            pltpu.make_async_copy(
                z_one.at[extra + number, pl.ds(0, rows), pl.ds(0, columns)],
                outs[out].at[pl.ds(row, rows), pl.ds(column, columns)],
                store_sem.at[number],
            )
        )
    for number in range(2 * extra):
        stores.append(
            pltpu.make_async_copy(
                z_one.at[number // 2, pl.ds(number % 2 * HALF_ROWS, HALF_ROWS)],
                dec_out.at[:, pl.ds(number * UNIT, UNIT)],
                store_sem.at[count + number],
            )
        )
    for store in stores:
        store.start()
    for u in range(count - a_out.shape[0], count):
        for side in range(2):
            copy_a(u, side).wait_send()
    for u in range(count - b_out.shape[0], count):
        for side in range(2):
            copy_b(u, side).wait_send()
    for number, device in enumerate((partner, x_side, y_side)):
        copy_v(number, device).wait_send()

    for store in stores:
        store.wait()

    @pl.when(outer)
    def _():
        copy_v(3, inward).wait_send()

        def drain(u, _):
            copy_in(u).wait_send()
            return 0

        lax.fori_loop(0, count + extra, drain, 0)

    @pl.when(inner)
    def _():
        copy_v(4, across).wait_send()
        copy_v(5, outward).wait_send()

        def drain(u, _):
            copy_across(u).wait_send()
            copy_out(u).wait_send()
            return 0

        lax.fori_loop(0, count + extra, drain, 0)


def sum_products(blocks, units, spots, shapes, lefts, rights, dec, vec):
    count, depth = len(units), rights[0].shape[0]
    extra = dec.shape[1] // (2 * UNIT)
    full = count + extra
    lefts = [a.reshape(4, 2, a.shape[0] // 8, depth) for a in lefts]
    slots = 3
    dma = pltpu.SemaphoreType.DMA
    return pl.pallas_call(
        partial(sum_kernel, blocks, units, spots),
        out_shape=tuple(jax.ShapeDtypeStruct(shape, BF) for shape in (*shapes, dec.shape))
        + (jax.ShapeDtypeStruct(vec.shape, F32),),
        in_specs=[pl.BlockSpec(memory_space=pltpu.VMEM)] * 2
        + [pl.BlockSpec(memory_space=pl.ANY)] * (len(lefts) + len(rights)),
        out_specs=(pl.BlockSpec(memory_space=pl.ANY),) * (len(shapes) + 1)
        + (pl.BlockSpec(memory_space=pltpu.VMEM),),
        scratch_shapes=[
            pltpu.VMEM((len(blocks), 4, ROWS, depth), BF),
            pltpu.VMEM((len(blocks), 4, ROWS, depth), BF),
            pltpu.VMEM((count, depth, UNIT), BF),
            pltpu.VMEM((count, depth, UNIT), BF),
            pltpu.VMEM((slots, 2, 2, ROWS, HALF), BF),
            pltpu.VMEM((count, 2, 2, ROWS, HALF), BF),
            pltpu.VMEM((slots, 2, ROWS, HALF), BF),
            pltpu.VMEM((count, 2, ROWS, HALF), BF),
            pltpu.VMEM((4, ROWS, UNIT), F32),
            pltpu.VMEM((full, ROWS, UNIT), BF),
            pltpu.VMEM((full, ROWS, UNIT), BF),
            pltpu.VMEM((full, ROWS, UNIT), BF),
            pltpu.VMEM((6, *vec.shape), F32),
            pltpu.VMEM((6, *vec.shape), F32),
            dma((len(blocks), 3)),
            dma((count, 3)),
            dma((slots, 2)),
            dma((count, 2)),
            dma((slots, 2)),
            dma((count, 2)),
            dma((full, 2)),
            dma((full, 2)),
            dma((6,)),
            dma((6,)),
            dma((count + 2 * extra,)),
        ],
        compiler_params=pltpu.CompilerParams(
            collective_id=0, has_side_effects=True, vmem_limit_bytes=58 * 2**20
        ),
        cost_estimate=pl.CostEstimate(
            flops=8 * 2 * count * ROWS * UNIT * depth,
            bytes_accessed=300 * 2**20,
            transcendentals=0,
        ),
    )(vec, dec, *lefts, *rights)


def block_forward(h, weights, gains, bias, heads, skip):
    wqkv, wout, wup, wdown = weights
    width = h.shape[1]
    normed_a = layer_norm(h, gains[0]).astype(BF)
    query = matmul(normed_a[skip:], wqkv[:, :width]).astype(BF)
    keys = matmul(normed_a, wqkv[:, width : 2 * width]).astype(BF)
    values = matmul(normed_a, wqkv[:, 2 * width :]).astype(BF)
    mixed_t, lse = attend(query.T, keys, values.T, bias, width // heads)
    middle = h[skip:] + left_t(mixed_t, wout)
    normed_b = layer_norm(middle, gains[1]).astype(BF)
    before = matmul(normed_b, wup)
    hidden = jax.nn.gelu(before, approximate=False).astype(BF)
    end = middle + matmul(hidden, wdown)
    return end, (h, normed_a, query, keys, values, mixed_t, lse, middle, normed_b, before, hidden)


def block_backward(saved, grad, weights, gains, bias, heads, skip):
    wqkv, wout, wup, wdown = weights
    h, normed_a, query, keys, values, mixed_t, lse, middle, normed_b, before, hidden = saved
    width = h.shape[1]
    dbranch = grad.astype(BF)
    after, gelu_pull = jax.vjp(partial(jax.nn.gelu, approximate=False), before)
    dbefore = gelu_pull(right_t(dbranch, wdown))[0].astype(BF)
    dmiddle, dgain_two = norm_back(middle, gains[1], right_t(dbefore, wup))
    dmiddle = dmiddle + grad
    dattn = dmiddle.astype(BF)
    dmixed = right_t(dattn, wout).astype(BF)
    dqt, dkeys, dvalues = attend_back(query, keys, values, dmixed, bias, lse, width // heads)
    dquery = dqt.T
    if skip:
        dquery = jnp.pad(dquery, ((skip, 0), (0, 0)))
        dmiddle = jnp.pad(dmiddle, ((skip, 0), (0, 0)))
    dqkv = jnp.concatenate([dquery, dkeys, dvalues], 1)
    dh, dgain_one = norm_back(h, gains[0], right_t(dqkv, wqkv))
    factors = ((normed_a.T, dqkv), (mixed_t, dattn), (normed_b.T, dbefore), (hidden.T, dbranch))
    return (dh + dmiddle, factors, (dgain_one, dgain_two))


def reduce_rows(grad):
    return lax.psum_scatter(grad.astype(BF), "fsdp", scatter_dimension=0, tiled=True)


def sum_gradients(factors, encoded, dseen, inputs, dh_low, dec, vector_grad, local_loss):
    lefts = [pair[0] for pair in factors] + [encoded.T]
    owners = lax.axis_size("fsdp")
    own = PD // owners
    first = inputs.T.reshape(owners, own, VIS)
    lefts.append(jnp.pad(first, ((0, 0), (0, ROWS - own), (0, 0))).reshape(-1, VIS))
    rights = [pair[1] for pair in factors] + [dseen, dh_low]
    blocks, units, spots = [], [], []

    def add(left, sub, right, out, row, rows, column, columns):
        blocks.append((left, sub))
        for n in range(0, columns, UNIT):
            units.append((len(blocks) - 1, right, n))
            spots.append((out, row, rows, column + n, UNIT))

    add(4, 0, 4, 1, 0, ROWS, 4 * D + FF, DD)
    for n in range(FF // owners // ROWS):
        add(3, n, 3, 2, n * ROWS, ROWS, 0, D)
    add(2, 0, 2, 1, 0, ROWS, 4 * D, FF)
    add(1, 0, 1, 1, 0, ROWS, 3 * D, D)
    add(0, 0, 0, 1, 0, ROWS, 0, 3 * D)
    add(5, 0, 5, 0, 0, own, 0, D)
    shapes = ((own, D), (ROWS, 4 * D + FF + DD), (FF // owners, D))
    length = vector_grad.shape[0]
    rows = -(-(length + 1) // (8 * LANES)) * 8
    vec = jnp.concatenate(
        [vector_grad, local_loss[None], jnp.zeros((rows * LANES - length - 1,), F32)]
    )
    used = dec.shape[1]
    dec = jnp.pad(dec, ((0, 0), (0, -used % (2 * UNIT))))
    *parts, dec, vec = sum_products(
        tuple(blocks), tuple(units), tuple(spots), shapes, lefts, rights, dec, vec.reshape(rows, LANES)
    )
    vec = vec.reshape(-1)
    return parts, dec[:, :used], vec[:length], vec[length]


def enc_split(wide, down):
    return (
        (wide[:, : 3 * D], wide[:, 3 * D : 4 * D], wide[:, 4 * D : 4 * D + FF], down),
        wide[:, 4 * D + FF :],
    )


def dec_split(wide, down):
    return (
        (wide[:, : 3 * DD], wide[:, 3 * DD : 4 * DD], wide[:, 4 * DD : 4 * DD + DFF], down),
        wide[:, 4 * DD + DFF :],
    )


def advance(weight, mom, avg, grad, rate):
    grad = grad + DECAY * weight
    buf = MOMENTUM * mom + grad
    new = weight - rate * (grad + MOMENTUM * buf)
    return (buf, new, AVERAGE * avg + (1.0 - AVERAGE) * new)


def arrange(valid, masked, scene_ids):
    slots = valid.shape[0]
    live = valid > 0
    kinds = jnp.stack([live & (masked == 0), live & (masked > 0), ~live], 1)
    index = jnp.arange(slots, dtype=jnp.int32)
    ranks = matmul((index[None, :] < index[:, None]).astype(BF), kinds.astype(BF)).astype(jnp.int32)
    n_seen, n_hid = [jnp.sum(kinds[:, i].astype(jnp.int32)) for i in range(2)]
    empty = ranks[:, 2]
    to_empty = jnp.where(empty < VIS - n_seen, n_seen + empty, n_seen + n_hid + empty)
    place = jnp.where(
        kinds[:, 0], ranks[:, 0], jnp.where(kinds[:, 1], VIS + ranks[:, 1], to_empty)
    )
    return (place[None, :] == index[:, None]).astype(BF), n_seen, n_hid


def exact_pick(pick, array):
    high = lax.reduce_precision(array, 8, 7)
    rest = array - high
    mid = lax.reduce_precision(rest, 8, 7)
    low = rest - mid
    return (
        matmul(pick, high.astype(BF)) + matmul(pick, mid.astype(BF)) + matmul(pick, low.astype(BF))
    )


def body(
    pixels,
    masked,
    valid,
    scene_ids,
    gsd_index,
    coords,
    embed,
    wide_enc,
    enc_down,
    wide_dec,
    dec_down,
    vectors,
    embed_mom,
    wide_enc_mom,
    enc_down_mom,
    wide_dec_mom,
    dec_down_mom,
    vector_mom,
    embed_avg,
    wide_enc_avg,
    enc_down_avg,
    wide_dec_avg,
    dec_down_avg,
    vector_avg,
):
    slots = pixels.shape[0]
    w_embed, w_enc, w_enc_down, w_dec, w_dec_down = [
        lax.all_gather(w.astype(BF), "fsdp", axis=0, tiled=True)
        for w in (embed, wide_enc, enc_down, wide_dec, dec_down)
    ]
    enc_weights, w_link = enc_split(w_enc, w_enc_down)
    dec_weights, w_head = dec_split(w_dec, w_dec_down)
    rows_ok = valid.astype(jnp.float32)
    flags = rows_ok * masked.astype(jnp.float32)
    bands = pixels.reshape(slots, BANDS, PATCH * PATCH)
    weighted = bands * rows_ok[:, None, None]
    band_sum = jnp.sum(weighted, axis=(0, 2))
    counts = jnp.stack([jnp.sum(rows_ok), jnp.sum(flags)])
    band_sq = jnp.sum(weighted * bands, axis=(0, 2))
    stats = lax.psum(jnp.concatenate([band_sum, band_sq, counts]), ("dp", "fsdp"))
    band_sum, band_sq, counts = stats[:3], stats[3:6], stats[6:]
    n_pix = counts[0] * (PATCH * PATCH)
    mean = band_sum / n_pix
    var = band_sq / n_pix - mean * mean
    count = counts[1]

    pick, n_seen, n_hid = arrange(valid, masked, scene_ids)
    picked_pixels = exact_pick(pick, pixels)
    small = matmul(
        pick, jnp.concatenate([(scene_ids % 2)[:, None], coords], 1).astype(BF)
    )
    odd, coord = small[:, 0], small[:, 1:]
    cent = picked_pixels.reshape(slots, BANDS, PATCH * PATCH) - mean[None, :, None]
    normed = (cent * lax.rsqrt(var + EPS)[None, :, None]).reshape(slots, PD)
    level = jnp.where(odd == 0, gsd_index[0], gsd_index[1]).astype(jnp.float32)
    scale = jnp.exp2(0.5 * level - 1.0)
    index = jnp.arange(slots, dtype=jnp.int32)
    kept = index[:VIS] < n_seen
    hidden_ok = index[:HID] < n_hid
    live = jnp.concatenate([kept, hidden_ok])
    keptf = kept.astype(jnp.float32)[:, None]
    allow = live[:, None] & (odd[:, None] == odd[None, :]) | (index[:, None] == index[None, :])
    bias = jnp.where(allow, 0.0, NEGATIVE)
    bias_enc, bias_dec = bias[:VIS, :VIS], bias[:, VIS:]

    gains_enc = (vectors[:D], vectors[D : 2 * D])
    gain_enc_out = vectors[2 * D : 3 * D]
    base = 3 * D
    gains_dec = (vectors[base : base + DD], vectors[base + DD : base + 2 * DD])
    gain_dec_out = vectors[base + 2 * DD : base + 3 * DD]
    token = vectors[base + 3 * DD :]

    inputs = normed[:VIS].astype(BF)
    h_start = matmul(inputs, w_embed) + positions(coord[:VIS], scale[:VIS], D)
    h_end, enc_saved = block_forward(h_start, enc_weights, gains_enc, bias_enc, HEADS, 0)
    encoded = layer_norm(h_end, gain_enc_out).astype(BF)
    seen_out = matmul(encoded, w_link)
    y_start = positions(coord, scale, DD) + jnp.concatenate(
        [jnp.where(kept[:, None], seen_out, token), jnp.broadcast_to(token, (HID, DD))]
    )
    y_end, dec_saved = block_forward(y_start, dec_weights, gains_dec, bias_dec, DHEADS, VIS)
    decoded = layer_norm(y_end, gain_dec_out).astype(BF)
    pred = matmul(decoded, w_head)
    flag = hidden_ok.astype(jnp.float32)
    losses, loss_pull = jax.vjp(lambda values: row_loss(values, normed[VIS:]), pred)
    local_loss = jnp.sum(flag * losses)
    dpred = loss_pull(flag / count)[0].astype(BF)
    dy_end, dgain_dec_out = norm_back(y_end, gain_dec_out, right_t(dpred, w_head))
    dy_start, dec_factors, dgains_dec = block_backward(
        dec_saved, dy_end, dec_weights, gains_dec, bias_dec, DHEADS, VIS
    )
    owners = lax.axis_size("fsdp")
    dec_grads = [matmul(*pair).astype(BF) for pair in dec_factors]
    down_grad = dec_grads[3].reshape(owners, -1, DD // owners, DD)
    down_grad = down_grad.transpose(0, 2, 1, 3).reshape(DD, DFF)
    dec_grads = jnp.concatenate(
        [*dec_grads[:3], left_t(decoded, dpred).astype(BF), down_grad], 1
    )
    dy_start, dec_grads = lax.optimization_barrier((dy_start, dec_grads))
    dec_sum = reduce_rows(dec_grads)
    picked = dy_start[:VIS] * keptf
    dtoken = jnp.sum(dy_start, 0) - jnp.sum(picked, 0)
    dseen = picked.astype(BF)
    dh_end, dgain_enc_out = norm_back(h_end, gain_enc_out, right_t(dseen, w_link))
    dh_start, enc_factors, dgains_enc = block_backward(
        enc_saved, dh_end, enc_weights, gains_enc, bias_enc, HEADS, 0
    )
    dh_low = dh_start.astype(BF)
    vector_grad = jnp.concatenate(
        [
            dgains_enc[0],
            dgains_enc[1],
            dgain_enc_out,
            dgains_dec[0],
            dgains_dec[1],
            dgain_dec_out,
            dtoken,
        ]
    )
    if (lax.axis_size("dp"), lax.axis_size("fsdp")) == (4, 8):
        enc_parts, dec_sum, vector_grad, loss_sum = sum_gradients(
            enc_factors, encoded, dseen, inputs, dh_low, dec_sum, vector_grad, local_loss
        )
    else:
        enc_grads = [matmul(*pair).astype(BF) for pair in enc_factors]
        link_grad = left_t(encoded, dseen).astype(BF)
        enc_parts = lax.psum(
            (
                reduce_rows(left_t(inputs, dh_low)),
                reduce_rows(
                    jnp.concatenate([enc_grads[0], enc_grads[1], enc_grads[2], link_grad], 1)
                ),
                reduce_rows(enc_grads[3]),
            ),
            "dp",
        )
        vector_grad, loss_sum = lax.psum((vector_grad, local_loss), ("dp", "fsdp"))
        dec_sum = lax.psum(dec_sum, "dp")
    rows = dec_sum.shape[0]
    wide = wide_dec.shape[1]
    down = dec_sum[:, wide:].reshape(rows, -1, DD).transpose(1, 0, 2).reshape(-1, DD)
    dec_parts = (dec_sum[:, :wide], down)
    shard_grads = [g.astype(F32) for g in (*enc_parts, *dec_parts)]
    rate = STEP_UNIT * (PD * TOK_DEV * lax.axis_size("dp") * lax.axis_size("fsdp")) ** 0.5
    weights = (embed, wide_enc, enc_down, wide_dec, dec_down)
    moms = (embed_mom, wide_enc_mom, enc_down_mom, wide_dec_mom, dec_down_mom)
    avgs = (embed_avg, wide_enc_avg, enc_down_avg, wide_dec_avg, dec_down_avg)
    outs = []
    for number in range(5):
        buf, new, avg = advance(
            weights[number], moms[number], avgs[number], shard_grads[number], rate
        )
        outs += [buf, new, avg, new.astype(jnp.bfloat16)]
    return (*outs, *advance(vectors, vector_mom, vector_avg, vector_grad, rate), loss_sum, count)


def solution(mesh):
    both, rows = P(("dp", "fsdp")), P("fsdp", None)
    placed = (P(("dp", "fsdp"), None), both, both, both, both, P(("dp", "fsdp"), None))
    states = (rows,) * 5 + (P(),)
    return jax.shard_map(
        body,
        mesh=mesh,
        in_specs=placed + states * 3,
        out_specs=(rows,) * 20 + (P(),) * 5,
        check_vma=False,
    )
```

```python
from functools import partial

import jax
import jax.numpy as jnp
from jax import lax
from jax.experimental import pallas as pl
from jax.experimental.pallas import tpu as pltpu
from jax.sharding import PartitionSpec as P

D = 1024
HEADS = 16
FF = 4096
DD = 512
DHEADS = 16
DFF = 2048
PATCH = 16
BANDS = 3
TOK_DEV = 768
PD = 768
LOWD = 192
VIS = 192
HID = TOK_DEV - VIS

EPS = 1e-06
MOMENTUM = 0.9
DECAY = 0.0001
AVERAGE = 0.9
STEP_UNIT = 0.003
NEGATIVE = -1e30
LANES = 128
BF = jnp.bfloat16
F32 = jnp.float32


def matmul(left, right):
    return jnp.dot(left, right, preferred_element_type=jnp.float32)


def left_t(left, right):
    return lax.dot_general(
        left, right, (((0,), (0,)), ((), ())), preferred_element_type=jnp.float32
    )


def right_t(left, right):
    return lax.dot_general(
        left, right, (((1,), (1,)), ((), ())), preferred_element_type=jnp.float32
    )


def layer_norm(h, gain):
    mean = jnp.mean(h, -1, keepdims=True)
    cent = h - mean
    var = jnp.mean(cent * cent, -1, keepdims=True)
    return cent * lax.rsqrt(var + EPS) * gain


def norm_back(h, gain, grad):
    result, pull = jax.vjp(layer_norm, h, gain)
    return pull(grad)


def gelu_parts(before):
    below = 0.5 * (1.0 + lax.erf(before * 0.5**0.5))
    slope = below + before * jnp.exp(before * before * -0.5) * (0.5 / jnp.pi) ** 0.5
    return before * below, slope


def positions(coord, scale, width):
    quarter = width // 4
    omega = 10000.0 ** (-jnp.arange(quarter, dtype=jnp.float32) / quarter)
    angle_x = coord[:, 0:1] * scale[:, None] * omega[None, :]
    angle_y = coord[:, 1:2] * scale[:, None] * omega[None, :]
    return jnp.concatenate(
        [jnp.sin(angle_x), jnp.cos(angle_x), jnp.sin(angle_y), jnp.cos(angle_y)], -1
    )


def row_loss(pred, normed):
    rows = normed.shape[0]
    coarse = jnp.mean(normed.reshape(rows, BANDS, PATCH // 2, 2, PATCH // 2, 2), axis=(3, 5))
    upper = jnp.repeat(jnp.repeat(coarse, 2, axis=2), 2, axis=3).reshape(rows, PD)
    err_high = pred[:, :PD] - (normed - upper)
    err_low = pred[:, PD:] - coarse.reshape(rows, LOWD)
    return jnp.mean(jnp.sqrt(err_high * err_high + 1.0) - 1.0, -1) + jnp.mean(err_low * err_low, -1)


def attend_kernel(size, qt_ref, k_ref, vt_ref, bias_ref, ot_ref, lse_ref):
    per = LANES // size
    row_head = lax.broadcasted_iota(jnp.int32, qt_ref.shape, 0) // size
    factor = size ** (-0.5)
    for j in range(per):
        query = jnp.where(row_head == j, qt_ref[...].astype(F32), 0.0).astype(BF)
        scores = matmul(k_ref[...], query) * factor + bias_ref[...]
        top = jnp.max(scores, 0, keepdims=True)
        probs = jnp.exp(scores - top)
        total = jnp.sum(probs, 0, keepdims=True)
        probs = (probs * (1.0 / total)).astype(BF)
        rows = slice(j * size, (j + 1) * size)
        ot_ref[rows, :] = matmul(vt_ref[rows, :], probs).astype(BF)
        lse_ref[0, j : j + 1, :] = top + jnp.log(total)


def attend(qt, keys, vt, bias, size):
    width, queries = qt.shape
    rows = keys.shape[0]
    groups, per = width // LANES, LANES // size
    return pl.pallas_call(
        partial(attend_kernel, size),
        grid=(groups,),
        out_shape=(
            jax.ShapeDtypeStruct((width, queries), BF),
            jax.ShapeDtypeStruct((groups, per, queries), F32),
        ),
        in_specs=[
            pl.BlockSpec((LANES, queries), lambda g: (g, 0)),
            pl.BlockSpec((rows, LANES), lambda g: (0, g)),
            pl.BlockSpec((LANES, rows), lambda g: (g, 0)),
            pl.BlockSpec((rows, queries), lambda g: (0, 0)),
        ],
        out_specs=(
            pl.BlockSpec((LANES, queries), lambda g: (g, 0)),
            pl.BlockSpec((1, per, queries), lambda g: (g, 0, 0)),
        ),
        compiler_params=pltpu.CompilerParams(vmem_limit_bytes=40 * 2**20),
        cost_estimate=pl.CostEstimate(
            flops=4 * rows * queries * width * per,
            bytes_accessed=4 * rows * queries,
            transcendentals=rows * queries * width // size,
        ),
    )(qt, keys, vt, bias)


def attend_back_kernel(
    size,
    qt_ref,
    q_ref,
    k_ref,
    kt_ref,
    v_ref,
    do_ref,
    dot_ref,
    bias_ref,
    *rest,
):
    *lse_ref, dqt_ref, dk_ref, dv_ref = rest
    per = LANES // size
    row_head = lax.broadcasted_iota(jnp.int32, qt_ref.shape, 0) // size
    lane_head = lax.broadcasted_iota(jnp.int32, dk_ref.shape, 1) // size
    factor = size ** (-0.5)
    dkeys = jnp.zeros(dk_ref.shape, F32)
    dvalues = jnp.zeros(dv_ref.shape, F32)
    for j in range(per):
        query = jnp.where(row_head == j, qt_ref[...].astype(F32), 0.0).astype(BF)
        dout = jnp.where(row_head == j, dot_ref[...].astype(F32), 0.0).astype(BF)
        scores = matmul(k_ref[...], query) * factor + bias_ref[...]
        if lse_ref:
            probs = jnp.exp(scores - lse_ref[0][0, j : j + 1, :])
        else:
            probs = jnp.exp(scores - jnp.max(scores, 0, keepdims=True))
            probs = probs * (1.0 / jnp.sum(probs, 0, keepdims=True))
        dvalues = jnp.where(lane_head == j, matmul(probs.astype(BF), do_ref[...]), dvalues)
        dprobs = matmul(v_ref[...], dout)
        delta = jnp.sum(dprobs * probs, 0, keepdims=True)
        dscores = (probs * (dprobs - delta)).astype(BF)
        dkeys = jnp.where(lane_head == j, matmul(dscores, q_ref[...]), dkeys)
        rows = slice(j * size, (j + 1) * size)
        dqt_ref[rows, :] = (matmul(kt_ref[rows, :], dscores) * factor).astype(BF)
    dk_ref[...] = (dkeys * factor).astype(BF)
    dv_ref[...] = dvalues.astype(BF)


def attend_back(query, keys, values, dmixed, bias, lse, size):
    queries, width = query.shape
    rows = keys.shape[0]
    groups, per = width // LANES, LANES // size
    tall = lambda n: pl.BlockSpec((n, LANES), lambda g: (0, g))
    flat = lambda n: pl.BlockSpec((LANES, n), lambda g: (g, 0))
    return pl.pallas_call(
        partial(attend_back_kernel, size),
        grid=(groups,),
        out_shape=(
            jax.ShapeDtypeStruct((width, queries), BF),
            jax.ShapeDtypeStruct((rows, width), BF),
            jax.ShapeDtypeStruct((rows, width), BF),
        ),
        in_specs=[
            flat(queries),
            tall(queries),
            tall(rows),
            flat(rows),
            tall(rows),
            tall(queries),
            flat(queries),
            pl.BlockSpec((rows, queries), lambda g: (0, 0)),
        ]
        + [pl.BlockSpec((1, per, queries), lambda g: (g, 0, 0))] * (lse is not None),
        out_specs=(flat(queries), tall(rows), tall(rows)),
        compiler_params=pltpu.CompilerParams(vmem_limit_bytes=48 * 2**20),
        cost_estimate=pl.CostEstimate(
            flops=10 * rows * queries * width * per,
            bytes_accessed=4 * rows * queries,
            transcendentals=rows * queries * width // size,
        ),
    )(query.T, query, keys, keys.T, values, dmixed, dmixed.T, bias, *([] if lse is None else [lse]))


MESH = pl.DeviceIdType.MESH
UNIT = 512
HALF = UNIT // 2
ROWS = 128
HALF_ROWS = ROWS // 2
LAGS = (2, 4, 6, 8, 11)


def put(source, target, send, recv, device):
    return pltpu.make_async_remote_copy(
        src_ref=source,
        dst_ref=target,
        send_sem=send,
        recv_sem=recv,
        device_id=device,
        device_id_type=MESH,
    )


def sum_kernel(blocks, units, spots, vec_ref, dec_ref, *refs):
    n_left = max(b[0] for b in blocks) + 1
    n_right = max(u[1] for u in units) + 1
    lefts, rights = refs[:n_left], refs[n_left : n_left + n_right]
    outs = refs[n_left + n_right : n_left + n_right + 3]
    dec_out, vec_out = refs[n_left + n_right + 3 : n_left + n_right + 5]
    (
        xo,
        xp,
        yo,
        yp,
        a_out,
        a_in,
        b_out,
        b_in,
        sums,
        z_out,
        z_one,
        z_two,
        v_in,
        v_out,
        left_sem,
        right_sem,
        a_send,
        a_recv,
        b_send,
        b_recv,
        z_send,
        z_recv,
        v_send,
        v_recv,
        store_sem,
    ) = refs[n_left + n_right + 5 :]
    count = len(units)
    extra = z_one.shape[0] - count
    z, f = lax.axis_index("dp"), lax.axis_index("fsdp")
    core, place = f % 2, f // 2
    x, y = place % 2, place // 2
    partner = (z, f + 1 - 2 * core)
    x_side = (z, f + 2 - 4 * x)
    y_side = (z, f + 4 - 8 * y)
    at_x, at_y, at_far = place + 1 - 2 * x, place + 2 - 4 * y, 3 - place
    low = z < 2
    outer = (z == 0) | (z == 3)
    inner = (z == 1) | (z == 2)
    inward = (jnp.where(low, 1, 2), f)
    across = (3 - z, f)
    outward = (jnp.where(low, 0, 3), f)

    barrier = pltpu.get_barrier_semaphore()
    for device in (partner, x_side, y_side):
        pl.semaphore_signal(barrier, inc=1, device_id=device, device_id_type=MESH)

    @pl.when(outer)
    def _():
        pl.semaphore_signal(barrier, inc=1, device_id=inward, device_id_type=MESH)
        pl.semaphore_wait(barrier, 4)

    @pl.when(inner)
    def _():
        pl.semaphore_signal(barrier, inc=1, device_id=across, device_id_type=MESH)
        pl.semaphore_signal(barrier, inc=1, device_id=outward, device_id_type=MESH)
        pl.semaphore_wait(barrier, 5)

    def swap_left(source, b):
        return put(source, xp.at[b], left_sem.at[b, 1], left_sem.at[b, 2], partner)

    def swap_right(source, u):
        return put(source, yp.at[u], right_sem.at[u, 1], right_sem.at[u, 2], partner)

    for number, (block, right, column) in enumerate(units):
        if number == 0 or block != units[number - 1][0]:
            left, sub = blocks[block]
            rows = pl.ds(sub * ROWS, ROWS)
            swap_left(lefts[left].at[:, 1 - core, rows], block).start()
            pltpu.make_async_copy(
                lefts[left].at[:, core, rows], xo.at[block], left_sem.at[block, 0]
            ).start()
        piece = rights[right].at[:, pl.ds(column, UNIT)]
        swap_right(piece, number).start()
        pltpu.make_async_copy(piece, yo.at[number], right_sem.at[number, 0]).start()

    starts = [n for n in range(1, count) if units[n][0] != units[n - 1][0]]

    def block_of(u):
        return sum([jnp.where(u >= n, 1, 0) for n in starts], jnp.int32(0))

    first, second = pl.ds(0, HALF), pl.ds(HALF, HALF)

    def part(u, owner, columns):
        b = block_of(u)
        return matmul(xo[b, owner], yo[u, :, columns]) + matmul(xp[b, owner], yp[u, :, columns])

    def copy_a(u, side):
        slot = u % a_out.shape[0]
        return put(
            a_out.at[slot, side],
            a_in.at[u, side],
            a_send.at[slot, side],
            a_recv.at[u, side],
            (x_side, y_side)[side],
        )

    def copy_b(u, side):
        slot = u % b_out.shape[0]
        return put(
            b_out.at[slot, side],
            b_in.at[u, side],
            b_send.at[slot, side],
            b_recv.at[u, side],
            (y_side, x_side)[side],
        )

    def copy_in(u):
        return put(z_out.at[u], z_one.at[u], z_send.at[u, 0], z_recv.at[u, 0], inward)

    def copy_across(u):
        return put(z_out.at[u], z_two.at[u], z_send.at[u, 0], z_recv.at[u, 1], across)

    def copy_out(u):
        return put(z_one.at[u], z_one.at[u], z_send.at[u, 1], z_recv.at[u, 0], outward)

    def copy_v(step, device):
        return put(v_out.at[step], v_in.at[step], v_send.at[step], v_recv.at[step], device)

    def ready(n):
        halves = [
            dec_ref[:, pl.ds(pl.multiple_of((2 * n + part) * UNIT, UNIT), UNIT)] for part in range(2)
        ]
        return jnp.concatenate(halves, 0).astype(F32)

    def send_in(u, value):
        z_out[u] = value.astype(BF)
        copy_in(u).start()

    def add_in(u, value):
        copy_in(u).wait_recv()
        z_out[u] = (value + z_one[u].astype(F32)).astype(BF)
        copy_across(u).start()

    def add_across(u):
        copy_across(u).wait_recv()
        z_one[u] = (z_out[u].astype(F32) + z_two[u].astype(F32)).astype(BF)
        copy_out(u).start()

    def take(u):
        copy_out(u).wait_recv()

    def step(i, _):
        def stage(lag, also=None):
            u = i - lag
            ok = (u >= 0) & (u < count)
            if also is not None:
                ok = ok & also
            return u, pl.when(ok)

        u0, when = stage(0)

        @when
        def _():
            u = u0
            b = block_of(u)

            @pl.when((u == 0) | (b != block_of(u - 1)))
            def _():
                pltpu.make_async_copy(xo.at[b], xo.at[b], left_sem.at[b, 0]).wait()
                swap_left(xo.at[b], b).wait()

            pltpu.make_async_copy(yo.at[u], yo.at[u], right_sem.at[u, 0]).wait()
            swap_right(yo.at[u], u).wait()

            @pl.when(u >= a_out.shape[0])
            def _():
                for side in range(2):
                    copy_a(u - a_out.shape[0], side).wait_send()

            slot = u % a_out.shape[0]
            a_out[slot, 0, 0] = part(u, at_x, first).astype(BF)
            a_out[slot, 0, 1] = part(u, at_far, first).astype(BF)
            copy_a(u, 0).start()
            a_out[slot, 1, 0] = part(u, at_y, second).astype(BF)
            a_out[slot, 1, 1] = part(u, at_far, second).astype(BF)
            copy_a(u, 1).start()

        u1, when = stage(LAGS[0])

        @when
        def _():
            u = u1
            slot = u % b_out.shape[0]

            @pl.when(u >= b_out.shape[0])
            def _():
                for side in range(2):
                    copy_b(u - b_out.shape[0], side).wait_send()

            copy_a(u, 0).wait_recv()
            b_out[slot, 0] = (part(u, at_y, first) + a_in[u, 0, 1].astype(F32)).astype(BF)
            copy_b(u, 0).start()
            copy_a(u, 1).wait_recv()
            b_out[slot, 1] = (part(u, at_x, second) + a_in[u, 1, 1].astype(F32)).astype(BF)
            copy_b(u, 1).start()

        u2, when = stage(LAGS[1])

        @when
        def _():
            u = u2
            copy_b(u, 0).wait_recv()
            copy_b(u, 1).wait_recv()
            for side, columns in enumerate((first, second)):
                total = part(u, place, columns) + a_in[u, side, 0].astype(F32)
                sums[u % 4, :, columns] = total + b_in[u, side].astype(F32)

            @pl.when(outer)
            def _():
                send_in(u + extra, sums[u % 4])

        u3, when = stage(LAGS[2], inner)

        @when
        def _():
            add_in(u3 + extra, sums[u3 % 4])

        u4, when = stage(LAGS[3], inner)

        @when
        def _():
            add_across(u4 + extra)

        u5, when = stage(LAGS[4], outer)

        @when
        def _():
            take(u5 + extra)

        @pl.when((i < extra) & outer)
        def _():
            send_in(i, ready(i))

        one, two, three = [lag - LAGS[1] for lag in LAGS[2:]]

        @pl.when((i >= one) & (i < extra + one) & inner)
        def _():
            add_in(i - one, ready(i - one))

        @pl.when((i >= two) & (i < extra + two) & inner)
        def _():
            add_across(i - two)

        @pl.when((i >= three) & (i < extra + three) & outer)
        def _():
            take(i - three)

        for number, device in enumerate((partner, x_side, y_side)):

            @pl.when(i == number)
            def _():
                if number == 0:
                    v_out[0] = vec_ref[...]
                else:
                    copy_v(number - 1, (partner, x_side, y_side)[number - 1]).wait_recv()
                    v_out[number] = v_out[number - 1] + v_in[number - 1]
                copy_v(number, device).start()

        @pl.when(i == 3)
        def _():
            copy_v(2, y_side).wait_recv()
            v_out[3] = v_out[2] + v_in[2]

            @pl.when(outer)
            def _():
                copy_v(3, inward).start()

        @pl.when((i == 4) & inner)
        def _():
            copy_v(3, inward).wait_recv()
            v_out[4] = v_out[3] + v_in[3]
            copy_v(4, across).start()

        @pl.when((i == 5) & inner)
        def _():
            copy_v(4, across).wait_recv()
            v_out[5] = v_out[4] + v_in[4]
            copy_v(5, outward).start()
            vec_out[...] = v_out[5]

        @pl.when((i == 7) & outer)
        def _():
            copy_v(5, outward).wait_recv()
            vec_out[...] = v_in[5]

        return 0

    lax.fori_loop(0, count + LAGS[4], step, 0)

    stores = []
    for number, (out, row, rows, column, columns) in enumerate(spots):
        stores.append(
            pltpu.make_async_copy(
                z_one.at[extra + number, pl.ds(0, rows), pl.ds(0, columns)],
                outs[out].at[pl.ds(row, rows), pl.ds(column, columns)],
                store_sem.at[number],
            )
        )
    for number in range(2 * extra):
        stores.append(
            pltpu.make_async_copy(
                z_one.at[number // 2, pl.ds(number % 2 * HALF_ROWS, HALF_ROWS)],
                dec_out.at[:, pl.ds(number * UNIT, UNIT)],
                store_sem.at[count + number],
            )
        )
    for store in stores:
        store.start()
    for u in range(count - a_out.shape[0], count):
        for side in range(2):
            copy_a(u, side).wait_send()
    for u in range(count - b_out.shape[0], count):
        for side in range(2):
            copy_b(u, side).wait_send()
    for number, device in enumerate((partner, x_side, y_side)):
        copy_v(number, device).wait_send()

    for store in stores:
        store.wait()

    @pl.when(outer)
    def _():
        copy_v(3, inward).wait_send()

        def drain(u, _):
            copy_in(u).wait_send()
            return 0

        lax.fori_loop(0, count + extra, drain, 0)

    @pl.when(inner)
    def _():
        copy_v(4, across).wait_send()
        copy_v(5, outward).wait_send()

        def drain(u, _):
            copy_across(u).wait_send()
            copy_out(u).wait_send()
            return 0

        lax.fori_loop(0, count + extra, drain, 0)


def sum_products(blocks, units, spots, shapes, lefts, rights, dec, vec):
    count, depth = len(units), rights[0].shape[0]
    extra = dec.shape[1] // (2 * UNIT)
    full = count + extra
    lefts = [a.reshape(4, 2, a.shape[0] // 8, depth) for a in lefts]
    slots = 3
    dma = pltpu.SemaphoreType.DMA
    return pl.pallas_call(
        partial(sum_kernel, blocks, units, spots),
        out_shape=tuple(jax.ShapeDtypeStruct(shape, BF) for shape in (*shapes, dec.shape))
        + (jax.ShapeDtypeStruct(vec.shape, F32),),
        in_specs=[pl.BlockSpec(memory_space=pltpu.VMEM)] * 2
        + [pl.BlockSpec(memory_space=pl.ANY)] * (len(lefts) + len(rights)),
        out_specs=(pl.BlockSpec(memory_space=pl.ANY),) * (len(shapes) + 1)
        + (pl.BlockSpec(memory_space=pltpu.VMEM),),
        scratch_shapes=[
            pltpu.VMEM((len(blocks), 4, ROWS, depth), BF),
            pltpu.VMEM((len(blocks), 4, ROWS, depth), BF),
            pltpu.VMEM((count, depth, UNIT), BF),
            pltpu.VMEM((count, depth, UNIT), BF),
            pltpu.VMEM((slots, 2, 2, ROWS, HALF), BF),
            pltpu.VMEM((count, 2, 2, ROWS, HALF), BF),
            pltpu.VMEM((slots, 2, ROWS, HALF), BF),
            pltpu.VMEM((count, 2, ROWS, HALF), BF),
            pltpu.VMEM((4, ROWS, UNIT), F32),
            pltpu.VMEM((full, ROWS, UNIT), BF),
            pltpu.VMEM((full, ROWS, UNIT), BF),
            pltpu.VMEM((full, ROWS, UNIT), BF),
            pltpu.VMEM((6, *vec.shape), F32),
            pltpu.VMEM((6, *vec.shape), F32),
            dma((len(blocks), 3)),
            dma((count, 3)),
            dma((slots, 2)),
            dma((count, 2)),
            dma((slots, 2)),
            dma((count, 2)),
            dma((full, 2)),
            dma((full, 2)),
            dma((6,)),
            dma((6,)),
            dma((count + 2 * extra,)),
        ],
        compiler_params=pltpu.CompilerParams(
            collective_id=0, has_side_effects=True, vmem_limit_bytes=58 * 2**20
        ),
        cost_estimate=pl.CostEstimate(
            flops=8 * 2 * count * ROWS * UNIT * depth,
            bytes_accessed=300 * 2**20,
            transcendentals=0,
        ),
    )(vec, dec, *lefts, *rights)


def encoder_pieces(shapes):
    (own, width), (rows, _), (tall, _) = shapes
    pieces = [(0, 0, own, 0, width, 0)]
    pieces += [(1, 0, rows, n * D, D, (1, 2, 0)[n]) for n in range(3)]
    pieces += [(1, 0, rows, 3 * D, D, 1)]
    pieces += [(1, 0, rows, 4 * D + n * D, D, (2, 0, 1, 2)[n]) for n in range(FF // D)]
    pieces += [(2, n * rows, rows, 0, D, (0, 1, 2, 0)[n]) for n in range(tall // rows)]
    pieces += [(1, 0, rows, 4 * D + FF, DD, 0)]
    return pieces


def norm_rows(h, gain):
    mean = jnp.mean(h, -1, keepdims=True)
    cent = h - mean
    var = jnp.mean(cent * cent, -1, keepdims=True)
    return (cent * lax.rsqrt(var + EPS) * gain).astype(BF)


def encoder_kernel(
    picked_ref,
    stats_ref,
    pos_ref,
    bias_ref,
    gains_ref,
    embed_ref,
    wide_ref,
    down_ref,
    wide_out,
    down_out,
    stats_out,
    inputs_ref,
    start_ref,
    a_ref,
    qkv_ref,
    mixed_ref,
    middle_ref,
    b_ref,
    slope_ref,
    hidden_ref,
    end_ref,
    z_ref,
    seen_ref,
    w_embed,
    w_wide,
    w_down,
    v_in,
    v_out,
    load_sem,
    store_sem,
    send_sem,
    recv_sem,
    v_send,
    v_recv,
):
    shards, gathered = (embed_ref, wide_ref, down_ref), (w_embed, w_wide, w_down)
    pieces = encoder_pieces([ref.shape for ref in shards])
    count = len(pieces)
    z, f = lax.axis_index("dp"), lax.axis_index("fsdp")
    core, place = f % 2, f // 2
    x, y = place % 2, place // 2
    f_x, f_y, f_far = f + 2 - 4 * x, f + 4 - 8 * y, f + 6 - 4 * x - 8 * y
    partner = (z, f + 1 - 2 * core)
    x_side, y_side, z_side = (z, f_x), (z, f_y), (z + 1 - 2 * (z % 2), f)
    outer = (z == 0) | (z == 3)
    inner = (z == 1) | (z == 2)
    across = (3 - z, f)

    barrier = pltpu.get_barrier_semaphore()
    for device in (partner, x_side, y_side, z_side):
        pl.semaphore_signal(barrier, inc=1, device_id=device, device_id_type=MESH)

    @pl.when(outer)
    def _():
        pl.semaphore_wait(barrier, 4)

    @pl.when(inner)
    def _():
        pl.semaphore_signal(barrier, inc=1, device_id=across, device_id_type=MESH)
        pl.semaphore_wait(barrier, 5)

    loads = [
        pltpu.make_async_copy(shard, whole.at[f], load_sem.at[n])
        for n, (shard, whole) in enumerate(zip(shards, gathered))
    ]
    for load in loads:
        load.start()

    def spot(t, owner, half=None):
        array, row, rows, column, columns, _ = pieces[t]
        if half is not None:
            columns //= 2
            column += half * columns
        return gathered[array].at[owner, pl.ds(row, rows), pl.ds(column, columns)]

    def move(t, owner, send, recv, device, half=None):
        target = spot(t, owner, half)
        source = target
        if send < 3:
            array, row, rows, column, columns, _ = pieces[t]
            source = shards[array].at[pl.ds(row, rows), pl.ds(column, columns)]
        return put(source, target, send_sem.at[t, send], recv_sem.at[t, recv], device)

    def own_x(t):
        return move(t, f, 0, 0, x_side)

    def own_y(t):
        return move(t, f, 1, 1, y_side)

    def own_core(t):
        return move(t, f, 2, 4, partner)

    def far_x(t):
        return move(t, f_y, 3, 2, x_side, 0)

    def far_y(t):
        return move(t, f_x, 4, 3, y_side, 1)

    def to_core(t, n):
        return move(t, (f_x, f_y, f_far)[n], 5 + n, 5 + n, partner)

    def to_z(t, n):
        return move(t, (f_x, f_y, f_far)[n], 8 + n, 8 + n, z_side)

    def brings(t, then, other=None):
        kind = pieces[t][5]
        if kind == 0:
            then()
            return
        pl.when(z % 2 == kind - 1)(then)
        if other is not None:
            pl.when(z % 2 != kind - 1)(other)

    def first(t):
        own_core(t).start()

        def then():
            own_x(t).start()
            own_y(t).start()

        brings(t, then)

    def second(t):
        def then():
            own_x(t).wait_recv()
            far_y(t).start()
            own_y(t).wait_recv()
            far_x(t).start()
            for n in range(2):
                to_core(t, n).start()
                if pieces[t][5]:
                    to_z(t, n).start()

        brings(t, then)

    def third(t):
        def then():
            far_x(t).wait_recv()
            far_y(t).wait_recv()
            to_core(t, 2).start()
            if pieces[t][5]:
                to_z(t, 2).start()

        brings(t, then)

    def taken(t, n):
        def other():
            to_z(t, n).wait_recv()
            to_core(t, n).start()

        brings(t, lambda: None, other)

    def whole(t):
        own_core(t).wait_recv()
        for n in range(3):
            to_core(t, n).wait_recv()

    def drain(t):
        own_core(t).wait_send()
        for n in range(3):
            to_core(t, n).wait_send()

        def then():
            for copy in (own_x(t), own_y(t), far_x(t), far_y(t)):
                copy.wait_send()
            if pieces[t][5]:
                for n in range(3):
                    to_z(t, n).wait_send()

        brings(t, then)

    def copy_v(step, device):
        return put(v_out.at[step], v_in.at[step], v_send.at[step], v_recv.at[step], device)

    sides = (partner, x_side, y_side)

    def statistics(i):
        if i <= 3:
            if i == 0:
                v_out[0] = stats_ref[...]
            else:
                copy_v(i - 1, sides[i - 1]).wait_recv()
                v_out[i] = v_out[i - 1] + v_in[i - 1]
            if i < 3:
                copy_v(i, sides[i]).start()
            else:

                @pl.when(outer)
                def _():
                    copy_v(3, z_side).start()

        if i == 4:

            @pl.when(inner)
            def _():
                copy_v(3, z_side).wait_recv()
                v_out[4] = v_out[3] + v_in[3]
                copy_v(4, across).start()

        if i == 5:

            @pl.when(inner)
            def _():
                copy_v(4, across).wait_recv()
                v_out[5] = v_out[4] + v_in[4]
                copy_v(5, z_side).start()
                stats_out[...] = v_out[5]

            @pl.when(outer)
            def _():
                copy_v(5, z_side).wait_recv()
                stats_out[...] = v_in[5]

    def columns_of(t):
        array, row, rows, column, columns, _ = pieces[t]
        weight = gathered[array][:, row : row + rows, column : column + columns]
        return weight.reshape(-1, columns)

    def embed_step():
        pixels = stats_out[6:7, :] * (PATCH * PATCH)
        for band in range(BANDS):
            mean = stats_out[band : band + 1, :] / pixels
            var = stats_out[BANDS + band : BANDS + band + 1, :] / pixels - mean * mean
            rate = lax.rsqrt(var + EPS)
            for part in range(PATCH * PATCH // LANES):
                lanes = pl.ds(band * PATCH * PATCH + part * LANES, LANES)
                inputs_ref[:, lanes] = ((picked_ref[:, lanes] - mean) * rate).astype(BF)
        start_ref[...] = matmul(inputs_ref[...], columns_of(0)) + pos_ref[...]
        a_ref[...] = norm_rows(start_ref[...], gains_ref[0:1, :])

    def qkv_step(n):
        qkv_ref[:, n * D : (n + 1) * D] = matmul(a_ref[...], columns_of(1 + n)).astype(BF)

    def attention_step():
        size = D // HEADS
        lane_head = lax.broadcasted_iota(jnp.int32, (VIS, LANES), 1) // size

        def group(g, _):
            query, keys, values = [
                qkv_ref[:, pl.ds(pl.multiple_of(n * D + g * LANES, LANES), LANES)] for n in range(3)
            ]
            mixed = jnp.zeros((VIS, LANES), F32)
            for j in range(LANES // size):
                one = jnp.where(lane_head == j, query.astype(F32), 0.0).astype(BF)
                scores = right_t(one, keys) * size ** (-0.5) + bias_ref[...]
                probs = jnp.exp(scores - jnp.max(scores, -1, keepdims=True))
                probs = probs * (1.0 / jnp.sum(probs, -1, keepdims=True))
                mixed = jnp.where(lane_head == j, matmul(probs.astype(BF), values), mixed)
            mixed_ref[:, pl.ds(pl.multiple_of(g * LANES, LANES), LANES)] = mixed.astype(BF)
            return 0

        lax.fori_loop(0, D // LANES, group, 0)

    def out_step():
        middle_ref[...] = start_ref[...] + matmul(mixed_ref[...], columns_of(4))
        b_ref[...] = norm_rows(middle_ref[...], gains_ref[1:2, :])

    def up_step(n):
        columns = slice(n * D, (n + 1) * D)
        after, slope = gelu_parts(matmul(b_ref[...], columns_of(5 + n)))
        hidden_ref[:, columns] = after.astype(BF)
        slope_ref[:, columns] = slope

    def down_step(n):
        rows, owners = w_wide.shape[1], w_down.shape[0]
        tall = w_down.shape[1]
        parts = [hidden_ref[:, o * tall + n * rows : o * tall + (n + 1) * rows] for o in range(owners)]
        total = matmul(jnp.concatenate(parts, 1), columns_of(9 + n))
        end_ref[...] = (middle_ref[...] if n == 0 else end_ref[...]) + total

    def link_step():
        z_ref[...] = norm_rows(end_ref[...], gains_ref[2:3, :])
        seen_ref[...] = matmul(z_ref[...], columns_of(count - 1))

    work = [(6, 0, embed_step), (6, 1, partial(qkv_step, 0)), (7, 2, partial(qkv_step, 1))]
    work += [(8, 3, partial(qkv_step, 2)), (8, None, attention_step), (9, 4, out_step)]
    work += [(at, 5 + n, partial(up_step, n)) for n, at in enumerate((10, 10, 12, 13))]
    work += [(at, 9 + n, partial(down_step, n)) for n, at in enumerate((13, 15, 16, 16))]
    work += [(17, count - 1, link_step)]
    stores = []

    for load in loads:
        load.wait()
    first(0)
    first(1)
    for i in range(18):
        if i + 2 < count:
            first(i + 2)
        statistics(i)
        if i < count:
            second(i)
        if 0 <= i - 1 < count:
            third(i - 1)
        if 0 <= i - 3 < count:
            taken(i - 3, 0)
            taken(i - 3, 1)
        if 0 <= i - 4 < count:
            taken(i - 4, 2)
        for at, piece, run in work:
            if at != i:
                continue
            if piece is not None:
                whole(piece)
                array, row, rows, column, columns, _ = pieces[piece]
                if array:
                    where = (slice(None), pl.ds(row, rows), pl.ds(column, columns))
                    store = pltpu.make_async_copy(
                        gathered[array].at[where],
                        (None, wide_out, down_out)[array].at[where],
                        store_sem.at[piece],
                    )
                    store.start()
                    stores.append(store)
            run()
    for store in stores:
        store.wait()
    for t in range(count):
        drain(t)
    for step in range(3):
        copy_v(step, sides[step]).wait_send()

    @pl.when(outer)
    def _():
        copy_v(3, z_side).wait_send()

    @pl.when(inner)
    def _():
        copy_v(4, across).wait_send()
        copy_v(5, z_side).wait_send()


def encoder_forward(picked, stats, pos, bias, gains, embed, wide, down):
    owners = lax.axis_size("fsdp")
    shapes = [w.shape for w in (embed, wide, down)]
    count = len(encoder_pieces(shapes))
    full = [jax.ShapeDtypeStruct((owners, *shape), BF) for shape in shapes[1:]]
    local = [
        jax.ShapeDtypeStruct((8, LANES), F32),
        jax.ShapeDtypeStruct((VIS, PD), BF),
        jax.ShapeDtypeStruct((VIS, D), F32),
        jax.ShapeDtypeStruct((VIS, D), BF),
        jax.ShapeDtypeStruct((VIS, 3 * D), BF),
        jax.ShapeDtypeStruct((VIS, D), BF),
        jax.ShapeDtypeStruct((VIS, D), F32),
        jax.ShapeDtypeStruct((VIS, D), BF),
        jax.ShapeDtypeStruct((VIS, FF), F32),
        jax.ShapeDtypeStruct((VIS, FF), BF),
        jax.ShapeDtypeStruct((VIS, D), F32),
        jax.ShapeDtypeStruct((VIS, D), BF),
        jax.ShapeDtypeStruct((VIS, DD), F32),
    ]
    vmem, anywhere = pl.BlockSpec(memory_space=pltpu.VMEM), pl.BlockSpec(memory_space=pl.ANY)
    dma = pltpu.SemaphoreType.DMA
    wide_full, down_full, *rest = pl.pallas_call(
        encoder_kernel,
        out_shape=(*full, *local),
        in_specs=[vmem] * 5 + [anywhere] * 3,
        out_specs=(anywhere,) * 2 + (vmem,) * len(local),
        scratch_shapes=[pltpu.VMEM((owners, *shape), BF) for shape in shapes]
        + [
            pltpu.VMEM((6, 8, LANES), F32),
            pltpu.VMEM((6, 8, LANES), F32),
            dma((3,)),
            dma((count,)),
            dma((count, 11)),
            dma((count, 11)),
            dma((6,)),
            dma((6,)),
        ],
        compiler_params=pltpu.CompilerParams(
            collective_id=1, has_side_effects=True, vmem_limit_bytes=56 * 2**20
        ),
        cost_estimate=pl.CostEstimate(
            flops=2 * VIS * 14 * 2**20, bytes_accessed=200 * 2**20, transcendentals=0
        ),
    )(picked, stats, pos, bias, gains, embed, wide, down)
    return (wide_full.reshape(D, -1), down_full.reshape(FF, D), *rest)


def block_forward(h, weights, gains, bias, heads, skip):
    wqkv, wout, wup, wdown = weights
    width = h.shape[1]
    normed_a = layer_norm(h, gains[0]).astype(BF)
    query = matmul(normed_a[skip:], wqkv[:, :width]).astype(BF)
    keys = matmul(normed_a, wqkv[:, width : 2 * width]).astype(BF)
    values = matmul(normed_a, wqkv[:, 2 * width :]).astype(BF)
    mixed_t, lse = attend(query.T, keys, values.T, bias, width // heads)
    middle = h[skip:] + left_t(mixed_t, wout)
    normed_b = layer_norm(middle, gains[1]).astype(BF)
    after, slope = gelu_parts(matmul(normed_b, wup))
    hidden = after.astype(BF)
    end = middle + matmul(hidden, wdown)
    return end, (h, normed_a, query, keys, values, mixed_t, lse, middle, normed_b, slope, hidden)


def block_backward(saved, grad, weights, gains, bias, heads, skip):
    wqkv, wout, wup, wdown = weights
    h, normed_a, query, keys, values, mixed_t, lse, middle, normed_b, slope, hidden = saved
    width = h.shape[1]
    dbranch = grad.astype(BF)
    dbefore = (right_t(dbranch, wdown) * slope).astype(BF)
    dmiddle, dgain_two = norm_back(middle, gains[1], right_t(dbefore, wup))
    dmiddle = dmiddle + grad
    dattn = dmiddle.astype(BF)
    dmixed = right_t(dattn, wout).astype(BF)
    dqt, dkeys, dvalues = attend_back(query, keys, values, dmixed, bias, lse, width // heads)
    dquery = dqt.T
    if skip:
        dquery = jnp.pad(dquery, ((skip, 0), (0, 0)))
        dmiddle = jnp.pad(dmiddle, ((skip, 0), (0, 0)))
    dqkv = jnp.concatenate([dquery, dkeys, dvalues], 1)
    dh, dgain_one = norm_back(h, gains[0], right_t(dqkv, wqkv))
    factors = ((normed_a.T, dqkv), (mixed_t, dattn), (normed_b.T, dbefore), (hidden.T, dbranch))
    return (dh + dmiddle, factors, (dgain_one, dgain_two))


def reduce_rows(grad):
    return lax.psum_scatter(grad.astype(BF), "fsdp", scatter_dimension=0, tiled=True)


def sum_gradients(factors, encoded, dseen, inputs, dh_low, dec, vector_grad, local_loss):
    lefts = [pair[0] for pair in factors] + [encoded.T]
    owners = lax.axis_size("fsdp")
    own = PD // owners
    first = inputs.T.reshape(owners, own, VIS)
    lefts.append(jnp.pad(first, ((0, 0), (0, ROWS - own), (0, 0))).reshape(-1, VIS))
    rights = [pair[1] for pair in factors] + [dseen, dh_low]
    blocks, units, spots = [], [], []

    def add(left, sub, right, out, row, rows, column, columns):
        blocks.append((left, sub))
        for n in range(0, columns, UNIT):
            units.append((len(blocks) - 1, right, n))
            spots.append((out, row, rows, column + n, UNIT))

    add(4, 0, 4, 1, 0, ROWS, 4 * D + FF, DD)
    for n in range(FF // owners // ROWS):
        add(3, n, 3, 2, n * ROWS, ROWS, 0, D)
    add(2, 0, 2, 1, 0, ROWS, 4 * D, FF)
    add(1, 0, 1, 1, 0, ROWS, 3 * D, D)
    add(0, 0, 0, 1, 0, ROWS, 0, 3 * D)
    add(5, 0, 5, 0, 0, own, 0, D)
    shapes = ((own, D), (ROWS, 4 * D + FF + DD), (FF // owners, D))
    length = vector_grad.shape[0]
    rows = -(-(length + 1) // (8 * LANES)) * 8
    vec = jnp.concatenate(
        [vector_grad, local_loss[None], jnp.zeros((rows * LANES - length - 1,), F32)]
    )
    used = dec.shape[1]
    dec = jnp.pad(dec, ((0, 0), (0, -used % (2 * UNIT))))
    *parts, dec, vec = sum_products(
        tuple(blocks), tuple(units), tuple(spots), shapes, lefts, rights, dec, vec.reshape(rows, LANES)
    )
    vec = vec.reshape(-1)
    return parts, dec[:, :used], vec[:length], vec[length]


def enc_split(wide, down):
    return (
        (wide[:, : 3 * D], wide[:, 3 * D : 4 * D], wide[:, 4 * D : 4 * D + FF], down),
        wide[:, 4 * D + FF :],
    )


def dec_split(wide, down):
    return (
        (wide[:, : 3 * DD], wide[:, 3 * DD : 4 * DD], wide[:, 4 * DD : 4 * DD + DFF], down),
        wide[:, 4 * DD + DFF :],
    )


def advance(weight, mom, avg, grad, rate):
    grad = grad + DECAY * weight
    buf = MOMENTUM * mom + grad
    new = weight - rate * (grad + MOMENTUM * buf)
    return (buf, new, AVERAGE * avg + (1.0 - AVERAGE) * new)


def arrange(valid, masked, scene_ids):
    slots = valid.shape[0]
    live = valid > 0
    kinds = jnp.stack([live & (masked == 0), live & (masked > 0), ~live], 1)
    index = jnp.arange(slots, dtype=jnp.int32)
    ranks = matmul((index[None, :] < index[:, None]).astype(BF), kinds.astype(BF)).astype(jnp.int32)
    n_seen, n_hid = [jnp.sum(kinds[:, i].astype(jnp.int32)) for i in range(2)]
    empty = ranks[:, 2]
    to_empty = jnp.where(empty < VIS - n_seen, n_seen + empty, n_seen + n_hid + empty)
    place = jnp.where(
        kinds[:, 0], ranks[:, 0], jnp.where(kinds[:, 1], VIS + ranks[:, 1], to_empty)
    )
    return (place[None, :] == index[:, None]).astype(BF), n_seen, n_hid


def exact_pick(pick, array):
    high = lax.reduce_precision(array, 8, 7)
    rest = array - high
    mid = lax.reduce_precision(rest, 8, 7)
    low = rest - mid
    return (
        matmul(pick, high.astype(BF)) + matmul(pick, mid.astype(BF)) + matmul(pick, low.astype(BF))
    )


def body(
    pixels,
    masked,
    valid,
    scene_ids,
    gsd_index,
    coords,
    embed,
    wide_enc,
    enc_down,
    wide_dec,
    dec_down,
    vectors,
    embed_mom,
    wide_enc_mom,
    enc_down_mom,
    wide_dec_mom,
    dec_down_mom,
    vector_mom,
    embed_avg,
    wide_enc_avg,
    enc_down_avg,
    wide_dec_avg,
    dec_down_avg,
    vector_avg,
):
    slots = pixels.shape[0]
    fast = (lax.axis_size("dp"), lax.axis_size("fsdp")) == (4, 8)
    w_dec, w_dec_down = [
        lax.all_gather(w.astype(BF), "fsdp", axis=0, tiled=True) for w in (wide_dec, dec_down)
    ]
    dec_weights, w_head = dec_split(w_dec, w_dec_down)
    rows_ok = valid.astype(jnp.float32)
    flags = rows_ok * masked.astype(jnp.float32)
    bands = pixels.reshape(slots, BANDS, PATCH * PATCH)
    weighted = bands * rows_ok[:, None, None]
    band_sum = jnp.sum(weighted, axis=(0, 2))
    counts = jnp.stack([jnp.sum(rows_ok), jnp.sum(flags)])
    band_sq = jnp.sum(weighted * bands, axis=(0, 2))
    stats = jnp.concatenate([band_sum, band_sq, counts])

    pick, n_seen, n_hid = arrange(valid, masked, scene_ids)
    picked_pixels = exact_pick(pick, pixels)
    small = matmul(
        pick, jnp.concatenate([(scene_ids % 2)[:, None], coords], 1).astype(BF)
    )
    odd, coord = small[:, 0], small[:, 1:]
    level = jnp.where(odd == 0, gsd_index[0], gsd_index[1]).astype(jnp.float32)
    scale = jnp.exp2(0.5 * level - 1.0)
    index = jnp.arange(slots, dtype=jnp.int32)
    kept = index[:VIS] < n_seen
    hidden_ok = index[:HID] < n_hid
    live = jnp.concatenate([kept, hidden_ok])
    keptf = kept.astype(jnp.float32)[:, None]
    allow = live[:, None] & (odd[:, None] == odd[None, :]) | (index[:, None] == index[None, :])
    bias = jnp.where(allow, 0.0, NEGATIVE)
    bias_enc, bias_dec = bias[:VIS, :VIS], bias[:, VIS:]

    gains_enc = (vectors[:D], vectors[D : 2 * D])
    gain_enc_out = vectors[2 * D : 3 * D]
    base = 3 * D
    gains_dec = (vectors[base : base + DD], vectors[base + DD : base + 2 * DD])
    gain_dec_out = vectors[base + 2 * DD : base + 3 * DD]
    token = vectors[base + 3 * DD :]

    pos_enc = positions(coord[:VIS], scale[:VIS], D)
    low_enc = [w.astype(BF) for w in (embed, wide_enc, enc_down)]
    if fast:
        gains = jnp.pad(vectors[: 3 * D].reshape(3, D), ((0, 5), (0, 0)))
        stats = jnp.broadcast_to(stats[:, None], (8, LANES))
        w_enc, w_enc_down, stats, inputs, h_start, *saved, h_end, encoded, seen_out = encoder_forward(
            picked_pixels[:VIS], stats, pos_enc, bias_enc.T, gains, *low_enc
        )
        normed_a, qkv, mixed, *saved = saved
        enc_saved = (h_start, normed_a, *jnp.split(qkv, 3, 1), mixed.T, None, *saved)
        enc_weights, w_link = enc_split(w_enc, w_enc_down)
        stats = stats[:, 0]
    else:
        stats = lax.psum(stats, ("dp", "fsdp"))
    band_sum, band_sq, counts = stats[:3], stats[3:6], stats[6:]
    n_pix = counts[0] * (PATCH * PATCH)
    mean = band_sum / n_pix
    var = band_sq / n_pix - mean * mean
    count = counts[1]
    cent = picked_pixels.reshape(slots, BANDS, PATCH * PATCH) - mean[None, :, None]
    normed = (cent * lax.rsqrt(var + EPS)[None, :, None]).reshape(slots, PD)
    if not fast:
        w_embed, w_enc, w_enc_down = [
            lax.all_gather(w, "fsdp", axis=0, tiled=True) for w in low_enc
        ]
        enc_weights, w_link = enc_split(w_enc, w_enc_down)
        inputs = normed[:VIS].astype(BF)
        h_start = matmul(inputs, w_embed) + pos_enc
        h_end, enc_saved = block_forward(h_start, enc_weights, gains_enc, bias_enc, HEADS, 0)
        encoded = layer_norm(h_end, gain_enc_out).astype(BF)
        seen_out = matmul(encoded, w_link)
    y_start = positions(coord, scale, DD) + jnp.concatenate(
        [jnp.where(kept[:, None], seen_out, token), jnp.broadcast_to(token, (HID, DD))]
    )
    y_end, dec_saved = block_forward(y_start, dec_weights, gains_dec, bias_dec, DHEADS, VIS)
    decoded = layer_norm(y_end, gain_dec_out).astype(BF)
    pred = matmul(decoded, w_head)
    flag = hidden_ok.astype(jnp.float32)
    losses, loss_pull = jax.vjp(lambda values: row_loss(values, normed[VIS:]), pred)
    local_loss = jnp.sum(flag * losses)
    dpred = loss_pull(flag / count)[0].astype(BF)
    dy_end, dgain_dec_out = norm_back(y_end, gain_dec_out, right_t(dpred, w_head))
    dy_start, dec_factors, dgains_dec = block_backward(
        dec_saved, dy_end, dec_weights, gains_dec, bias_dec, DHEADS, VIS
    )
    owners = lax.axis_size("fsdp")
    dec_grads = [matmul(*pair).astype(BF) for pair in dec_factors]
    down_grad = dec_grads[3].reshape(owners, -1, DD // owners, DD)
    down_grad = down_grad.transpose(0, 2, 1, 3).reshape(DD, DFF)
    dec_grads = jnp.concatenate(
        [*dec_grads[:3], left_t(decoded, dpred).astype(BF), down_grad], 1
    )
    dy_start, dec_grads = lax.optimization_barrier((dy_start, dec_grads))
    dec_sum = reduce_rows(dec_grads)
    picked = dy_start[:VIS] * keptf
    dtoken = jnp.sum(dy_start, 0) - jnp.sum(picked, 0)
    dseen = picked.astype(BF)
    dh_end, dgain_enc_out = norm_back(h_end, gain_enc_out, right_t(dseen, w_link))
    dh_start, enc_factors, dgains_enc = block_backward(
        enc_saved, dh_end, enc_weights, gains_enc, bias_enc, HEADS, 0
    )
    dh_low = dh_start.astype(BF)
    vector_grad = jnp.concatenate(
        [
            dgains_enc[0],
            dgains_enc[1],
            dgain_enc_out,
            dgains_dec[0],
            dgains_dec[1],
            dgain_dec_out,
            dtoken,
        ]
    )
    if fast:
        enc_parts, dec_sum, vector_grad, loss_sum = sum_gradients(
            enc_factors, encoded, dseen, inputs, dh_low, dec_sum, vector_grad, local_loss
        )
    else:
        enc_grads = [matmul(*pair).astype(BF) for pair in enc_factors]
        link_grad = left_t(encoded, dseen).astype(BF)
        enc_parts = lax.psum(
            (
                reduce_rows(left_t(inputs, dh_low)),
                reduce_rows(
                    jnp.concatenate([enc_grads[0], enc_grads[1], enc_grads[2], link_grad], 1)
                ),
                reduce_rows(enc_grads[3]),
            ),
            "dp",
        )
        vector_grad, loss_sum = lax.psum((vector_grad, local_loss), ("dp", "fsdp"))
        dec_sum = lax.psum(dec_sum, "dp")
    rows = dec_sum.shape[0]
    wide = wide_dec.shape[1]
    down = dec_sum[:, wide:].reshape(rows, -1, DD).transpose(1, 0, 2).reshape(-1, DD)
    dec_parts = (dec_sum[:, :wide], down)
    shard_grads = [g.astype(F32) for g in (*enc_parts, *dec_parts)]
    rate = STEP_UNIT * (PD * TOK_DEV * lax.axis_size("dp") * lax.axis_size("fsdp")) ** 0.5
    weights = (embed, wide_enc, enc_down, wide_dec, dec_down)
    moms = (embed_mom, wide_enc_mom, enc_down_mom, wide_dec_mom, dec_down_mom)
    avgs = (embed_avg, wide_enc_avg, enc_down_avg, wide_dec_avg, dec_down_avg)
    outs = []
    for number in range(5):
        buf, new, avg = advance(
            weights[number], moms[number], avgs[number], shard_grads[number], rate
        )
        outs += [buf, new, avg, new.astype(jnp.bfloat16)]
    return (*outs, *advance(vectors, vector_mom, vector_avg, vector_grad, rate), loss_sum, count)


def solution(mesh):
    both, rows = P(("dp", "fsdp")), P("fsdp", None)
    placed = (P(("dp", "fsdp"), None), both, both, both, both, P(("dp", "fsdp"), None))
    states = (rows,) * 5 + (P(),)
    return jax.shard_map(
        body,
        mesh=mesh,
        in_specs=placed + states * 3,
        out_specs=(rows,) * 20 + (P(),) * 5,
        check_vma=False,
    )
```

```python
from functools import partial

import jax
import jax.numpy as jnp
from jax import lax
from jax.experimental import pallas as pl
from jax.experimental.pallas import tpu as pltpu
from jax.sharding import PartitionSpec as P

D = 1024
HEADS = 16
FF = 4096
DD = 512
DHEADS = 16
DFF = 2048
PATCH = 16
BANDS = 3
TOK_DEV = 768
PD = 768
LOWD = 192
VIS = 192
HID = TOK_DEV - VIS

EPS = 1e-06
MOMENTUM = 0.9
DECAY = 0.0001
AVERAGE = 0.9
STEP_UNIT = 0.003
NEGATIVE = -1e30
LANES = 128
BF = jnp.bfloat16
F32 = jnp.float32


def matmul(left, right):
    return jnp.dot(left, right, preferred_element_type=jnp.float32)


def left_t(left, right):
    return lax.dot_general(
        left, right, (((0,), (0,)), ((), ())), preferred_element_type=jnp.float32
    )


def right_t(left, right):
    return lax.dot_general(
        left, right, (((1,), (1,)), ((), ())), preferred_element_type=jnp.float32
    )


def layer_norm(h, gain):
    mean = jnp.mean(h, -1, keepdims=True)
    cent = h - mean
    var = jnp.mean(cent * cent, -1, keepdims=True)
    return cent * lax.rsqrt(var + EPS) * gain


def norm_back(h, gain, grad):
    result, pull = jax.vjp(layer_norm, h, gain)
    return pull(grad)


def gelu_parts(before):
    below = 0.5 * (1.0 + lax.erf(before * 0.5**0.5))
    slope = below + before * jnp.exp(before * before * -0.5) * (0.5 / jnp.pi) ** 0.5
    return before * below, slope


def positions(coord, scale, width):
    quarter = width // 4
    omega = 10000.0 ** (-jnp.arange(quarter, dtype=jnp.float32) / quarter)
    angle_x = coord[:, 0:1] * scale[:, None] * omega[None, :]
    angle_y = coord[:, 1:2] * scale[:, None] * omega[None, :]
    return jnp.concatenate(
        [jnp.sin(angle_x), jnp.cos(angle_x), jnp.sin(angle_y), jnp.cos(angle_y)], -1
    )


def row_loss(pred, normed):
    rows = normed.shape[0]
    coarse = jnp.mean(normed.reshape(rows, BANDS, PATCH // 2, 2, PATCH // 2, 2), axis=(3, 5))
    upper = jnp.repeat(jnp.repeat(coarse, 2, axis=2), 2, axis=3).reshape(rows, PD)
    err_high = pred[:, :PD] - (normed - upper)
    err_low = pred[:, PD:] - coarse.reshape(rows, LOWD)
    return jnp.mean(jnp.sqrt(err_high * err_high + 1.0) - 1.0, -1) + jnp.mean(err_low * err_low, -1)


def attend_kernel(size, qt_ref, k_ref, vt_ref, bias_ref, ot_ref, lse_ref):
    per = LANES // size
    row_head = lax.broadcasted_iota(jnp.int32, qt_ref.shape, 0) // size
    factor = size ** (-0.5)
    for j in range(per):
        query = jnp.where(row_head == j, qt_ref[...].astype(F32), 0.0).astype(BF)
        scores = matmul(k_ref[...], query) * factor + bias_ref[...]
        top = jnp.max(scores, 0, keepdims=True)
        probs = jnp.exp(scores - top)
        total = jnp.sum(probs, 0, keepdims=True)
        probs = (probs * (1.0 / total)).astype(BF)
        rows = slice(j * size, (j + 1) * size)
        ot_ref[rows, :] = matmul(vt_ref[rows, :], probs).astype(BF)
        lse_ref[0, j : j + 1, :] = top + jnp.log(total)


def attend(qt, keys, vt, bias, size):
    width, queries = qt.shape
    rows = keys.shape[0]
    groups, per = width // LANES, LANES // size
    return pl.pallas_call(
        partial(attend_kernel, size),
        grid=(groups,),
        out_shape=(
            jax.ShapeDtypeStruct((width, queries), BF),
            jax.ShapeDtypeStruct((groups, per, queries), F32),
        ),
        in_specs=[
            pl.BlockSpec((LANES, queries), lambda g: (g, 0)),
            pl.BlockSpec((rows, LANES), lambda g: (0, g)),
            pl.BlockSpec((LANES, rows), lambda g: (g, 0)),
            pl.BlockSpec((rows, queries), lambda g: (0, 0)),
        ],
        out_specs=(
            pl.BlockSpec((LANES, queries), lambda g: (g, 0)),
            pl.BlockSpec((1, per, queries), lambda g: (g, 0, 0)),
        ),
        compiler_params=pltpu.CompilerParams(vmem_limit_bytes=40 * 2**20),
        cost_estimate=pl.CostEstimate(
            flops=4 * rows * queries * width * per,
            bytes_accessed=4 * rows * queries,
            transcendentals=rows * queries * width // size,
        ),
    )(qt, keys, vt, bias)


def attend_back_kernel(
    size,
    qt_ref,
    q_ref,
    k_ref,
    kt_ref,
    v_ref,
    do_ref,
    dot_ref,
    bias_ref,
    *rest,
):
    *lse_ref, dqt_ref, dk_ref, dv_ref = rest
    per = LANES // size
    row_head = lax.broadcasted_iota(jnp.int32, qt_ref.shape, 0) // size
    lane_head = lax.broadcasted_iota(jnp.int32, dk_ref.shape, 1) // size
    factor = size ** (-0.5)
    dkeys = jnp.zeros(dk_ref.shape, F32)
    dvalues = jnp.zeros(dv_ref.shape, F32)
    for j in range(per):
        query = jnp.where(row_head == j, qt_ref[...].astype(F32), 0.0).astype(BF)
        dout = jnp.where(row_head == j, dot_ref[...].astype(F32), 0.0).astype(BF)
        scores = matmul(k_ref[...], query) * factor + bias_ref[...]
        if lse_ref:
            probs = jnp.exp(scores - lse_ref[0][0, j : j + 1, :])
        else:
            probs = jnp.exp(scores - jnp.max(scores, 0, keepdims=True))
            probs = probs * (1.0 / jnp.sum(probs, 0, keepdims=True))
        dvalues = jnp.where(lane_head == j, matmul(probs.astype(BF), do_ref[...]), dvalues)
        dprobs = matmul(v_ref[...], dout)
        delta = jnp.sum(dprobs * probs, 0, keepdims=True)
        dscores = (probs * (dprobs - delta)).astype(BF)
        dkeys = jnp.where(lane_head == j, matmul(dscores, q_ref[...]), dkeys)
        rows = slice(j * size, (j + 1) * size)
        dqt_ref[rows, :] = (matmul(kt_ref[rows, :], dscores) * factor).astype(BF)
    dk_ref[...] = (dkeys * factor).astype(BF)
    dv_ref[...] = dvalues.astype(BF)


def attend_back(query, keys, values, dmixed, bias, lse, size):
    queries, width = query.shape
    rows = keys.shape[0]
    groups, per = width // LANES, LANES // size
    tall = lambda n: pl.BlockSpec((n, LANES), lambda g: (0, g))
    flat = lambda n: pl.BlockSpec((LANES, n), lambda g: (g, 0))
    return pl.pallas_call(
        partial(attend_back_kernel, size),
        grid=(groups,),
        out_shape=(
            jax.ShapeDtypeStruct((width, queries), BF),
            jax.ShapeDtypeStruct((rows, width), BF),
            jax.ShapeDtypeStruct((rows, width), BF),
        ),
        in_specs=[
            flat(queries),
            tall(queries),
            tall(rows),
            flat(rows),
            tall(rows),
            tall(queries),
            flat(queries),
            pl.BlockSpec((rows, queries), lambda g: (0, 0)),
        ]
        + [pl.BlockSpec((1, per, queries), lambda g: (g, 0, 0))] * (lse is not None),
        out_specs=(flat(queries), tall(rows), tall(rows)),
        compiler_params=pltpu.CompilerParams(vmem_limit_bytes=48 * 2**20),
        cost_estimate=pl.CostEstimate(
            flops=10 * rows * queries * width * per,
            bytes_accessed=4 * rows * queries,
            transcendentals=rows * queries * width // size,
        ),
    )(query.T, query, keys, keys.T, values, dmixed, dmixed.T, bias, *([] if lse is None else [lse]))


MESH = pl.DeviceIdType.MESH
UNIT = 512
HALF = UNIT // 2
ROWS = 128
HALF_ROWS = ROWS // 2
LAGS = (2, 4, 6, 8, 11)


def put(source, target, send, recv, device):
    return pltpu.make_async_remote_copy(
        src_ref=source,
        dst_ref=target,
        send_sem=send,
        recv_sem=recv,
        device_id=device,
        device_id_type=MESH,
    )


def sum_kernel(blocks, units, spots, vec_ref, dec_ref, *refs):
    n_left = max(b[0] for b in blocks) + 1
    n_right = max(u[1] for u in units) + 1
    lefts, rights = refs[:n_left], refs[n_left : n_left + n_right]
    outs = refs[n_left + n_right : n_left + n_right + 3]
    dec_out, vec_out = refs[n_left + n_right + 3 : n_left + n_right + 5]
    (
        xo,
        xp,
        yo,
        yp,
        a_out,
        a_in,
        b_out,
        b_in,
        sums,
        z_out,
        z_one,
        z_two,
        v_in,
        v_out,
        left_sem,
        right_sem,
        a_send,
        a_recv,
        b_send,
        b_recv,
        z_send,
        z_recv,
        v_send,
        v_recv,
        store_sem,
    ) = refs[n_left + n_right + 5 :]
    count = len(units)
    extra = z_one.shape[0] - count
    z, f = lax.axis_index("dp"), lax.axis_index("fsdp")
    core, place = f % 2, f // 2
    x, y = place % 2, place // 2
    partner = (z, f + 1 - 2 * core)
    x_side = (z, f + 2 - 4 * x)
    y_side = (z, f + 4 - 8 * y)
    at_x, at_y, at_far = place + 1 - 2 * x, place + 2 - 4 * y, 3 - place
    low = z < 2
    outer = (z == 0) | (z == 3)
    inner = (z == 1) | (z == 2)
    inward = (jnp.where(low, 1, 2), f)
    across = (3 - z, f)
    outward = (jnp.where(low, 0, 3), f)

    barrier = pltpu.get_barrier_semaphore()
    for device in (partner, x_side, y_side):
        pl.semaphore_signal(barrier, inc=1, device_id=device, device_id_type=MESH)

    @pl.when(outer)
    def _():
        pl.semaphore_signal(barrier, inc=1, device_id=inward, device_id_type=MESH)
        pl.semaphore_wait(barrier, 4)

    @pl.when(inner)
    def _():
        pl.semaphore_signal(barrier, inc=1, device_id=across, device_id_type=MESH)
        pl.semaphore_signal(barrier, inc=1, device_id=outward, device_id_type=MESH)
        pl.semaphore_wait(barrier, 5)

    def swap_left(source, b):
        return put(source, xp.at[b], left_sem.at[b, 1], left_sem.at[b, 2], partner)

    def swap_right(source, u):
        return put(source, yp.at[u], right_sem.at[u, 1], right_sem.at[u, 2], partner)

    for number, (block, right, column) in enumerate(units):
        if number == 0 or block != units[number - 1][0]:
            left, sub = blocks[block]
            rows = pl.ds(sub * ROWS, ROWS)
            swap_left(lefts[left].at[:, 1 - core, rows], block).start()
            pltpu.make_async_copy(
                lefts[left].at[:, core, rows], xo.at[block], left_sem.at[block, 0]
            ).start()
        piece = rights[right].at[:, pl.ds(column, UNIT)]
        swap_right(piece, number).start()
        pltpu.make_async_copy(piece, yo.at[number], right_sem.at[number, 0]).start()

    starts = [n for n in range(1, count) if units[n][0] != units[n - 1][0]]

    def block_of(u):
        return sum([jnp.where(u >= n, 1, 0) for n in starts], jnp.int32(0))

    first, second = pl.ds(0, HALF), pl.ds(HALF, HALF)

    def part(u, owner, columns):
        b = block_of(u)
        return matmul(xo[b, owner], yo[u, :, columns]) + matmul(xp[b, owner], yp[u, :, columns])

    def copy_a(u, side):
        slot = u % a_out.shape[0]
        return put(
            a_out.at[slot, side],
            a_in.at[u, side],
            a_send.at[slot, side],
            a_recv.at[u, side],
            (x_side, y_side)[side],
        )

    def copy_b(u, side):
        slot = u % b_out.shape[0]
        return put(
            b_out.at[slot, side],
            b_in.at[u, side],
            b_send.at[slot, side],
            b_recv.at[u, side],
            (y_side, x_side)[side],
        )

    def copy_in(u):
        return put(z_out.at[u], z_one.at[u], z_send.at[u, 0], z_recv.at[u, 0], inward)

    def copy_across(u):
        return put(z_out.at[u], z_two.at[u], z_send.at[u, 0], z_recv.at[u, 1], across)

    def copy_out(u):
        return put(z_one.at[u], z_one.at[u], z_send.at[u, 1], z_recv.at[u, 0], outward)

    def copy_v(step, device):
        return put(v_out.at[step], v_in.at[step], v_send.at[step], v_recv.at[step], device)

    def ready(n):
        halves = [
            dec_ref[:, pl.ds(pl.multiple_of((2 * n + part) * UNIT, UNIT), UNIT)] for part in range(2)
        ]
        return jnp.concatenate(halves, 0).astype(F32)

    def send_in(u, value):
        z_out[u] = value.astype(BF)
        copy_in(u).start()

    def add_in(u, value):
        copy_in(u).wait_recv()
        z_out[u] = (value + z_one[u].astype(F32)).astype(BF)
        copy_across(u).start()

    def add_across(u):
        copy_across(u).wait_recv()
        z_one[u] = (z_out[u].astype(F32) + z_two[u].astype(F32)).astype(BF)
        copy_out(u).start()

    def take(u):
        copy_out(u).wait_recv()

    def step(i, _):
        def stage(lag, also=None):
            u = i - lag
            ok = (u >= 0) & (u < count)
            if also is not None:
                ok = ok & also
            return u, pl.when(ok)

        u0, when = stage(0)

        @when
        def _():
            u = u0
            b = block_of(u)

            @pl.when((u == 0) | (b != block_of(u - 1)))
            def _():
                pltpu.make_async_copy(xo.at[b], xo.at[b], left_sem.at[b, 0]).wait()
                swap_left(xo.at[b], b).wait()

            pltpu.make_async_copy(yo.at[u], yo.at[u], right_sem.at[u, 0]).wait()
            swap_right(yo.at[u], u).wait()

            @pl.when(u >= a_out.shape[0])
            def _():
                for side in range(2):
                    copy_a(u - a_out.shape[0], side).wait_send()

            slot = u % a_out.shape[0]
            a_out[slot, 0, 0] = part(u, at_x, first).astype(BF)
            a_out[slot, 0, 1] = part(u, at_far, first).astype(BF)
            copy_a(u, 0).start()
            a_out[slot, 1, 0] = part(u, at_y, second).astype(BF)
            a_out[slot, 1, 1] = part(u, at_far, second).astype(BF)
            copy_a(u, 1).start()

        u1, when = stage(LAGS[0])

        @when
        def _():
            u = u1
            slot = u % b_out.shape[0]

            @pl.when(u >= b_out.shape[0])
            def _():
                for side in range(2):
                    copy_b(u - b_out.shape[0], side).wait_send()

            copy_a(u, 0).wait_recv()
            b_out[slot, 0] = (part(u, at_y, first) + a_in[u, 0, 1].astype(F32)).astype(BF)
            copy_b(u, 0).start()
            copy_a(u, 1).wait_recv()
            b_out[slot, 1] = (part(u, at_x, second) + a_in[u, 1, 1].astype(F32)).astype(BF)
            copy_b(u, 1).start()

        u2, when = stage(LAGS[1])

        @when
        def _():
            u = u2
            copy_b(u, 0).wait_recv()
            copy_b(u, 1).wait_recv()
            for side, columns in enumerate((first, second)):
                total = part(u, place, columns) + a_in[u, side, 0].astype(F32)
                sums[u % 4, :, columns] = total + b_in[u, side].astype(F32)

            @pl.when(outer)
            def _():
                send_in(u + extra, sums[u % 4])

        u3, when = stage(LAGS[2], inner)

        @when
        def _():
            add_in(u3 + extra, sums[u3 % 4])

        u4, when = stage(LAGS[3], inner)

        @when
        def _():
            add_across(u4 + extra)

        u5, when = stage(LAGS[4], outer)

        @when
        def _():
            take(u5 + extra)

        @pl.when((i < extra) & outer)
        def _():
            send_in(i, ready(i))

        one, two, three = [lag - LAGS[1] for lag in LAGS[2:]]

        @pl.when((i >= one) & (i < extra + one) & inner)
        def _():
            add_in(i - one, ready(i - one))

        @pl.when((i >= two) & (i < extra + two) & inner)
        def _():
            add_across(i - two)

        @pl.when((i >= three) & (i < extra + three) & outer)
        def _():
            take(i - three)

        for number, device in enumerate((partner, x_side, y_side)):

            @pl.when(i == number)
            def _():
                if number == 0:
                    v_out[0] = vec_ref[...]
                else:
                    copy_v(number - 1, (partner, x_side, y_side)[number - 1]).wait_recv()
                    v_out[number] = v_out[number - 1] + v_in[number - 1]
                copy_v(number, device).start()

        @pl.when(i == 3)
        def _():
            copy_v(2, y_side).wait_recv()
            v_out[3] = v_out[2] + v_in[2]

            @pl.when(outer)
            def _():
                copy_v(3, inward).start()

        @pl.when((i == 4) & inner)
        def _():
            copy_v(3, inward).wait_recv()
            v_out[4] = v_out[3] + v_in[3]
            copy_v(4, across).start()

        @pl.when((i == 5) & inner)
        def _():
            copy_v(4, across).wait_recv()
            v_out[5] = v_out[4] + v_in[4]
            copy_v(5, outward).start()
            vec_out[...] = v_out[5]

        @pl.when((i == 7) & outer)
        def _():
            copy_v(5, outward).wait_recv()
            vec_out[...] = v_in[5]

        return 0

    lax.fori_loop(0, count + LAGS[4], step, 0)

    stores = []
    for number, (out, row, rows, column, columns) in enumerate(spots):
        stores.append(
            pltpu.make_async_copy(
                z_one.at[extra + number, pl.ds(0, rows), pl.ds(0, columns)],
                outs[out].at[pl.ds(row, rows), pl.ds(column, columns)],
                store_sem.at[number],
            )
        )
    for number in range(2 * extra):
        stores.append(
            pltpu.make_async_copy(
                z_one.at[number // 2, pl.ds(number % 2 * HALF_ROWS, HALF_ROWS)],
                dec_out.at[:, pl.ds(number * UNIT, UNIT)],
                store_sem.at[count + number],
            )
        )
    for store in stores:
        store.start()
    for u in range(count - a_out.shape[0], count):
        for side in range(2):
            copy_a(u, side).wait_send()
    for u in range(count - b_out.shape[0], count):
        for side in range(2):
            copy_b(u, side).wait_send()
    for number, device in enumerate((partner, x_side, y_side)):
        copy_v(number, device).wait_send()

    for store in stores:
        store.wait()

    @pl.when(outer)
    def _():
        copy_v(3, inward).wait_send()

        def drain(u, _):
            copy_in(u).wait_send()
            return 0

        lax.fori_loop(0, count + extra, drain, 0)

    @pl.when(inner)
    def _():
        copy_v(4, across).wait_send()
        copy_v(5, outward).wait_send()

        def drain(u, _):
            copy_across(u).wait_send()
            copy_out(u).wait_send()
            return 0

        lax.fori_loop(0, count + extra, drain, 0)


def sum_products(blocks, units, spots, shapes, lefts, rights, dec, vec):
    count, depth = len(units), rights[0].shape[0]
    extra = dec.shape[1] // (2 * UNIT)
    full = count + extra
    lefts = [a.reshape(4, 2, a.shape[0] // 8, depth) for a in lefts]
    slots = 3
    dma = pltpu.SemaphoreType.DMA
    return pl.pallas_call(
        partial(sum_kernel, blocks, units, spots),
        out_shape=tuple(jax.ShapeDtypeStruct(shape, BF) for shape in (*shapes, dec.shape))
        + (jax.ShapeDtypeStruct(vec.shape, F32),),
        in_specs=[pl.BlockSpec(memory_space=pltpu.VMEM)] * 2
        + [pl.BlockSpec(memory_space=pl.ANY)] * (len(lefts) + len(rights)),
        out_specs=(pl.BlockSpec(memory_space=pl.ANY),) * (len(shapes) + 1)
        + (pl.BlockSpec(memory_space=pltpu.VMEM),),
        scratch_shapes=[
            pltpu.VMEM((len(blocks), 4, ROWS, depth), BF),
            pltpu.VMEM((len(blocks), 4, ROWS, depth), BF),
            pltpu.VMEM((count, depth, UNIT), BF),
            pltpu.VMEM((count, depth, UNIT), BF),
            pltpu.VMEM((slots, 2, 2, ROWS, HALF), BF),
            pltpu.VMEM((count, 2, 2, ROWS, HALF), BF),
            pltpu.VMEM((slots, 2, ROWS, HALF), BF),
            pltpu.VMEM((count, 2, ROWS, HALF), BF),
            pltpu.VMEM((4, ROWS, UNIT), F32),
            pltpu.VMEM((full, ROWS, UNIT), BF),
            pltpu.VMEM((full, ROWS, UNIT), BF),
            pltpu.VMEM((full, ROWS, UNIT), BF),
            pltpu.VMEM((6, *vec.shape), F32),
            pltpu.VMEM((6, *vec.shape), F32),
            dma((len(blocks), 3)),
            dma((count, 3)),
            dma((slots, 2)),
            dma((count, 2)),
            dma((slots, 2)),
            dma((count, 2)),
            dma((full, 2)),
            dma((full, 2)),
            dma((6,)),
            dma((6,)),
            dma((count + 2 * extra,)),
        ],
        compiler_params=pltpu.CompilerParams(
            collective_id=0, has_side_effects=True, vmem_limit_bytes=58 * 2**20
        ),
        cost_estimate=pl.CostEstimate(
            flops=8 * 2 * count * ROWS * UNIT * depth,
            bytes_accessed=300 * 2**20,
            transcendentals=0,
        ),
    )(vec, dec, *lefts, *rights)


def encoder_pieces(shapes):
    (own, width), (rows, _), (tall, _) = shapes
    pieces = [(0, 0, own, 0, width, 0)]
    pieces += [(1, 0, rows, n * D, D, (1, 2, 0)[n]) for n in range(3)]
    pieces += [(1, 0, rows, 3 * D, D, 1)]
    pieces += [(1, 0, rows, 4 * D + n * D, D, (2, 0, 1, 2)[n]) for n in range(FF // D)]
    pieces += [(2, n * rows, rows, 0, D, (0, 1, 2, 0)[n]) for n in range(tall // rows)]
    pieces += [(1, 0, rows, 4 * D + FF, DD, 0)]
    return pieces


def norm_rows(h, gain):
    mean = jnp.mean(h, -1, keepdims=True)
    cent = h - mean
    var = jnp.mean(cent * cent, -1, keepdims=True)
    return (cent * lax.rsqrt(var + EPS) * gain).astype(BF)


def encoder_kernel(
    picked_ref,
    stats_ref,
    pos_ref,
    bias_ref,
    gains_ref,
    embed_ref,
    wide_ref,
    down_ref,
    wide_out,
    down_out,
    stats_out,
    inputs_ref,
    start_ref,
    a_ref,
    qkv_ref,
    mixed_ref,
    middle_ref,
    b_ref,
    slope_ref,
    hidden_ref,
    end_ref,
    z_ref,
    seen_ref,
    w_embed,
    w_wide,
    w_down,
    v_in,
    v_out,
    load_sem,
    store_sem,
    send_sem,
    recv_sem,
    v_send,
    v_recv,
):
    shards, gathered = (embed_ref, wide_ref, down_ref), (w_embed, w_wide, w_down)
    pieces = encoder_pieces([ref.shape for ref in shards])
    count = len(pieces)
    z, f = lax.axis_index("dp"), lax.axis_index("fsdp")
    core, place = f % 2, f // 2
    x, y = place % 2, place // 2
    f_x, f_y, f_far = f + 2 - 4 * x, f + 4 - 8 * y, f + 6 - 4 * x - 8 * y
    partner = (z, f + 1 - 2 * core)
    x_side, y_side, z_side = (z, f_x), (z, f_y), (z + 1 - 2 * (z % 2), f)
    outer = (z == 0) | (z == 3)
    inner = (z == 1) | (z == 2)
    across = (3 - z, f)

    barrier = pltpu.get_barrier_semaphore()
    for device in (partner, x_side, y_side, z_side):
        pl.semaphore_signal(barrier, inc=1, device_id=device, device_id_type=MESH)

    @pl.when(outer)
    def _():
        pl.semaphore_wait(barrier, 4)

    @pl.when(inner)
    def _():
        pl.semaphore_signal(barrier, inc=1, device_id=across, device_id_type=MESH)
        pl.semaphore_wait(barrier, 5)

    loads = [
        pltpu.make_async_copy(shard, whole.at[f], load_sem.at[n])
        for n, (shard, whole) in enumerate(zip(shards, gathered))
    ]
    for load in loads:
        load.start()

    def spot(t, owner, half=None):
        array, row, rows, column, columns, _ = pieces[t]
        if half is not None:
            columns //= 2
            column += half * columns
        return gathered[array].at[owner, pl.ds(row, rows), pl.ds(column, columns)]

    def move(t, owner, send, recv, device, half=None):
        target = spot(t, owner, half)
        source = target
        if send < 3:
            array, row, rows, column, columns, _ = pieces[t]
            source = shards[array].at[pl.ds(row, rows), pl.ds(column, columns)]
        return put(source, target, send_sem.at[t, send], recv_sem.at[t, recv], device)

    def own_x(t):
        return move(t, f, 0, 0, x_side)

    def own_y(t):
        return move(t, f, 1, 1, y_side)

    def own_core(t):
        return move(t, f, 2, 4, partner)

    def far_x(t):
        return move(t, f_y, 3, 2, x_side, 0)

    def far_y(t):
        return move(t, f_x, 4, 3, y_side, 1)

    def to_core(t, n):
        return move(t, (f_x, f_y, f_far)[n], 5 + n, 5 + n, partner)

    def to_z(t, n):
        return move(t, (f_x, f_y, f_far)[n], 8 + n, 8 + n, z_side)

    def brings(t, then, other=None):
        kind = pieces[t][5]
        if kind == 0:
            then()
            return
        pl.when(z % 2 == kind - 1)(then)
        if other is not None:
            pl.when(z % 2 != kind - 1)(other)

    def first(t):
        own_core(t).start()

        def then():
            own_x(t).start()
            own_y(t).start()

        brings(t, then)

    def second(t):
        def then():
            own_x(t).wait_recv()
            far_y(t).start()
            own_y(t).wait_recv()
            far_x(t).start()
            for n in range(2):
                to_core(t, n).start()
                if pieces[t][5]:
                    to_z(t, n).start()

        brings(t, then)

    def third(t):
        def then():
            far_x(t).wait_recv()
            far_y(t).wait_recv()
            to_core(t, 2).start()
            if pieces[t][5]:
                to_z(t, 2).start()

        brings(t, then)

    def taken(t, n):
        def other():
            to_z(t, n).wait_recv()
            to_core(t, n).start()

        brings(t, lambda: None, other)

    def whole(t):
        own_core(t).wait_recv()
        for n in range(3):
            to_core(t, n).wait_recv()

    def drain(t):
        own_core(t).wait_send()
        for n in range(3):
            to_core(t, n).wait_send()

        def then():
            for copy in (own_x(t), own_y(t), far_x(t), far_y(t)):
                copy.wait_send()
            if pieces[t][5]:
                for n in range(3):
                    to_z(t, n).wait_send()

        brings(t, then)

    def copy_v(step, device):
        return put(v_out.at[step], v_in.at[step], v_send.at[step], v_recv.at[step], device)

    sides = (partner, x_side, y_side)

    def statistics(i):
        if i <= 3:
            if i == 0:
                v_out[0] = stats_ref[...]
            else:
                copy_v(i - 1, sides[i - 1]).wait_recv()
                v_out[i] = v_out[i - 1] + v_in[i - 1]
            if i < 3:
                copy_v(i, sides[i]).start()
            else:

                @pl.when(outer)
                def _():
                    copy_v(3, z_side).start()

        if i == 4:

            @pl.when(inner)
            def _():
                copy_v(3, z_side).wait_recv()
                v_out[4] = v_out[3] + v_in[3]
                copy_v(4, across).start()

        if i == 5:

            @pl.when(inner)
            def _():
                copy_v(4, across).wait_recv()
                v_out[5] = v_out[4] + v_in[4]
                copy_v(5, z_side).start()
                stats_out[...] = v_out[5]

            @pl.when(outer)
            def _():
                copy_v(5, z_side).wait_recv()
                stats_out[...] = v_in[5]

    def columns_of(t):
        array, row, rows, column, columns, _ = pieces[t]
        weight = gathered[array][:, row : row + rows, column : column + columns]
        return weight.reshape(-1, columns)

    def embed_step():
        pixels = stats_out[6:7, :] * (PATCH * PATCH)
        for band in range(BANDS):
            mean = stats_out[band : band + 1, :] / pixels
            var = stats_out[BANDS + band : BANDS + band + 1, :] / pixels - mean * mean
            rate = lax.rsqrt(var + EPS)
            for part in range(PATCH * PATCH // LANES):
                lanes = pl.ds(band * PATCH * PATCH + part * LANES, LANES)
                inputs_ref[:, lanes] = ((picked_ref[:, lanes] - mean) * rate).astype(BF)
        start_ref[...] = matmul(inputs_ref[...], columns_of(0)) + pos_ref[...]
        a_ref[...] = norm_rows(start_ref[...], gains_ref[0:1, :])

    def qkv_step(n):
        qkv_ref[:, n * D : (n + 1) * D] = matmul(a_ref[...], columns_of(1 + n)).astype(BF)

    def attention_step():
        size = D // HEADS
        lane_head = lax.broadcasted_iota(jnp.int32, (VIS, LANES), 1) // size

        def group(g, _):
            query, keys, values = [
                qkv_ref[:, pl.ds(pl.multiple_of(n * D + g * LANES, LANES), LANES)] for n in range(3)
            ]
            mixed = jnp.zeros((VIS, LANES), F32)
            for j in range(LANES // size):
                one = jnp.where(lane_head == j, query.astype(F32), 0.0).astype(BF)
                scores = right_t(one, keys) * size ** (-0.5) + bias_ref[...]
                probs = jnp.exp(scores - jnp.max(scores, -1, keepdims=True))
                probs = probs * (1.0 / jnp.sum(probs, -1, keepdims=True))
                mixed = jnp.where(lane_head == j, matmul(probs.astype(BF), values), mixed)
            mixed_ref[:, pl.ds(pl.multiple_of(g * LANES, LANES), LANES)] = mixed.astype(BF)
            return 0

        lax.fori_loop(0, D // LANES, group, 0)

    def out_step():
        middle_ref[...] = start_ref[...] + matmul(mixed_ref[...], columns_of(4))
        b_ref[...] = norm_rows(middle_ref[...], gains_ref[1:2, :])

    def up_step(n):
        columns = slice(n * D, (n + 1) * D)
        after, slope = gelu_parts(matmul(b_ref[...], columns_of(5 + n)))
        hidden_ref[:, columns] = after.astype(BF)
        slope_ref[:, columns] = slope

    def down_step(n):
        rows, owners = w_wide.shape[1], w_down.shape[0]
        tall = w_down.shape[1]
        parts = [hidden_ref[:, o * tall + n * rows : o * tall + (n + 1) * rows] for o in range(owners)]
        total = matmul(jnp.concatenate(parts, 1), columns_of(9 + n))
        end_ref[...] = (middle_ref[...] if n == 0 else end_ref[...]) + total

    def link_step():
        z_ref[...] = norm_rows(end_ref[...], gains_ref[2:3, :])
        seen_ref[...] = matmul(z_ref[...], columns_of(count - 1))

    work = [(6, 0, embed_step), (6, 1, partial(qkv_step, 0)), (7, 2, partial(qkv_step, 1))]
    work += [(8, 3, partial(qkv_step, 2)), (8, None, attention_step), (9, 4, out_step)]
    work += [(at, 5 + n, partial(up_step, n)) for n, at in enumerate((10, 10, 12, 13))]
    work += [(at, 9 + n, partial(down_step, n)) for n, at in enumerate((13, 15, 16, 16))]
    work += [(17, count - 1, link_step)]
    stores = []

    for load in loads:
        load.wait()
    first(0)
    first(1)
    for i in range(18):
        if i + 2 < count:
            first(i + 2)
        statistics(i)
        if i < count:
            second(i)
        if 0 <= i - 1 < count:
            third(i - 1)
        if 0 <= i - 3 < count:
            taken(i - 3, 0)
            taken(i - 3, 1)
        if 0 <= i - 4 < count:
            taken(i - 4, 2)
        for at, piece, run in work:
            if at != i:
                continue
            if piece is not None:
                whole(piece)
                array, row, rows, column, columns, _ = pieces[piece]
                if array:
                    where = (slice(None), pl.ds(row, rows), pl.ds(column, columns))
                    store = pltpu.make_async_copy(
                        gathered[array].at[where],
                        (None, wide_out, down_out)[array].at[where],
                        store_sem.at[piece],
                    )
                    store.start()
                    stores.append(store)
            run()
    for store in stores:
        store.wait()
    for t in range(count):
        drain(t)
    for step in range(3):
        copy_v(step, sides[step]).wait_send()

    @pl.when(outer)
    def _():
        copy_v(3, z_side).wait_send()

    @pl.when(inner)
    def _():
        copy_v(4, across).wait_send()
        copy_v(5, z_side).wait_send()


def encoder_forward(picked, stats, pos, bias, gains, embed, wide, down):
    owners = lax.axis_size("fsdp")
    shapes = [w.shape for w in (embed, wide, down)]
    count = len(encoder_pieces(shapes))
    full = [jax.ShapeDtypeStruct((owners, *shape), BF) for shape in shapes[1:]]
    local = [
        jax.ShapeDtypeStruct((8, LANES), F32),
        jax.ShapeDtypeStruct((VIS, PD), BF),
        jax.ShapeDtypeStruct((VIS, D), F32),
        jax.ShapeDtypeStruct((VIS, D), BF),
        jax.ShapeDtypeStruct((VIS, 3 * D), BF),
        jax.ShapeDtypeStruct((VIS, D), BF),
        jax.ShapeDtypeStruct((VIS, D), F32),
        jax.ShapeDtypeStruct((VIS, D), BF),
        jax.ShapeDtypeStruct((VIS, FF), F32),
        jax.ShapeDtypeStruct((VIS, FF), BF),
        jax.ShapeDtypeStruct((VIS, D), F32),
        jax.ShapeDtypeStruct((VIS, D), BF),
        jax.ShapeDtypeStruct((VIS, DD), F32),
    ]
    vmem, anywhere = pl.BlockSpec(memory_space=pltpu.VMEM), pl.BlockSpec(memory_space=pl.ANY)
    dma = pltpu.SemaphoreType.DMA
    wide_full, down_full, *rest = pl.pallas_call(
        encoder_kernel,
        out_shape=(*full, *local),
        in_specs=[vmem] * 5 + [anywhere] * 3,
        out_specs=(anywhere,) * 2 + (vmem,) * len(local),
        scratch_shapes=[pltpu.VMEM((owners, *shape), BF) for shape in shapes]
        + [
            pltpu.VMEM((6, 8, LANES), F32),
            pltpu.VMEM((6, 8, LANES), F32),
            dma((3,)),
            dma((count,)),
            dma((count, 11)),
            dma((count, 11)),
            dma((6,)),
            dma((6,)),
        ],
        compiler_params=pltpu.CompilerParams(
            collective_id=1, has_side_effects=True, vmem_limit_bytes=56 * 2**20
        ),
        cost_estimate=pl.CostEstimate(
            flops=2 * VIS * 14 * 2**20, bytes_accessed=200 * 2**20, transcendentals=0
        ),
    )(picked, stats, pos, bias, gains, embed, wide, down)
    return (wide_full.reshape(D, -1), down_full.reshape(FF, D), *rest)


LOWP = 256
HEADP = PD + LOWP
BLOCK = HID // 2


def normalize(h):
    cent = h - jnp.mean(h, -1, keepdims=True)
    rate = lax.rsqrt(jnp.mean(cent * cent, -1, keepdims=True) + EPS)
    return cent * rate, rate


def normalize_back(unit, rate, gain, grad):
    scaled = grad * gain
    along = jnp.mean(scaled * unit, -1, keepdims=True)
    dh = rate * (scaled - jnp.mean(scaled, -1, keepdims=True) - unit * along)
    return dh, jnp.sum(grad * unit, 0, keepdims=True)


def exact_product(array, weight):
    high = array.astype(BF)
    rest = array - high.astype(F32)
    mid = rest.astype(BF)
    low = (rest - mid.astype(F32)).astype(BF)
    return matmul(high, weight) + matmul(mid, weight) + matmul(low, weight)


def decoder_kernel(
    owners,
    pos_ref,
    seen_ref,
    kept_ref,
    flag_ref,
    picked_ref,
    stats_ref,
    bias_ref,
    gains_ref,
    pool_ref,
    spread_ref,
    wide_ref,
    down_ref,
    grads_ref,
    dy_ref,
    vec_ref,
    y_ref,
    a_ref,
    q_ref,
    k_ref,
    v_ref,
    mixed_t,
    mixed_ref,
    lse_ref,
    head_ref,
    b_ref,
    hidden_ref,
    z_ref,
    dpred_ref,
    dbranch_ref,
    dbefore_ref,
    dattn_ref,
    dmixed_ref,
    dmiddle_ref,
    dq_ref,
    dk_ref,
    dv_ref,
    loss_ref,
):
    size = DD // DHEADS
    per = LANES // size
    factor = size ** (-0.5)
    gain_one, gain_two, gain_out = [gains_ref[n : n + 1, :] for n in range(3)]
    token = gains_ref[3:4, :]
    lane_head = lax.broadcasted_iota(jnp.int32, (HID, LANES), 1) // size
    key_head = lax.broadcasted_iota(jnp.int32, (TOK_DEV, LANES), 1) // size
    vec_ref[...] = jnp.zeros_like(vec_ref)
    loss_ref[...] = jnp.zeros_like(loss_ref)
    head_ref[...] = jnp.zeros_like(head_ref)
    head_ref[:, : PD + LOWD] = wide_ref[:, 4 * DD + DFF :]

    def project(rows, with_query):
        a = (normalize(y_ref[rows, :])[0] * gain_one).astype(BF)
        a_ref[rows, :] = a
        k_ref[rows, :] = matmul(a, wide_ref[:, DD : 2 * DD]).astype(BF)
        v_ref[rows, :] = matmul(a, wide_ref[:, 2 * DD : 3 * DD]).astype(BF)
        return a

    y_ref[:VIS, :] = pos_ref[:VIS, :] + jnp.where(kept_ref[...] > 0, seen_ref[...], token)
    y_ref[VIS:, :] = pos_ref[VIS:, :] + token
    project(slice(0, VIS), False)

    def hidden_rows(n):
        start = pl.multiple_of(n * BLOCK, BLOCK)
        return pl.ds(start, BLOCK), pl.ds(pl.multiple_of(start + VIS, 32), BLOCK)

    def project_hidden(n, _):
        rows, all_rows = hidden_rows(n)
        a = project(all_rows, True)
        q_ref[rows, :] = matmul(a, wide_ref[:, :DD]).astype(BF)
        return 0

    lax.fori_loop(0, 2, project_hidden, 0)

    def only(array, head_of, j):
        return jnp.where(head_of == j, array.astype(F32), 0.0).astype(BF)

    def attend_group(g, _):
        lanes = pl.ds(pl.multiple_of(g * LANES, LANES), LANES)
        keys, query = k_ref[:, lanes], q_ref[:, lanes]
        values_t = v_ref[:, lanes].T
        for j in range(per):
            scores = right_t(keys, only(query, lane_head, j)) * factor + bias_ref[...]
            top = jnp.max(scores, 0, keepdims=True)
            probs = jnp.exp(scores - top)
            total = jnp.sum(probs, 0, keepdims=True)
            probs = (probs * (1.0 / total)).astype(BF)
            rows = slice(j * size, (j + 1) * size)
            mixed_t[g, rows, :] = matmul(values_t[rows, :], probs).astype(BF)
            lse_ref[g, j : j + 1, :] = top + jnp.log(total)
        mixed_ref[:, lanes] = mixed_t[g].T
        return 0

    lax.fori_loop(0, DD // LANES, attend_group, 0)

    pixels = stats_ref[6:7, :] * (PATCH * PATCH)
    flagged = stats_ref[7:8, 0:1]

    def follow(n, _):
        rows, all_rows = hidden_rows(n)
        middle = y_ref[all_rows, :] + matmul(mixed_ref[rows, :], wide_ref[:, 3 * DD : 4 * DD])
        unit_b, rate_b = normalize(middle)
        b = (unit_b * gain_two).astype(BF)
        b_ref[rows, :] = b
        after, slope = gelu_parts(matmul(b, wide_ref[:, 4 * DD : 4 * DD + DFF]))
        hidden_ref[rows, :] = after.astype(BF)
        unit_z, rate_z = normalize(middle + matmul(hidden_ref[rows, :], down_ref[...]))
        z = (unit_z * gain_out).astype(BF)
        z_ref[rows, :] = z
        pred = matmul(z, head_ref[...])
        parts = []
        for part in range(PD // LANES):
            band = part * LANES // (PATCH * PATCH)
            mean = stats_ref[band : band + 1, :] / pixels
            var = stats_ref[BANDS + band : BANDS + band + 1, :] / pixels - mean * mean
            lanes = slice(part * LANES, (part + 1) * LANES)
            parts.append((picked_ref[rows, lanes] - mean) * lax.rsqrt(var + EPS))
        normed = jnp.concatenate(parts, 1)
        coarse = exact_product(normed, pool_ref[...])
        err_high = pred[:, :PD] - (normed - exact_product(coarse, spread_ref[...]))
        err_low = pred[:, PD:] - coarse
        flag = flag_ref[rows, :]
        length = jnp.sqrt(err_high * err_high + 1.0)
        loss_ref[:, :PD] += jnp.sum((length - 1.0) * flag, 0, keepdims=True) * (1.0 / PD)
        loss_ref[:, PD:] += jnp.sum(err_low * err_low * flag, 0, keepdims=True) * (1.0 / LOWD)
        share = flag / flagged
        dpred_ref[rows, :PD] = (err_high / length * (share * (1.0 / PD))).astype(BF)
        dpred_ref[rows, PD:] = (err_low * (share * (2.0 / LOWD))).astype(BF)
        dz = right_t(dpred_ref[rows, :], head_ref[...])
        dend, dgain = normalize_back(unit_z, rate_z, gain_out, dz)
        vec_ref[2:3, :] += dgain
        dbranch_ref[rows, :] = dend.astype(BF)
        dhidden = right_t(dbranch_ref[rows, :], down_ref[...])
        dbefore_ref[rows, :] = (dhidden * slope).astype(BF)
        db = right_t(dbefore_ref[rows, :], wide_ref[:, 4 * DD : 4 * DD + DFF])
        dmiddle, dgain = normalize_back(unit_b, rate_b, gain_two, db)
        vec_ref[1:2, :] += dgain
        dmiddle = dmiddle + dend
        dmiddle_ref[rows, :] = dmiddle
        dattn_ref[rows, :] = dmiddle.astype(BF)
        dmixed = right_t(dattn_ref[rows, :], wide_ref[:, 3 * DD : 4 * DD])
        dmixed_ref[rows, :] = dmixed.astype(BF)
        return 0

    lax.fori_loop(0, 2, follow, 0)

    tall = DFF // owners
    rows = DD // owners
    down_grad = left_t(hidden_ref[...], dbranch_ref[...]).astype(BF)
    for owner in range(owners):
        for part in range(tall // rows):
            start = owner * tall + part * rows
            grads_ref[owner * rows : (owner + 1) * rows, part * DD : (part + 1) * DD] = down_grad[
                start : start + rows, :
            ]
    wide = DFF
    for g in range(DD // LANES):
        grads_ref[g * LANES : (g + 1) * LANES, wide + 3 * DD : wide + 4 * DD] = matmul(
            mixed_t[g], dattn_ref[...]
        ).astype(BF)
    grads_ref[:, wide + 4 * DD : wide + 4 * DD + DFF] = left_t(
        b_ref[...], dbefore_ref[...]
    ).astype(BF)
    grads_ref[:, wide + 4 * DD + DFF :] = left_t(z_ref[...], dpred_ref[...]).astype(BF)[
        :, : PD + LOWD
    ]

    def attend_back_group(g, _):
        lanes = pl.ds(pl.multiple_of(g * LANES, LANES), LANES)
        query, keys, values, dout = [r[:, lanes] for r in (q_ref, k_ref, v_ref, dmixed_ref)]
        keys_t = keys.T
        dkeys = jnp.zeros((TOK_DEV, LANES), F32)
        dvalues = jnp.zeros((TOK_DEV, LANES), F32)
        dquery = []
        for j in range(per):
            scores = right_t(keys, only(query, lane_head, j)) * factor + bias_ref[...]
            probs = jnp.exp(scores - lse_ref[g, j : j + 1, :])
            dvalues = jnp.where(key_head == j, matmul(probs.astype(BF), dout), dvalues)
            dprobs = right_t(values, only(dout, lane_head, j))
            delta = jnp.sum(dprobs * probs, 0, keepdims=True)
            dscores = (probs * (dprobs - delta)).astype(BF)
            dkeys = jnp.where(key_head == j, matmul(dscores, query), dkeys)
            dquery.append(matmul(keys_t[j * size : (j + 1) * size, :], dscores))
        dq_ref[:, lanes] = (jnp.concatenate(dquery, 0) * factor).astype(BF).T
        dk_ref[:, lanes] = (dkeys * factor).astype(BF)
        dv_ref[:, lanes] = dvalues.astype(BF)
        return 0

    lax.fori_loop(0, DD // LANES, attend_back_group, 0)

    for n, ref in enumerate((dk_ref, dv_ref)):
        grads_ref[:, wide + (n + 1) * DD : wide + (n + 2) * DD] = left_t(
            a_ref[...], ref[...]
        ).astype(BF)
    grads_ref[:, wide : wide + DD] = left_t(a_ref[VIS:, :], dq_ref[...]).astype(BF)

    def start_rows(rows, da):
        unit, rate = normalize(y_ref[rows, :])
        da = da + right_t(dk_ref[rows, :], wide_ref[:, DD : 2 * DD])
        da = da + right_t(dv_ref[rows, :], wide_ref[:, 2 * DD : 3 * DD])
        dh, dgain = normalize_back(unit, rate, gain_one, da)
        vec_ref[0:1, :] += dgain
        return dh

    dy = start_rows(slice(0, VIS), 0.0)
    dy_ref[...] = dy
    vec_ref[3:4, :] += jnp.sum(jnp.where(kept_ref[...] > 0, 0.0, dy), 0, keepdims=True)

    def start_hidden(n, _):
        rows, all_rows = hidden_rows(n)
        dy = start_rows(all_rows, right_t(dq_ref[rows, :], wide_ref[:, :DD]))
        vec_ref[3:4, :] += jnp.sum(dy + dmiddle_ref[rows, :], 0, keepdims=True)
        return 0

    lax.fori_loop(0, 2, start_hidden, 0)
    vec_ref[4:5, :] = loss_ref[:, :DD] + loss_ref[:, DD:]


def decoder_step(pos, seen, kept, flag, picked, stats, bias, vectors, wide, down):
    index = jnp.arange(PD)
    band, row, column = index // PATCH**2, index // PATCH % PATCH, index % PATCH
    low = band * (PATCH // 2) ** 2 + row // 2 * (PATCH // 2) + column // 2
    spread = low[None, :] == jnp.arange(LOWP)[:, None]
    gains = jnp.pad(vectors.reshape(4, DD), ((0, 4), (0, 0)))
    owners = lax.axis_size("fsdp")
    scratch = [
        ((TOK_DEV, DD), F32),
        ((TOK_DEV, DD), BF),
        ((HID, DD), BF),
        ((TOK_DEV, DD), BF),
        ((TOK_DEV, DD), BF),
        ((DD // LANES, LANES, HID), BF),
        ((HID, DD), BF),
        ((DD // LANES, LANES * DHEADS // DD, HID), F32),
        ((DD, HEADP), BF),
        ((HID, DD), BF),
        ((HID, DFF), BF),
        ((HID, DD), BF),
        ((HID, HEADP), BF),
        ((HID, DD), BF),
        ((HID, DFF), BF),
        ((HID, DD), BF),
        ((HID, DD), BF),
        ((HID, DD), F32),
        ((HID, DD), BF),
        ((TOK_DEV, DD), BF),
        ((TOK_DEV, DD), BF),
        ((1, HEADP), F32),
    ]
    vmem = pl.BlockSpec(memory_space=pltpu.VMEM)
    grads, dy, vec = pl.pallas_call(
        partial(decoder_kernel, owners),
        out_shape=(
            jax.ShapeDtypeStruct((DD, DFF + wide.shape[1]), BF),
            jax.ShapeDtypeStruct((VIS, DD), F32),
            jax.ShapeDtypeStruct((8, DD), F32),
        ),
        in_specs=[vmem] * 12,
        out_specs=(vmem,) * 3,
        scratch_shapes=[pltpu.VMEM(*entry) for entry in scratch],
        compiler_params=pltpu.CompilerParams(vmem_limit_bytes=60 * 2**20),
        cost_estimate=pl.CostEstimate(
            flops=40 * 10**9, bytes_accessed=40 * 2**20, transcendentals=2 * 10**7
        ),
    )(
        pos,
        seen,
        kept.astype(F32)[:, None],
        flag[:, None],
        picked,
        stats,
        bias,
        gains,
        (spread.T * 0.25).astype(BF),
        spread.astype(BF),
        wide,
        down,
    )
    return grads, dy, vec[:3], vec[3], jnp.sum(vec[4])


def block_forward(h, weights, gains, bias, heads, skip):
    wqkv, wout, wup, wdown = weights
    width = h.shape[1]
    normed_a = layer_norm(h, gains[0]).astype(BF)
    query = matmul(normed_a[skip:], wqkv[:, :width]).astype(BF)
    keys = matmul(normed_a, wqkv[:, width : 2 * width]).astype(BF)
    values = matmul(normed_a, wqkv[:, 2 * width :]).astype(BF)
    mixed_t, lse = attend(query.T, keys, values.T, bias, width // heads)
    middle = h[skip:] + left_t(mixed_t, wout)
    normed_b = layer_norm(middle, gains[1]).astype(BF)
    after, slope = gelu_parts(matmul(normed_b, wup))
    hidden = after.astype(BF)
    end = middle + matmul(hidden, wdown)
    return end, (h, normed_a, query, keys, values, mixed_t, lse, middle, normed_b, slope, hidden)


def block_backward(saved, grad, weights, gains, bias, heads, skip):
    wqkv, wout, wup, wdown = weights
    h, normed_a, query, keys, values, mixed_t, lse, middle, normed_b, slope, hidden = saved
    width = h.shape[1]
    dbranch = grad.astype(BF)
    dbefore = (right_t(dbranch, wdown) * slope).astype(BF)
    dmiddle, dgain_two = norm_back(middle, gains[1], right_t(dbefore, wup))
    dmiddle = dmiddle + grad
    dattn = dmiddle.astype(BF)
    dmixed = right_t(dattn, wout).astype(BF)
    dqt, dkeys, dvalues = attend_back(query, keys, values, dmixed, bias, lse, width // heads)
    dquery = dqt.T
    if skip:
        dquery = jnp.pad(dquery, ((skip, 0), (0, 0)))
        dmiddle = jnp.pad(dmiddle, ((skip, 0), (0, 0)))
    dqkv = jnp.concatenate([dquery, dkeys, dvalues], 1)
    dh, dgain_one = norm_back(h, gains[0], right_t(dqkv, wqkv))
    factors = ((normed_a.T, dqkv), (mixed_t, dattn), (normed_b.T, dbefore), (hidden.T, dbranch))
    return (dh + dmiddle, factors, (dgain_one, dgain_two))


def reduce_rows(grad):
    return lax.psum_scatter(grad.astype(BF), "fsdp", scatter_dimension=0, tiled=True)


def sum_gradients(factors, encoded, dseen, inputs, dh_low, dec, vector_grad, local_loss):
    lefts = [pair[0] for pair in factors] + [encoded.T]
    owners = lax.axis_size("fsdp")
    own = PD // owners
    first = inputs.T.reshape(owners, own, VIS)
    lefts.append(jnp.pad(first, ((0, 0), (0, ROWS - own), (0, 0))).reshape(-1, VIS))
    rights = [pair[1] for pair in factors] + [dseen, dh_low]
    blocks, units, spots = [], [], []

    def add(left, sub, right, out, row, rows, column, columns):
        blocks.append((left, sub))
        for n in range(0, columns, UNIT):
            units.append((len(blocks) - 1, right, n))
            spots.append((out, row, rows, column + n, UNIT))

    add(4, 0, 4, 1, 0, ROWS, 4 * D + FF, DD)
    for n in range(FF // owners // ROWS):
        add(3, n, 3, 2, n * ROWS, ROWS, 0, D)
    add(2, 0, 2, 1, 0, ROWS, 4 * D, FF)
    add(1, 0, 1, 1, 0, ROWS, 3 * D, D)
    add(0, 0, 0, 1, 0, ROWS, 0, 3 * D)
    add(5, 0, 5, 0, 0, own, 0, D)
    shapes = ((own, D), (ROWS, 4 * D + FF + DD), (FF // owners, D))
    length = vector_grad.shape[0]
    rows = -(-(length + 1) // (8 * LANES)) * 8
    vec = jnp.concatenate(
        [vector_grad, local_loss[None], jnp.zeros((rows * LANES - length - 1,), F32)]
    )
    used = dec.shape[1]
    dec = jnp.pad(dec, ((0, 0), (0, -used % (2 * UNIT))))
    *parts, dec, vec = sum_products(
        tuple(blocks), tuple(units), tuple(spots), shapes, lefts, rights, dec, vec.reshape(rows, LANES)
    )
    vec = vec.reshape(-1)
    return parts, dec[:, :used], vec[:length], vec[length]


def enc_split(wide, down):
    return (
        (wide[:, : 3 * D], wide[:, 3 * D : 4 * D], wide[:, 4 * D : 4 * D + FF], down),
        wide[:, 4 * D + FF :],
    )


def advance(weight, mom, avg, grad, rate):
    grad = grad + DECAY * weight
    buf = MOMENTUM * mom + grad
    new = weight - rate * (grad + MOMENTUM * buf)
    return (buf, new, AVERAGE * avg + (1.0 - AVERAGE) * new)


def arrange(valid, masked, scene_ids):
    slots = valid.shape[0]
    live = valid > 0
    kinds = jnp.stack([live & (masked == 0), live & (masked > 0), ~live], 1)
    index = jnp.arange(slots, dtype=jnp.int32)
    ranks = matmul((index[None, :] < index[:, None]).astype(BF), kinds.astype(BF)).astype(jnp.int32)
    n_seen, n_hid = [jnp.sum(kinds[:, i].astype(jnp.int32)) for i in range(2)]
    empty = ranks[:, 2]
    to_empty = jnp.where(empty < VIS - n_seen, n_seen + empty, n_seen + n_hid + empty)
    place = jnp.where(
        kinds[:, 0], ranks[:, 0], jnp.where(kinds[:, 1], VIS + ranks[:, 1], to_empty)
    )
    return (place[None, :] == index[:, None]).astype(BF), n_seen, n_hid


def exact_pick(pick, array):
    high = lax.reduce_precision(array, 8, 7)
    rest = array - high
    mid = lax.reduce_precision(rest, 8, 7)
    low = rest - mid
    return (
        matmul(pick, high.astype(BF)) + matmul(pick, mid.astype(BF)) + matmul(pick, low.astype(BF))
    )


def body(
    pixels,
    masked,
    valid,
    scene_ids,
    gsd_index,
    coords,
    embed,
    wide_enc,
    enc_down,
    wide_dec,
    dec_down,
    vectors,
    embed_mom,
    wide_enc_mom,
    enc_down_mom,
    wide_dec_mom,
    dec_down_mom,
    vector_mom,
    embed_avg,
    wide_enc_avg,
    enc_down_avg,
    wide_dec_avg,
    dec_down_avg,
    vector_avg,
):
    slots = pixels.shape[0]
    fast = (lax.axis_size("dp"), lax.axis_size("fsdp")) == (4, 8)
    w_dec, w_dec_down = [
        lax.all_gather(w.astype(BF), "fsdp", axis=0, tiled=True) for w in (wide_dec, dec_down)
    ]
    rows_ok = valid.astype(jnp.float32)
    flags = rows_ok * masked.astype(jnp.float32)
    bands = pixels.reshape(slots, BANDS, PATCH * PATCH)
    weighted = bands * rows_ok[:, None, None]
    band_sum = jnp.sum(weighted, axis=(0, 2))
    counts = jnp.stack([jnp.sum(rows_ok), jnp.sum(flags)])
    band_sq = jnp.sum(weighted * bands, axis=(0, 2))
    stats = jnp.concatenate([band_sum, band_sq, counts])

    pick, n_seen, n_hid = arrange(valid, masked, scene_ids)
    picked_pixels = exact_pick(pick, pixels)
    small = matmul(
        pick, jnp.concatenate([(scene_ids % 2)[:, None], coords], 1).astype(BF)
    )
    odd, coord = small[:, 0], small[:, 1:]
    level = jnp.where(odd == 0, gsd_index[0], gsd_index[1]).astype(jnp.float32)
    scale = jnp.exp2(0.5 * level - 1.0)
    index = jnp.arange(slots, dtype=jnp.int32)
    kept = index[:VIS] < n_seen
    hidden_ok = index[:HID] < n_hid
    live = jnp.concatenate([kept, hidden_ok])
    keptf = kept.astype(jnp.float32)[:, None]
    allow = live[:, None] & (odd[:, None] == odd[None, :]) | (index[:, None] == index[None, :])
    bias = jnp.where(allow, 0.0, NEGATIVE)
    bias_enc, bias_dec = bias[:VIS, :VIS], bias[:, VIS:]

    gains_enc = (vectors[:D], vectors[D : 2 * D])
    gain_enc_out = vectors[2 * D : 3 * D]
    pos_enc = positions(coord[:VIS], scale[:VIS], D)
    low_enc = [w.astype(BF) for w in (embed, wide_enc, enc_down)]
    if fast:
        gains = jnp.pad(vectors[: 3 * D].reshape(3, D), ((0, 5), (0, 0)))
        stats = jnp.broadcast_to(stats[:, None], (8, LANES))
        w_enc, w_enc_down, stats, inputs, h_start, *saved, h_end, encoded, seen_out = encoder_forward(
            picked_pixels[:VIS], stats, pos_enc, bias_enc.T, gains, *low_enc
        )
        normed_a, qkv, mixed, *saved = saved
        enc_saved = (h_start, normed_a, *jnp.split(qkv, 3, 1), mixed.T, None, *saved)
        enc_weights, w_link = enc_split(w_enc, w_enc_down)
    else:
        stats = jnp.broadcast_to(lax.psum(stats, ("dp", "fsdp"))[:, None], (8, LANES))
    count = stats[7, 0]
    if not fast:
        w_embed, w_enc, w_enc_down = [
            lax.all_gather(w, "fsdp", axis=0, tiled=True) for w in low_enc
        ]
        enc_weights, w_link = enc_split(w_enc, w_enc_down)
        mean = jnp.repeat(stats[:3, 0] / (stats[6, 0] * (PATCH * PATCH)), PATCH * PATCH)
        square = jnp.repeat(stats[3:6, 0] / (stats[6, 0] * (PATCH * PATCH)), PATCH * PATCH)
        rate = lax.rsqrt(square - mean * mean + EPS)
        inputs = ((picked_pixels[:VIS] - mean) * rate).astype(BF)
        h_start = matmul(inputs, w_embed) + pos_enc
        h_end, enc_saved = block_forward(h_start, enc_weights, gains_enc, bias_enc, HEADS, 0)
        encoded = layer_norm(h_end, gain_enc_out).astype(BF)
        seen_out = matmul(encoded, w_link)
    pos_dec = positions(coord, scale, DD)
    dec_grads, dy_seen, dgains_dec, dtoken, local_loss = decoder_step(
        pos_dec,
        seen_out,
        kept,
        hidden_ok.astype(F32),
        picked_pixels[VIS:],
        stats,
        bias_dec,
        vectors[3 * D :],
        w_dec,
        w_dec_down,
    )
    dec_sum = reduce_rows(dec_grads)
    dseen = (dy_seen * keptf).astype(BF)
    dh_end, dgain_enc_out = norm_back(h_end, gain_enc_out, right_t(dseen, w_link))
    dh_start, enc_factors, dgains_enc = block_backward(
        enc_saved, dh_end, enc_weights, gains_enc, bias_enc, HEADS, 0
    )
    dh_low = dh_start.astype(BF)
    vector_grad = jnp.concatenate(
        [
            dgains_enc[0],
            dgains_enc[1],
            dgain_enc_out,
            dgains_dec.reshape(-1),
            dtoken,
        ]
    )
    if fast:
        enc_parts, dec_sum, vector_grad, loss_sum = sum_gradients(
            enc_factors, encoded, dseen, inputs, dh_low, dec_sum, vector_grad, local_loss
        )
    else:
        enc_grads = [matmul(*pair).astype(BF) for pair in enc_factors]
        link_grad = left_t(encoded, dseen).astype(BF)
        enc_parts = lax.psum(
            (
                reduce_rows(left_t(inputs, dh_low)),
                reduce_rows(
                    jnp.concatenate([enc_grads[0], enc_grads[1], enc_grads[2], link_grad], 1)
                ),
                reduce_rows(enc_grads[3]),
            ),
            "dp",
        )
        vector_grad, loss_sum = lax.psum((vector_grad, local_loss), ("dp", "fsdp"))
        dec_sum = lax.psum(dec_sum, "dp")
    rows = dec_sum.shape[0]
    down = dec_sum[:, :DFF].reshape(rows, -1, DD).transpose(1, 0, 2).reshape(-1, DD)
    dec_parts = (dec_sum[:, DFF:], down)
    shard_grads = [g.astype(F32) for g in (*enc_parts, *dec_parts)]
    rate = STEP_UNIT * (PD * TOK_DEV * lax.axis_size("dp") * lax.axis_size("fsdp")) ** 0.5
    weights = (embed, wide_enc, enc_down, wide_dec, dec_down)
    moms = (embed_mom, wide_enc_mom, enc_down_mom, wide_dec_mom, dec_down_mom)
    avgs = (embed_avg, wide_enc_avg, enc_down_avg, wide_dec_avg, dec_down_avg)
    outs = []
    for number in range(5):
        buf, new, avg = advance(
            weights[number], moms[number], avgs[number], shard_grads[number], rate
        )
        outs += [buf, new, avg, new.astype(jnp.bfloat16)]
    return (*outs, *advance(vectors, vector_mom, vector_avg, vector_grad, rate), loss_sum, count)


def solution(mesh):
    both, rows = P(("dp", "fsdp")), P("fsdp", None)
    placed = (P(("dp", "fsdp"), None), both, both, both, both, P(("dp", "fsdp"), None))
    states = (rows,) * 5 + (P(),)
    return jax.shard_map(
        body,
        mesh=mesh,
        in_specs=placed + states * 3,
        out_specs=(rows,) * 20 + (P(),) * 5,
        check_vma=False,
    )
```

```python
from functools import partial

import jax
import jax.numpy as jnp
from jax import lax
from jax.experimental import pallas as pl
from jax.experimental.pallas import tpu as pltpu
from jax.sharding import PartitionSpec as P

D = 1024
HEADS = 16
FF = 4096
DD = 512
DHEADS = 16
DFF = 2048
PATCH = 16
BANDS = 3
TOK_DEV = 768
PD = 768
LOWD = 192
VIS = 192
HID = TOK_DEV - VIS

EPS = 1e-06
MOMENTUM = 0.9
DECAY = 0.0001
AVERAGE = 0.9
STEP_UNIT = 0.003
NEGATIVE = -1e30
LANES = 128
BF = jnp.bfloat16
F32 = jnp.float32


def matmul(left, right):
    return jnp.dot(left, right, preferred_element_type=jnp.float32)


def left_t(left, right):
    return lax.dot_general(
        left, right, (((0,), (0,)), ((), ())), preferred_element_type=jnp.float32
    )


def right_t(left, right):
    return lax.dot_general(
        left, right, (((1,), (1,)), ((), ())), preferred_element_type=jnp.float32
    )


def layer_norm(h, gain):
    mean = jnp.mean(h, -1, keepdims=True)
    cent = h - mean
    var = jnp.mean(cent * cent, -1, keepdims=True)
    return cent * lax.rsqrt(var + EPS) * gain


def norm_back(h, gain, grad):
    result, pull = jax.vjp(layer_norm, h, gain)
    return pull(grad)


def gelu_parts(before):
    below = 0.5 * (1.0 + lax.erf(before * 0.5**0.5))
    slope = below + before * jnp.exp(before * before * -0.5) * (0.5 / jnp.pi) ** 0.5
    return before * below, slope


def positions(coord, scale, width):
    quarter = width // 4
    omega = 10000.0 ** (-jnp.arange(quarter, dtype=jnp.float32) / quarter)
    angle_x = coord[:, 0:1] * scale[:, None] * omega[None, :]
    angle_y = coord[:, 1:2] * scale[:, None] * omega[None, :]
    return jnp.concatenate(
        [jnp.sin(angle_x), jnp.cos(angle_x), jnp.sin(angle_y), jnp.cos(angle_y)], -1
    )


def row_loss(pred, normed):
    rows = normed.shape[0]
    coarse = jnp.mean(normed.reshape(rows, BANDS, PATCH // 2, 2, PATCH // 2, 2), axis=(3, 5))
    upper = jnp.repeat(jnp.repeat(coarse, 2, axis=2), 2, axis=3).reshape(rows, PD)
    err_high = pred[:, :PD] - (normed - upper)
    err_low = pred[:, PD:] - coarse.reshape(rows, LOWD)
    return jnp.mean(jnp.sqrt(err_high * err_high + 1.0) - 1.0, -1) + jnp.mean(err_low * err_low, -1)


def attend_kernel(size, qt_ref, k_ref, vt_ref, bias_ref, ot_ref, lse_ref):
    per = LANES // size
    row_head = lax.broadcasted_iota(jnp.int32, qt_ref.shape, 0) // size
    factor = size ** (-0.5)
    for j in range(per):
        query = jnp.where(row_head == j, qt_ref[...].astype(F32), 0.0).astype(BF)
        scores = matmul(k_ref[...], query) * factor + bias_ref[...]
        top = jnp.max(scores, 0, keepdims=True)
        probs = jnp.exp(scores - top)
        total = jnp.sum(probs, 0, keepdims=True)
        probs = (probs * (1.0 / total)).astype(BF)
        rows = slice(j * size, (j + 1) * size)
        ot_ref[rows, :] = matmul(vt_ref[rows, :], probs).astype(BF)
        lse_ref[0, j : j + 1, :] = top + jnp.log(total)


def attend(qt, keys, vt, bias, size):
    width, queries = qt.shape
    rows = keys.shape[0]
    groups, per = width // LANES, LANES // size
    return pl.pallas_call(
        partial(attend_kernel, size),
        grid=(groups,),
        out_shape=(
            jax.ShapeDtypeStruct((width, queries), BF),
            jax.ShapeDtypeStruct((groups, per, queries), F32),
        ),
        in_specs=[
            pl.BlockSpec((LANES, queries), lambda g: (g, 0)),
            pl.BlockSpec((rows, LANES), lambda g: (0, g)),
            pl.BlockSpec((LANES, rows), lambda g: (g, 0)),
            pl.BlockSpec((rows, queries), lambda g: (0, 0)),
        ],
        out_specs=(
            pl.BlockSpec((LANES, queries), lambda g: (g, 0)),
            pl.BlockSpec((1, per, queries), lambda g: (g, 0, 0)),
        ),
        compiler_params=pltpu.CompilerParams(vmem_limit_bytes=40 * 2**20),
        cost_estimate=pl.CostEstimate(
            flops=4 * rows * queries * width * per,
            bytes_accessed=4 * rows * queries,
            transcendentals=rows * queries * width // size,
        ),
    )(qt, keys, vt, bias)


def attend_back_kernel(
    size,
    qt_ref,
    q_ref,
    k_ref,
    kt_ref,
    v_ref,
    do_ref,
    dot_ref,
    bias_ref,
    *rest,
):
    *lse_ref, dqt_ref, dk_ref, dv_ref = rest
    per = LANES // size
    row_head = lax.broadcasted_iota(jnp.int32, qt_ref.shape, 0) // size
    lane_head = lax.broadcasted_iota(jnp.int32, dk_ref.shape, 1) // size
    factor = size ** (-0.5)
    dkeys = jnp.zeros(dk_ref.shape, F32)
    dvalues = jnp.zeros(dv_ref.shape, F32)
    for j in range(per):
        query = jnp.where(row_head == j, qt_ref[...].astype(F32), 0.0).astype(BF)
        dout = jnp.where(row_head == j, dot_ref[...].astype(F32), 0.0).astype(BF)
        scores = matmul(k_ref[...], query) * factor + bias_ref[...]
        if lse_ref:
            probs = jnp.exp(scores - lse_ref[0][0, j : j + 1, :])
        else:
            probs = jnp.exp(scores - jnp.max(scores, 0, keepdims=True))
            probs = probs * (1.0 / jnp.sum(probs, 0, keepdims=True))
        dvalues = jnp.where(lane_head == j, matmul(probs.astype(BF), do_ref[...]), dvalues)
        dprobs = matmul(v_ref[...], dout)
        delta = jnp.sum(dprobs * probs, 0, keepdims=True)
        dscores = (probs * (dprobs - delta)).astype(BF)
        dkeys = jnp.where(lane_head == j, matmul(dscores, q_ref[...]), dkeys)
        rows = slice(j * size, (j + 1) * size)
        dqt_ref[rows, :] = (matmul(kt_ref[rows, :], dscores) * factor).astype(BF)
    dk_ref[...] = (dkeys * factor).astype(BF)
    dv_ref[...] = dvalues.astype(BF)


def attend_back(query, keys, values, dmixed, bias, lse, size):
    queries, width = query.shape
    rows = keys.shape[0]
    groups, per = width // LANES, LANES // size
    tall = lambda n: pl.BlockSpec((n, LANES), lambda g: (0, g))
    flat = lambda n: pl.BlockSpec((LANES, n), lambda g: (g, 0))
    return pl.pallas_call(
        partial(attend_back_kernel, size),
        grid=(groups,),
        out_shape=(
            jax.ShapeDtypeStruct((width, queries), BF),
            jax.ShapeDtypeStruct((rows, width), BF),
            jax.ShapeDtypeStruct((rows, width), BF),
        ),
        in_specs=[
            flat(queries),
            tall(queries),
            tall(rows),
            flat(rows),
            tall(rows),
            tall(queries),
            flat(queries),
            pl.BlockSpec((rows, queries), lambda g: (0, 0)),
        ]
        + [pl.BlockSpec((1, per, queries), lambda g: (g, 0, 0))] * (lse is not None),
        out_specs=(flat(queries), tall(rows), tall(rows)),
        compiler_params=pltpu.CompilerParams(vmem_limit_bytes=48 * 2**20),
        cost_estimate=pl.CostEstimate(
            flops=10 * rows * queries * width * per,
            bytes_accessed=4 * rows * queries,
            transcendentals=rows * queries * width // size,
        ),
    )(query.T, query, keys, keys.T, values, dmixed, dmixed.T, bias, *([] if lse is None else [lse]))


MESH = pl.DeviceIdType.MESH
UNIT = 512
HALF = UNIT // 2
ROWS = 128
HALF_ROWS = ROWS // 2
LAGS = (2, 4, 6, 8, 11)


def put(source, target, send, recv, device):
    return pltpu.make_async_remote_copy(
        src_ref=source,
        dst_ref=target,
        send_sem=send,
        recv_sem=recv,
        device_id=device,
        device_id_type=MESH,
    )


def back_kernel(
    dec_units,
    blocks,
    units,
    spots,
    dy_ref,
    kept_ref,
    vec_ref,
    gains_ref,
    bias_ref,
    qkv_ref,
    dec_ref,
    end_ref,
    middle_ref,
    start_ref,
    slope_ref,
    wide_ref,
    down_ref,
    *refs,
):
    n_left = max(b[0] for b in blocks) + 1
    lefts, refs = refs[:n_left], refs[n_left:]
    outs, refs = refs[:5], refs[5:]
    vec_out, refs = refs[0], refs[1:]
    (
        xo,
        xp,
        yo,
        yp,
        do,
        dp,
        products,
        a_out,
        a_in,
        b_out,
        b_in,
        sums,
        z_out,
        z_one,
        z_two,
        v_in,
        v_out,
        wide_buf,
        down_buf,
        slope_buf,
        h_buf,
        dend_ref,
        dmid_ref,
        dbranch_ref,
        dmixed_ref,
        dqkv_ref,
        grad_vec,
        wide_sem,
        down_sem,
        slope_sem,
        h_sem,
        dec_sem,
        left_sem,
        right_sem,
        a_send,
        a_recv,
        b_send,
        b_recv,
        z_send,
        z_recv,
        v_send,
        v_recv,
        store_sem,
    ) = refs
    count = dec_units + len(units)
    z, f = lax.axis_index("dp"), lax.axis_index("fsdp")
    core, place = f % 2, f // 2
    x, y = place % 2, place // 2
    partner = (z, f + 1 - 2 * core)
    x_side = (z, f + 2 - 4 * x)
    y_side = (z, f + 4 - 8 * y)
    at_x, at_y, at_far = place + 1 - 2 * x, place + 2 - 4 * y, 3 - place
    low = z < 2
    outer = (z == 0) | (z == 3)
    inner = (z == 1) | (z == 2)
    inward = (jnp.where(low, 1, 2), f)
    across = (3 - z, f)
    outward = (jnp.where(low, 0, 3), f)

    ring = wide_buf.shape[0]
    up_chunks, out_chunks, qkv_chunks = FF // UNIT, D // UNIT, 3 * D // UNIT
    chunks = 1 + up_chunks + out_chunks + qkv_chunks

    def wide_copy(w):
        inside = jnp.where(w < 1 + up_chunks, 4 * D + UNIT * (w - 1), 3 * D + UNIT * (w - 1 - up_chunks))
        column = jnp.where(
            w == 0,
            4 * D + FF,
            jnp.where(w < 1 + up_chunks + out_chunks, inside, UNIT * (w - 1 - up_chunks - out_chunks)),
        )
        return pltpu.make_async_copy(
            wide_ref.at[:, pl.ds(pl.multiple_of(column, UNIT), UNIT)],
            wide_buf.at[w % ring],
            wide_sem.at[w % ring],
        )

    def down_copy(j):
        rows = pl.ds(pl.multiple_of(j * UNIT, UNIT), UNIT)
        return pltpu.make_async_copy(down_ref.at[rows], down_buf.at[j % 2], down_sem.at[j % 2])

    def slope_copy(j):
        columns = pl.ds(pl.multiple_of(j * UNIT, UNIT), UNIT)
        return pltpu.make_async_copy(slope_ref.at[:, columns], slope_buf.at[j % 2], slope_sem.at[j % 2])

    def h_copy(source):
        return pltpu.make_async_copy(source, h_buf, h_sem.at[0])

    h_copy(end_ref).start()
    for n in range(ring):
        wide_copy(n).start()
    for n in range(2):
        down_copy(n).start()
        slope_copy(n).start()

    barrier = pltpu.get_barrier_semaphore()
    for device in (partner, x_side, y_side):
        pl.semaphore_signal(barrier, inc=1, device_id=device, device_id_type=MESH)

    @pl.when(outer)
    def _():
        pl.semaphore_signal(barrier, inc=1, device_id=inward, device_id_type=MESH)
        pl.semaphore_wait(barrier, 4)

    @pl.when(inner)
    def _():
        pl.semaphore_signal(barrier, inc=1, device_id=across, device_id_type=MESH)
        pl.semaphore_signal(barrier, inc=1, device_id=outward, device_id_type=MESH)
        pl.semaphore_wait(barrier, 5)

    def swap_dec(source, n):
        return put(source, dp.at[n], dec_sem.at[n, 1], dec_sem.at[n, 2], partner)

    def swap_left(source, b):
        return put(source, xp.at[b], left_sem.at[b, 1], left_sem.at[b, 2], partner)

    def swap_right(r):
        return put(yo.at[r], yp.at[r], right_sem.at[r, 0], right_sem.at[r, 1], partner)

    for n in range(dec_units):
        swap_dec(dec_ref.at[:, 1 - core, n], n).start()
        pltpu.make_async_copy(dec_ref.at[:, core, n], do.at[n], dec_sem.at[n, 0]).start()
    for b, (left, sub) in enumerate(blocks):
        rows = pl.ds(sub * ROWS, ROWS)
        swap_left(lefts[left].at[:, 1 - core, rows], b).start()
        pltpu.make_async_copy(lefts[left].at[:, core, rows], xo.at[b], left_sem.at[b, 0]).start()

    firsts = 1 + out_chunks
    single = next(n for n in range(1, len(units)) if units[n][1] >= firsts)
    starts = [n for n in range(1, len(units)) if units[n][0] != units[n - 1][0]]

    def block_of(e):
        return sum([jnp.where(e >= n, 1, 0) for n in starts], jnp.int32(0))

    def right_of(e):
        early = jnp.where(e == 0, 0, 1 + (e + out_chunks - 1) % out_chunks)
        return jnp.where(e < single, early, e - single + firsts)

    first, second = pl.ds(0, HALF), pl.ds(HALF, HALF)

    def part(u, owner, columns, k):
        @pl.when(u < dec_units)
        def _():
            n = jnp.minimum(u, dec_units - 1)
            products[k] = do[n, owner, :, columns].astype(F32) + dp[n, owner, :, columns].astype(F32)

        @pl.when(u >= dec_units)
        def _():
            e = jnp.maximum(u - dec_units, 0)
            b, r = block_of(e), right_of(e)
            total = matmul(xo[b, owner], yo[r, :, columns])
            products[k] = total + matmul(xp[b, owner], yp[r, :, columns])

        return products[k]

    def copy_a(u, side):
        slot = u % a_out.shape[0]
        return put(
            a_out.at[slot, side],
            a_in.at[u, side],
            a_send.at[slot, side],
            a_recv.at[u, side],
            (x_side, y_side)[side],
        )

    def copy_b(u, side):
        slot = u % b_out.shape[0]
        return put(
            b_out.at[slot, side],
            b_in.at[u, side],
            b_send.at[slot, side],
            b_recv.at[u, side],
            (y_side, x_side)[side],
        )

    z_slots = z_out.shape[0]

    def copy_in(u):
        return put(z_out.at[u % z_slots], z_one.at[u], z_send.at[u, 0], z_recv.at[u, 0], inward)

    def copy_across(u):
        return put(z_out.at[u % z_slots], z_two.at[u], z_send.at[u, 0], z_recv.at[u, 1], across)

    def copy_out(u):
        return put(z_one.at[u], z_one.at[u], z_send.at[u, 1], z_recv.at[u, 0], outward)

    def copy_v(step, device):
        return put(v_out.at[step], v_in.at[step], v_send.at[step], v_recv.at[step], device)

    gain_one, gain_two, gain_out = [gains_ref[n : n + 1, :] for n in range(3)]

    def give(r, value):
        yo[r] = value
        swap_right(r).start()

    def columns_at(n):
        return slice(n * UNIT, (n + 1) * UNIT)

    def back_link():
        dseen = jnp.where(kept_ref[...] > 0, dy_ref[...], 0.0).astype(BF)
        give(0, dseen)
        wide_copy(0).wait()
        h_copy(end_ref).wait()
        unit, rate = normalize(h_buf[...])
        dend, dgain = normalize_back(unit, rate, gain_out, right_t(dseen, wide_buf[0]))
        grad_vec[...] = vec_ref[...]
        grad_vec[2:3, :] = dgain
        dend_ref[...] = dend
        dbranch_ref[...] = dend.astype(BF)
        for n in range(out_chunks):
            give(1 + n, dbranch_ref[:, columns_at(n)])
        wide_copy(ring).start()
        h_copy(middle_ref).start()
        dmid_ref[...] = jnp.zeros_like(dmid_ref)

    def back_hidden(j):
        w = 1 + j
        down_copy(j).wait()
        slope_copy(j).wait()
        wide_copy(w).wait()
        dhidden = right_t(dbranch_ref[...], down_buf[j % 2])
        dbefore = (dhidden * slope_buf[j % 2]).astype(BF)
        give(firsts + j, dbefore)
        dmid_ref[...] += right_t(dbefore, wide_buf[w % ring])
        wide_copy(w + ring).start()

        @pl.when(j + 2 < up_chunks)
        def _():
            down_copy(j + 2).start()
            slope_copy(j + 2).start()

    def back_out():
        h_copy(middle_ref).wait()
        unit, rate = normalize(h_buf[...])
        dmiddle, dgain = normalize_back(unit, rate, gain_two, dmid_ref[...])
        grad_vec[1:2, :] = dgain
        dmiddle = dmiddle + dend_ref[...]
        dend_ref[...] = dmiddle
        dattn = dmiddle.astype(BF)
        dmixed = jnp.zeros((VIS, D), F32)
        for n in range(out_chunks):
            w = 1 + up_chunks + n
            piece = dattn[:, columns_at(n)]
            give(firsts + up_chunks + n, piece)
            wide_copy(w).wait()
            dmixed = dmixed + right_t(piece, wide_buf[w % ring])
            wide_copy(w + ring).start()
        dmixed_ref[...] = dmixed.astype(BF)
        h_copy(start_ref).start()
        dmid_ref[...] = jnp.zeros_like(dmid_ref)

    size = D // HEADS
    lane_head = lax.broadcasted_iota(jnp.int32, (VIS, LANES), 1) // size

    def only(array, j):
        return jnp.where(lane_head == j, array.astype(F32), 0.0).astype(BF)

    def back_attention(g):
        at = [pl.ds(pl.multiple_of(n * D + g * LANES, LANES), LANES) for n in range(3)]
        query, keys, values = [qkv_ref[:, lanes] for lanes in at]
        dout = dmixed_ref[:, at[0]]
        keys_t = keys.T
        factor = size ** (-0.5)
        dkeys, dvalues = jnp.zeros((VIS, LANES), F32), jnp.zeros((VIS, LANES), F32)
        dquery = []
        for j in range(LANES // size):
            scores = right_t(keys, only(query, j)) * factor + bias_ref[...]
            probs = jnp.exp(scores - jnp.max(scores, 0, keepdims=True))
            probs = probs * (1.0 / jnp.sum(probs, 0, keepdims=True))
            dvalues = jnp.where(lane_head == j, matmul(probs.astype(BF), dout), dvalues)
            dprobs = right_t(values, only(dout, j))
            delta = jnp.sum(dprobs * probs, 0, keepdims=True)
            dscores = (probs * (dprobs - delta)).astype(BF)
            dkeys = jnp.where(lane_head == j, matmul(dscores, query), dkeys)
            dquery.append(matmul(keys_t[j * size : (j + 1) * size, :], dscores))
        dqkv_ref[:, at[0]] = (jnp.concatenate(dquery, 0) * factor).astype(BF).T
        dqkv_ref[:, at[1]] = (dkeys * factor).astype(BF)
        dqkv_ref[:, at[2]] = dvalues.astype(BF)

    def give_qkv():
        for c in range(qkv_chunks):
            give(firsts + up_chunks + out_chunks + c, dqkv_ref[:, columns_at(c)])

    def back_qkv(c):
        w = 1 + up_chunks + out_chunks + c
        wide_copy(w).wait()
        piece = dqkv_ref[:, pl.ds(pl.multiple_of(c * UNIT, UNIT), UNIT)]
        dmid_ref[...] += right_t(piece, wide_buf[w % ring])

        @pl.when(w + ring < chunks)
        def _():
            wide_copy(w + ring).start()

    def back_start():
        h_copy(start_ref).wait()
        unit, rate = normalize(h_buf[...])
        dh, dgain = normalize_back(unit, rate, gain_one, dmid_ref[...])
        grad_vec[0:1, :] = dgain
        dh = (dh + dend_ref[...]).astype(BF)
        for n in range(out_chunks):
            give(firsts + up_chunks + out_chunks + qkv_chunks + n, dh[:, columns_at(n)])

    at_hidden = 1
    at_out = at_hidden + up_chunks
    at_attention = at_out + 1
    groups = D // LANES
    at_qkv = at_attention + groups
    at_start = at_qkv + qkv_chunks
    at_vec = at_start + 1

    def step(i, _):
        def stage(lag, also=None):
            u = i - lag
            ok = (u >= 0) & (u < count)
            if also is not None:
                ok = ok & also
            return u, pl.when(ok)

        u0, when = stage(0)

        @when
        def _():
            u = u0

            @pl.when(u < dec_units)
            def _():
                pltpu.make_async_copy(do.at[u], do.at[u], dec_sem.at[u, 0]).wait()
                swap_dec(do.at[u], u).wait()

            @pl.when(u == dec_units)
            def _():
                for b in range(len(blocks)):
                    pltpu.make_async_copy(xo.at[b], xo.at[b], left_sem.at[b, 0]).wait()
                    swap_left(xo.at[b], b).wait()
                for r in range(firsts):
                    swap_right(r).wait()

            @pl.when(u >= dec_units + single)
            def _():
                swap_right(u - dec_units - single + firsts).wait()

            @pl.when(u >= a_out.shape[0])
            def _():
                for side in range(2):
                    copy_a(u - a_out.shape[0], side).wait_send()

            slot = u % a_out.shape[0]
            a_out[slot, 0, 0] = part(u, at_x, first, 0).astype(BF)
            a_out[slot, 0, 1] = part(u, at_far, first, 1).astype(BF)
            copy_a(u, 0).start()
            a_out[slot, 1, 0] = part(u, at_y, second, 2).astype(BF)
            a_out[slot, 1, 1] = part(u, at_far, second, 3).astype(BF)
            copy_a(u, 1).start()

        u1, when = stage(LAGS[0])

        @when
        def _():
            u = u1
            slot = u % b_out.shape[0]

            @pl.when(u >= b_out.shape[0])
            def _():
                for side in range(2):
                    copy_b(u - b_out.shape[0], side).wait_send()

            copy_a(u, 0).wait_recv()
            b_out[slot, 0] = (part(u, at_y, first, 0) + a_in[u, 0, 1].astype(F32)).astype(BF)
            copy_b(u, 0).start()
            copy_a(u, 1).wait_recv()
            b_out[slot, 1] = (part(u, at_x, second, 1) + a_in[u, 1, 1].astype(F32)).astype(BF)
            copy_b(u, 1).start()

        u2, when = stage(LAGS[1])

        @when
        def _():
            u = u2
            copy_b(u, 0).wait_recv()
            copy_b(u, 1).wait_recv()
            for side, columns in enumerate((first, second)):
                total = part(u, place, columns, side) + a_in[u, side, 0].astype(F32)
                sums[u % 4, :, columns] = total + b_in[u, side].astype(F32)

            @pl.when(outer)
            def _():
                @pl.when(u >= z_slots)
                def _():
                    copy_in(u - z_slots).wait_send()

                z_out[u % z_slots] = sums[u % 4].astype(BF)
                copy_in(u).start()

        u3, when = stage(LAGS[2], inner)

        @when
        def _():
            u = u3
            copy_in(u).wait_recv()

            @pl.when(u >= z_slots)
            def _():
                copy_across(u - z_slots).wait_send()

            z_out[u % z_slots] = (sums[u % 4] + z_one[u].astype(F32)).astype(BF)
            copy_across(u).start()

        u4, when = stage(LAGS[3], inner)

        @when
        def _():
            u = u4
            copy_across(u).wait_recv()
            z_one[u] = (z_out[u % z_slots].astype(F32) + z_two[u].astype(F32)).astype(BF)
            copy_out(u).start()

        u5, when = stage(LAGS[4], outer)

        @when
        def _():
            copy_out(u5).wait_recv()

        pl.when(i == 0)(back_link)

        @pl.when((i >= at_hidden) & (i < at_hidden + up_chunks))
        def _():
            back_hidden(i - at_hidden)

        pl.when(i == at_out)(back_out)

        @pl.when((i >= at_attention) & (i < at_attention + groups))
        def _():
            back_attention(i - at_attention)

        pl.when(i == at_qkv)(give_qkv)

        @pl.when((i >= at_qkv) & (i < at_qkv + qkv_chunks))
        def _():
            back_qkv(i - at_qkv)

        pl.when(i == at_start)(back_start)

        for number, device in enumerate((partner, x_side, y_side)):

            @pl.when(i == at_vec + number)
            def _():
                if number == 0:
                    v_out[0] = grad_vec[...]
                else:
                    copy_v(number - 1, (partner, x_side, y_side)[number - 1]).wait_recv()
                    v_out[number] = v_out[number - 1] + v_in[number - 1]
                copy_v(number, device).start()

        @pl.when(i == at_vec + 3)
        def _():
            copy_v(2, y_side).wait_recv()
            v_out[3] = v_out[2] + v_in[2]

            @pl.when(outer)
            def _():
                copy_v(3, inward).start()

        @pl.when((i == at_vec + 4) & inner)
        def _():
            copy_v(3, inward).wait_recv()
            v_out[4] = v_out[3] + v_in[3]
            copy_v(4, across).start()

        @pl.when((i == at_vec + 5) & inner)
        def _():
            copy_v(4, across).wait_recv()
            v_out[5] = v_out[4] + v_in[4]
            copy_v(5, outward).start()
            vec_out[...] = v_out[5]

        @pl.when((i == at_vec + 7) & outer)
        def _():
            copy_v(5, outward).wait_recv()
            vec_out[...] = v_in[5]

        return 0

    lax.fori_loop(0, count + LAGS[4], step, 0)

    stores = []
    for n, (u, start, out, row, rows, column) in enumerate(spots):
        stores.append(
            pltpu.make_async_copy(
                z_one.at[u, pl.ds(start, rows)],
                outs[out].at[pl.ds(row, rows), pl.ds(column, UNIT)],
                store_sem.at[n],
            )
        )
    for store in stores:
        store.start()
    for u in range(count - a_out.shape[0], count):
        for side in range(2):
            copy_a(u, side).wait_send()
    for u in range(count - b_out.shape[0], count):
        for side in range(2):
            copy_b(u, side).wait_send()
    for number, device in enumerate((partner, x_side, y_side)):
        copy_v(number, device).wait_send()
    for store in stores:
        store.wait()

    @pl.when(outer)
    def _():
        copy_v(3, inward).wait_send()
        for u in range(count - z_slots, count):
            copy_in(u).wait_send()

    @pl.when(inner)
    def _():
        copy_v(4, across).wait_send()
        copy_v(5, outward).wait_send()
        for u in range(count - z_slots, count):
            copy_across(u).wait_send()

        def drain(u, _):
            copy_out(u).wait_send()
            return 0

        lax.fori_loop(0, count, drain, 0)


def encoder_back(dy, kept, vec, gains, bias, qkv, dec, states, wide, down, lefts):
    owners = lax.axis_size("fsdp")
    own = PD // owners
    dec_units = dec.shape[1] * dec.shape[2] // ROWS
    dec = dec.reshape(4, 2, dec_units, ROWS, UNIT)
    half = ROWS // 2
    blocks, units, spots = [], [], []
    for n in range(2 * dec_units):
        place = (4, n * half, half, 0) if n < DFF // DD else (3, 0, half, (n - DFF // DD) * UNIT)
        spots.append((n // 2, n % 2 * half, *place))

    def add(left, sub, right, out, row, rows, column, columns):
        blocks.append((left, sub))
        for n in range(columns // UNIT):
            spots.append((dec_units + len(units), 0, out, row, rows, column + n * UNIT))
            units.append((len(blocks) - 1, right + n))

    subs = FF // owners // ROWS
    add(0, 0, 0, 1, 0, ROWS, 4 * D + FF, DD)
    for n in range(subs):
        add(1, n, 1, 2, n * ROWS, ROWS, 0, D)
    right = 1 + D // UNIT
    add(2, 0, right, 1, 0, ROWS, 4 * D, FF)
    right += FF // UNIT
    add(3, 0, right, 1, 0, ROWS, 3 * D, D)
    right += D // UNIT
    add(4, 0, right, 1, 0, ROWS, 0, 3 * D)
    right += 3 * D // UNIT
    add(5, 0, right, 0, 0, own, 0, D)
    right += D // UNIT
    count = dec_units + len(units)
    shapes = ((own, D), (ROWS, 4 * D + FF + DD), (FF // owners, D), (half, 10 * UNIT), (DFF // owners, DD))
    lefts = [a.reshape(4, 2, -1, VIS) for a in lefts]
    slots = 3
    dma = pltpu.SemaphoreType.DMA
    vmem, anywhere = pl.BlockSpec(memory_space=pltpu.VMEM), pl.BlockSpec(memory_space=pl.ANY)
    return pl.pallas_call(
        partial(back_kernel, dec_units, tuple(blocks), tuple(units), tuple(spots)),
        out_shape=tuple(jax.ShapeDtypeStruct(shape, BF) for shape in shapes)
        + (jax.ShapeDtypeStruct(vec.shape, F32),),
        in_specs=[vmem] * 6 + [anywhere] * (7 + len(lefts)),
        out_specs=(anywhere,) * len(shapes) + (vmem,),
        scratch_shapes=[
            pltpu.VMEM((len(blocks), 4, ROWS, VIS), BF),
            pltpu.VMEM((len(blocks), 4, ROWS, VIS), BF),
            pltpu.VMEM((right, VIS, UNIT), BF),
            pltpu.VMEM((right, VIS, UNIT), BF),
            pltpu.VMEM((dec_units, 4, ROWS, UNIT), BF),
            pltpu.VMEM((dec_units, 4, ROWS, UNIT), BF),
            pltpu.VMEM((4, ROWS, HALF), F32),
            pltpu.VMEM((slots, 2, 2, ROWS, HALF), BF),
            pltpu.VMEM((count, 2, 2, ROWS, HALF), BF),
            pltpu.VMEM((slots, 2, ROWS, HALF), BF),
            pltpu.VMEM((count, 2, ROWS, HALF), BF),
            pltpu.VMEM((4, ROWS, UNIT), F32),
            pltpu.VMEM((6, ROWS, UNIT), BF),
            pltpu.VMEM((count, ROWS, UNIT), BF),
            pltpu.VMEM((count, ROWS, UNIT), BF),
            pltpu.VMEM((6, *vec.shape), F32),
            pltpu.VMEM((6, *vec.shape), F32),
            pltpu.VMEM((3, D, UNIT), BF),
            pltpu.VMEM((2, UNIT, D), BF),
            pltpu.VMEM((2, VIS, UNIT), F32),
            pltpu.VMEM((VIS, D), F32),
            pltpu.VMEM((VIS, D), F32),
            pltpu.VMEM((VIS, D), F32),
            pltpu.VMEM((VIS, D), BF),
            pltpu.VMEM((VIS, D), BF),
            pltpu.VMEM((VIS, 3 * D), BF),
            pltpu.VMEM(vec.shape, F32),
            dma((3,)),
            dma((2,)),
            dma((2,)),
            dma((1,)),
            dma((dec_units, 3)),
            dma((len(blocks), 3)),
            dma((right, 2)),
            dma((slots, 2)),
            dma((count, 2)),
            dma((slots, 2)),
            dma((count, 2)),
            dma((count, 2)),
            dma((count, 2)),
            dma((6,)),
            dma((6,)),
            dma((count + dec_units,)),
        ],
        compiler_params=pltpu.CompilerParams(
            collective_id=0, has_side_effects=True, vmem_limit_bytes=61 * 2**20
        ),
        cost_estimate=pl.CostEstimate(
            flops=30 * 10**9, bytes_accessed=300 * 2**20, transcendentals=0
        ),
    )(dy, kept, vec, gains, bias, qkv, dec, *states, wide, down, *lefts)


def encoder_pieces(shapes):
    (own, width), (rows, _), (tall, _) = shapes
    pieces = [(0, 0, own, 0, width, 0)]
    pieces += [(1, 0, rows, n * D, D, (1, 2, 0)[n]) for n in range(3)]
    pieces += [(1, 0, rows, 3 * D, D, 1)]
    pieces += [(1, 0, rows, 4 * D + n * D, D, (2, 0, 1, 2)[n]) for n in range(FF // D)]
    pieces += [(2, n * rows, rows, 0, D, (0, 1, 2, 0)[n]) for n in range(tall // rows)]
    pieces += [(1, 0, rows, 4 * D + FF, DD, 0)]
    return pieces


def norm_rows(h, gain):
    mean = jnp.mean(h, -1, keepdims=True)
    cent = h - mean
    var = jnp.mean(cent * cent, -1, keepdims=True)
    return (cent * lax.rsqrt(var + EPS) * gain).astype(BF)


def encoder_kernel(
    picked_ref,
    stats_ref,
    pos_ref,
    bias_ref,
    gains_ref,
    embed_ref,
    wide_ref,
    down_ref,
    wide_out,
    down_out,
    stats_out,
    inputs_t,
    a_t,
    mixed_t,
    b_t,
    hidden_t,
    z_t,
    start_ref,
    qkv_ref,
    middle_ref,
    slope_ref,
    end_ref,
    seen_ref,
    inputs_ref,
    a_ref,
    mixed_ref,
    b_ref,
    hidden_ref,
    z_ref,
    w_embed,
    w_wide,
    w_down,
    v_in,
    v_out,
    load_sem,
    store_sem,
    send_sem,
    recv_sem,
    v_send,
    v_recv,
):
    shards, gathered = (embed_ref, wide_ref, down_ref), (w_embed, w_wide, w_down)
    pieces = encoder_pieces([ref.shape for ref in shards])
    count = len(pieces)
    z, f = lax.axis_index("dp"), lax.axis_index("fsdp")
    core, place = f % 2, f // 2
    x, y = place % 2, place // 2
    f_x, f_y, f_far = f + 2 - 4 * x, f + 4 - 8 * y, f + 6 - 4 * x - 8 * y
    partner = (z, f + 1 - 2 * core)
    x_side, y_side, z_side = (z, f_x), (z, f_y), (z + 1 - 2 * (z % 2), f)
    outer = (z == 0) | (z == 3)
    inner = (z == 1) | (z == 2)
    across = (3 - z, f)

    barrier = pltpu.get_barrier_semaphore()
    for device in (partner, x_side, y_side, z_side):
        pl.semaphore_signal(barrier, inc=1, device_id=device, device_id_type=MESH)

    @pl.when(outer)
    def _():
        pl.semaphore_wait(barrier, 4)

    @pl.when(inner)
    def _():
        pl.semaphore_signal(barrier, inc=1, device_id=across, device_id_type=MESH)
        pl.semaphore_wait(barrier, 5)

    loads = [
        pltpu.make_async_copy(shard, whole.at[f], load_sem.at[n])
        for n, (shard, whole) in enumerate(zip(shards, gathered))
    ]
    for load in loads:
        load.start()

    def spot(t, owner, half=None):
        array, row, rows, column, columns, _ = pieces[t]
        if half is not None:
            columns //= 2
            column += half * columns
        return gathered[array].at[owner, pl.ds(row, rows), pl.ds(column, columns)]

    def move(t, owner, send, recv, device, half=None):
        target = spot(t, owner, half)
        source = target
        if send < 3:
            array, row, rows, column, columns, _ = pieces[t]
            source = shards[array].at[pl.ds(row, rows), pl.ds(column, columns)]
        return put(source, target, send_sem.at[t, send], recv_sem.at[t, recv], device)

    def own_x(t):
        return move(t, f, 0, 0, x_side)

    def own_y(t):
        return move(t, f, 1, 1, y_side)

    def own_core(t):
        return move(t, f, 2, 4, partner)

    def far_x(t):
        return move(t, f_y, 3, 2, x_side, 0)

    def far_y(t):
        return move(t, f_x, 4, 3, y_side, 1)

    def to_core(t, n):
        return move(t, (f_x, f_y, f_far)[n], 5 + n, 5 + n, partner)

    def to_z(t, n):
        return move(t, (f_x, f_y, f_far)[n], 8 + n, 8 + n, z_side)

    def brings(t, then, other=None):
        kind = pieces[t][5]
        if kind == 0:
            then()
            return
        pl.when(z % 2 == kind - 1)(then)
        if other is not None:
            pl.when(z % 2 != kind - 1)(other)

    def first(t):
        own_core(t).start()

        def then():
            own_x(t).start()
            own_y(t).start()

        brings(t, then)

    def second(t):
        def then():
            own_x(t).wait_recv()
            far_y(t).start()
            own_y(t).wait_recv()
            far_x(t).start()
            for n in range(2):
                to_core(t, n).start()
                if pieces[t][5]:
                    to_z(t, n).start()

        brings(t, then)

    def third(t):
        def then():
            far_x(t).wait_recv()
            far_y(t).wait_recv()
            to_core(t, 2).start()
            if pieces[t][5]:
                to_z(t, 2).start()

        brings(t, then)

    def taken(t, n):
        def other():
            to_z(t, n).wait_recv()
            to_core(t, n).start()

        brings(t, lambda: None, other)

    def whole(t):
        own_core(t).wait_recv()
        for n in range(3):
            to_core(t, n).wait_recv()

    def drain(t):
        own_core(t).wait_send()
        for n in range(3):
            to_core(t, n).wait_send()

        def then():
            for copy in (own_x(t), own_y(t), far_x(t), far_y(t)):
                copy.wait_send()
            if pieces[t][5]:
                for n in range(3):
                    to_z(t, n).wait_send()

        brings(t, then)

    def copy_v(step, device):
        return put(v_out.at[step], v_in.at[step], v_send.at[step], v_recv.at[step], device)

    sides = (partner, x_side, y_side)

    def statistics(i):
        if i <= 3:
            if i == 0:
                v_out[0] = stats_ref[...]
            else:
                copy_v(i - 1, sides[i - 1]).wait_recv()
                v_out[i] = v_out[i - 1] + v_in[i - 1]
            if i < 3:
                copy_v(i, sides[i]).start()
            else:

                @pl.when(outer)
                def _():
                    copy_v(3, z_side).start()

        if i == 4:

            @pl.when(inner)
            def _():
                copy_v(3, z_side).wait_recv()
                v_out[4] = v_out[3] + v_in[3]
                copy_v(4, across).start()

        if i == 5:

            @pl.when(inner)
            def _():
                copy_v(4, across).wait_recv()
                v_out[5] = v_out[4] + v_in[4]
                copy_v(5, z_side).start()
                stats_out[...] = v_out[5]

            @pl.when(outer)
            def _():
                copy_v(5, z_side).wait_recv()
                stats_out[...] = v_in[5]

    def turn(source, target, start=0, width=D):
        for lane in range(start, start + width, LANES):
            target[lane : lane + LANES, :] = source[:, lane : lane + LANES].T

    def columns_of(t):
        array, row, rows, column, columns, _ = pieces[t]
        weight = gathered[array][:, row : row + rows, column : column + columns]
        return weight.reshape(-1, columns)

    def embed_step():
        pixels = stats_out[6:7, :] * (PATCH * PATCH)
        for band in range(BANDS):
            mean = stats_out[band : band + 1, :] / pixels
            var = stats_out[BANDS + band : BANDS + band + 1, :] / pixels - mean * mean
            rate = lax.rsqrt(var + EPS)
            for part in range(PATCH * PATCH // LANES):
                lanes = pl.ds(band * PATCH * PATCH + part * LANES, LANES)
                inputs_ref[:, lanes] = ((picked_ref[:, lanes] - mean) * rate).astype(BF)
        start_ref[...] = matmul(inputs_ref[...], columns_of(0)) + pos_ref[...]
        a_ref[...] = norm_rows(start_ref[...], gains_ref[0:1, :])
        own = w_embed.shape[1]
        flipped = jnp.concatenate(
            [inputs_ref[:, lane : lane + LANES].T for lane in range(0, PD, LANES)], 0
        )
        inputs_t[...] = jnp.zeros_like(inputs_t)
        for owner in range(w_embed.shape[0]):
            inputs_t[owner, :own, :] = flipped[owner * own : (owner + 1) * own, :]
        turn(a_ref, a_t)

    def qkv_step(n):
        qkv_ref[:, n * D : (n + 1) * D] = matmul(a_ref[...], columns_of(1 + n)).astype(BF)

    def attention_step():
        size = D // HEADS
        lane_head = lax.broadcasted_iota(jnp.int32, (VIS, LANES), 1) // size

        def group(g, _):
            query, keys, values = [
                qkv_ref[:, pl.ds(pl.multiple_of(n * D + g * LANES, LANES), LANES)] for n in range(3)
            ]
            mixed = jnp.zeros((VIS, LANES), F32)
            for j in range(LANES // size):
                one = jnp.where(lane_head == j, query.astype(F32), 0.0).astype(BF)
                scores = right_t(one, keys) * size ** (-0.5) + bias_ref[...]
                probs = jnp.exp(scores - jnp.max(scores, -1, keepdims=True))
                probs = probs * (1.0 / jnp.sum(probs, -1, keepdims=True))
                mixed = jnp.where(lane_head == j, matmul(probs.astype(BF), values), mixed)
            mixed_ref[:, pl.ds(pl.multiple_of(g * LANES, LANES), LANES)] = mixed.astype(BF)
            return 0

        lax.fori_loop(0, D // LANES, group, 0)

    def out_step():
        turn(mixed_ref, mixed_t)
        middle_ref[...] = start_ref[...] + matmul(mixed_ref[...], columns_of(4))
        b_ref[...] = norm_rows(middle_ref[...], gains_ref[1:2, :])
        turn(b_ref, b_t)

    def up_step(n):
        columns = slice(n * D, (n + 1) * D)
        after, slope = gelu_parts(matmul(b_ref[...], columns_of(5 + n)))
        hidden_ref[:, columns] = after.astype(BF)
        slope_ref[:, columns] = slope
        turn(hidden_ref, hidden_t, n * D)

    def down_step(n):
        rows, owners = w_wide.shape[1], w_down.shape[0]
        tall = w_down.shape[1]
        parts = [hidden_ref[:, o * tall + n * rows : o * tall + (n + 1) * rows] for o in range(owners)]
        total = matmul(jnp.concatenate(parts, 1), columns_of(9 + n))
        end_ref[...] = (middle_ref[...] if n == 0 else end_ref[...]) + total

    def link_step():
        z_ref[...] = norm_rows(end_ref[...], gains_ref[2:3, :])
        turn(z_ref, z_t)
        seen_ref[...] = matmul(z_ref[...], columns_of(count - 1))

    work = [(6, 0, embed_step), (6, 1, partial(qkv_step, 0)), (7, 2, partial(qkv_step, 1))]
    work += [(8, 3, partial(qkv_step, 2)), (8, None, attention_step), (9, 4, out_step)]
    work += [(at, 5 + n, partial(up_step, n)) for n, at in enumerate((10, 10, 12, 13))]
    work += [(at, 9 + n, partial(down_step, n)) for n, at in enumerate((13, 15, 16, 16))]
    work += [(17, count - 1, link_step)]
    stores = []

    for load in loads:
        load.wait()
    first(0)
    first(1)
    for i in range(18):
        if i + 2 < count:
            first(i + 2)
        statistics(i)
        if i < count:
            second(i)
        if 0 <= i - 1 < count:
            third(i - 1)
        if 0 <= i - 3 < count:
            taken(i - 3, 0)
            taken(i - 3, 1)
        if 0 <= i - 4 < count:
            taken(i - 4, 2)
        for at, piece, run in work:
            if at != i:
                continue
            if piece is not None:
                whole(piece)
                array, row, rows, column, columns, _ = pieces[piece]
                if array:
                    where = (slice(None), pl.ds(row, rows), pl.ds(column, columns))
                    store = pltpu.make_async_copy(
                        gathered[array].at[where],
                        (None, wide_out, down_out)[array].at[where],
                        store_sem.at[piece],
                    )
                    store.start()
                    stores.append(store)
            run()
    for store in stores:
        store.wait()
    for t in range(count):
        drain(t)
    for step in range(3):
        copy_v(step, sides[step]).wait_send()

    @pl.when(outer)
    def _():
        copy_v(3, z_side).wait_send()

    @pl.when(inner)
    def _():
        copy_v(4, across).wait_send()
        copy_v(5, z_side).wait_send()


def encoder_forward(picked, stats, pos, bias, gains, embed, wide, down):
    owners = lax.axis_size("fsdp")
    shapes = [w.shape for w in (embed, wide, down)]
    count = len(encoder_pieces(shapes))
    full = [jax.ShapeDtypeStruct((owners, *shape), BF) for shape in shapes[1:]]
    local = [
        jax.ShapeDtypeStruct((8, LANES), F32),
        jax.ShapeDtypeStruct((owners, ROWS, VIS), BF),
        *[jax.ShapeDtypeStruct((width, VIS), BF) for width in (D, D, D, FF, D)],
        jax.ShapeDtypeStruct((VIS, D), F32),
        jax.ShapeDtypeStruct((VIS, 3 * D), BF),
        jax.ShapeDtypeStruct((VIS, D), F32),
        jax.ShapeDtypeStruct((VIS, FF), F32),
        jax.ShapeDtypeStruct((VIS, D), F32),
        jax.ShapeDtypeStruct((VIS, DD), F32),
    ]
    vmem, anywhere = pl.BlockSpec(memory_space=pltpu.VMEM), pl.BlockSpec(memory_space=pl.ANY)
    dma = pltpu.SemaphoreType.DMA
    wide_full, down_full, *rest = pl.pallas_call(
        encoder_kernel,
        out_shape=(*full, *local),
        in_specs=[vmem] * 5 + [anywhere] * 3,
        out_specs=(anywhere,) * 2 + (vmem,) * len(local),
        scratch_shapes=[pltpu.VMEM((VIS, width), BF) for width in (PD, D, D, D, FF, D)]
        + [pltpu.VMEM((owners, *shape), BF) for shape in shapes]
        + [
            pltpu.VMEM((6, 8, LANES), F32),
            pltpu.VMEM((6, 8, LANES), F32),
            dma((3,)),
            dma((count,)),
            dma((count, 11)),
            dma((count, 11)),
            dma((6,)),
            dma((6,)),
        ],
        compiler_params=pltpu.CompilerParams(
            collective_id=1, has_side_effects=True, vmem_limit_bytes=56 * 2**20
        ),
        cost_estimate=pl.CostEstimate(
            flops=2 * VIS * 14 * 2**20, bytes_accessed=200 * 2**20, transcendentals=0
        ),
    )(picked, stats, pos, bias, gains, embed, wide, down)
    return (wide_full.reshape(D, -1), down_full.reshape(FF, D), *rest)


LOWP = 256
HEADP = PD + LOWP
BLOCK = HID // 2


def normalize(h):
    cent = h - jnp.mean(h, -1, keepdims=True)
    rate = lax.rsqrt(jnp.mean(cent * cent, -1, keepdims=True) + EPS)
    return cent * rate, rate


def normalize_back(unit, rate, gain, grad):
    scaled = grad * gain
    along = jnp.mean(scaled * unit, -1, keepdims=True)
    dh = rate * (scaled - jnp.mean(scaled, -1, keepdims=True) - unit * along)
    return dh, jnp.sum(grad * unit, 0, keepdims=True)


def exact_product(array, weight):
    high = array.astype(BF)
    rest = array - high.astype(F32)
    mid = rest.astype(BF)
    low = (rest - mid.astype(F32)).astype(BF)
    return matmul(high, weight) + matmul(mid, weight) + matmul(low, weight)


def decoder_kernel(
    owners,
    pos_ref,
    seen_ref,
    kept_ref,
    flag_ref,
    picked_ref,
    stats_ref,
    bias_ref,
    gains_ref,
    pool_ref,
    spread_ref,
    wide_ref,
    down_ref,
    grads_ref,
    dy_ref,
    vec_ref,
    y_ref,
    a_ref,
    q_ref,
    k_ref,
    v_ref,
    mixed_t,
    mixed_ref,
    lse_ref,
    head_ref,
    b_ref,
    hidden_ref,
    z_ref,
    dpred_ref,
    dbranch_ref,
    dbefore_ref,
    dattn_ref,
    dmixed_ref,
    dmiddle_ref,
    dq_ref,
    dk_ref,
    dv_ref,
    loss_ref,
):
    size = DD // DHEADS
    per = LANES // size
    factor = size ** (-0.5)
    gain_one, gain_two, gain_out = [gains_ref[n : n + 1, :] for n in range(3)]
    token = gains_ref[3:4, :]
    lane_head = lax.broadcasted_iota(jnp.int32, (HID, LANES), 1) // size
    key_head = lax.broadcasted_iota(jnp.int32, (TOK_DEV, LANES), 1) // size
    vec_ref[...] = jnp.zeros_like(vec_ref)
    loss_ref[...] = jnp.zeros_like(loss_ref)
    head_ref[...] = jnp.zeros_like(head_ref)
    head_ref[:, : PD + LOWD] = wide_ref[:, 4 * DD + DFF :]

    def project(rows, with_query):
        a = (normalize(y_ref[rows, :])[0] * gain_one).astype(BF)
        a_ref[rows, :] = a
        k_ref[rows, :] = matmul(a, wide_ref[:, DD : 2 * DD]).astype(BF)
        v_ref[rows, :] = matmul(a, wide_ref[:, 2 * DD : 3 * DD]).astype(BF)
        return a

    y_ref[:VIS, :] = pos_ref[:VIS, :] + jnp.where(kept_ref[...] > 0, seen_ref[...], token)
    y_ref[VIS:, :] = pos_ref[VIS:, :] + token
    project(slice(0, VIS), False)

    def hidden_rows(n):
        start = pl.multiple_of(n * BLOCK, BLOCK)
        return pl.ds(start, BLOCK), pl.ds(pl.multiple_of(start + VIS, 32), BLOCK)

    def project_hidden(n, _):
        rows, all_rows = hidden_rows(n)
        a = project(all_rows, True)
        q_ref[rows, :] = matmul(a, wide_ref[:, :DD]).astype(BF)
        return 0

    lax.fori_loop(0, 2, project_hidden, 0)

    def only(array, head_of, j):
        return jnp.where(head_of == j, array.astype(F32), 0.0).astype(BF)

    def attend_group(g, _):
        lanes = pl.ds(pl.multiple_of(g * LANES, LANES), LANES)
        keys, query = k_ref[:, lanes], q_ref[:, lanes]
        values_t = v_ref[:, lanes].T
        for j in range(per):
            scores = right_t(keys, only(query, lane_head, j)) * factor + bias_ref[...]
            top = jnp.max(scores, 0, keepdims=True)
            probs = jnp.exp(scores - top)
            total = jnp.sum(probs, 0, keepdims=True)
            probs = (probs * (1.0 / total)).astype(BF)
            rows = slice(j * size, (j + 1) * size)
            mixed_t[g, rows, :] = matmul(values_t[rows, :], probs).astype(BF)
            lse_ref[g, j : j + 1, :] = top + jnp.log(total)
        mixed_ref[:, lanes] = mixed_t[g].T
        return 0

    lax.fori_loop(0, DD // LANES, attend_group, 0)

    pixels = stats_ref[6:7, :] * (PATCH * PATCH)
    flagged = stats_ref[7:8, 0:1]

    def follow(n, _):
        rows, all_rows = hidden_rows(n)
        middle = y_ref[all_rows, :] + matmul(mixed_ref[rows, :], wide_ref[:, 3 * DD : 4 * DD])
        unit_b, rate_b = normalize(middle)
        b = (unit_b * gain_two).astype(BF)
        b_ref[rows, :] = b
        after, slope = gelu_parts(matmul(b, wide_ref[:, 4 * DD : 4 * DD + DFF]))
        hidden_ref[rows, :] = after.astype(BF)
        unit_z, rate_z = normalize(middle + matmul(hidden_ref[rows, :], down_ref[...]))
        z = (unit_z * gain_out).astype(BF)
        z_ref[rows, :] = z
        pred = matmul(z, head_ref[...])
        parts = []
        for part in range(PD // LANES):
            band = part * LANES // (PATCH * PATCH)
            mean = stats_ref[band : band + 1, :] / pixels
            var = stats_ref[BANDS + band : BANDS + band + 1, :] / pixels - mean * mean
            lanes = slice(part * LANES, (part + 1) * LANES)
            parts.append((picked_ref[rows, lanes] - mean) * lax.rsqrt(var + EPS))
        normed = jnp.concatenate(parts, 1)
        coarse = exact_product(normed, pool_ref[...])
        err_high = pred[:, :PD] - (normed - exact_product(coarse, spread_ref[...]))
        err_low = pred[:, PD:] - coarse
        flag = flag_ref[rows, :]
        length = jnp.sqrt(err_high * err_high + 1.0)
        loss_ref[:, :PD] += jnp.sum((length - 1.0) * flag, 0, keepdims=True) * (1.0 / PD)
        loss_ref[:, PD:] += jnp.sum(err_low * err_low * flag, 0, keepdims=True) * (1.0 / LOWD)
        share = flag / flagged
        dpred_ref[rows, :PD] = (err_high / length * (share * (1.0 / PD))).astype(BF)
        dpred_ref[rows, PD:] = (err_low * (share * (2.0 / LOWD))).astype(BF)
        dz = right_t(dpred_ref[rows, :], head_ref[...])
        dend, dgain = normalize_back(unit_z, rate_z, gain_out, dz)
        vec_ref[2:3, :] += dgain
        dbranch_ref[rows, :] = dend.astype(BF)
        dhidden = right_t(dbranch_ref[rows, :], down_ref[...])
        dbefore_ref[rows, :] = (dhidden * slope).astype(BF)
        db = right_t(dbefore_ref[rows, :], wide_ref[:, 4 * DD : 4 * DD + DFF])
        dmiddle, dgain = normalize_back(unit_b, rate_b, gain_two, db)
        vec_ref[1:2, :] += dgain
        dmiddle = dmiddle + dend
        dmiddle_ref[rows, :] = dmiddle
        dattn_ref[rows, :] = dmiddle.astype(BF)
        dmixed = right_t(dattn_ref[rows, :], wide_ref[:, 3 * DD : 4 * DD])
        dmixed_ref[rows, :] = dmixed.astype(BF)
        return 0

    lax.fori_loop(0, 2, follow, 0)

    rows = DD // owners

    def store(block, grad):
        grads_ref[:, block] = grad.astype(BF).reshape(owners, rows, UNIT)

    parts = DFF // DD
    down_grad = left_t(hidden_ref[...], dbranch_ref[...]).astype(BF)
    down_grad = down_grad.reshape(owners, parts, rows, UNIT)
    for part in range(parts):
        grads_ref[:, part] = down_grad[:, part]
    store(
        parts + 3,
        jnp.concatenate([matmul(mixed_t[g], dattn_ref[...]) for g in range(DD // LANES)], 0),
    )
    for n in range(DFF // UNIT):
        store(parts + 4 + n, left_t(b_ref[...], dbefore_ref[:, n * UNIT : (n + 1) * UNIT]))
    for n in range(HEADP // UNIT):
        store(parts + 8 + n, left_t(z_ref[...], dpred_ref[:, n * UNIT : (n + 1) * UNIT]))

    def attend_back_group(g, _):
        lanes = pl.ds(pl.multiple_of(g * LANES, LANES), LANES)
        query, keys, values, dout = [r[:, lanes] for r in (q_ref, k_ref, v_ref, dmixed_ref)]
        keys_t = keys.T
        dkeys = jnp.zeros((TOK_DEV, LANES), F32)
        dvalues = jnp.zeros((TOK_DEV, LANES), F32)
        dquery = []
        for j in range(per):
            scores = right_t(keys, only(query, lane_head, j)) * factor + bias_ref[...]
            probs = jnp.exp(scores - lse_ref[g, j : j + 1, :])
            dvalues = jnp.where(key_head == j, matmul(probs.astype(BF), dout), dvalues)
            dprobs = right_t(values, only(dout, lane_head, j))
            delta = jnp.sum(dprobs * probs, 0, keepdims=True)
            dscores = (probs * (dprobs - delta)).astype(BF)
            dkeys = jnp.where(key_head == j, matmul(dscores, query), dkeys)
            dquery.append(matmul(keys_t[j * size : (j + 1) * size, :], dscores))
        dq_ref[:, lanes] = (jnp.concatenate(dquery, 0) * factor).astype(BF).T
        dk_ref[:, lanes] = (dkeys * factor).astype(BF)
        dv_ref[:, lanes] = dvalues.astype(BF)
        return 0

    lax.fori_loop(0, DD // LANES, attend_back_group, 0)

    store(parts, left_t(a_ref[VIS:, :], dq_ref[...]))
    store(parts + 1, left_t(a_ref[...], dk_ref[...]))
    store(parts + 2, left_t(a_ref[...], dv_ref[...]))

    def start_rows(rows, da):
        unit, rate = normalize(y_ref[rows, :])
        da = da + right_t(dk_ref[rows, :], wide_ref[:, DD : 2 * DD])
        da = da + right_t(dv_ref[rows, :], wide_ref[:, 2 * DD : 3 * DD])
        dh, dgain = normalize_back(unit, rate, gain_one, da)
        vec_ref[0:1, :] += dgain
        return dh

    dy = start_rows(slice(0, VIS), 0.0)
    dy_ref[...] = dy
    vec_ref[3:4, :] += jnp.sum(jnp.where(kept_ref[...] > 0, 0.0, dy), 0, keepdims=True)

    def start_hidden(n, _):
        rows, all_rows = hidden_rows(n)
        dy = start_rows(all_rows, right_t(dq_ref[rows, :], wide_ref[:, :DD]))
        vec_ref[3:4, :] += jnp.sum(dy + dmiddle_ref[rows, :], 0, keepdims=True)
        return 0

    lax.fori_loop(0, 2, start_hidden, 0)
    vec_ref[4:5, :] = loss_ref[:, :DD] + loss_ref[:, DD:]


def decoder_step(pos, seen, kept, flag, picked, stats, bias, vectors, wide, down):
    index = jnp.arange(PD)
    band, row, column = index // PATCH**2, index // PATCH % PATCH, index % PATCH
    low = band * (PATCH // 2) ** 2 + row // 2 * (PATCH // 2) + column // 2
    spread = low[None, :] == jnp.arange(LOWP)[:, None]
    gains = jnp.pad(vectors.reshape(4, DD), ((0, 4), (0, 0)))
    owners = lax.axis_size("fsdp")
    scratch = [
        ((TOK_DEV, DD), F32),
        ((TOK_DEV, DD), BF),
        ((HID, DD), BF),
        ((TOK_DEV, DD), BF),
        ((TOK_DEV, DD), BF),
        ((DD // LANES, LANES, HID), BF),
        ((HID, DD), BF),
        ((DD // LANES, LANES * DHEADS // DD, HID), F32),
        ((DD, HEADP), BF),
        ((HID, DD), BF),
        ((HID, DFF), BF),
        ((HID, DD), BF),
        ((HID, HEADP), BF),
        ((HID, DD), BF),
        ((HID, DFF), BF),
        ((HID, DD), BF),
        ((HID, DD), BF),
        ((HID, DD), F32),
        ((HID, DD), BF),
        ((TOK_DEV, DD), BF),
        ((TOK_DEV, DD), BF),
        ((1, HEADP), F32),
    ]
    vmem = pl.BlockSpec(memory_space=pltpu.VMEM)
    grads, dy, vec = pl.pallas_call(
        partial(decoder_kernel, owners),
        out_shape=(
            jax.ShapeDtypeStruct((owners, DFF // DD + 10, DD // owners, UNIT), BF),
            jax.ShapeDtypeStruct((VIS, DD), F32),
            jax.ShapeDtypeStruct((8, DD), F32),
        ),
        in_specs=[vmem] * 12,
        out_specs=(vmem,) * 3,
        scratch_shapes=[pltpu.VMEM(*entry) for entry in scratch],
        compiler_params=pltpu.CompilerParams(vmem_limit_bytes=60 * 2**20),
        cost_estimate=pl.CostEstimate(
            flops=40 * 10**9, bytes_accessed=40 * 2**20, transcendentals=2 * 10**7
        ),
    )(
        pos,
        seen,
        kept.astype(F32)[:, None],
        flag[:, None],
        picked,
        stats,
        bias,
        gains,
        (spread.T * 0.25).astype(BF),
        spread.astype(BF),
        wide,
        down,
    )
    return grads, dy, vec[:4].reshape(-1), jnp.sum(vec[4])


def block_forward(h, weights, gains, bias, heads, skip):
    wqkv, wout, wup, wdown = weights
    width = h.shape[1]
    normed_a = layer_norm(h, gains[0]).astype(BF)
    query = matmul(normed_a[skip:], wqkv[:, :width]).astype(BF)
    keys = matmul(normed_a, wqkv[:, width : 2 * width]).astype(BF)
    values = matmul(normed_a, wqkv[:, 2 * width :]).astype(BF)
    mixed_t, lse = attend(query.T, keys, values.T, bias, width // heads)
    middle = h[skip:] + left_t(mixed_t, wout)
    normed_b = layer_norm(middle, gains[1]).astype(BF)
    after, slope = gelu_parts(matmul(normed_b, wup))
    hidden = after.astype(BF)
    end = middle + matmul(hidden, wdown)
    return end, (h, normed_a, query, keys, values, mixed_t, lse, middle, normed_b, slope, hidden)


def block_backward(saved, grad, weights, gains, bias, heads, skip):
    wqkv, wout, wup, wdown = weights
    h, normed_a, query, keys, values, mixed_t, lse, middle, normed_b, slope, hidden = saved
    width = h.shape[1]
    dbranch = grad.astype(BF)
    dbefore = (right_t(dbranch, wdown) * slope).astype(BF)
    dmiddle, dgain_two = norm_back(middle, gains[1], right_t(dbefore, wup))
    dmiddle = dmiddle + grad
    dattn = dmiddle.astype(BF)
    dmixed = right_t(dattn, wout).astype(BF)
    dqt, dkeys, dvalues = attend_back(query, keys, values, dmixed, bias, lse, width // heads)
    dquery = dqt.T
    if skip:
        dquery = jnp.pad(dquery, ((skip, 0), (0, 0)))
        dmiddle = jnp.pad(dmiddle, ((skip, 0), (0, 0)))
    dqkv = jnp.concatenate([dquery, dkeys, dvalues], 1)
    dh, dgain_one = norm_back(h, gains[0], right_t(dqkv, wqkv))
    factors = ((normed_a.T, dqkv), (mixed_t, dattn), (normed_b.T, dbefore), (hidden.T, dbranch))
    return (dh + dmiddle, factors, (dgain_one, dgain_two))


def reduce_rows(grad):
    return lax.psum_scatter(grad.astype(BF), "fsdp", scatter_dimension=0, tiled=True)


def enc_split(wide, down):
    return (
        (wide[:, : 3 * D], wide[:, 3 * D : 4 * D], wide[:, 4 * D : 4 * D + FF], down),
        wide[:, 4 * D + FF :],
    )


def advance(weight, mom, avg, grad, rate):
    grad = grad + DECAY * weight
    buf = MOMENTUM * mom + grad
    new = weight - rate * (grad + MOMENTUM * buf)
    return (buf, new, AVERAGE * avg + (1.0 - AVERAGE) * new)


def arrange(valid, masked, scene_ids):
    slots = valid.shape[0]
    live = valid > 0
    kinds = jnp.stack([live & (masked == 0), live & (masked > 0), ~live], 1)
    index = jnp.arange(slots, dtype=jnp.int32)
    ranks = matmul((index[None, :] < index[:, None]).astype(BF), kinds.astype(BF)).astype(jnp.int32)
    n_seen, n_hid = [jnp.sum(kinds[:, i].astype(jnp.int32)) for i in range(2)]
    empty = ranks[:, 2]
    to_empty = jnp.where(empty < VIS - n_seen, n_seen + empty, n_seen + n_hid + empty)
    place = jnp.where(
        kinds[:, 0], ranks[:, 0], jnp.where(kinds[:, 1], VIS + ranks[:, 1], to_empty)
    )
    return (place[None, :] == index[:, None]).astype(BF), n_seen, n_hid


def exact_pick(pick, array):
    high = lax.reduce_precision(array, 8, 7)
    rest = array - high
    mid = lax.reduce_precision(rest, 8, 7)
    low = rest - mid
    return (
        matmul(pick, high.astype(BF)) + matmul(pick, mid.astype(BF)) + matmul(pick, low.astype(BF))
    )


def body(
    pixels,
    masked,
    valid,
    scene_ids,
    gsd_index,
    coords,
    embed,
    wide_enc,
    enc_down,
    wide_dec,
    dec_down,
    vectors,
    embed_mom,
    wide_enc_mom,
    enc_down_mom,
    wide_dec_mom,
    dec_down_mom,
    vector_mom,
    embed_avg,
    wide_enc_avg,
    enc_down_avg,
    wide_dec_avg,
    dec_down_avg,
    vector_avg,
):
    slots = pixels.shape[0]
    fast = (lax.axis_size("dp"), lax.axis_size("fsdp")) == (4, 8)
    w_dec, w_dec_down = [
        lax.all_gather(w.astype(BF), "fsdp", axis=0, tiled=True) for w in (wide_dec, dec_down)
    ]
    rows_ok = valid.astype(jnp.float32)
    flags = rows_ok * masked.astype(jnp.float32)
    bands = pixels.reshape(slots, BANDS, PATCH * PATCH)
    weighted = bands * rows_ok[:, None, None]
    band_sum = jnp.sum(weighted, axis=(0, 2))
    counts = jnp.stack([jnp.sum(rows_ok), jnp.sum(flags)])
    band_sq = jnp.sum(weighted * bands, axis=(0, 2))
    stats = jnp.concatenate([band_sum, band_sq, counts])

    pick, n_seen, n_hid = arrange(valid, masked, scene_ids)
    picked_pixels = exact_pick(pick, pixels)
    small = matmul(
        pick, jnp.concatenate([(scene_ids % 2)[:, None], coords], 1).astype(BF)
    )
    odd, coord = small[:, 0], small[:, 1:]
    level = jnp.where(odd == 0, gsd_index[0], gsd_index[1]).astype(jnp.float32)
    scale = jnp.exp2(0.5 * level - 1.0)
    index = jnp.arange(slots, dtype=jnp.int32)
    kept = index[:VIS] < n_seen
    hidden_ok = index[:HID] < n_hid
    live = jnp.concatenate([kept, hidden_ok])
    keptf = kept.astype(jnp.float32)[:, None]
    allow = live[:, None] & (odd[:, None] == odd[None, :]) | (index[:, None] == index[None, :])
    bias = jnp.where(allow, 0.0, NEGATIVE)
    bias_enc, bias_dec = bias[:VIS, :VIS], bias[:, VIS:]

    gains_enc = (vectors[:D], vectors[D : 2 * D])
    gain_enc_out = vectors[2 * D : 3 * D]
    pos_enc = positions(coord[:VIS], scale[:VIS], D)
    low_enc = [w.astype(BF) for w in (embed, wide_enc, enc_down)]
    if fast:
        gains = jnp.pad(vectors[: 3 * D].reshape(3, D), ((0, 5), (0, 0)))
        stats = jnp.broadcast_to(stats[:, None], (8, LANES))
        w_enc, w_enc_down, stats, *factors, h_start, qkv, middle, slope, h_end, seen_out = (
            encoder_forward(picked_pixels[:VIS], stats, pos_enc, bias_enc.T, gains, *low_enc)
        )
    else:
        stats = jnp.broadcast_to(lax.psum(stats, ("dp", "fsdp"))[:, None], (8, LANES))
    count = stats[7, 0]
    if not fast:
        w_embed, w_enc, w_enc_down = [
            lax.all_gather(w, "fsdp", axis=0, tiled=True) for w in low_enc
        ]
        enc_weights, w_link = enc_split(w_enc, w_enc_down)
        mean = jnp.repeat(stats[:3, 0] / (stats[6, 0] * (PATCH * PATCH)), PATCH * PATCH)
        square = jnp.repeat(stats[3:6, 0] / (stats[6, 0] * (PATCH * PATCH)), PATCH * PATCH)
        rate = lax.rsqrt(square - mean * mean + EPS)
        inputs = ((picked_pixels[:VIS] - mean) * rate).astype(BF)
        h_start = matmul(inputs, w_embed) + pos_enc
        h_end, enc_saved = block_forward(h_start, enc_weights, gains_enc, bias_enc, HEADS, 0)
        encoded = layer_norm(h_end, gain_enc_out).astype(BF)
        seen_out = matmul(encoded, w_link)
    pos_dec = positions(coord, scale, DD)
    dec_grads, dy_seen, dec_vec, local_loss = decoder_step(
        pos_dec,
        seen_out,
        kept,
        hidden_ok.astype(F32),
        picked_pixels[VIS:],
        stats,
        bias_dec,
        vectors[3 * D :],
        w_dec,
        w_dec_down,
    )
    wide = wide_dec.shape[1]
    if fast:
        vec = jnp.concatenate([jnp.zeros((3 * D,), F32), dec_vec, local_loss[None]])
        vec = jnp.pad(vec, (0, 8 * D - vec.shape[0])).reshape(8, D)
        inputs_t, a_t, mixed_t, b_t, hidden_t, z_t = factors
        *enc_parts, dec_wide, dec_tall, vec = encoder_back(
            dy_seen,
            keptf,
            vec,
            gains,
            bias_enc,
            qkv,
            dec_grads,
            (h_end, middle, h_start, slope),
            w_enc,
            w_enc_down,
            (z_t, hidden_t, b_t, mixed_t, a_t, inputs_t),
        )
        dec_parts = (dec_wide[:, :wide], dec_tall)
        vector_grad, loss_sum = vec[:5].reshape(-1), vec[5, 0]
    else:
        dseen = (dy_seen * keptf).astype(BF)
        dh_end, dgain_enc_out = norm_back(h_end, gain_enc_out, right_t(dseen, w_link))
        dh_start, enc_factors, dgains_enc = block_backward(
            enc_saved, dh_end, enc_weights, gains_enc, bias_enc, HEADS, 0
        )
        enc_grads = [matmul(*pair).astype(BF) for pair in enc_factors]
        link_grad = left_t(encoded, dseen).astype(BF)
        enc_parts = lax.psum(
            (
                reduce_rows(left_t(inputs, dh_start.astype(BF))),
                reduce_rows(
                    jnp.concatenate([enc_grads[0], enc_grads[1], enc_grads[2], link_grad], 1)
                ),
                reduce_rows(enc_grads[3]),
            ),
            "dp",
        )
        dec_sum = lax.psum(reduce_rows(dec_grads), "dp")[0]
        rows, parts = dec_sum.shape[1], DFF // DD
        dec_parts = (
            dec_sum[parts:].transpose(1, 0, 2).reshape(rows, -1)[:, :wide],
            dec_sum[:parts].reshape(-1, DD),
        )
        vector_grad = jnp.concatenate([*dgains_enc, dgain_enc_out, dec_vec])
        vector_grad, loss_sum = lax.psum((vector_grad, local_loss), ("dp", "fsdp"))
    shard_grads = [g.astype(F32) for g in (*enc_parts, *dec_parts)]
    rate = STEP_UNIT * (PD * TOK_DEV * lax.axis_size("dp") * lax.axis_size("fsdp")) ** 0.5
    weights = (embed, wide_enc, enc_down, wide_dec, dec_down)
    moms = (embed_mom, wide_enc_mom, enc_down_mom, wide_dec_mom, dec_down_mom)
    avgs = (embed_avg, wide_enc_avg, enc_down_avg, wide_dec_avg, dec_down_avg)
    outs = []
    for number in range(5):
        buf, new, avg = advance(
            weights[number], moms[number], avgs[number], shard_grads[number], rate
        )
        outs += [buf, new, avg, new.astype(jnp.bfloat16)]
    return (*outs, *advance(vectors, vector_mom, vector_avg, vector_grad, rate), loss_sum, count)


def solution(mesh):
    both, rows = P(("dp", "fsdp")), P("fsdp", None)
    placed = (P(("dp", "fsdp"), None), both, both, both, both, P(("dp", "fsdp"), None))
    states = (rows,) * 5 + (P(),)
    return jax.shard_map(
        body,
        mesh=mesh,
        in_specs=placed + states * 3,
        out_specs=(rows,) * 20 + (P(),) * 5,
        check_vma=False,
    )
```

```python
from functools import partial

import jax
import jax.numpy as jnp
from jax import lax
from jax.experimental import pallas as pl
from jax.experimental.pallas import tpu as pltpu
from jax.sharding import PartitionSpec as P

D = 1024
HEADS = 16
FF = 4096
DD = 512
DHEADS = 16
DFF = 2048
PATCH = 16
BANDS = 3
TOK_DEV = 768
PD = 768
LOWD = 192
VIS = 192
HID = TOK_DEV - VIS

EPS = 1e-06
MOMENTUM = 0.9
DECAY = 0.0001
AVERAGE = 0.9
STEP_UNIT = 0.003
NEGATIVE = -1e30
LANES = 128
BF = jnp.bfloat16
F32 = jnp.float32


def matmul(left, right):
    return jnp.dot(left, right, preferred_element_type=jnp.float32)


def left_t(left, right):
    return lax.dot_general(
        left, right, (((0,), (0,)), ((), ())), preferred_element_type=jnp.float32
    )


def right_t(left, right):
    return lax.dot_general(
        left, right, (((1,), (1,)), ((), ())), preferred_element_type=jnp.float32
    )


def layer_norm(h, gain):
    mean = jnp.mean(h, -1, keepdims=True)
    cent = h - mean
    var = jnp.mean(cent * cent, -1, keepdims=True)
    return cent * lax.rsqrt(var + EPS) * gain


def norm_back(h, gain, grad):
    result, pull = jax.vjp(layer_norm, h, gain)
    return pull(grad)


def gelu_parts(before):
    below = 0.5 * (1.0 + lax.erf(before * 0.5**0.5))
    slope = below + before * jnp.exp(before * before * -0.5) * (0.5 / jnp.pi) ** 0.5
    return before * below, slope


def positions(coord, scale, width):
    quarter = width // 4
    omega = 10000.0 ** (-jnp.arange(quarter, dtype=jnp.float32) / quarter)
    angle_x = coord[:, 0:1] * scale[:, None] * omega[None, :]
    angle_y = coord[:, 1:2] * scale[:, None] * omega[None, :]
    return jnp.concatenate(
        [jnp.sin(angle_x), jnp.cos(angle_x), jnp.sin(angle_y), jnp.cos(angle_y)], -1
    )


def row_loss(pred, normed):
    rows = normed.shape[0]
    coarse = jnp.mean(normed.reshape(rows, BANDS, PATCH // 2, 2, PATCH // 2, 2), axis=(3, 5))
    upper = jnp.repeat(jnp.repeat(coarse, 2, axis=2), 2, axis=3).reshape(rows, PD)
    err_high = pred[:, :PD] - (normed - upper)
    err_low = pred[:, PD:] - coarse.reshape(rows, LOWD)
    return jnp.mean(jnp.sqrt(err_high * err_high + 1.0) - 1.0, -1) + jnp.mean(err_low * err_low, -1)


def attend_kernel(size, qt_ref, k_ref, vt_ref, bias_ref, ot_ref, lse_ref):
    per = LANES // size
    row_head = lax.broadcasted_iota(jnp.int32, qt_ref.shape, 0) // size
    factor = size ** (-0.5)
    for j in range(per):
        query = jnp.where(row_head == j, qt_ref[...].astype(F32), 0.0).astype(BF)
        scores = matmul(k_ref[...], query) * factor + bias_ref[...]
        top = jnp.max(scores, 0, keepdims=True)
        probs = jnp.exp(scores - top)
        total = jnp.sum(probs, 0, keepdims=True)
        probs = (probs * (1.0 / total)).astype(BF)
        rows = slice(j * size, (j + 1) * size)
        ot_ref[rows, :] = matmul(vt_ref[rows, :], probs).astype(BF)
        lse_ref[0, j : j + 1, :] = top + jnp.log(total)


def attend(qt, keys, vt, bias, size):
    width, queries = qt.shape
    rows = keys.shape[0]
    groups, per = width // LANES, LANES // size
    return pl.pallas_call(
        partial(attend_kernel, size),
        grid=(groups,),
        out_shape=(
            jax.ShapeDtypeStruct((width, queries), BF),
            jax.ShapeDtypeStruct((groups, per, queries), F32),
        ),
        in_specs=[
            pl.BlockSpec((LANES, queries), lambda g: (g, 0)),
            pl.BlockSpec((rows, LANES), lambda g: (0, g)),
            pl.BlockSpec((LANES, rows), lambda g: (g, 0)),
            pl.BlockSpec((rows, queries), lambda g: (0, 0)),
        ],
        out_specs=(
            pl.BlockSpec((LANES, queries), lambda g: (g, 0)),
            pl.BlockSpec((1, per, queries), lambda g: (g, 0, 0)),
        ),
        compiler_params=pltpu.CompilerParams(vmem_limit_bytes=40 * 2**20),
        cost_estimate=pl.CostEstimate(
            flops=4 * rows * queries * width * per,
            bytes_accessed=4 * rows * queries,
            transcendentals=rows * queries * width // size,
        ),
    )(qt, keys, vt, bias)


def attend_back_kernel(
    size,
    qt_ref,
    q_ref,
    k_ref,
    kt_ref,
    v_ref,
    do_ref,
    dot_ref,
    bias_ref,
    *rest,
):
    *lse_ref, dqt_ref, dk_ref, dv_ref = rest
    per = LANES // size
    row_head = lax.broadcasted_iota(jnp.int32, qt_ref.shape, 0) // size
    lane_head = lax.broadcasted_iota(jnp.int32, dk_ref.shape, 1) // size
    factor = size ** (-0.5)
    dkeys = jnp.zeros(dk_ref.shape, F32)
    dvalues = jnp.zeros(dv_ref.shape, F32)
    for j in range(per):
        query = jnp.where(row_head == j, qt_ref[...].astype(F32), 0.0).astype(BF)
        dout = jnp.where(row_head == j, dot_ref[...].astype(F32), 0.0).astype(BF)
        scores = matmul(k_ref[...], query) * factor + bias_ref[...]
        if lse_ref:
            probs = jnp.exp(scores - lse_ref[0][0, j : j + 1, :])
        else:
            probs = jnp.exp(scores - jnp.max(scores, 0, keepdims=True))
            probs = probs * (1.0 / jnp.sum(probs, 0, keepdims=True))
        dvalues = jnp.where(lane_head == j, matmul(probs.astype(BF), do_ref[...]), dvalues)
        dprobs = matmul(v_ref[...], dout)
        delta = jnp.sum(dprobs * probs, 0, keepdims=True)
        dscores = (probs * (dprobs - delta)).astype(BF)
        dkeys = jnp.where(lane_head == j, matmul(dscores, q_ref[...]), dkeys)
        rows = slice(j * size, (j + 1) * size)
        dqt_ref[rows, :] = (matmul(kt_ref[rows, :], dscores) * factor).astype(BF)
    dk_ref[...] = (dkeys * factor).astype(BF)
    dv_ref[...] = dvalues.astype(BF)


def attend_back(query, keys, values, dmixed, bias, lse, size):
    queries, width = query.shape
    rows = keys.shape[0]
    groups, per = width // LANES, LANES // size
    tall = lambda n: pl.BlockSpec((n, LANES), lambda g: (0, g))
    flat = lambda n: pl.BlockSpec((LANES, n), lambda g: (g, 0))
    return pl.pallas_call(
        partial(attend_back_kernel, size),
        grid=(groups,),
        out_shape=(
            jax.ShapeDtypeStruct((width, queries), BF),
            jax.ShapeDtypeStruct((rows, width), BF),
            jax.ShapeDtypeStruct((rows, width), BF),
        ),
        in_specs=[
            flat(queries),
            tall(queries),
            tall(rows),
            flat(rows),
            tall(rows),
            tall(queries),
            flat(queries),
            pl.BlockSpec((rows, queries), lambda g: (0, 0)),
        ]
        + [pl.BlockSpec((1, per, queries), lambda g: (g, 0, 0))] * (lse is not None),
        out_specs=(flat(queries), tall(rows), tall(rows)),
        compiler_params=pltpu.CompilerParams(vmem_limit_bytes=48 * 2**20),
        cost_estimate=pl.CostEstimate(
            flops=10 * rows * queries * width * per,
            bytes_accessed=4 * rows * queries,
            transcendentals=rows * queries * width // size,
        ),
    )(query.T, query, keys, keys.T, values, dmixed, dmixed.T, bias, *([] if lse is None else [lse]))


MESH = pl.DeviceIdType.MESH
UNIT = 512
HALF = UNIT // 2
ROWS = 128
HALF_ROWS = ROWS // 2
LAGS = (2, 4, 6, 8, 11)


def put(source, target, send, recv, device):
    return pltpu.make_async_remote_copy(
        src_ref=source,
        dst_ref=target,
        send_sem=send,
        recv_sem=recv,
        device_id=device,
        device_id_type=MESH,
    )


def back_kernel(
    dec_units,
    blocks,
    units,
    spots,
    dy_ref,
    kept_ref,
    vec_ref,
    gains_ref,
    bias_ref,
    qkv_ref,
    dec_ref,
    end_ref,
    middle_ref,
    start_ref,
    slope_ref,
    wide_ref,
    down_ref,
    *refs,
):
    n_left = max(b[0] for b in blocks) + 1
    lefts, refs = refs[:n_left], refs[n_left:]
    outs, refs = refs[:5], refs[5:]
    vec_out, refs = refs[0], refs[1:]
    (
        xo,
        xp,
        yo,
        yp,
        do,
        dp,
        products,
        a_out,
        a_in,
        b_out,
        b_in,
        sums,
        z_out,
        z_one,
        z_two,
        v_in,
        v_out,
        wide_buf,
        down_buf,
        slope_buf,
        h_buf,
        dend_ref,
        dmid_ref,
        dbranch_ref,
        dmixed_ref,
        dqkv_ref,
        grad_vec,
        wide_sem,
        down_sem,
        slope_sem,
        h_sem,
        dec_sem,
        left_sem,
        right_sem,
        a_send,
        a_recv,
        b_send,
        b_recv,
        z_send,
        z_recv,
        v_send,
        v_recv,
        store_sem,
    ) = refs
    count = dec_units + len(units)
    z, f = lax.axis_index("dp"), lax.axis_index("fsdp")
    core, place = f % 2, f // 2
    x, y = place % 2, place // 2
    partner = (z, f + 1 - 2 * core)
    x_side = (z, f + 2 - 4 * x)
    y_side = (z, f + 4 - 8 * y)
    at_x, at_y, at_far = place + 1 - 2 * x, place + 2 - 4 * y, 3 - place
    low = z < 2
    outer = (z == 0) | (z == 3)
    inner = (z == 1) | (z == 2)
    inward = (jnp.where(low, 1, 2), f)
    across = (3 - z, f)
    outward = (jnp.where(low, 0, 3), f)

    ring = wide_buf.shape[0]
    up_chunks, out_chunks, qkv_chunks = FF // UNIT, D // UNIT, 3 * D // UNIT
    chunks = 1 + up_chunks + out_chunks + qkv_chunks

    def wide_copy(w):
        inside = jnp.where(w < 1 + up_chunks, 4 * D + UNIT * (w - 1), 3 * D + UNIT * (w - 1 - up_chunks))
        column = jnp.where(
            w == 0,
            4 * D + FF,
            jnp.where(w < 1 + up_chunks + out_chunks, inside, UNIT * (w - 1 - up_chunks - out_chunks)),
        )
        return pltpu.make_async_copy(
            wide_ref.at[:, pl.ds(pl.multiple_of(column, UNIT), UNIT)],
            wide_buf.at[w % ring],
            wide_sem.at[w % ring],
        )

    def down_copy(j):
        rows = pl.ds(pl.multiple_of(j * UNIT, UNIT), UNIT)
        return pltpu.make_async_copy(down_ref.at[rows], down_buf.at[j % 2], down_sem.at[j % 2])

    def slope_copy(j):
        columns = pl.ds(pl.multiple_of(j * UNIT, UNIT), UNIT)
        return pltpu.make_async_copy(slope_ref.at[:, columns], slope_buf.at[j % 2], slope_sem.at[j % 2])

    def h_copy(source):
        return pltpu.make_async_copy(source, h_buf, h_sem.at[0])

    h_copy(end_ref).start()
    for n in range(ring):
        wide_copy(n).start()
    for n in range(2):
        down_copy(n).start()
        slope_copy(n).start()

    barrier = pltpu.get_barrier_semaphore()
    for device in (partner, x_side, y_side):
        pl.semaphore_signal(barrier, inc=1, device_id=device, device_id_type=MESH)

    @pl.when(outer)
    def _():
        pl.semaphore_signal(barrier, inc=1, device_id=inward, device_id_type=MESH)
        pl.semaphore_wait(barrier, 4)

    @pl.when(inner)
    def _():
        pl.semaphore_signal(barrier, inc=1, device_id=across, device_id_type=MESH)
        pl.semaphore_signal(barrier, inc=1, device_id=outward, device_id_type=MESH)
        pl.semaphore_wait(barrier, 5)

    def swap_dec(source, n):
        return put(source, dp.at[n], dec_sem.at[n, 1], dec_sem.at[n, 2], partner)

    def swap_left(source, b):
        return put(source, xp.at[b], left_sem.at[b, 1], left_sem.at[b, 2], partner)

    def swap_right(r):
        return put(yo.at[r], yp.at[r], right_sem.at[r, 0], right_sem.at[r, 1], partner)

    for n in range(dec_units):
        swap_dec(dec_ref.at[:, 1 - core, n], n).start()
        pltpu.make_async_copy(dec_ref.at[:, core, n], do.at[n], dec_sem.at[n, 0]).start()
    for b, (left, sub) in enumerate(blocks):
        rows = pl.ds(sub * ROWS, ROWS)
        swap_left(lefts[left].at[:, 1 - core, rows], b).start()
        pltpu.make_async_copy(lefts[left].at[:, core, rows], xo.at[b], left_sem.at[b, 0]).start()

    firsts = 1 + out_chunks
    single = next(n for n in range(1, len(units)) if units[n][1] >= firsts)
    starts = [n for n in range(1, len(units)) if units[n][0] != units[n - 1][0]]

    def block_of(e):
        return sum([jnp.where(e >= n, 1, 0) for n in starts], jnp.int32(0))

    def right_of(e):
        early = jnp.where(e == 0, 0, 1 + (e + out_chunks - 1) % out_chunks)
        return jnp.where(e < single, early, e - single + firsts)

    first, second = pl.ds(0, HALF), pl.ds(HALF, HALF)

    def part(u, owner, columns, k):
        @pl.when(u < dec_units)
        def _():
            n = jnp.minimum(u, dec_units - 1)
            products[k] = do[n, owner, :, columns].astype(F32) + dp[n, owner, :, columns].astype(F32)

        @pl.when(u >= dec_units)
        def _():
            e = jnp.maximum(u - dec_units, 0)
            b, r = block_of(e), right_of(e)
            total = matmul(xo[b, owner], yo[r, :, columns])
            products[k] = total + matmul(xp[b, owner], yp[r, :, columns])

        return products[k]

    def copy_a(u, side):
        slot = u % a_out.shape[0]
        return put(
            a_out.at[slot, side],
            a_in.at[u, side],
            a_send.at[slot, side],
            a_recv.at[u, side],
            (x_side, y_side)[side],
        )

    def copy_b(u, side):
        slot = u % b_out.shape[0]
        return put(
            b_out.at[slot, side],
            b_in.at[u, side],
            b_send.at[slot, side],
            b_recv.at[u, side],
            (y_side, x_side)[side],
        )

    z_slots = z_out.shape[0]

    def copy_in(u):
        return put(z_out.at[u % z_slots], z_one.at[u], z_send.at[u, 0], z_recv.at[u, 0], inward)

    def copy_across(u):
        return put(z_out.at[u % z_slots], z_two.at[u], z_send.at[u, 0], z_recv.at[u, 1], across)

    def copy_out(u):
        return put(z_one.at[u], z_one.at[u], z_send.at[u, 1], z_recv.at[u, 0], outward)

    def copy_v(step, device):
        return put(v_out.at[step], v_in.at[step], v_send.at[step], v_recv.at[step], device)

    gain_one, gain_two, gain_out = [gains_ref[n : n + 1, :] for n in range(3)]

    def give(r, value):
        yo[r] = value
        swap_right(r).start()

    def columns_at(n):
        return slice(n * UNIT, (n + 1) * UNIT)

    def back_link():
        dseen = jnp.where(kept_ref[...] > 0, dy_ref[...], 0.0).astype(BF)
        give(0, dseen)
        wide_copy(0).wait()
        h_copy(end_ref).wait()
        unit, rate = normalize(h_buf[...])
        dend, dgain = normalize_back(unit, rate, gain_out, right_t(dseen, wide_buf[0]))
        grad_vec[...] = vec_ref[...]
        grad_vec[2:3, :] = dgain
        dend_ref[...] = dend
        dbranch_ref[...] = dend.astype(BF)
        for n in range(out_chunks):
            give(1 + n, dbranch_ref[:, columns_at(n)])
        wide_copy(ring).start()
        h_copy(middle_ref).start()
        dmid_ref[...] = jnp.zeros_like(dmid_ref)

    def back_hidden(j):
        w = 1 + j
        down_copy(j).wait()
        slope_copy(j).wait()
        wide_copy(w).wait()
        dhidden = right_t(dbranch_ref[...], down_buf[j % 2])
        dbefore = (dhidden * slope_buf[j % 2]).astype(BF)
        give(firsts + j, dbefore)
        dmid_ref[...] += right_t(dbefore, wide_buf[w % ring])
        wide_copy(w + ring).start()

        @pl.when(j + 2 < up_chunks)
        def _():
            down_copy(j + 2).start()
            slope_copy(j + 2).start()

    def back_out():
        h_copy(middle_ref).wait()
        unit, rate = normalize(h_buf[...])
        dmiddle, dgain = normalize_back(unit, rate, gain_two, dmid_ref[...])
        grad_vec[1:2, :] = dgain
        dmiddle = dmiddle + dend_ref[...]
        dend_ref[...] = dmiddle
        dattn = dmiddle.astype(BF)
        dmixed = jnp.zeros((VIS, D), F32)
        for n in range(out_chunks):
            w = 1 + up_chunks + n
            piece = dattn[:, columns_at(n)]
            give(firsts + up_chunks + n, piece)
            wide_copy(w).wait()
            dmixed = dmixed + right_t(piece, wide_buf[w % ring])
            wide_copy(w + ring).start()
        dmixed_ref[...] = dmixed.astype(BF)
        h_copy(start_ref).start()
        dmid_ref[...] = jnp.zeros_like(dmid_ref)

    size = D // HEADS
    lane_head = lax.broadcasted_iota(jnp.int32, (VIS, LANES), 1) // size

    def only(array, j):
        return jnp.where(lane_head == j, array.astype(F32), 0.0).astype(BF)

    def back_attention(g):
        at = [pl.ds(pl.multiple_of(n * D + g * LANES, LANES), LANES) for n in range(3)]
        query, keys, values = [qkv_ref[:, lanes] for lanes in at]
        dout = dmixed_ref[:, at[0]]
        keys_t = keys.T
        factor = size ** (-0.5)
        dkeys, dvalues = jnp.zeros((VIS, LANES), F32), jnp.zeros((VIS, LANES), F32)
        dquery = []
        for j in range(LANES // size):
            scores = right_t(keys, only(query, j)) * factor + bias_ref[...]
            probs = jnp.exp(scores - jnp.max(scores, 0, keepdims=True))
            probs = probs * (1.0 / jnp.sum(probs, 0, keepdims=True))
            dvalues = jnp.where(lane_head == j, matmul(probs.astype(BF), dout), dvalues)
            dprobs = right_t(values, only(dout, j))
            delta = jnp.sum(dprobs * probs, 0, keepdims=True)
            dscores = (probs * (dprobs - delta)).astype(BF)
            dkeys = jnp.where(lane_head == j, matmul(dscores, query), dkeys)
            dquery.append(matmul(keys_t[j * size : (j + 1) * size, :], dscores))
        dqkv_ref[:, at[0]] = (jnp.concatenate(dquery, 0) * factor).astype(BF).T
        dqkv_ref[:, at[1]] = (dkeys * factor).astype(BF)
        dqkv_ref[:, at[2]] = dvalues.astype(BF)

    def give_qkv():
        for c in range(qkv_chunks):
            give(firsts + up_chunks + out_chunks + c, dqkv_ref[:, columns_at(c)])

    def back_qkv(c):
        w = 1 + up_chunks + out_chunks + c
        wide_copy(w).wait()
        piece = dqkv_ref[:, pl.ds(pl.multiple_of(c * UNIT, UNIT), UNIT)]
        dmid_ref[...] += right_t(piece, wide_buf[w % ring])

        @pl.when(w + ring < chunks)
        def _():
            wide_copy(w + ring).start()

    def back_start():
        h_copy(start_ref).wait()
        unit, rate = normalize(h_buf[...])
        dh, dgain = normalize_back(unit, rate, gain_one, dmid_ref[...])
        grad_vec[0:1, :] = dgain
        dh = (dh + dend_ref[...]).astype(BF)
        for n in range(out_chunks):
            give(firsts + up_chunks + out_chunks + qkv_chunks + n, dh[:, columns_at(n)])

    at_hidden = 1
    at_out = at_hidden + up_chunks
    at_attention = at_out + 1
    groups = D // LANES
    at_qkv = at_attention + groups
    at_start = at_qkv + qkv_chunks
    at_vec = at_start + 1

    def step(i, _):
        def stage(lag, also=None):
            u = i - lag
            ok = (u >= 0) & (u < count)
            if also is not None:
                ok = ok & also
            return u, pl.when(ok)

        u0, when = stage(0)

        @when
        def _():
            u = u0

            @pl.when(u < dec_units)
            def _():
                pltpu.make_async_copy(do.at[u], do.at[u], dec_sem.at[u, 0]).wait()
                swap_dec(do.at[u], u).wait()

            @pl.when(u == dec_units)
            def _():
                for b in range(len(blocks)):
                    pltpu.make_async_copy(xo.at[b], xo.at[b], left_sem.at[b, 0]).wait()
                    swap_left(xo.at[b], b).wait()
                for r in range(firsts):
                    swap_right(r).wait()

            @pl.when(u >= dec_units + single)
            def _():
                swap_right(u - dec_units - single + firsts).wait()

            @pl.when(u >= a_out.shape[0])
            def _():
                for side in range(2):
                    copy_a(u - a_out.shape[0], side).wait_send()

            slot = u % a_out.shape[0]
            a_out[slot, 0, 0] = part(u, at_x, first, 0).astype(BF)
            a_out[slot, 0, 1] = part(u, at_far, first, 1).astype(BF)
            copy_a(u, 0).start()
            a_out[slot, 1, 0] = part(u, at_y, second, 2).astype(BF)
            a_out[slot, 1, 1] = part(u, at_far, second, 3).astype(BF)
            copy_a(u, 1).start()

        u1, when = stage(LAGS[0])

        @when
        def _():
            u = u1
            slot = u % b_out.shape[0]

            @pl.when(u >= b_out.shape[0])
            def _():
                for side in range(2):
                    copy_b(u - b_out.shape[0], side).wait_send()

            copy_a(u, 0).wait_recv()
            b_out[slot, 0] = (part(u, at_y, first, 0) + a_in[u, 0, 1].astype(F32)).astype(BF)
            copy_b(u, 0).start()
            copy_a(u, 1).wait_recv()
            b_out[slot, 1] = (part(u, at_x, second, 1) + a_in[u, 1, 1].astype(F32)).astype(BF)
            copy_b(u, 1).start()

        u2, when = stage(LAGS[1])

        @when
        def _():
            u = u2
            copy_b(u, 0).wait_recv()
            copy_b(u, 1).wait_recv()
            for side, columns in enumerate((first, second)):
                total = part(u, place, columns, side) + a_in[u, side, 0].astype(F32)
                sums[u % 4, :, columns] = total + b_in[u, side].astype(F32)

            @pl.when(outer)
            def _():
                @pl.when(u >= z_slots)
                def _():
                    copy_in(u - z_slots).wait_send()

                z_out[u % z_slots] = sums[u % 4].astype(BF)
                copy_in(u).start()

        u3, when = stage(LAGS[2], inner)

        @when
        def _():
            u = u3
            copy_in(u).wait_recv()

            @pl.when(u >= z_slots)
            def _():
                copy_across(u - z_slots).wait_send()

            z_out[u % z_slots] = (sums[u % 4] + z_one[u].astype(F32)).astype(BF)
            copy_across(u).start()

        u4, when = stage(LAGS[3], inner)

        @when
        def _():
            u = u4
            copy_across(u).wait_recv()
            z_one[u] = (z_out[u % z_slots].astype(F32) + z_two[u].astype(F32)).astype(BF)
            copy_out(u).start()

        u5, when = stage(LAGS[4], outer)

        @when
        def _():
            copy_out(u5).wait_recv()

        pl.when(i == 0)(back_link)

        @pl.when((i >= at_hidden) & (i < at_hidden + up_chunks))
        def _():
            back_hidden(i - at_hidden)

        pl.when(i == at_out)(back_out)

        @pl.when((i >= at_attention) & (i < at_attention + groups))
        def _():
            back_attention(i - at_attention)

        pl.when(i == at_qkv)(give_qkv)

        @pl.when((i >= at_qkv) & (i < at_qkv + qkv_chunks))
        def _():
            back_qkv(i - at_qkv)

        pl.when(i == at_start)(back_start)

        for number, device in enumerate((partner, x_side, y_side)):

            @pl.when(i == at_vec + number)
            def _():
                if number == 0:
                    v_out[0] = grad_vec[...]
                else:
                    copy_v(number - 1, (partner, x_side, y_side)[number - 1]).wait_recv()
                    v_out[number] = v_out[number - 1] + v_in[number - 1]
                copy_v(number, device).start()

        @pl.when(i == at_vec + 3)
        def _():
            copy_v(2, y_side).wait_recv()
            v_out[3] = v_out[2] + v_in[2]

            @pl.when(outer)
            def _():
                copy_v(3, inward).start()

        @pl.when((i == at_vec + 4) & inner)
        def _():
            copy_v(3, inward).wait_recv()
            v_out[4] = v_out[3] + v_in[3]
            copy_v(4, across).start()

        @pl.when((i == at_vec + 5) & inner)
        def _():
            copy_v(4, across).wait_recv()
            v_out[5] = v_out[4] + v_in[4]
            copy_v(5, outward).start()
            vec_out[...] = v_out[5]

        @pl.when((i == at_vec + 7) & outer)
        def _():
            copy_v(5, outward).wait_recv()
            vec_out[...] = v_in[5]

        return 0

    lax.fori_loop(0, count + LAGS[4], step, 0)

    stores = []
    for n, (u, start, out, row, rows, column) in enumerate(spots):
        stores.append(
            pltpu.make_async_copy(
                z_one.at[u, pl.ds(start, rows)],
                outs[out].at[pl.ds(row, rows), pl.ds(column, UNIT)],
                store_sem.at[n],
            )
        )
    for store in stores:
        store.start()
    for u in range(count - a_out.shape[0], count):
        for side in range(2):
            copy_a(u, side).wait_send()
    for u in range(count - b_out.shape[0], count):
        for side in range(2):
            copy_b(u, side).wait_send()
    for number, device in enumerate((partner, x_side, y_side)):
        copy_v(number, device).wait_send()
    for store in stores:
        store.wait()

    @pl.when(outer)
    def _():
        copy_v(3, inward).wait_send()
        for u in range(count - z_slots, count):
            copy_in(u).wait_send()

    @pl.when(inner)
    def _():
        copy_v(4, across).wait_send()
        copy_v(5, outward).wait_send()
        for u in range(count - z_slots, count):
            copy_across(u).wait_send()

        def drain(u, _):
            copy_out(u).wait_send()
            return 0

        lax.fori_loop(0, count, drain, 0)


def encoder_back(dy, kept, vec, gains, bias, qkv, dec, states, wide, down, lefts):
    owners = lax.axis_size("fsdp")
    own = PD // owners
    dec_units = dec.shape[1] * dec.shape[2] // ROWS
    dec = dec.reshape(4, 2, dec_units, ROWS, UNIT)
    half = ROWS // 2
    blocks, units, spots = [], [], []
    for n in range(2 * dec_units):
        place = (4, n * half, half, 0) if n < DFF // DD else (3, 0, half, (n - DFF // DD) * UNIT)
        spots.append((n // 2, n % 2 * half, *place))

    def add(left, sub, right, out, row, rows, column, columns):
        blocks.append((left, sub))
        for n in range(columns // UNIT):
            spots.append((dec_units + len(units), 0, out, row, rows, column + n * UNIT))
            units.append((len(blocks) - 1, right + n))

    subs = FF // owners // ROWS
    add(0, 0, 0, 1, 0, ROWS, 4 * D + FF, DD)
    for n in range(subs):
        add(1, n, 1, 2, n * ROWS, ROWS, 0, D)
    right = 1 + D // UNIT
    add(2, 0, right, 1, 0, ROWS, 4 * D, FF)
    right += FF // UNIT
    add(3, 0, right, 1, 0, ROWS, 3 * D, D)
    right += D // UNIT
    add(4, 0, right, 1, 0, ROWS, 0, 3 * D)
    right += 3 * D // UNIT
    add(5, 0, right, 0, 0, own, 0, D)
    right += D // UNIT
    count = dec_units + len(units)
    shapes = ((own, D), (ROWS, 4 * D + FF + DD), (FF // owners, D), (half, 10 * UNIT), (DFF // owners, DD))
    lefts = [a.reshape(4, 2, -1, VIS) for a in lefts]
    slots = 3
    dma = pltpu.SemaphoreType.DMA
    vmem, anywhere = pl.BlockSpec(memory_space=pltpu.VMEM), pl.BlockSpec(memory_space=pl.ANY)
    return pl.pallas_call(
        partial(back_kernel, dec_units, tuple(blocks), tuple(units), tuple(spots)),
        out_shape=tuple(jax.ShapeDtypeStruct(shape, BF) for shape in shapes)
        + (jax.ShapeDtypeStruct(vec.shape, F32),),
        in_specs=[vmem] * 6 + [anywhere] * (7 + len(lefts)),
        out_specs=(anywhere,) * len(shapes) + (vmem,),
        scratch_shapes=[
            pltpu.VMEM((len(blocks), 4, ROWS, VIS), BF),
            pltpu.VMEM((len(blocks), 4, ROWS, VIS), BF),
            pltpu.VMEM((right, VIS, UNIT), BF),
            pltpu.VMEM((right, VIS, UNIT), BF),
            pltpu.VMEM((dec_units, 4, ROWS, UNIT), BF),
            pltpu.VMEM((dec_units, 4, ROWS, UNIT), BF),
            pltpu.VMEM((4, ROWS, HALF), F32),
            pltpu.VMEM((slots, 2, 2, ROWS, HALF), BF),
            pltpu.VMEM((count, 2, 2, ROWS, HALF), BF),
            pltpu.VMEM((slots, 2, ROWS, HALF), BF),
            pltpu.VMEM((count, 2, ROWS, HALF), BF),
            pltpu.VMEM((4, ROWS, UNIT), F32),
            pltpu.VMEM((6, ROWS, UNIT), BF),
            pltpu.VMEM((count, ROWS, UNIT), BF),
            pltpu.VMEM((count, ROWS, UNIT), BF),
            pltpu.VMEM((6, *vec.shape), F32),
            pltpu.VMEM((6, *vec.shape), F32),
            pltpu.VMEM((3, D, UNIT), BF),
            pltpu.VMEM((2, UNIT, D), BF),
            pltpu.VMEM((2, VIS, UNIT), F32),
            pltpu.VMEM((VIS, D), F32),
            pltpu.VMEM((VIS, D), F32),
            pltpu.VMEM((VIS, D), F32),
            pltpu.VMEM((VIS, D), BF),
            pltpu.VMEM((VIS, D), BF),
            pltpu.VMEM((VIS, 3 * D), BF),
            pltpu.VMEM(vec.shape, F32),
            dma((3,)),
            dma((2,)),
            dma((2,)),
            dma((1,)),
            dma((dec_units, 3)),
            dma((len(blocks), 3)),
            dma((right, 2)),
            dma((slots, 2)),
            dma((count, 2)),
            dma((slots, 2)),
            dma((count, 2)),
            dma((count, 2)),
            dma((count, 2)),
            dma((6,)),
            dma((6,)),
            dma((count + dec_units,)),
        ],
        compiler_params=pltpu.CompilerParams(
            collective_id=0, has_side_effects=True, vmem_limit_bytes=61 * 2**20
        ),
        cost_estimate=pl.CostEstimate(
            flops=30 * 10**9, bytes_accessed=300 * 2**20, transcendentals=0
        ),
    )(dy, kept, vec, gains, bias, qkv, dec, *states, wide, down, *lefts)


def encoder_pieces(shapes):
    (own, width), (rows, _), (tall, _) = shapes
    pieces = [(0, 0, own, 0, width, 0)]
    pieces += [(1, 0, rows, n * D, D, (1, 2, 0)[n]) for n in range(3)]
    pieces += [(1, 0, rows, 3 * D, D, 1)]
    pieces += [(1, 0, rows, 4 * D + n * D, D, (2, 0, 1, 2)[n]) for n in range(FF // D)]
    pieces += [(2, n * rows, rows, 0, D, (0, 1, 2, 0)[n]) for n in range(tall // rows)]
    pieces += [(1, 0, rows, 4 * D + FF, DD, 0)]
    return pieces


def norm_rows(h, gain):
    mean = jnp.mean(h, -1, keepdims=True)
    cent = h - mean
    var = jnp.mean(cent * cent, -1, keepdims=True)
    return (cent * lax.rsqrt(var + EPS) * gain).astype(BF)


def encoder_kernel(
    pixels_ref,
    row_ref,
    column_ref,
    scale_ref,
    omega_ref,
    gains_ref,
    embed_ref,
    wide_ref,
    down_ref,
    wide_out,
    down_out,
    stats_out,
    by_row,
    by_column,
    picked_out,
    pos_out,
    bias_out,
    inputs_t,
    a_t,
    mixed_t,
    b_t,
    hidden_t,
    z_t,
    start_ref,
    qkv_ref,
    middle_ref,
    slope_ref,
    end_ref,
    seen_ref,
    inputs_ref,
    a_ref,
    mixed_ref,
    b_ref,
    hidden_ref,
    z_ref,
    w_embed,
    w_wide,
    w_down,
    stage_ref,
    pick_ref,
    high_ref,
    mid_ref,
    low_ref,
    picked_ref,
    pos_ref,
    bias_ref,
    v_in,
    v_out,
    load_sem,
    store_sem,
    send_sem,
    recv_sem,
    v_send,
    v_recv,
):
    shards, gathered = (embed_ref, wide_ref, down_ref), (w_embed, w_wide, w_down)
    pieces = encoder_pieces([ref.shape for ref in shards])
    count = len(pieces)
    z, f = lax.axis_index("dp"), lax.axis_index("fsdp")
    core, place = f % 2, f // 2
    x, y = place % 2, place // 2
    f_x, f_y, f_far = f + 2 - 4 * x, f + 4 - 8 * y, f + 6 - 4 * x - 8 * y
    partner = (z, f + 1 - 2 * core)
    x_side, y_side, z_side = (z, f_x), (z, f_y), (z + 1 - 2 * (z % 2), f)
    outer = (z == 0) | (z == 3)
    inner = (z == 1) | (z == 2)
    across = (3 - z, f)

    barrier = pltpu.get_barrier_semaphore()
    for device in (partner, x_side, y_side, z_side):
        pl.semaphore_signal(barrier, inc=1, device_id=device, device_id_type=MESH)

    @pl.when(outer)
    def _():
        pl.semaphore_wait(barrier, 4)

    @pl.when(inner)
    def _():
        pl.semaphore_signal(barrier, inc=1, device_id=across, device_id_type=MESH)
        pl.semaphore_wait(barrier, 5)

    stages = stage_ref.shape[0]

    def load(t):
        array, row, rows, column, columns, _ = pieces[t]
        return pltpu.make_async_copy(
            shards[array].at[pl.ds(row, rows), pl.ds(column, columns)],
            stage_ref.at[t % stages, pl.ds(0, rows), pl.ds(0, columns)],
            load_sem.at[t % stages],
        )

    for t in range(stages):
        load(t).start()

    def spot(t, owner, half=None):
        array, row, rows, column, columns, _ = pieces[t]
        if half is not None:
            columns //= 2
            column += half * columns
        return gathered[array].at[owner, pl.ds(row, rows), pl.ds(column, columns)]

    def move(t, owner, send, recv, device, half=None):
        target = spot(t, owner, half)
        return put(target, target, send_sem.at[t, send], recv_sem.at[t, recv], device)

    def own_x(t):
        return move(t, f, 0, 0, x_side)

    def own_y(t):
        return move(t, f, 1, 1, y_side)

    def own_core(t):
        return move(t, f, 2, 4, partner)

    def far_x(t):
        return move(t, f_y, 3, 2, x_side, 0)

    def far_y(t):
        return move(t, f_x, 4, 3, y_side, 1)

    def to_core(t, n):
        return move(t, (f_x, f_y, f_far)[n], 5 + n, 5 + n, partner)

    def to_z(t, n):
        return move(t, (f_x, f_y, f_far)[n], 8 + n, 8 + n, z_side)

    def brings(t, then, other=None):
        kind = pieces[t][5]
        if kind == 0:
            then()
            return
        pl.when(z % 2 == kind - 1)(then)
        if other is not None:
            pl.when(z % 2 != kind - 1)(other)

    def first(t):
        load(t).wait()
        array, row, rows, column, columns, _ = pieces[t]
        spot(t, f)[...] = stage_ref[t % stages, :rows, :columns].astype(BF)
        if t + stages < count:
            load(t + stages).start()
        own_core(t).start()

        def then():
            own_x(t).start()
            own_y(t).start()

        brings(t, then)

    def second(t):
        def then():
            own_x(t).wait_recv()
            far_y(t).start()
            own_y(t).wait_recv()
            far_x(t).start()
            for n in range(2):
                to_core(t, n).start()
                if pieces[t][5]:
                    to_z(t, n).start()

        brings(t, then)

    def third(t):
        def then():
            far_x(t).wait_recv()
            far_y(t).wait_recv()
            to_core(t, 2).start()
            if pieces[t][5]:
                to_z(t, 2).start()

        brings(t, then)

    def taken(t, n):
        def other():
            to_z(t, n).wait_recv()
            to_core(t, n).start()

        brings(t, lambda: None, other)

    def whole(t):
        own_core(t).wait_recv()
        for n in range(3):
            to_core(t, n).wait_recv()

    def drain(t):
        own_core(t).wait_send()
        for n in range(3):
            to_core(t, n).wait_send()

        def then():
            for copy in (own_x(t), own_y(t), far_x(t), far_y(t)):
                copy.wait_send()
            if pieces[t][5]:
                for n in range(3):
                    to_z(t, n).wait_send()

        brings(t, then)

    def copy_v(step, device):
        return put(v_out.at[step], v_in.at[step], v_send.at[step], v_recv.at[step], device)

    sides = (partner, x_side, y_side)

    def statistics(i):
        if i <= 3:
            if i > 0:
                copy_v(i - 1, sides[i - 1]).wait_recv()
                v_out[i] = v_out[i - 1] + v_in[i - 1]
            if i < 3:
                copy_v(i, sides[i]).start()
            else:

                @pl.when(outer)
                def _():
                    copy_v(3, z_side).start()

        if i == 4:

            @pl.when(inner)
            def _():
                copy_v(3, z_side).wait_recv()
                v_out[4] = v_out[3] + v_in[3]
                copy_v(4, across).start()

        if i == 5:

            @pl.when(inner)
            def _():
                copy_v(4, across).wait_recv()
                v_out[5] = v_out[4] + v_in[4]
                copy_v(5, z_side).start()
                stats_out[...] = v_out[5]

            @pl.when(outer)
            def _():
                copy_v(5, z_side).wait_recv()
                stats_out[...] = v_in[5]

    def turn(source, target, start=0, width=D):
        for lane in range(start, start + width, LANES):
            target[lane : lane + LANES, :] = source[:, lane : lane + LANES].T

    def columns_of(t):
        array, row, rows, column, columns, _ = pieces[t]
        weight = gathered[array][:, row : row + rows, column : column + columns]
        return weight.reshape(-1, columns)

    def local_statistics():
        pixels = pixels_ref[...]
        weighted = pixels * column_ref[:, 0:1]
        sums = jnp.sum(weighted, 0, keepdims=True)
        squares = jnp.sum(weighted * pixels, 0, keepdims=True)
        live = row_ref[0:1, :]
        totals = [r[:, n * PATCH**2 : (n + 1) * PATCH**2] for r in (sums, squares) for n in range(BANDS)]
        for n, total in enumerate((*totals, live, live * row_ref[1:2, :])):
            v_out[0, n : n + 1, :] = jnp.broadcast_to(jnp.sum(total, 1, keepdims=True), (1, LANES))

    def arrange_step():
        slots = (TOK_DEV, TOK_DEV)
        down, along = [lax.broadcasted_iota(jnp.int32, slots, n) for n in range(2)]
        live, masked = row_ref[0:1, :], row_ref[1:2, :]
        seen, hid = live * (1.0 - masked), live * masked
        kind = lax.broadcasted_iota(jnp.int32, row_ref.shape, 0)
        kinds = jnp.where(kind == 0, seen, jnp.where(kind == 1, hid, 1.0 - live))
        ranks = matmul(kinds.astype(BF), jnp.where(down < along, 1.0, 0.0).astype(BF))
        n_seen, n_hid = [jnp.sum(r, 1, keepdims=True) for r in (seen, hid)]
        empty = ranks[2:3, :]
        place = jnp.where(empty < VIS - n_seen, n_seen + empty, n_seen + n_hid + empty)
        place = jnp.where(hid > 0, VIS + ranks[1:2, :], place)
        place = jnp.where(seen > 0, ranks[0:1, :], place)
        pick_ref[...] = jnp.where(down == place.astype(jnp.int32), 1.0, 0.0).astype(BF)
        facts = row_ref[...].astype(BF)
        by_row[...] = right_t(facts, pick_ref[...])
        by_column[...] = right_t(pick_ref[...], facts)
        pixels = pixels_ref[...]
        high = pixels.astype(BF)
        rest = pixels - high.astype(F32)
        mid = rest.astype(BF)
        high_ref[...], mid_ref[...] = high, mid
        low_ref[...] = (rest - mid.astype(F32)).astype(BF)

    def pick_rows(rows):
        pick = pick_ref[rows, :]
        return matmul(pick, high_ref[...]) + matmul(pick, mid_ref[...]) + matmul(pick, low_ref[...])

    def pick_step():
        picked_ref[...] = pick_rows(slice(0, VIS))
        same = by_column[:VIS, 2:3] == by_row[2:3, :VIS]
        shape = (VIS, VIS)
        bias_out[...] = mask_bias(by_column[:VIS, 0:1] > 0, same, shape, 0)
        bias_ref[...] = mask_bias(by_row[0:1, :VIS] > 0, same, shape, 0, 1)

    def position_rows(target, rows, width, row):
        quarter = width // 4
        odd = by_column[rows, 2:3] > 0
        scale = jnp.where(odd, scale_ref[1:2, 0:1], scale_ref[0:1, 0:1])
        for n in range(2):
            angle = by_column[rows, 3 + n : 4 + n] * scale * omega_ref[row : row + 1, :quarter]
            target[rows, 2 * n * quarter : (2 * n + 1) * quarter] = jnp.sin(angle)
            target[rows, (2 * n + 1) * quarter : (2 * n + 2) * quarter] = jnp.cos(angle)

    def hidden_step(n):
        rows = slice(n * VIS, (n + 1) * VIS)
        if n > 0:
            picked_out[(n - 1) * VIS : n * VIS, :] = pick_rows(rows)
        position_rows(pos_out, rows, DD, 1)

    def embed_step():
        pixels = stats_out[6:7, :] * (PATCH * PATCH)
        for band in range(BANDS):
            mean = stats_out[band : band + 1, :] / pixels
            var = stats_out[BANDS + band : BANDS + band + 1, :] / pixels - mean * mean
            rate = lax.rsqrt(var + EPS)
            for part in range(PATCH * PATCH // LANES):
                lanes = pl.ds(band * PATCH * PATCH + part * LANES, LANES)
                inputs_ref[:, lanes] = ((picked_ref[:, lanes] - mean) * rate).astype(BF)
        start_ref[...] = matmul(inputs_ref[...], columns_of(0)) + pos_ref[...]
        a_ref[...] = norm_rows(start_ref[...], gains_ref[0:1, :])
        own = w_embed.shape[1]
        flipped = jnp.concatenate(
            [inputs_ref[:, lane : lane + LANES].T for lane in range(0, PD, LANES)], 0
        )
        inputs_t[...] = jnp.zeros_like(inputs_t)
        for owner in range(w_embed.shape[0]):
            inputs_t[owner, :own, :] = flipped[owner * own : (owner + 1) * own, :]
        turn(a_ref, a_t)

    def qkv_step(n):
        qkv_ref[:, n * D : (n + 1) * D] = matmul(a_ref[...], columns_of(1 + n)).astype(BF)

    def attention_step():
        size = D // HEADS
        lane_head = lax.broadcasted_iota(jnp.int32, (VIS, LANES), 1) // size

        def group(g, _):
            query, keys, values = [
                qkv_ref[:, pl.ds(pl.multiple_of(n * D + g * LANES, LANES), LANES)] for n in range(3)
            ]
            mixed = jnp.zeros((VIS, LANES), F32)
            for j in range(LANES // size):
                one = jnp.where(lane_head == j, query.astype(F32), 0.0).astype(BF)
                scores = right_t(one, keys) * size ** (-0.5) + bias_ref[...]
                probs = jnp.exp(scores - jnp.max(scores, -1, keepdims=True))
                probs = probs * (1.0 / jnp.sum(probs, -1, keepdims=True))
                mixed = jnp.where(lane_head == j, matmul(probs.astype(BF), values), mixed)
            mixed_ref[:, pl.ds(pl.multiple_of(g * LANES, LANES), LANES)] = mixed.astype(BF)
            return 0

        lax.fori_loop(0, D // LANES, group, 0)

    def out_step():
        turn(mixed_ref, mixed_t)
        middle_ref[...] = start_ref[...] + matmul(mixed_ref[...], columns_of(4))
        b_ref[...] = norm_rows(middle_ref[...], gains_ref[1:2, :])
        turn(b_ref, b_t)

    def up_step(n):
        columns = slice(n * D, (n + 1) * D)
        after, slope = gelu_parts(matmul(b_ref[...], columns_of(5 + n)))
        hidden_ref[:, columns] = after.astype(BF)
        slope_ref[:, columns] = slope
        turn(hidden_ref, hidden_t, n * D)

    def down_step(n):
        rows, owners = w_wide.shape[1], w_down.shape[0]
        tall = w_down.shape[1]
        parts = [hidden_ref[:, o * tall + n * rows : o * tall + (n + 1) * rows] for o in range(owners)]
        total = matmul(jnp.concatenate(parts, 1), columns_of(9 + n))
        end_ref[...] = (middle_ref[...] if n == 0 else end_ref[...]) + total

    def link_step():
        z_ref[...] = norm_rows(end_ref[...], gains_ref[2:3, :])
        turn(z_ref, z_t)
        seen_ref[...] = matmul(z_ref[...], columns_of(count - 1))

    work = [(0, None, arrange_step), (1, None, pick_step)]
    work += [(2, None, partial(position_rows, pos_ref, slice(0, VIS), D, 0))]
    work += [(at, None, partial(hidden_step, n)) for n, at in enumerate((3, 4, 11, 14))]
    work += [(6, 0, embed_step), (6, 1, partial(qkv_step, 0)), (7, 2, partial(qkv_step, 1))]
    work += [(8, 3, partial(qkv_step, 2)), (8, None, attention_step), (9, 4, out_step)]
    work += [(at, 5 + n, partial(up_step, n)) for n, at in enumerate((10, 10, 12, 13))]
    work += [(at, 9 + n, partial(down_step, n)) for n, at in enumerate((13, 15, 16, 16))]
    work += [(17, count - 1, link_step)]
    stores = []

    first(0)
    local_statistics()
    first(1)
    for i in range(18):
        if i + 2 < count:
            first(i + 2)
        statistics(i)
        if i < count:
            second(i)
        if 0 <= i - 1 < count:
            third(i - 1)
        if 0 <= i - 3 < count:
            taken(i - 3, 0)
            taken(i - 3, 1)
        if 0 <= i - 4 < count:
            taken(i - 4, 2)
        for at, piece, run in work:
            if at != i:
                continue
            if piece is not None:
                whole(piece)
                array, row, rows, column, columns, _ = pieces[piece]
                if array:
                    where = (slice(None), pl.ds(row, rows), pl.ds(column, columns))
                    store = pltpu.make_async_copy(
                        gathered[array].at[where],
                        (None, wide_out, down_out)[array].at[where],
                        store_sem.at[piece],
                    )
                    store.start()
                    stores.append(store)
            run()
    for store in stores:
        store.wait()
    for t in range(count):
        drain(t)
    for step in range(3):
        copy_v(step, sides[step]).wait_send()

    @pl.when(outer)
    def _():
        copy_v(3, z_side).wait_send()

    @pl.when(inner)
    def _():
        copy_v(4, across).wait_send()
        copy_v(5, z_side).wait_send()


def encoder_forward(pixels, facts, scale, gains, embed, wide, down):
    owners = lax.axis_size("fsdp")
    shapes = [w.shape for w in (embed, wide, down)]
    count = len(encoder_pieces(shapes))
    omega = [
        10000.0 ** (-jnp.arange(width // 4, dtype=jnp.float32) / (width // 4)) for width in (D, DD)
    ]
    omega = jnp.stack([omega[0], jnp.pad(omega[1], (0, D // 4 - DD // 4))] + [omega[0]] * 6)
    full = [jax.ShapeDtypeStruct((owners, *shape), BF) for shape in shapes[1:]]
    local = [
        jax.ShapeDtypeStruct((8, LANES), F32),
        jax.ShapeDtypeStruct((8, TOK_DEV), F32),
        jax.ShapeDtypeStruct((TOK_DEV, 8), F32),
        jax.ShapeDtypeStruct((HID, PD), F32),
        jax.ShapeDtypeStruct((TOK_DEV, DD), F32),
        jax.ShapeDtypeStruct((VIS, VIS), F32),
        jax.ShapeDtypeStruct((owners, ROWS, VIS), BF),
        *[jax.ShapeDtypeStruct((width, VIS), BF) for width in (D, D, D, FF, D)],
        jax.ShapeDtypeStruct((VIS, D), F32),
        jax.ShapeDtypeStruct((VIS, 3 * D), BF),
        jax.ShapeDtypeStruct((VIS, D), F32),
        jax.ShapeDtypeStruct((VIS, FF), F32),
        jax.ShapeDtypeStruct((VIS, D), F32),
        jax.ShapeDtypeStruct((VIS, DD), F32),
    ]
    vmem, anywhere = pl.BlockSpec(memory_space=pltpu.VMEM), pl.BlockSpec(memory_space=pl.ANY)
    dma = pltpu.SemaphoreType.DMA
    wide_full, down_full, *rest = pl.pallas_call(
        encoder_kernel,
        out_shape=(*full, *local),
        in_specs=[vmem] * 6 + [anywhere] * 3,
        out_specs=(anywhere,) * 2 + (vmem,) * len(local),
        scratch_shapes=[pltpu.VMEM((VIS, width), BF) for width in (PD, D, D, D, FF, D)]
        + [pltpu.VMEM((owners, *shape), BF) for shape in shapes]
        + [
            pltpu.VMEM((4, ROWS, D), F32),
            *[pltpu.VMEM((TOK_DEV, PD), BF)] * 4,
            pltpu.VMEM((VIS, PD), F32),
            pltpu.VMEM((VIS, D), F32),
            pltpu.VMEM((VIS, VIS), F32),
            pltpu.VMEM((6, 8, LANES), F32),
            pltpu.VMEM((6, 8, LANES), F32),
            dma((4,)),
            dma((count,)),
            dma((count, 11)),
            dma((count, 11)),
            dma((6,)),
            dma((6,)),
        ],
        compiler_params=pltpu.CompilerParams(
            collective_id=1, has_side_effects=True, vmem_limit_bytes=60 * 2**20
        ),
        cost_estimate=pl.CostEstimate(
            flops=2 * VIS * 14 * 2**20, bytes_accessed=200 * 2**20, transcendentals=0
        ),
    )(pixels, facts, facts.T, scale, omega, gains, embed, wide, down)
    return (wide_full.reshape(D, -1), down_full.reshape(FF, D), *rest)


LOWP = 256
HEADP = PD + LOWP
BLOCK = HID // 2


def mask_bias(live, same, shape, offset, keys=0):
    key, query = [lax.broadcasted_iota(jnp.int32, shape, (keys + n) % 2) for n in range(2)]
    return jnp.where((live & same) | (key + offset == query), 0.0, NEGATIVE)


def normalize(h):
    cent = h - jnp.mean(h, -1, keepdims=True)
    rate = lax.rsqrt(jnp.mean(cent * cent, -1, keepdims=True) + EPS)
    return cent * rate, rate


def normalize_back(unit, rate, gain, grad):
    scaled = grad * gain
    along = jnp.mean(scaled * unit, -1, keepdims=True)
    dh = rate * (scaled - jnp.mean(scaled, -1, keepdims=True) - unit * along)
    return dh, jnp.sum(grad * unit, 0, keepdims=True)


def exact_product(array, weight):
    high = array.astype(BF)
    rest = array - high.astype(F32)
    mid = rest.astype(BF)
    low = (rest - mid.astype(F32)).astype(BF)
    return matmul(high, weight) + matmul(mid, weight) + matmul(low, weight)


def decoder_kernel(
    owners,
    pos_ref,
    seen_ref,
    row_ref,
    column_ref,
    picked_ref,
    stats_ref,
    gains_ref,
    pool_ref,
    spread_ref,
    wide_ref,
    down_ref,
    grads_ref,
    dy_ref,
    vec_ref,
    y_ref,
    a_ref,
    q_ref,
    k_ref,
    v_ref,
    mixed_t,
    mixed_ref,
    lse_ref,
    head_ref,
    b_ref,
    hidden_ref,
    z_ref,
    dpred_ref,
    dbranch_ref,
    dbefore_ref,
    dattn_ref,
    dmixed_ref,
    dmiddle_ref,
    dq_ref,
    dk_ref,
    dv_ref,
    loss_ref,
    bias_ref,
):
    size = DD // DHEADS
    per = LANES // size
    factor = size ** (-0.5)
    gain_one, gain_two, gain_out = [gains_ref[n : n + 1, :] for n in range(3)]
    token = gains_ref[3:4, :]
    lane_head = lax.broadcasted_iota(jnp.int32, (HID, LANES), 1) // size
    key_head = lax.broadcasted_iota(jnp.int32, (TOK_DEV, LANES), 1) // size
    kept = column_ref[:VIS, 0:1] > 0
    for start in range(0, TOK_DEV, VIS):
        rows = slice(start, start + VIS)
        bias_ref[rows, :] = mask_bias(
            column_ref[rows, 0:1] > 0,
            column_ref[rows, 2:3] == row_ref[2:3, VIS:],
            (VIS, HID),
            start - VIS,
        )
    vec_ref[...] = jnp.zeros_like(vec_ref)
    loss_ref[...] = jnp.zeros_like(loss_ref)
    head_ref[...] = jnp.zeros_like(head_ref)
    head_ref[:, : PD + LOWD] = wide_ref[:, 4 * DD + DFF :]

    def project(rows, with_query):
        a = (normalize(y_ref[rows, :])[0] * gain_one).astype(BF)
        a_ref[rows, :] = a
        k_ref[rows, :] = matmul(a, wide_ref[:, DD : 2 * DD]).astype(BF)
        v_ref[rows, :] = matmul(a, wide_ref[:, 2 * DD : 3 * DD]).astype(BF)
        return a

    y_ref[:VIS, :] = pos_ref[:VIS, :] + jnp.where(kept, seen_ref[...], token)
    y_ref[VIS:, :] = pos_ref[VIS:, :] + token
    project(slice(0, VIS), False)

    def hidden_rows(n):
        start = pl.multiple_of(n * BLOCK, BLOCK)
        return pl.ds(start, BLOCK), pl.ds(pl.multiple_of(start + VIS, 32), BLOCK)

    def project_hidden(n, _):
        rows, all_rows = hidden_rows(n)
        a = project(all_rows, True)
        q_ref[rows, :] = matmul(a, wide_ref[:, :DD]).astype(BF)
        return 0

    lax.fori_loop(0, 2, project_hidden, 0)

    def only(array, head_of, j):
        return jnp.where(head_of == j, array.astype(F32), 0.0).astype(BF)

    def attend_group(g, _):
        lanes = pl.ds(pl.multiple_of(g * LANES, LANES), LANES)
        keys, query = k_ref[:, lanes], q_ref[:, lanes]
        values_t = v_ref[:, lanes].T
        for j in range(per):
            scores = right_t(keys, only(query, lane_head, j)) * factor + bias_ref[...]
            top = jnp.max(scores, 0, keepdims=True)
            probs = jnp.exp(scores - top)
            total = jnp.sum(probs, 0, keepdims=True)
            probs = (probs * (1.0 / total)).astype(BF)
            rows = slice(j * size, (j + 1) * size)
            mixed_t[g, rows, :] = matmul(values_t[rows, :], probs).astype(BF)
            lse_ref[g, j : j + 1, :] = top + jnp.log(total)
        mixed_ref[:, lanes] = mixed_t[g].T
        return 0

    lax.fori_loop(0, DD // LANES, attend_group, 0)

    pixels = stats_ref[6:7, :] * (PATCH * PATCH)
    flagged = stats_ref[7:8, 0:1]

    def follow(n, _):
        rows, all_rows = hidden_rows(n)
        middle = y_ref[all_rows, :] + matmul(mixed_ref[rows, :], wide_ref[:, 3 * DD : 4 * DD])
        unit_b, rate_b = normalize(middle)
        b = (unit_b * gain_two).astype(BF)
        b_ref[rows, :] = b
        after, slope = gelu_parts(matmul(b, wide_ref[:, 4 * DD : 4 * DD + DFF]))
        hidden_ref[rows, :] = after.astype(BF)
        unit_z, rate_z = normalize(middle + matmul(hidden_ref[rows, :], down_ref[...]))
        z = (unit_z * gain_out).astype(BF)
        z_ref[rows, :] = z
        pred = matmul(z, head_ref[...])
        parts = []
        for part in range(PD // LANES):
            band = part * LANES // (PATCH * PATCH)
            mean = stats_ref[band : band + 1, :] / pixels
            var = stats_ref[BANDS + band : BANDS + band + 1, :] / pixels - mean * mean
            lanes = slice(part * LANES, (part + 1) * LANES)
            parts.append((picked_ref[rows, lanes] - mean) * lax.rsqrt(var + EPS))
        normed = jnp.concatenate(parts, 1)
        coarse = exact_product(normed, pool_ref[...])
        err_high = pred[:, :PD] - (normed - exact_product(coarse, spread_ref[...]))
        err_low = pred[:, PD:] - coarse
        flag = column_ref[all_rows, 0:1]
        length = jnp.sqrt(err_high * err_high + 1.0)
        loss_ref[:, :PD] += jnp.sum((length - 1.0) * flag, 0, keepdims=True) * (1.0 / PD)
        loss_ref[:, PD:] += jnp.sum(err_low * err_low * flag, 0, keepdims=True) * (1.0 / LOWD)
        share = flag / flagged
        dpred_ref[rows, :PD] = (err_high / length * (share * (1.0 / PD))).astype(BF)
        dpred_ref[rows, PD:] = (err_low * (share * (2.0 / LOWD))).astype(BF)
        dz = right_t(dpred_ref[rows, :], head_ref[...])
        dend, dgain = normalize_back(unit_z, rate_z, gain_out, dz)
        vec_ref[2:3, :] += dgain
        dbranch_ref[rows, :] = dend.astype(BF)
        dhidden = right_t(dbranch_ref[rows, :], down_ref[...])
        dbefore_ref[rows, :] = (dhidden * slope).astype(BF)
        db = right_t(dbefore_ref[rows, :], wide_ref[:, 4 * DD : 4 * DD + DFF])
        dmiddle, dgain = normalize_back(unit_b, rate_b, gain_two, db)
        vec_ref[1:2, :] += dgain
        dmiddle = dmiddle + dend
        dmiddle_ref[rows, :] = dmiddle
        dattn_ref[rows, :] = dmiddle.astype(BF)
        dmixed = right_t(dattn_ref[rows, :], wide_ref[:, 3 * DD : 4 * DD])
        dmixed_ref[rows, :] = dmixed.astype(BF)
        return 0

    lax.fori_loop(0, 2, follow, 0)

    rows = DD // owners

    def store(block, grad):
        grads_ref[:, block] = grad.astype(BF).reshape(owners, rows, UNIT)

    parts = DFF // DD
    down_grad = left_t(hidden_ref[...], dbranch_ref[...]).astype(BF)
    down_grad = down_grad.reshape(owners, parts, rows, UNIT)
    for part in range(parts):
        grads_ref[:, part] = down_grad[:, part]
    store(
        parts + 3,
        jnp.concatenate([matmul(mixed_t[g], dattn_ref[...]) for g in range(DD // LANES)], 0),
    )
    for n in range(DFF // UNIT):
        store(parts + 4 + n, left_t(b_ref[...], dbefore_ref[:, n * UNIT : (n + 1) * UNIT]))
    for n in range(HEADP // UNIT):
        store(parts + 8 + n, left_t(z_ref[...], dpred_ref[:, n * UNIT : (n + 1) * UNIT]))

    def attend_back_group(g, _):
        lanes = pl.ds(pl.multiple_of(g * LANES, LANES), LANES)
        query, keys, values, dout = [r[:, lanes] for r in (q_ref, k_ref, v_ref, dmixed_ref)]
        keys_t = keys.T
        dkeys = jnp.zeros((TOK_DEV, LANES), F32)
        dvalues = jnp.zeros((TOK_DEV, LANES), F32)
        dquery = []
        for j in range(per):
            scores = right_t(keys, only(query, lane_head, j)) * factor + bias_ref[...]
            probs = jnp.exp(scores - lse_ref[g, j : j + 1, :])
            dvalues = jnp.where(key_head == j, matmul(probs.astype(BF), dout), dvalues)
            dprobs = right_t(values, only(dout, lane_head, j))
            delta = jnp.sum(dprobs * probs, 0, keepdims=True)
            dscores = (probs * (dprobs - delta)).astype(BF)
            dkeys = jnp.where(key_head == j, matmul(dscores, query), dkeys)
            dquery.append(matmul(keys_t[j * size : (j + 1) * size, :], dscores))
        dq_ref[:, lanes] = (jnp.concatenate(dquery, 0) * factor).astype(BF).T
        dk_ref[:, lanes] = (dkeys * factor).astype(BF)
        dv_ref[:, lanes] = dvalues.astype(BF)
        return 0

    lax.fori_loop(0, DD // LANES, attend_back_group, 0)

    store(parts, left_t(a_ref[VIS:, :], dq_ref[...]))
    store(parts + 1, left_t(a_ref[...], dk_ref[...]))
    store(parts + 2, left_t(a_ref[...], dv_ref[...]))

    def start_rows(rows, da):
        unit, rate = normalize(y_ref[rows, :])
        da = da + right_t(dk_ref[rows, :], wide_ref[:, DD : 2 * DD])
        da = da + right_t(dv_ref[rows, :], wide_ref[:, 2 * DD : 3 * DD])
        dh, dgain = normalize_back(unit, rate, gain_one, da)
        vec_ref[0:1, :] += dgain
        return dh

    dy = start_rows(slice(0, VIS), 0.0)
    dy_ref[...] = dy
    vec_ref[3:4, :] += jnp.sum(jnp.where(kept, 0.0, dy), 0, keepdims=True)

    def start_hidden(n, _):
        rows, all_rows = hidden_rows(n)
        dy = start_rows(all_rows, right_t(dq_ref[rows, :], wide_ref[:, :DD]))
        vec_ref[3:4, :] += jnp.sum(dy + dmiddle_ref[rows, :], 0, keepdims=True)
        return 0

    lax.fori_loop(0, 2, start_hidden, 0)
    vec_ref[4:5, :] = loss_ref[:, :DD] + loss_ref[:, DD:]


def decoder_step(pos, seen, by_row, by_column, picked, stats, vectors, wide, down):
    index = jnp.arange(PD)
    band, row, column = index // PATCH**2, index // PATCH % PATCH, index % PATCH
    low = band * (PATCH // 2) ** 2 + row // 2 * (PATCH // 2) + column // 2
    spread = low[None, :] == jnp.arange(LOWP)[:, None]
    gains = jnp.pad(vectors.reshape(4, DD), ((0, 4), (0, 0)))
    owners = lax.axis_size("fsdp")
    scratch = [
        ((TOK_DEV, DD), F32),
        ((TOK_DEV, DD), BF),
        ((HID, DD), BF),
        ((TOK_DEV, DD), BF),
        ((TOK_DEV, DD), BF),
        ((DD // LANES, LANES, HID), BF),
        ((HID, DD), BF),
        ((DD // LANES, LANES * DHEADS // DD, HID), F32),
        ((DD, HEADP), BF),
        ((HID, DD), BF),
        ((HID, DFF), BF),
        ((HID, DD), BF),
        ((HID, HEADP), BF),
        ((HID, DD), BF),
        ((HID, DFF), BF),
        ((HID, DD), BF),
        ((HID, DD), BF),
        ((HID, DD), F32),
        ((HID, DD), BF),
        ((TOK_DEV, DD), BF),
        ((TOK_DEV, DD), BF),
        ((1, HEADP), F32),
        ((TOK_DEV, HID), F32),
    ]
    vmem = pl.BlockSpec(memory_space=pltpu.VMEM)
    grads, dy, vec = pl.pallas_call(
        partial(decoder_kernel, owners),
        out_shape=(
            jax.ShapeDtypeStruct((owners, DFF // DD + 10, DD // owners, UNIT), BF),
            jax.ShapeDtypeStruct((VIS, DD), F32),
            jax.ShapeDtypeStruct((8, DD), F32),
        ),
        in_specs=[vmem] * 11,
        out_specs=(vmem,) * 3,
        scratch_shapes=[pltpu.VMEM(*entry) for entry in scratch],
        compiler_params=pltpu.CompilerParams(vmem_limit_bytes=60 * 2**20),
        cost_estimate=pl.CostEstimate(
            flops=40 * 10**9, bytes_accessed=40 * 2**20, transcendentals=2 * 10**7
        ),
    )(
        pos,
        seen,
        by_row,
        by_column,
        picked,
        stats,
        gains,
        (spread.T * 0.25).astype(BF),
        spread.astype(BF),
        wide,
        down,
    )
    return grads, dy, vec[:4].reshape(-1), jnp.sum(vec[4])


def block_forward(h, weights, gains, bias, heads, skip):
    wqkv, wout, wup, wdown = weights
    width = h.shape[1]
    normed_a = layer_norm(h, gains[0]).astype(BF)
    query = matmul(normed_a[skip:], wqkv[:, :width]).astype(BF)
    keys = matmul(normed_a, wqkv[:, width : 2 * width]).astype(BF)
    values = matmul(normed_a, wqkv[:, 2 * width :]).astype(BF)
    mixed_t, lse = attend(query.T, keys, values.T, bias, width // heads)
    middle = h[skip:] + left_t(mixed_t, wout)
    normed_b = layer_norm(middle, gains[1]).astype(BF)
    after, slope = gelu_parts(matmul(normed_b, wup))
    hidden = after.astype(BF)
    end = middle + matmul(hidden, wdown)
    return end, (h, normed_a, query, keys, values, mixed_t, lse, middle, normed_b, slope, hidden)


def block_backward(saved, grad, weights, gains, bias, heads, skip):
    wqkv, wout, wup, wdown = weights
    h, normed_a, query, keys, values, mixed_t, lse, middle, normed_b, slope, hidden = saved
    width = h.shape[1]
    dbranch = grad.astype(BF)
    dbefore = (right_t(dbranch, wdown) * slope).astype(BF)
    dmiddle, dgain_two = norm_back(middle, gains[1], right_t(dbefore, wup))
    dmiddle = dmiddle + grad
    dattn = dmiddle.astype(BF)
    dmixed = right_t(dattn, wout).astype(BF)
    dqt, dkeys, dvalues = attend_back(query, keys, values, dmixed, bias, lse, width // heads)
    dquery = dqt.T
    if skip:
        dquery = jnp.pad(dquery, ((skip, 0), (0, 0)))
        dmiddle = jnp.pad(dmiddle, ((skip, 0), (0, 0)))
    dqkv = jnp.concatenate([dquery, dkeys, dvalues], 1)
    dh, dgain_one = norm_back(h, gains[0], right_t(dqkv, wqkv))
    factors = ((normed_a.T, dqkv), (mixed_t, dattn), (normed_b.T, dbefore), (hidden.T, dbranch))
    return (dh + dmiddle, factors, (dgain_one, dgain_two))


def reduce_rows(grad):
    return lax.psum_scatter(grad.astype(BF), "fsdp", scatter_dimension=0, tiled=True)


def enc_split(wide, down):
    return (
        (wide[:, : 3 * D], wide[:, 3 * D : 4 * D], wide[:, 4 * D : 4 * D + FF], down),
        wide[:, 4 * D + FF :],
    )


def advance(weight, mom, avg, grad, rate):
    grad = grad + DECAY * weight
    buf = MOMENTUM * mom + grad
    new = weight - rate * (grad + MOMENTUM * buf)
    return (buf, new, AVERAGE * avg + (1.0 - AVERAGE) * new)


def advance_kernel(rate, *refs):
    grads, weights, moms, avgs, outs = [refs[5 * n : 5 * n + 5] for n in range(4)] + [refs[20:]]

    def update(n):
        weight = weights[n][...]
        grad = grads[n][:, : weight.shape[1]].astype(F32)
        buf, new, avg = advance(weight, moms[n][...], avgs[n][...], grad, rate)
        outs[4 * n][...] = buf
        outs[4 * n + 1][...] = new
        outs[4 * n + 2][...] = avg
        outs[4 * n + 3][...] = new.astype(BF)

    pl.when(pl.program_id(0) == 0)(partial(update, 0))
    for n in range(1, 5):
        update(n)


def advance_all(rate, grads, weights, moms, avgs):
    steps = weights[3].shape[0] // 16

    def spec(n, array):
        if n == 0:
            return pl.BlockSpec(array.shape, lambda i: (0, 0))
        return pl.BlockSpec((array.shape[0] // steps, array.shape[1]), lambda i: (i, 0))

    arrays = [a for group in (grads, weights, moms, avgs) for a in group]
    outs = [(n, jax.ShapeDtypeStruct(w.shape, t)) for n, w in enumerate(weights) for t in (F32, F32, F32, BF)]
    size = sum(w.size for w in weights)
    return pl.pallas_call(
        partial(advance_kernel, rate),
        grid=(steps,),
        out_shape=[out for _, out in outs],
        in_specs=[spec(n % 5, a) for n, a in enumerate(arrays)],
        out_specs=[spec(n, out) for n, out in outs],
        compiler_params=pltpu.CompilerParams(vmem_limit_bytes=58 * 2**20),
        cost_estimate=pl.CostEstimate(flops=12 * size, bytes_accessed=28 * size, transcendentals=0),
    )(*arrays)


def arrange(valid, masked, scene_ids):
    slots = valid.shape[0]
    live = valid > 0
    kinds = jnp.stack([live & (masked == 0), live & (masked > 0), ~live], 1)
    index = jnp.arange(slots, dtype=jnp.int32)
    ranks = matmul((index[None, :] < index[:, None]).astype(BF), kinds.astype(BF)).astype(jnp.int32)
    n_seen, n_hid = [jnp.sum(kinds[:, i].astype(jnp.int32)) for i in range(2)]
    empty = ranks[:, 2]
    to_empty = jnp.where(empty < VIS - n_seen, n_seen + empty, n_seen + n_hid + empty)
    place = jnp.where(
        kinds[:, 0], ranks[:, 0], jnp.where(kinds[:, 1], VIS + ranks[:, 1], to_empty)
    )
    return (place[None, :] == index[:, None]).astype(BF), n_seen, n_hid


def exact_pick(pick, array):
    high = lax.reduce_precision(array, 8, 7)
    rest = array - high
    mid = lax.reduce_precision(rest, 8, 7)
    low = rest - mid
    return (
        matmul(pick, high.astype(BF)) + matmul(pick, mid.astype(BF)) + matmul(pick, low.astype(BF))
    )


def body(
    pixels,
    masked,
    valid,
    scene_ids,
    gsd_index,
    coords,
    embed,
    wide_enc,
    enc_down,
    wide_dec,
    dec_down,
    vectors,
    embed_mom,
    wide_enc_mom,
    enc_down_mom,
    wide_dec_mom,
    dec_down_mom,
    vector_mom,
    embed_avg,
    wide_enc_avg,
    enc_down_avg,
    wide_dec_avg,
    dec_down_avg,
    vector_avg,
):
    slots = pixels.shape[0]
    fast = (lax.axis_size("dp"), lax.axis_size("fsdp")) == (4, 8)
    w_dec, w_dec_down = [
        lax.all_gather(w.astype(BF), "fsdp", axis=0, tiled=True) for w in (wide_dec, dec_down)
    ]
    levels = jnp.exp2(0.5 * gsd_index.astype(jnp.float32) - 1.0)
    gains_enc = (vectors[:D], vectors[D : 2 * D])
    gain_enc_out = vectors[2 * D : 3 * D]
    if fast:
        facts = jnp.stack([valid, masked, scene_ids % 2, coords[:, 0], coords[:, 1]])
        facts = jnp.pad(facts, ((0, 3), (0, 0))).astype(F32)
        scale = jnp.pad(jnp.broadcast_to(levels[:, None], (2, LANES)), ((0, 6), (0, 0)))
        gains = jnp.pad(vectors[: 3 * D].reshape(3, D), ((0, 5), (0, 0)))
        w_enc, w_enc_down, stats, by_row, by_column, picked_hidden, pos_dec, bias_enc, *saved = (
            encoder_forward(pixels, facts, scale, gains, embed, wide_enc, enc_down)
        )
        *factors, h_start, qkv, middle, slope, h_end, seen_out = saved
    else:
        rows_ok = valid.astype(jnp.float32)
        flags = rows_ok * masked.astype(jnp.float32)
        bands = pixels.reshape(slots, BANDS, PATCH * PATCH)
        weighted = bands * rows_ok[:, None, None]
        band_sum = jnp.sum(weighted, axis=(0, 2))
        counts = jnp.stack([jnp.sum(rows_ok), jnp.sum(flags)])
        band_sq = jnp.sum(weighted * bands, axis=(0, 2))
        stats = jnp.concatenate([band_sum, band_sq, counts])
        stats = jnp.broadcast_to(lax.psum(stats, ("dp", "fsdp"))[:, None], (8, LANES))
        pick, n_seen, n_hid = arrange(valid, masked, scene_ids)
        picked_pixels = exact_pick(pick, pixels)
        picked_hidden = picked_pixels[VIS:]
        small = matmul(pick, jnp.concatenate([(scene_ids % 2)[:, None], coords], 1).astype(BF))
        odd, coord = small[:, 0], small[:, 1:]
        scale = jnp.where(odd == 0, levels[0], levels[1])
        index = jnp.arange(slots, dtype=jnp.int32)
        live = jnp.concatenate([index[:VIS] < n_seen, index[:HID] < n_hid])
        allow = live[:, None] & (odd[:, None] == odd[None, :]) | (index[:, None] == index[None, :])
        bias_enc = jnp.where(allow, 0.0, NEGATIVE)[:VIS, :VIS]
        by_row = jnp.pad(jnp.stack([live.astype(F32), odd, odd]), ((0, 5), (0, 0)))
        by_column = by_row.T
        pos_dec = positions(coord, scale, DD)
    count = stats[7, 0]
    if not fast:
        w_embed, w_enc, w_enc_down = [
            lax.all_gather(w.astype(BF), "fsdp", axis=0, tiled=True)
            for w in (embed, wide_enc, enc_down)
        ]
        enc_weights, w_link = enc_split(w_enc, w_enc_down)
        mean = jnp.repeat(stats[:3, 0] / (stats[6, 0] * (PATCH * PATCH)), PATCH * PATCH)
        square = jnp.repeat(stats[3:6, 0] / (stats[6, 0] * (PATCH * PATCH)), PATCH * PATCH)
        rate = lax.rsqrt(square - mean * mean + EPS)
        inputs = ((picked_pixels[:VIS] - mean) * rate).astype(BF)
        h_start = matmul(inputs, w_embed) + positions(coord[:VIS], scale[:VIS], D)
        h_end, enc_saved = block_forward(h_start, enc_weights, gains_enc, bias_enc, HEADS, 0)
        encoded = layer_norm(h_end, gain_enc_out).astype(BF)
        seen_out = matmul(encoded, w_link)
    dec_grads, dy_seen, dec_vec, local_loss = decoder_step(
        pos_dec,
        seen_out,
        by_row,
        by_column,
        picked_hidden,
        stats,
        vectors[3 * D :],
        w_dec,
        w_dec_down,
    )
    keptf = by_column[:VIS, 0:1]
    if fast:
        vec = jnp.concatenate([jnp.zeros((3 * D,), F32), dec_vec, local_loss[None]])
        vec = jnp.pad(vec, (0, 8 * D - vec.shape[0])).reshape(8, D)
        inputs_t, a_t, mixed_t, b_t, hidden_t, z_t = factors
        *enc_parts, dec_wide, dec_tall, vec = encoder_back(
            dy_seen,
            keptf,
            vec,
            gains,
            bias_enc,
            qkv,
            dec_grads,
            (h_end, middle, h_start, slope),
            w_enc,
            w_enc_down,
            (z_t, hidden_t, b_t, mixed_t, a_t, inputs_t),
        )
        dec_parts = (dec_wide, dec_tall)
        vector_grad, loss_sum = vec[:5].reshape(-1), vec[5, 0]
    else:
        dseen = (dy_seen * keptf).astype(BF)
        dh_end, dgain_enc_out = norm_back(h_end, gain_enc_out, right_t(dseen, w_link))
        dh_start, enc_factors, dgains_enc = block_backward(
            enc_saved, dh_end, enc_weights, gains_enc, bias_enc, HEADS, 0
        )
        enc_grads = [matmul(*pair).astype(BF) for pair in enc_factors]
        link_grad = left_t(encoded, dseen).astype(BF)
        enc_parts = lax.psum(
            (
                reduce_rows(left_t(inputs, dh_start.astype(BF))),
                reduce_rows(
                    jnp.concatenate([enc_grads[0], enc_grads[1], enc_grads[2], link_grad], 1)
                ),
                reduce_rows(enc_grads[3]),
            ),
            "dp",
        )
        dec_sum = lax.psum(reduce_rows(dec_grads), "dp")[0]
        rows, parts = dec_sum.shape[1], DFF // DD
        dec_parts = (
            dec_sum[parts:].transpose(1, 0, 2).reshape(rows, -1),
            dec_sum[:parts].reshape(-1, DD),
        )
        vector_grad = jnp.concatenate([*dgains_enc, dgain_enc_out, dec_vec])
        vector_grad, loss_sum = lax.psum((vector_grad, local_loss), ("dp", "fsdp"))
    grads = (*enc_parts, *dec_parts)
    rate = STEP_UNIT * (PD * TOK_DEV * lax.axis_size("dp") * lax.axis_size("fsdp")) ** 0.5
    weights = (embed, wide_enc, enc_down, wide_dec, dec_down)
    moms = (embed_mom, wide_enc_mom, enc_down_mom, wide_dec_mom, dec_down_mom)
    avgs = (embed_avg, wide_enc_avg, enc_down_avg, wide_dec_avg, dec_down_avg)
    outs = advance_all(rate, grads, weights, moms, avgs)
    return (*outs, *advance(vectors, vector_mom, vector_avg, vector_grad, rate), loss_sum, count)


def solution(mesh):
    both, rows = P(("dp", "fsdp")), P("fsdp", None)
    placed = (P(("dp", "fsdp"), None), both, both, both, both, P(("dp", "fsdp"), None))
    states = (rows,) * 5 + (P(),)
    return jax.shard_map(
        body,
        mesh=mesh,
        in_specs=placed + states * 3,
        out_specs=(rows,) * 20 + (P(),) * 5,
        check_vma=False,
    )
```

```python
from functools import partial

import jax
import jax.numpy as jnp
from jax import lax
from jax.experimental import pallas as pl
from jax.experimental.pallas import tpu as pltpu
from jax.sharding import PartitionSpec as P

D = 1024
HEADS = 16
FF = 4096
DD = 512
DHEADS = 16
DFF = 2048
PATCH = 16
BANDS = 3
TOK_DEV = 768
PD = 768
LOWD = 192
VIS = 192
HID = TOK_DEV - VIS

EPS = 1e-06
MOMENTUM = 0.9
DECAY = 0.0001
AVERAGE = 0.9
STEP_UNIT = 0.003
NEGATIVE = -1e30
LANES = 128
BF = jnp.bfloat16
F32 = jnp.float32


def matmul(left, right):
    return jnp.dot(left, right, preferred_element_type=jnp.float32)


def left_t(left, right):
    return lax.dot_general(
        left, right, (((0,), (0,)), ((), ())), preferred_element_type=jnp.float32
    )


def right_t(left, right):
    return lax.dot_general(
        left, right, (((1,), (1,)), ((), ())), preferred_element_type=jnp.float32
    )


def layer_norm(h, gain):
    mean = jnp.mean(h, -1, keepdims=True)
    cent = h - mean
    var = jnp.mean(cent * cent, -1, keepdims=True)
    return cent * lax.rsqrt(var + EPS) * gain


def norm_back(h, gain, grad):
    result, pull = jax.vjp(layer_norm, h, gain)
    return pull(grad)


def gelu_parts(before):
    below = 0.5 * (1.0 + lax.erf(before * 0.5**0.5))
    slope = below + before * jnp.exp(before * before * -0.5) * (0.5 / jnp.pi) ** 0.5
    return before * below, slope


def positions(coord, scale, width):
    quarter = width // 4
    omega = 10000.0 ** (-jnp.arange(quarter, dtype=jnp.float32) / quarter)
    angle_x = coord[:, 0:1] * scale[:, None] * omega[None, :]
    angle_y = coord[:, 1:2] * scale[:, None] * omega[None, :]
    return jnp.concatenate(
        [jnp.sin(angle_x), jnp.cos(angle_x), jnp.sin(angle_y), jnp.cos(angle_y)], -1
    )


def row_loss(pred, normed):
    rows = normed.shape[0]
    coarse = jnp.mean(normed.reshape(rows, BANDS, PATCH // 2, 2, PATCH // 2, 2), axis=(3, 5))
    upper = jnp.repeat(jnp.repeat(coarse, 2, axis=2), 2, axis=3).reshape(rows, PD)
    err_high = pred[:, :PD] - (normed - upper)
    err_low = pred[:, PD:] - coarse.reshape(rows, LOWD)
    return jnp.mean(jnp.sqrt(err_high * err_high + 1.0) - 1.0, -1) + jnp.mean(err_low * err_low, -1)


def attend_kernel(size, qt_ref, k_ref, vt_ref, bias_ref, ot_ref, lse_ref):
    per = LANES // size
    row_head = lax.broadcasted_iota(jnp.int32, qt_ref.shape, 0) // size
    factor = size ** (-0.5)
    for j in range(per):
        query = jnp.where(row_head == j, qt_ref[...].astype(F32), 0.0).astype(BF)
        scores = matmul(k_ref[...], query) * factor + bias_ref[...]
        top = jnp.max(scores, 0, keepdims=True)
        probs = jnp.exp(scores - top)
        total = jnp.sum(probs, 0, keepdims=True)
        probs = (probs * (1.0 / total)).astype(BF)
        rows = slice(j * size, (j + 1) * size)
        ot_ref[rows, :] = matmul(vt_ref[rows, :], probs).astype(BF)
        lse_ref[0, j : j + 1, :] = top + jnp.log(total)


def attend(qt, keys, vt, bias, size):
    width, queries = qt.shape
    rows = keys.shape[0]
    groups, per = width // LANES, LANES // size
    return pl.pallas_call(
        partial(attend_kernel, size),
        grid=(groups,),
        out_shape=(
            jax.ShapeDtypeStruct((width, queries), BF),
            jax.ShapeDtypeStruct((groups, per, queries), F32),
        ),
        in_specs=[
            pl.BlockSpec((LANES, queries), lambda g: (g, 0)),
            pl.BlockSpec((rows, LANES), lambda g: (0, g)),
            pl.BlockSpec((LANES, rows), lambda g: (g, 0)),
            pl.BlockSpec((rows, queries), lambda g: (0, 0)),
        ],
        out_specs=(
            pl.BlockSpec((LANES, queries), lambda g: (g, 0)),
            pl.BlockSpec((1, per, queries), lambda g: (g, 0, 0)),
        ),
        compiler_params=pltpu.CompilerParams(vmem_limit_bytes=40 * 2**20),
        cost_estimate=pl.CostEstimate(
            flops=4 * rows * queries * width * per,
            bytes_accessed=4 * rows * queries,
            transcendentals=rows * queries * width // size,
        ),
    )(qt, keys, vt, bias)


def attend_back_kernel(
    size,
    qt_ref,
    q_ref,
    k_ref,
    kt_ref,
    v_ref,
    do_ref,
    dot_ref,
    bias_ref,
    *rest,
):
    *lse_ref, dqt_ref, dk_ref, dv_ref = rest
    per = LANES // size
    row_head = lax.broadcasted_iota(jnp.int32, qt_ref.shape, 0) // size
    lane_head = lax.broadcasted_iota(jnp.int32, dk_ref.shape, 1) // size
    factor = size ** (-0.5)
    dkeys = jnp.zeros(dk_ref.shape, F32)
    dvalues = jnp.zeros(dv_ref.shape, F32)
    for j in range(per):
        query = jnp.where(row_head == j, qt_ref[...].astype(F32), 0.0).astype(BF)
        dout = jnp.where(row_head == j, dot_ref[...].astype(F32), 0.0).astype(BF)
        scores = matmul(k_ref[...], query) * factor + bias_ref[...]
        if lse_ref:
            probs = jnp.exp(scores - lse_ref[0][0, j : j + 1, :])
        else:
            probs = jnp.exp(scores - jnp.max(scores, 0, keepdims=True))
            probs = probs * (1.0 / jnp.sum(probs, 0, keepdims=True))
        dvalues = jnp.where(lane_head == j, matmul(probs.astype(BF), do_ref[...]), dvalues)
        dprobs = matmul(v_ref[...], dout)
        delta = jnp.sum(dprobs * probs, 0, keepdims=True)
        dscores = (probs * (dprobs - delta)).astype(BF)
        dkeys = jnp.where(lane_head == j, matmul(dscores, q_ref[...]), dkeys)
        rows = slice(j * size, (j + 1) * size)
        dqt_ref[rows, :] = (matmul(kt_ref[rows, :], dscores) * factor).astype(BF)
    dk_ref[...] = (dkeys * factor).astype(BF)
    dv_ref[...] = dvalues.astype(BF)


def attend_back(query, keys, values, dmixed, bias, lse, size):
    queries, width = query.shape
    rows = keys.shape[0]
    groups, per = width // LANES, LANES // size
    tall = lambda n: pl.BlockSpec((n, LANES), lambda g: (0, g))
    flat = lambda n: pl.BlockSpec((LANES, n), lambda g: (g, 0))
    return pl.pallas_call(
        partial(attend_back_kernel, size),
        grid=(groups,),
        out_shape=(
            jax.ShapeDtypeStruct((width, queries), BF),
            jax.ShapeDtypeStruct((rows, width), BF),
            jax.ShapeDtypeStruct((rows, width), BF),
        ),
        in_specs=[
            flat(queries),
            tall(queries),
            tall(rows),
            flat(rows),
            tall(rows),
            tall(queries),
            flat(queries),
            pl.BlockSpec((rows, queries), lambda g: (0, 0)),
        ]
        + [pl.BlockSpec((1, per, queries), lambda g: (g, 0, 0))] * (lse is not None),
        out_specs=(flat(queries), tall(rows), tall(rows)),
        compiler_params=pltpu.CompilerParams(vmem_limit_bytes=48 * 2**20),
        cost_estimate=pl.CostEstimate(
            flops=10 * rows * queries * width * per,
            bytes_accessed=4 * rows * queries,
            transcendentals=rows * queries * width // size,
        ),
    )(query.T, query, keys, keys.T, values, dmixed, dmixed.T, bias, *([] if lse is None else [lse]))


MESH = pl.DeviceIdType.MESH
UNIT = 512
HALF = UNIT // 2
ROWS = 128
HALF_ROWS = ROWS // 2
LAGS = (1, 2, 3, 4, 6)


def put(source, target, send, recv, device):
    return pltpu.make_async_remote_copy(
        src_ref=source,
        dst_ref=target,
        send_sem=send,
        recv_sem=recv,
        device_id=device,
        device_id_type=MESH,
    )


def back_kernel(
    dec_units,
    blocks,
    units,
    spots,
    dy_ref,
    column_ref,
    vec_ref,
    vectors_ref,
    bias_ref,
    qkv_ref,
    dec_ref,
    end_ref,
    middle_ref,
    start_ref,
    slope_ref,
    wide_ref,
    down_ref,
    *refs,
):
    n_left = max(b[0] for b in blocks) + 1
    lefts, refs = refs[:n_left], refs[n_left:]
    outs, refs = refs[:5], refs[5:]
    vec_out, refs = refs[0], refs[1:]
    (
        xo,
        xp,
        yo,
        yp,
        do,
        dp,
        products,
        a_out,
        a_in,
        b_out,
        b_in,
        sums,
        z_out,
        z_one,
        z_two,
        v_in,
        v_out,
        wide_buf,
        down_buf,
        slope_buf,
        h_buf,
        dend_ref,
        dmid_ref,
        dbranch_ref,
        dmixed_ref,
        dqkv_ref,
        grad_vec,
        wide_sem,
        down_sem,
        slope_sem,
        h_sem,
        dec_sem,
        left_sem,
        right_sem,
        a_send,
        a_recv,
        b_send,
        b_recv,
        z_send,
        z_recv,
        v_send,
        v_recv,
        store_sem,
    ) = refs
    count = dec_units + len(units)
    z, f = lax.axis_index("dp"), lax.axis_index("fsdp")
    core, place = f % 2, f // 2
    x, y = place % 2, place // 2
    partner = (z, f + 1 - 2 * core)
    x_side = (z, f + 2 - 4 * x)
    y_side = (z, f + 4 - 8 * y)
    at_x, at_y, at_far = place + 1 - 2 * x, place + 2 - 4 * y, 3 - place
    low = z < 2
    outer = (z == 0) | (z == 3)
    inner = (z == 1) | (z == 2)
    inward = (jnp.where(low, 1, 2), f)
    across = (3 - z, f)
    outward = (jnp.where(low, 0, 3), f)

    ring = wide_buf.shape[0]
    up_chunks, out_chunks, qkv_chunks = FF // UNIT, D // UNIT, 3 * D // UNIT
    chunks = 1 + up_chunks + out_chunks + qkv_chunks

    def wide_copy(w):
        inside = jnp.where(w < 1 + up_chunks, 4 * D + UNIT * (w - 1), 3 * D + UNIT * (w - 1 - up_chunks))
        column = jnp.where(
            w == 0,
            4 * D + FF,
            jnp.where(w < 1 + up_chunks + out_chunks, inside, UNIT * (w - 1 - up_chunks - out_chunks)),
        )
        return pltpu.make_async_copy(
            wide_ref.at[:, pl.ds(pl.multiple_of(column, UNIT), UNIT)],
            wide_buf.at[w % ring],
            wide_sem.at[w % ring],
        )

    def down_copy(j):
        rows = pl.ds(pl.multiple_of(j * UNIT, UNIT), UNIT)
        return pltpu.make_async_copy(down_ref.at[rows], down_buf.at[j % 2], down_sem.at[j % 2])

    def slope_copy(j):
        columns = pl.ds(pl.multiple_of(j * UNIT, UNIT), UNIT)
        return pltpu.make_async_copy(slope_ref.at[:, columns], slope_buf.at[j % 2], slope_sem.at[j % 2])

    def h_copy(source):
        return pltpu.make_async_copy(source, h_buf, h_sem.at[0])

    h_copy(end_ref).start()
    for n in range(ring):
        wide_copy(n).start()
    for n in range(2):
        down_copy(n).start()
        slope_copy(n).start()

    barrier = pltpu.get_barrier_semaphore()
    for device in (partner, x_side, y_side):
        pl.semaphore_signal(barrier, inc=1, device_id=device, device_id_type=MESH)

    @pl.when(outer)
    def _():
        pl.semaphore_signal(barrier, inc=1, device_id=inward, device_id_type=MESH)
        pl.semaphore_wait(barrier, 4)

    @pl.when(inner)
    def _():
        pl.semaphore_signal(barrier, inc=1, device_id=across, device_id_type=MESH)
        pl.semaphore_signal(barrier, inc=1, device_id=outward, device_id_type=MESH)
        pl.semaphore_wait(barrier, 5)

    def swap_dec(source, n):
        return put(source, dp.at[n], dec_sem.at[n, 1], dec_sem.at[n, 2], partner)

    def swap_left(source, b):
        return put(source, xp.at[b], left_sem.at[b, 1], left_sem.at[b, 2], partner)

    def swap_right(r):
        return put(yo.at[r], yp.at[r], right_sem.at[r, 0], right_sem.at[r, 1], partner)

    for n in range(dec_units):
        swap_dec(dec_ref.at[:, 1 - core, n], n).start()
        pltpu.make_async_copy(dec_ref.at[:, core, n], do.at[n], dec_sem.at[n, 0]).start()
    for b, (left, sub) in enumerate(blocks):
        rows = pl.ds(sub * ROWS, ROWS)
        swap_left(lefts[left].at[:, 1 - core, rows], b).start()
        pltpu.make_async_copy(lefts[left].at[:, core, rows], xo.at[b], left_sem.at[b, 0]).start()

    firsts = 1 + out_chunks
    single = next(n for n in range(1, len(units)) if units[n][1] >= firsts)
    starts = [n for n in range(1, len(units)) if units[n][0] != units[n - 1][0]]

    def block_of(e):
        return sum([jnp.where(e >= n, 1, 0) for n in starts], jnp.int32(0))

    def right_of(e):
        early = jnp.where(e == 0, 0, 1 + (e + out_chunks - 1) % out_chunks)
        return jnp.where(e < single, early, e - single + firsts)

    first, second = pl.ds(0, HALF), pl.ds(HALF, HALF)

    def part(u, owner, columns, k):
        @pl.when(u < dec_units)
        def _():
            n = jnp.minimum(u, dec_units - 1)
            products[k] = do[n, owner, :, columns].astype(F32) + dp[n, owner, :, columns].astype(F32)

        @pl.when(u >= dec_units)
        def _():
            e = jnp.maximum(u - dec_units, 0)
            b, r = block_of(e), right_of(e)
            total = matmul(xo[b, owner], yo[r, :, columns])
            products[k] = total + matmul(xp[b, owner], yp[r, :, columns])

        return products[k]

    def copy_a(u, side):
        slot = u % a_out.shape[0]
        return put(
            a_out.at[slot, side],
            a_in.at[u, side],
            a_send.at[slot, side],
            a_recv.at[u, side],
            (x_side, y_side)[side],
        )

    def copy_b(u, side):
        slot = u % b_out.shape[0]
        return put(
            b_out.at[slot, side],
            b_in.at[u, side],
            b_send.at[slot, side],
            b_recv.at[u, side],
            (y_side, x_side)[side],
        )

    z_slots = z_out.shape[0]

    def copy_in(u):
        return put(z_out.at[u % z_slots], z_one.at[u], z_send.at[u, 0], z_recv.at[u, 0], inward)

    def copy_across(u):
        return put(z_out.at[u % z_slots], z_two.at[u], z_send.at[u, 0], z_recv.at[u, 1], across)

    def copy_out(u):
        return put(z_one.at[u], z_one.at[u], z_send.at[u, 1], z_recv.at[u, 0], outward)

    def copy_v(step, device):
        return put(v_out.at[step], v_in.at[step], v_send.at[step], v_recv.at[step], device)

    gain_one, gain_two, gain_out = [vectors_ref[:, n * D : (n + 1) * D] for n in range(3)]

    def give(r, value):
        yo[r] = value
        swap_right(r).start()

    def columns_at(n):
        return slice(n * UNIT, (n + 1) * UNIT)

    def back_link():
        dseen = jnp.where(column_ref[:VIS, 0:1] > 0, dy_ref[...], 0.0).astype(BF)
        give(0, dseen)
        wide_copy(0).wait()
        h_copy(end_ref).wait()
        unit, rate = normalize(h_buf[...])
        dend, dgain = normalize_back(unit, rate, gain_out, right_t(dseen, wide_buf[0]))
        grad_vec[...] = vec_ref[...]
        grad_vec[2:3, :] = dgain
        dend_ref[...] = dend
        dbranch_ref[...] = dend.astype(BF)
        for n in range(out_chunks):
            give(1 + n, dbranch_ref[:, columns_at(n)])
        wide_copy(ring).start()
        h_copy(middle_ref).start()
        dmid_ref[...] = jnp.zeros_like(dmid_ref)

    def back_hidden(j):
        w = 1 + j
        down_copy(j).wait()
        slope_copy(j).wait()
        wide_copy(w).wait()
        dhidden = right_t(dbranch_ref[...], down_buf[j % 2])
        dbefore = (dhidden * slope_buf[j % 2]).astype(BF)
        give(firsts + j, dbefore)
        dmid_ref[...] += right_t(dbefore, wide_buf[w % ring])
        wide_copy(w + ring).start()

        @pl.when(j + 2 < up_chunks)
        def _():
            down_copy(j + 2).start()
            slope_copy(j + 2).start()

    def back_out():
        h_copy(middle_ref).wait()
        unit, rate = normalize(h_buf[...])
        dmiddle, dgain = normalize_back(unit, rate, gain_two, dmid_ref[...])
        grad_vec[1:2, :] = dgain
        dmiddle = dmiddle + dend_ref[...]
        dend_ref[...] = dmiddle
        dattn = dmiddle.astype(BF)
        dmixed = jnp.zeros((VIS, D), F32)
        for n in range(out_chunks):
            w = 1 + up_chunks + n
            piece = dattn[:, columns_at(n)]
            give(firsts + up_chunks + n, piece)
            wide_copy(w).wait()
            dmixed = dmixed + right_t(piece, wide_buf[w % ring])
            wide_copy(w + ring).start()
        dmixed_ref[...] = dmixed.astype(BF)
        h_copy(start_ref).start()
        dmid_ref[...] = jnp.zeros_like(dmid_ref)

    size = D // HEADS
    lane_head = lax.broadcasted_iota(jnp.int32, (VIS, LANES), 1) // size

    def only(array, j):
        return jnp.where(lane_head == j, array.astype(F32), 0.0).astype(BF)

    def back_attention(g):
        at = [pl.ds(pl.multiple_of(n * D + g * LANES, LANES), LANES) for n in range(3)]
        query, keys, values = [qkv_ref[:, lanes] for lanes in at]
        dout = dmixed_ref[:, at[0]]
        keys_t = keys.T
        factor = size ** (-0.5)
        dkeys, dvalues = jnp.zeros((VIS, LANES), F32), jnp.zeros((VIS, LANES), F32)
        dquery = []
        for j in range(LANES // size):
            scores = right_t(keys, only(query, j)) * factor + bias_ref[...]
            probs = jnp.exp(scores - jnp.max(scores, 0, keepdims=True))
            probs = probs * (1.0 / jnp.sum(probs, 0, keepdims=True))
            dvalues = jnp.where(lane_head == j, matmul(probs.astype(BF), dout), dvalues)
            dprobs = right_t(values, only(dout, j))
            delta = jnp.sum(dprobs * probs, 0, keepdims=True)
            dscores = (probs * (dprobs - delta)).astype(BF)
            dkeys = jnp.where(lane_head == j, matmul(dscores, query), dkeys)
            dquery.append(matmul(keys_t[j * size : (j + 1) * size, :], dscores))
        dqkv_ref[:, at[0]] = (jnp.concatenate(dquery, 0) * factor).astype(BF).T
        dqkv_ref[:, at[1]] = (dkeys * factor).astype(BF)
        dqkv_ref[:, at[2]] = dvalues.astype(BF)

    def give_qkv():
        for c in range(qkv_chunks):
            give(firsts + up_chunks + out_chunks + c, dqkv_ref[:, columns_at(c)])

    def back_qkv(c):
        w = 1 + up_chunks + out_chunks + c
        wide_copy(w).wait()
        piece = dqkv_ref[:, pl.ds(pl.multiple_of(c * UNIT, UNIT), UNIT)]
        dmid_ref[...] += right_t(piece, wide_buf[w % ring])

        @pl.when(w + ring < chunks)
        def _():
            wide_copy(w + ring).start()

    def back_start():
        h_copy(start_ref).wait()
        unit, rate = normalize(h_buf[...])
        dh, dgain = normalize_back(unit, rate, gain_one, dmid_ref[...])
        grad_vec[0:1, :] = dgain
        dh = (dh + dend_ref[...]).astype(BF)
        for n in range(out_chunks):
            give(firsts + up_chunks + out_chunks + qkv_chunks + n, dh[:, columns_at(n)])

    at_hidden = 1
    at_out = at_hidden + up_chunks
    at_attention = at_out + 1
    groups = D // LANES
    at_qkv = at_attention + groups
    at_start = at_qkv + qkv_chunks
    at_vec = at_start + 1

    def step(i, _):
        def stage(lag, also=None):
            u = i - lag
            ok = (u >= 0) & (u < count)
            if also is not None:
                ok = ok & also
            return u, pl.when(ok)

        u0, when = stage(0)

        @when
        def _():
            u = u0

            @pl.when(u < dec_units)
            def _():
                pltpu.make_async_copy(do.at[u], do.at[u], dec_sem.at[u, 0]).wait()
                swap_dec(do.at[u], u).wait()

            @pl.when(u == dec_units)
            def _():
                for b in range(len(blocks)):
                    pltpu.make_async_copy(xo.at[b], xo.at[b], left_sem.at[b, 0]).wait()
                    swap_left(xo.at[b], b).wait()
                for r in range(firsts):
                    swap_right(r).wait()

            @pl.when(u >= dec_units + single)
            def _():
                swap_right(u - dec_units - single + firsts).wait()

            @pl.when(u >= a_out.shape[0])
            def _():
                for side in range(2):
                    copy_a(u - a_out.shape[0], side).wait_send()

            slot = u % a_out.shape[0]
            a_out[slot, 0, 0] = part(u, at_x, first, 0).astype(BF)
            a_out[slot, 0, 1] = part(u, at_far, first, 1).astype(BF)
            copy_a(u, 0).start()
            a_out[slot, 1, 0] = part(u, at_y, second, 2).astype(BF)
            a_out[slot, 1, 1] = part(u, at_far, second, 3).astype(BF)
            copy_a(u, 1).start()

        u1, when = stage(LAGS[0])

        @when
        def _():
            u = u1
            slot = u % b_out.shape[0]

            @pl.when(u >= b_out.shape[0])
            def _():
                for side in range(2):
                    copy_b(u - b_out.shape[0], side).wait_send()

            copy_a(u, 0).wait_recv()
            b_out[slot, 0] = (part(u, at_y, first, 0) + a_in[u, 0, 1].astype(F32)).astype(BF)
            copy_b(u, 0).start()
            copy_a(u, 1).wait_recv()
            b_out[slot, 1] = (part(u, at_x, second, 1) + a_in[u, 1, 1].astype(F32)).astype(BF)
            copy_b(u, 1).start()

        u2, when = stage(LAGS[1])

        @when
        def _():
            u = u2
            copy_b(u, 0).wait_recv()
            copy_b(u, 1).wait_recv()
            for side, columns in enumerate((first, second)):
                total = part(u, place, columns, side) + a_in[u, side, 0].astype(F32)
                sums[u % 4, :, columns] = total + b_in[u, side].astype(F32)

            @pl.when(outer)
            def _():
                @pl.when(u >= z_slots)
                def _():
                    copy_in(u - z_slots).wait_send()

                z_out[u % z_slots] = sums[u % 4].astype(BF)
                copy_in(u).start()

        u3, when = stage(LAGS[2], inner)

        @when
        def _():
            u = u3
            copy_in(u).wait_recv()

            @pl.when(u >= z_slots)
            def _():
                copy_across(u - z_slots).wait_send()

            z_out[u % z_slots] = (sums[u % 4] + z_one[u].astype(F32)).astype(BF)
            copy_across(u).start()

        u4, when = stage(LAGS[3], inner)

        @when
        def _():
            u = u4
            copy_across(u).wait_recv()
            z_one[u] = (z_out[u % z_slots].astype(F32) + z_two[u].astype(F32)).astype(BF)
            copy_out(u).start()

        u5, when = stage(LAGS[4], outer)

        @when
        def _():
            copy_out(u5).wait_recv()

        pl.when(i == 0)(back_link)

        @pl.when((i >= at_hidden) & (i < at_hidden + up_chunks))
        def _():
            back_hidden(i - at_hidden)

        pl.when(i == at_out)(back_out)

        @pl.when((i >= at_attention) & (i < at_attention + groups))
        def _():
            back_attention(i - at_attention)

        pl.when(i == at_qkv)(give_qkv)

        @pl.when((i >= at_qkv) & (i < at_qkv + qkv_chunks))
        def _():
            back_qkv(i - at_qkv)

        pl.when(i == at_start)(back_start)

        for number, device in enumerate((partner, x_side, y_side)):

            @pl.when(i == at_vec + number)
            def _():
                if number == 0:
                    v_out[0] = grad_vec[...]
                else:
                    copy_v(number - 1, (partner, x_side, y_side)[number - 1]).wait_recv()
                    v_out[number] = v_out[number - 1] + v_in[number - 1]
                copy_v(number, device).start()

        @pl.when(i == at_vec + 3)
        def _():
            copy_v(2, y_side).wait_recv()
            v_out[3] = v_out[2] + v_in[2]

            @pl.when(outer)
            def _():
                copy_v(3, inward).start()

        @pl.when((i == at_vec + 4) & inner)
        def _():
            copy_v(3, inward).wait_recv()
            v_out[4] = v_out[3] + v_in[3]
            copy_v(4, across).start()

        @pl.when((i == at_vec + 5) & inner)
        def _():
            copy_v(4, across).wait_recv()
            v_out[5] = v_out[4] + v_in[4]
            copy_v(5, outward).start()
            vec_out[...] = v_out[5]

        @pl.when((i == at_vec + 7) & outer)
        def _():
            copy_v(5, outward).wait_recv()
            vec_out[...] = v_in[5]

        return 0

    lax.fori_loop(0, count + LAGS[4], step, 0)

    stores = []
    for n, (u, start, out, row, rows, column) in enumerate(spots):
        stores.append(
            pltpu.make_async_copy(
                z_one.at[u, pl.ds(start, rows)],
                outs[out].at[pl.ds(row, rows), pl.ds(column, UNIT)],
                store_sem.at[n],
            )
        )
    for store in stores:
        store.start()
    for u in range(count - a_out.shape[0], count):
        for side in range(2):
            copy_a(u, side).wait_send()
    for u in range(count - b_out.shape[0], count):
        for side in range(2):
            copy_b(u, side).wait_send()
    for number, device in enumerate((partner, x_side, y_side)):
        copy_v(number, device).wait_send()
    for store in stores:
        store.wait()

    @pl.when(outer)
    def _():
        copy_v(3, inward).wait_send()
        for u in range(count - z_slots, count):
            copy_in(u).wait_send()

    @pl.when(inner)
    def _():
        copy_v(4, across).wait_send()
        copy_v(5, outward).wait_send()
        for u in range(count - z_slots, count):
            copy_across(u).wait_send()

        def drain(u, _):
            copy_out(u).wait_send()
            return 0

        lax.fori_loop(0, count, drain, 0)


def encoder_back(dy, by_column, vec, vectors, bias, qkv, dec, states, wide, down, lefts):
    owners = lax.axis_size("fsdp")
    own = PD // owners
    dec_units = dec.shape[1] * dec.shape[2] // ROWS
    dec = dec.reshape(4, 2, dec_units, ROWS, UNIT)
    half = ROWS // 2
    blocks, units, spots = [], [], []
    for n in range(2 * dec_units):
        place = (4, n * half, half, 0) if n < DFF // DD else (3, 0, half, (n - DFF // DD) * UNIT)
        spots.append((n // 2, n % 2 * half, *place))

    def add(left, sub, right, out, row, rows, column, columns):
        blocks.append((left, sub))
        for n in range(columns // UNIT):
            spots.append((dec_units + len(units), 0, out, row, rows, column + n * UNIT))
            units.append((len(blocks) - 1, right + n))

    subs = FF // owners // ROWS
    add(0, 0, 0, 1, 0, ROWS, 4 * D + FF, DD)
    for n in range(subs):
        add(1, n, 1, 2, n * ROWS, ROWS, 0, D)
    right = 1 + D // UNIT
    add(2, 0, right, 1, 0, ROWS, 4 * D, FF)
    right += FF // UNIT
    add(3, 0, right, 1, 0, ROWS, 3 * D, D)
    right += D // UNIT
    add(4, 0, right, 1, 0, ROWS, 0, 3 * D)
    right += 3 * D // UNIT
    add(5, 0, right, 0, 0, own, 0, D)
    right += D // UNIT
    count = dec_units + len(units)
    shapes = ((own, D), (ROWS, 4 * D + FF + DD), (FF // owners, D), (half, 10 * UNIT), (DFF // owners, DD))
    lefts = [a.reshape(4, 2, -1, VIS) for a in lefts]
    slots = 3
    dma = pltpu.SemaphoreType.DMA
    vmem, anywhere = pl.BlockSpec(memory_space=pltpu.VMEM), pl.BlockSpec(memory_space=pl.ANY)
    return pl.pallas_call(
        partial(back_kernel, dec_units, tuple(blocks), tuple(units), tuple(spots)),
        out_shape=tuple(jax.ShapeDtypeStruct(shape, BF) for shape in shapes)
        + (jax.ShapeDtypeStruct(vec.shape, F32),),
        in_specs=[vmem] * 6 + [anywhere] * (7 + len(lefts)),
        out_specs=(anywhere,) * len(shapes) + (vmem,),
        scratch_shapes=[
            pltpu.VMEM((len(blocks), 4, ROWS, VIS), BF),
            pltpu.VMEM((len(blocks), 4, ROWS, VIS), BF),
            pltpu.VMEM((right, VIS, UNIT), BF),
            pltpu.VMEM((right, VIS, UNIT), BF),
            pltpu.VMEM((dec_units, 4, ROWS, UNIT), BF),
            pltpu.VMEM((dec_units, 4, ROWS, UNIT), BF),
            pltpu.VMEM((4, ROWS, HALF), F32),
            pltpu.VMEM((slots, 2, 2, ROWS, HALF), BF),
            pltpu.VMEM((count, 2, 2, ROWS, HALF), BF),
            pltpu.VMEM((slots, 2, ROWS, HALF), BF),
            pltpu.VMEM((count, 2, ROWS, HALF), BF),
            pltpu.VMEM((4, ROWS, UNIT), F32),
            pltpu.VMEM((6, ROWS, UNIT), BF),
            pltpu.VMEM((count, ROWS, UNIT), BF),
            pltpu.VMEM((count, ROWS, UNIT), BF),
            pltpu.VMEM((6, *vec.shape), F32),
            pltpu.VMEM((6, *vec.shape), F32),
            pltpu.VMEM((3, D, UNIT), BF),
            pltpu.VMEM((2, UNIT, D), BF),
            pltpu.VMEM((2, VIS, UNIT), F32),
            pltpu.VMEM((VIS, D), F32),
            pltpu.VMEM((VIS, D), F32),
            pltpu.VMEM((VIS, D), F32),
            pltpu.VMEM((VIS, D), BF),
            pltpu.VMEM((VIS, D), BF),
            pltpu.VMEM((VIS, 3 * D), BF),
            pltpu.VMEM(vec.shape, F32),
            dma((3,)),
            dma((2,)),
            dma((2,)),
            dma((1,)),
            dma((dec_units, 3)),
            dma((len(blocks), 3)),
            dma((right, 2)),
            dma((slots, 2)),
            dma((count, 2)),
            dma((slots, 2)),
            dma((count, 2)),
            dma((count, 2)),
            dma((count, 2)),
            dma((6,)),
            dma((6,)),
            dma((count + dec_units,)),
        ],
        compiler_params=pltpu.CompilerParams(
            collective_id=0, has_side_effects=True, vmem_limit_bytes=61 * 2**20
        ),
        cost_estimate=pl.CostEstimate(
            flops=30 * 10**9, bytes_accessed=300 * 2**20, transcendentals=0
        ),
    )(dy, by_column, vec, vectors, bias, qkv, dec, *states, wide, down, *lefts)


def encoder_pieces(shapes):
    (own, width), (rows, _), (tall, _), (dec_rows, dec_width), (dec_tall, _) = shapes
    half = dec_rows // 2
    pieces = [(3, n * half, half, 0, dec_width, n + 1) for n in range(2)]
    pieces += [(0, 0, own, 0, width, 0)]
    pieces += [(1, 0, rows, n * D, D, (1, 2, 0)[n]) for n in range(3)]
    pieces += [(1, 0, rows, 3 * D, D, 1)]
    pieces += [(1, 0, rows, 4 * D + n * D, D, (2, 0, 1, 2)[n]) for n in range(FF // D)]
    pieces += [(2, n * rows, rows, 0, D, (0, 1, 2, 0)[n]) for n in range(tall // rows)]
    pieces += [(1, 0, rows, 4 * D + FF, DD, 0)]
    pieces += [(4, 0, dec_tall, 0, DD, 0)]
    return pieces


def norm_rows(h, gain):
    mean = jnp.mean(h, -1, keepdims=True)
    cent = h - mean
    var = jnp.mean(cent * cent, -1, keepdims=True)
    return (cent * lax.rsqrt(var + EPS) * gain).astype(BF)


def encoder_kernel(
    pixels_ref,
    row_ref,
    column_ref,
    scale_ref,
    omega_ref,
    vectors_ref,
    embed_ref,
    wide_ref,
    down_ref,
    dec_wide_ref,
    dec_down_ref,
    wide_out,
    down_out,
    dec_wide_out,
    dec_down_out,
    picked_out,
    slope_out,
    stats_out,
    by_row,
    by_column,
    pos_out,
    bias_out,
    inputs_t,
    a_t,
    mixed_t,
    b_t,
    hidden_t,
    z_t,
    start_ref,
    qkv_ref,
    middle_ref,
    end_ref,
    seen_ref,
    inputs_ref,
    a_ref,
    mixed_ref,
    b_ref,
    hidden_ref,
    z_ref,
    w_embed,
    w_wide,
    w_down,
    stage_ref,
    pick_ref,
    high_ref,
    mid_ref,
    low_ref,
    picked_ref,
    pos_ref,
    bias_ref,
    dec_stage,
    dec_stage_down,
    dec_own,
    dec_own_down,
    slope_ref,
    hidden_pixels,
    v_in,
    v_out,
    load_sem,
    store_sem,
    send_sem,
    recv_sem,
    v_send,
    v_recv,
    side_sem,
):
    shards = (embed_ref, wide_ref, down_ref, dec_wide_ref, dec_down_ref)
    gathered = (w_embed, w_wide, w_down, dec_wide_out, dec_down_out)
    gain_one, gain_two, gain_out = [vectors_ref[:, n * D : (n + 1) * D] for n in range(3)]
    pieces = encoder_pieces([ref.shape for ref in shards])
    count, base = len(pieces), 2
    stores = []
    z, f = lax.axis_index("dp"), lax.axis_index("fsdp")
    core, place = f % 2, f // 2
    x, y = place % 2, place // 2
    f_x, f_y, f_far = f + 2 - 4 * x, f + 4 - 8 * y, f + 6 - 4 * x - 8 * y
    partner = (z, f + 1 - 2 * core)
    x_side, y_side, z_side = (z, f_x), (z, f_y), (z + 1 - 2 * (z % 2), f)
    outer = (z == 0) | (z == 3)
    inner = (z == 1) | (z == 2)
    across = (3 - z, f)

    barrier = pltpu.get_barrier_semaphore()
    for device in (partner, x_side, y_side, z_side):
        pl.semaphore_signal(barrier, inc=1, device_id=device, device_id_type=MESH)

    @pl.when(outer)
    def _():
        pl.semaphore_wait(barrier, 4)

    @pl.when(inner)
    def _():
        pl.semaphore_signal(barrier, inc=1, device_id=across, device_id_type=MESH)
        pl.semaphore_wait(barrier, 5)

    stages = stage_ref.shape[0]

    def load(t):
        array, row, rows, column, columns, _ = pieces[t]
        return pltpu.make_async_copy(
            shards[array].at[pl.ds(row, rows), pl.ds(column, columns)],
            stage_ref.at[staged[t], pl.ds(0, rows), pl.ds(0, columns)],
            load_sem.at[staged[t]],
        )

    encoder = [t for t, piece in enumerate(pieces) if piece[0] < 3]
    staged = {t: n % stages for n, t in enumerate(encoder)}
    after = dict(zip(encoder, encoder[stages:]))
    dec_loads = [
        pltpu.make_async_copy(dec_wide_ref, dec_stage, side_sem.at[0]),
        pltpu.make_async_copy(dec_down_ref, dec_stage_down, side_sem.at[1]),
    ]
    for copy in dec_loads:
        copy.start()
    for t in encoder[:stages]:
        load(t).start()

    def spot(t, owner, half=None):
        array, row, rows, column, columns, _ = pieces[t]
        if array > 2:
            if half is not None:
                rows //= 2
                row += half * rows
            return gathered[array].at[owner, pl.ds(row, rows)]
        if half is not None:
            columns //= 2
            column += half * columns
        return gathered[array].at[owner, pl.ds(row, rows), pl.ds(column, columns)]

    def move(t, owner, send, recv, device, half=None):
        target = source = spot(t, owner, half)
        array, row, rows = pieces[t][:3]
        if send < 3 and array > 2:
            source = (dec_own, dec_own_down)[array - 3].at[pl.ds(row, rows)]
        return put(source, target, send_sem.at[t, send], recv_sem.at[t, recv], device)

    def own_x(t):
        return move(t, f, 0, 0, x_side)

    def own_y(t):
        return move(t, f, 1, 1, y_side)

    def own_core(t):
        return move(t, f, 2, 4, partner)

    def far_x(t):
        return move(t, f_y, 3, 2, x_side, 0)

    def far_y(t):
        return move(t, f_x, 4, 3, y_side, 1)

    def to_core(t, n):
        return move(t, (f_x, f_y, f_far)[n], 5 + n, 5 + n, partner)

    def to_z(t, n):
        return move(t, (f_x, f_y, f_far)[n], 8 + n, 8 + n, z_side)

    def brings(t, then, other=None):
        kind = pieces[t][5]
        if kind == 0:
            then()
            return
        pl.when(z % 2 == kind - 1)(then)
        if other is not None:
            pl.when(z % 2 != kind - 1)(other)

    def first(t):
        array, row, rows, column, columns, _ = pieces[t]
        if array < 3:
            load(t).wait()
            spot(t, f)[...] = stage_ref[staged[t], :rows, :columns].astype(BF)
            if t in after:
                load(after[t]).start()
        else:
            if row == 0:
                dec_loads[array - 3].wait()
            own = (dec_own, dec_own_down)[array - 3]
            own[row : row + rows, :] = (dec_stage, dec_stage_down)[array - 3][
                row : row + rows, :
            ].astype(BF)
            store = pltpu.make_async_copy(own.at[pl.ds(row, rows)], spot(t, f), store_sem.at[t])
            store.start()
            stores.append(store)
        own_core(t).start()

        def then():
            own_x(t).start()
            own_y(t).start()

        brings(t, then)

    def second(t):
        def then():
            own_x(t).wait_recv()
            far_y(t).start()
            own_y(t).wait_recv()
            far_x(t).start()
            for n in range(2):
                to_core(t, n).start()
                if pieces[t][5]:
                    to_z(t, n).start()

        brings(t, then)

    def third(t):
        def then():
            far_x(t).wait_recv()
            far_y(t).wait_recv()
            to_core(t, 2).start()
            if pieces[t][5]:
                to_z(t, 2).start()

        brings(t, then)

    def taken(t, n):
        def other():
            to_z(t, n).wait_recv()
            to_core(t, n).start()

        brings(t, lambda: None, other)

    def whole(t):
        own_core(t).wait_recv()
        for n in range(3):
            to_core(t, n).wait_recv()

    def drain(t):
        own_core(t).wait_send()
        for n in range(3):
            to_core(t, n).wait_send()

        def then():
            for copy in (own_x(t), own_y(t), far_x(t), far_y(t)):
                copy.wait_send()
            if pieces[t][5]:
                for n in range(3):
                    to_z(t, n).wait_send()

        brings(t, then)

    def copy_v(step, device):
        return put(v_out.at[step], v_in.at[step], v_send.at[step], v_recv.at[step], device)

    sides = (partner, x_side, y_side)

    def statistics(i):
        if i <= 3:
            if i > 0:
                copy_v(i - 1, sides[i - 1]).wait_recv()
                v_out[i] = v_out[i - 1] + v_in[i - 1]
            if i < 3:
                copy_v(i, sides[i]).start()
            else:

                @pl.when(outer)
                def _():
                    copy_v(3, z_side).start()

        if i == 4:

            @pl.when(inner)
            def _():
                copy_v(3, z_side).wait_recv()
                v_out[4] = v_out[3] + v_in[3]
                copy_v(4, across).start()

        if i == 5:

            @pl.when(inner)
            def _():
                copy_v(4, across).wait_recv()
                v_out[5] = v_out[4] + v_in[4]
                copy_v(5, z_side).start()
                stats_out[...] = v_out[5]

            @pl.when(outer)
            def _():
                copy_v(5, z_side).wait_recv()
                stats_out[...] = v_in[5]

    def turn(source, target, start=0, width=D):
        for lane in range(start, start + width, LANES):
            target[lane : lane + LANES, :] = source[:, lane : lane + LANES].T

    def columns_of(t):
        array, row, rows, column, columns, _ = pieces[t]
        weight = gathered[array][:, row : row + rows, column : column + columns]
        return weight.reshape(-1, columns)

    def local_statistics():
        pixels = pixels_ref[...]
        weighted = pixels * column_ref[:, 0:1]
        sums = jnp.sum(weighted, 0, keepdims=True)
        squares = jnp.sum(weighted * pixels, 0, keepdims=True)
        live = row_ref[0:1, :]
        totals = [r[:, n * PATCH**2 : (n + 1) * PATCH**2] for r in (sums, squares) for n in range(BANDS)]
        for n, total in enumerate((*totals, live, live * row_ref[1:2, :])):
            v_out[0, n : n + 1, :] = jnp.broadcast_to(jnp.sum(total, 1, keepdims=True), (1, LANES))

    def arrange_step():
        slots = (TOK_DEV, TOK_DEV)
        down, along = [lax.broadcasted_iota(jnp.int32, slots, n) for n in range(2)]
        live, masked = row_ref[0:1, :], row_ref[1:2, :]
        seen, hid = live * (1.0 - masked), live * masked
        kind = lax.broadcasted_iota(jnp.int32, row_ref.shape, 0)
        kinds = jnp.where(kind == 0, seen, jnp.where(kind == 1, hid, 1.0 - live))
        ranks = matmul(kinds.astype(BF), jnp.where(down < along, 1.0, 0.0).astype(BF))
        n_seen, n_hid = [jnp.sum(r, 1, keepdims=True) for r in (seen, hid)]
        empty = ranks[2:3, :]
        place = jnp.where(empty < VIS - n_seen, n_seen + empty, n_seen + n_hid + empty)
        place = jnp.where(hid > 0, VIS + ranks[1:2, :], place)
        place = jnp.where(seen > 0, ranks[0:1, :], place)
        pick_ref[...] = jnp.where(down == place.astype(jnp.int32), 1.0, 0.0).astype(BF)
        facts = row_ref[...].astype(BF)
        by_row[...] = right_t(facts, pick_ref[...])
        by_column[...] = right_t(pick_ref[...], facts)
        pixels = pixels_ref[...]
        high = pixels.astype(BF)
        rest = pixels - high.astype(F32)
        mid = rest.astype(BF)
        high_ref[...], mid_ref[...] = high, mid
        low_ref[...] = (rest - mid.astype(F32)).astype(BF)

    def pick_rows(rows):
        pick = pick_ref[rows, :]
        return matmul(pick, high_ref[...]) + matmul(pick, mid_ref[...]) + matmul(pick, low_ref[...])

    def pick_step():
        picked_ref[...] = pick_rows(slice(0, VIS))
        same = by_column[:VIS, 2:3] == by_row[2:3, :VIS]
        shape = (VIS, VIS)
        bias_out[...] = mask_bias(by_column[:VIS, 0:1] > 0, same, shape, 0)
        bias_ref[...] = mask_bias(by_row[0:1, :VIS] > 0, same, shape, 0, 1)

    def position_rows(target, rows, width, row):
        quarter = width // 4
        odd = by_column[rows, 2:3] > 0
        scale = jnp.where(odd, scale_ref[1:2, 0:1], scale_ref[0:1, 0:1])
        for n in range(2):
            angle = by_column[rows, 3 + n : 4 + n] * scale * omega_ref[row : row + 1, :quarter]
            target[rows, 2 * n * quarter : (2 * n + 1) * quarter] = jnp.sin(angle)
            target[rows, (2 * n + 1) * quarter : (2 * n + 2) * quarter] = jnp.cos(angle)

    def pixel_store(n):
        return pltpu.make_async_copy(
            hidden_pixels, picked_out.at[pl.ds((n - 1) * VIS, VIS)], side_sem.at[4]
        )

    def hidden_step(n):
        rows = slice(n * VIS, (n + 1) * VIS)
        if n > 0:
            if n > 1:
                pixel_store(n - 1).wait()
            hidden_pixels[...] = pick_rows(rows)
            pixel_store(n).start()
        position_rows(pos_out, rows, DD, 1)

    def embed_step():
        pixels = stats_out[6:7, :] * (PATCH * PATCH)
        for band in range(BANDS):
            mean = stats_out[band : band + 1, :] / pixels
            var = stats_out[BANDS + band : BANDS + band + 1, :] / pixels - mean * mean
            rate = lax.rsqrt(var + EPS)
            for part in range(PATCH * PATCH // LANES):
                lanes = pl.ds(band * PATCH * PATCH + part * LANES, LANES)
                inputs_ref[:, lanes] = ((picked_ref[:, lanes] - mean) * rate).astype(BF)
        start_ref[...] = matmul(inputs_ref[...], columns_of(base)) + pos_ref[...]
        a_ref[...] = norm_rows(start_ref[...], gain_one)
        own = w_embed.shape[1]
        flipped = jnp.concatenate(
            [inputs_ref[:, lane : lane + LANES].T for lane in range(0, PD, LANES)], 0
        )
        inputs_t[...] = jnp.zeros_like(inputs_t)
        for owner in range(w_embed.shape[0]):
            inputs_t[owner, :own, :] = flipped[owner * own : (owner + 1) * own, :]
        turn(a_ref, a_t)

    def qkv_step(n):
        qkv_ref[:, n * D : (n + 1) * D] = matmul(a_ref[...], columns_of(base + 1 + n)).astype(BF)

    def attention_step():
        size = D // HEADS
        lane_head = lax.broadcasted_iota(jnp.int32, (VIS, LANES), 1) // size

        def group(g, _):
            query, keys, values = [
                qkv_ref[:, pl.ds(pl.multiple_of(n * D + g * LANES, LANES), LANES)] for n in range(3)
            ]
            mixed = jnp.zeros((VIS, LANES), F32)
            for j in range(LANES // size):
                one = jnp.where(lane_head == j, query.astype(F32), 0.0).astype(BF)
                scores = right_t(one, keys) * size ** (-0.5) + bias_ref[...]
                probs = jnp.exp(scores - jnp.max(scores, -1, keepdims=True))
                probs = probs * (1.0 / jnp.sum(probs, -1, keepdims=True))
                mixed = jnp.where(lane_head == j, matmul(probs.astype(BF), values), mixed)
            mixed_ref[:, pl.ds(pl.multiple_of(g * LANES, LANES), LANES)] = mixed.astype(BF)
            return 0

        lax.fori_loop(0, D // LANES, group, 0)

    def out_step():
        turn(mixed_ref, mixed_t)
        middle_ref[...] = start_ref[...] + matmul(mixed_ref[...], columns_of(base + 4))
        b_ref[...] = norm_rows(middle_ref[...], gain_two)
        turn(b_ref, b_t)

    def slope_store(n):
        return pltpu.make_async_copy(
            slope_ref.at[n % 2], slope_out.at[:, pl.ds(n * D, D)], side_sem.at[2 + n % 2]
        )

    def up_step(n):
        columns = slice(n * D, (n + 1) * D)
        after, slope = gelu_parts(matmul(b_ref[...], columns_of(base + 5 + n)))
        hidden_ref[:, columns] = after.astype(BF)
        if n > 1:
            slope_store(n - 2).wait()
        slope_ref[n % 2] = slope
        slope_store(n).start()
        turn(hidden_ref, hidden_t, n * D)

    def down_step(n):
        rows, owners = w_wide.shape[1], w_down.shape[0]
        tall = w_down.shape[1]
        parts = [hidden_ref[:, o * tall + n * rows : o * tall + (n + 1) * rows] for o in range(owners)]
        total = matmul(jnp.concatenate(parts, 1), columns_of(base + 9 + n))
        end_ref[...] = (middle_ref[...] if n == 0 else end_ref[...]) + total

    def link_step():
        z_ref[...] = norm_rows(end_ref[...], gain_out)
        turn(z_ref, z_t)
        seen_ref[...] = matmul(z_ref[...], columns_of(base + 13))

    work = [(0, None, arrange_step), (1, None, pick_step)]
    work += [(2, None, partial(position_rows, pos_ref, slice(0, VIS), D, 0))]
    work += [(at, None, partial(hidden_step, n)) for n, at in enumerate((3, 4, 11, 14))]
    work += [(6, base, embed_step), (8, base + 1, partial(qkv_step, 0))]
    work += [(9, base + 2, partial(qkv_step, 1)), (9, base + 3, partial(qkv_step, 2))]
    work += [(9, None, attention_step), (11, base + 4, out_step)]
    work += [(at, base + 5 + n, partial(up_step, n)) for n, at in enumerate((12, 12, 14, 15))]
    work += [(at, base + 9 + n, partial(down_step, n)) for n, at in enumerate((15, 17, 18, 18))]
    work += [(19, base + 13, link_step)]

    first(0)
    local_statistics()
    first(1)
    for i in range(20):
        if i + 2 < count:
            first(i + 2)
        statistics(i)
        if i < count:
            second(i)
        if 0 <= i - 1 < count:
            third(i - 1)
        if 0 <= i - 3 < count:
            taken(i - 3, 0)
            taken(i - 3, 1)
        if 0 <= i - 4 < count:
            taken(i - 4, 2)
        for at, piece, run in work:
            if at != i:
                continue
            if piece is not None:
                whole(piece)
                array, row, rows, column, columns, _ = pieces[piece]
                if array:
                    where = (slice(None), pl.ds(row, rows), pl.ds(column, columns))
                    store = pltpu.make_async_copy(
                        gathered[array].at[where],
                        (None, wide_out, down_out)[array].at[where],
                        store_sem.at[piece],
                    )
                    store.start()
                    stores.append(store)
            run()
    for t, piece in enumerate(pieces):
        if piece[0] > 2:
            whole(t)
    for n in range(2):
        slope_store(FF // D - 2 + n).wait()
    pixel_store(HID // VIS).wait()
    for store in stores:
        store.wait()
    for t in range(count):
        drain(t)
    for step in range(3):
        copy_v(step, sides[step]).wait_send()

    @pl.when(outer)
    def _():
        copy_v(3, z_side).wait_send()

    @pl.when(inner)
    def _():
        copy_v(4, across).wait_send()
        copy_v(5, z_side).wait_send()


def encoder_forward(pixels, facts, scale, vectors, *shards):
    owners = lax.axis_size("fsdp")
    shapes = [w.shape for w in shards]
    count = len(encoder_pieces(shapes))
    omega = [
        10000.0 ** (-jnp.arange(width // 4, dtype=jnp.float32) / (width // 4)) for width in (D, DD)
    ]
    omega = jnp.stack([omega[0], jnp.pad(omega[1], (0, D // 4 - DD // 4))] + [omega[0]] * 6)
    full = [jax.ShapeDtypeStruct((owners, *shape), BF) for shape in shapes[1:]]
    full += [jax.ShapeDtypeStruct((HID, PD), F32), jax.ShapeDtypeStruct((VIS, FF), F32)]
    local = [
        jax.ShapeDtypeStruct((8, LANES), F32),
        jax.ShapeDtypeStruct((8, TOK_DEV), F32),
        jax.ShapeDtypeStruct((TOK_DEV, 8), F32),
        jax.ShapeDtypeStruct((TOK_DEV, DD), F32),
        jax.ShapeDtypeStruct((VIS, VIS), F32),
        jax.ShapeDtypeStruct((owners, ROWS, VIS), BF),
        *[jax.ShapeDtypeStruct((width, VIS), BF) for width in (D, D, D, FF, D)],
        jax.ShapeDtypeStruct((VIS, D), F32),
        jax.ShapeDtypeStruct((VIS, 3 * D), BF),
        jax.ShapeDtypeStruct((VIS, D), F32),
        jax.ShapeDtypeStruct((VIS, D), F32),
        jax.ShapeDtypeStruct((VIS, DD), F32),
    ]
    vmem, anywhere = pl.BlockSpec(memory_space=pltpu.VMEM), pl.BlockSpec(memory_space=pl.ANY)
    dma = pltpu.SemaphoreType.DMA
    wide_full, down_full, dec_wide, dec_down, *rest = pl.pallas_call(
        encoder_kernel,
        out_shape=(*full, *local),
        in_specs=[vmem] * 6 + [anywhere] * len(shards),
        out_specs=(anywhere,) * len(full) + (vmem,) * len(local),
        scratch_shapes=[pltpu.VMEM((VIS, width), BF) for width in (PD, D, D, D, FF, D)]
        + [pltpu.VMEM((owners, *shape), BF) for shape in shapes[:3]]
        + [
            pltpu.VMEM((4, ROWS, D), F32),
            *[pltpu.VMEM((TOK_DEV, PD), BF)] * 4,
            pltpu.VMEM((VIS, PD), F32),
            pltpu.VMEM((VIS, D), F32),
            pltpu.VMEM((VIS, VIS), F32),
            *[pltpu.VMEM(shape, F32) for shape in shapes[3:]],
            *[pltpu.VMEM(shape, BF) for shape in shapes[3:]],
            pltpu.VMEM((2, VIS, D), F32),
            pltpu.VMEM((VIS, PD), F32),
            pltpu.VMEM((6, 8, LANES), F32),
            pltpu.VMEM((6, 8, LANES), F32),
            dma((4,)),
            dma((count,)),
            dma((count, 11)),
            dma((count, 11)),
            dma((6,)),
            dma((6,)),
            dma((5,)),
        ],
        compiler_params=pltpu.CompilerParams(
            collective_id=1, has_side_effects=True, vmem_limit_bytes=60 * 2**20
        ),
        cost_estimate=pl.CostEstimate(
            flops=2 * VIS * 14 * 2**20, bytes_accessed=200 * 2**20, transcendentals=0
        ),
    )(pixels, facts, facts.T, scale, omega, vectors, *shards)
    return (
        wide_full.reshape(D, -1),
        down_full.reshape(FF, D),
        dec_wide.reshape(DD, -1),
        dec_down.reshape(DFF, DD),
        *rest,
    )


LOWP = 256
HEADP = PD + LOWP
BLOCK = HID // 2


def mask_bias(live, same, shape, offset, keys=0):
    key, query = [lax.broadcasted_iota(jnp.int32, shape, (keys + n) % 2) for n in range(2)]
    return jnp.where((live & same) | (key + offset == query), 0.0, NEGATIVE)


def normalize(h):
    cent = h - jnp.mean(h, -1, keepdims=True)
    rate = lax.rsqrt(jnp.mean(cent * cent, -1, keepdims=True) + EPS)
    return cent * rate, rate


def normalize_back(unit, rate, gain, grad):
    scaled = grad * gain
    along = jnp.mean(scaled * unit, -1, keepdims=True)
    dh = rate * (scaled - jnp.mean(scaled, -1, keepdims=True) - unit * along)
    return dh, jnp.sum(grad * unit, 0, keepdims=True)


def exact_product(array, weight):
    high = array.astype(BF)
    rest = array - high.astype(F32)
    mid = rest.astype(BF)
    low = (rest - mid.astype(F32)).astype(BF)
    return matmul(high, weight) + matmul(mid, weight) + matmul(low, weight)


def decoder_kernel(
    owners,
    pos_ref,
    seen_ref,
    row_ref,
    column_ref,
    picked_ref,
    stats_ref,
    vectors_ref,
    wide_ref,
    down_ref,
    grads_ref,
    dy_ref,
    vec_out,
    y_ref,
    a_ref,
    q_ref,
    k_ref,
    v_ref,
    mixed_t,
    mixed_ref,
    lse_ref,
    head_ref,
    b_ref,
    hidden_ref,
    z_ref,
    dpred_ref,
    dbranch_ref,
    dbefore_ref,
    dattn_ref,
    dmixed_ref,
    dmiddle_ref,
    dq_ref,
    dk_ref,
    dv_ref,
    loss_ref,
    bias_ref,
    pool_ref,
    spread_ref,
    vec_ref,
):
    size = DD // DHEADS
    per = LANES // size
    factor = size ** (-0.5)
    gain_one, gain_two, gain_out, token = [
        vectors_ref[:, 3 * D + n * DD : 3 * D + (n + 1) * DD] for n in range(4)
    ]

    def pooled(shape, pixels):
        pixel, low = [lax.broadcasted_iota(jnp.int32, shape, (pixels + n) % 2) for n in range(2)]
        row, column = (pixel >> 4) & 15, pixel & 15
        return ((pixel >> 8) << 6) + ((row >> 1) << 3) + (column >> 1) == low

    pool_ref[...] = jnp.where(pooled((PD, LOWP), 0), 0.25, 0.0).astype(BF)
    spread_ref[...] = jnp.where(pooled((LOWP, PD), 1), 1.0, 0.0).astype(BF)
    lane_head = lax.broadcasted_iota(jnp.int32, (HID, LANES), 1) // size
    key_head = lax.broadcasted_iota(jnp.int32, (TOK_DEV, LANES), 1) // size
    kept = column_ref[:VIS, 0:1] > 0
    for start in range(0, TOK_DEV, VIS):
        rows = slice(start, start + VIS)
        bias_ref[rows, :] = mask_bias(
            column_ref[rows, 0:1] > 0,
            column_ref[rows, 2:3] == row_ref[2:3, VIS:],
            (VIS, HID),
            start - VIS,
        )
    vec_ref[...] = jnp.zeros_like(vec_ref)
    loss_ref[...] = jnp.zeros_like(loss_ref)
    head_ref[...] = jnp.zeros_like(head_ref)
    head_ref[:, : PD + LOWD] = wide_ref[:, 4 * DD + DFF :]

    def project(rows, with_query):
        a = (normalize(y_ref[rows, :])[0] * gain_one).astype(BF)
        a_ref[rows, :] = a
        k_ref[rows, :] = matmul(a, wide_ref[:, DD : 2 * DD]).astype(BF)
        v_ref[rows, :] = matmul(a, wide_ref[:, 2 * DD : 3 * DD]).astype(BF)
        return a

    y_ref[:VIS, :] = pos_ref[:VIS, :] + jnp.where(kept, seen_ref[...], token)
    y_ref[VIS:, :] = pos_ref[VIS:, :] + token
    project(slice(0, VIS), False)

    def hidden_rows(n):
        start = pl.multiple_of(n * BLOCK, BLOCK)
        return pl.ds(start, BLOCK), pl.ds(pl.multiple_of(start + VIS, 32), BLOCK)

    def project_hidden(n, _):
        rows, all_rows = hidden_rows(n)
        a = project(all_rows, True)
        q_ref[rows, :] = matmul(a, wide_ref[:, :DD]).astype(BF)
        return 0

    lax.fori_loop(0, 2, project_hidden, 0)

    def only(array, head_of, j):
        return jnp.where(head_of == j, array.astype(F32), 0.0).astype(BF)

    def attend_group(g, _):
        lanes = pl.ds(pl.multiple_of(g * LANES, LANES), LANES)
        keys, query = k_ref[:, lanes], q_ref[:, lanes]
        values_t = v_ref[:, lanes].T
        for j in range(per):
            scores = right_t(keys, only(query, lane_head, j)) * factor + bias_ref[...]
            top = jnp.max(scores, 0, keepdims=True)
            probs = jnp.exp(scores - top)
            total = jnp.sum(probs, 0, keepdims=True)
            probs = (probs * (1.0 / total)).astype(BF)
            rows = slice(j * size, (j + 1) * size)
            mixed_t[g, rows, :] = matmul(values_t[rows, :], probs).astype(BF)
            lse_ref[g, j : j + 1, :] = top + jnp.log(total)
        mixed_ref[:, lanes] = mixed_t[g].T
        return 0

    lax.fori_loop(0, DD // LANES, attend_group, 0)

    pixels = stats_ref[6:7, :] * (PATCH * PATCH)
    flagged = stats_ref[7:8, 0:1]

    def follow(n, _):
        rows, all_rows = hidden_rows(n)
        middle = y_ref[all_rows, :] + matmul(mixed_ref[rows, :], wide_ref[:, 3 * DD : 4 * DD])
        unit_b, rate_b = normalize(middle)
        b = (unit_b * gain_two).astype(BF)
        b_ref[rows, :] = b
        after, slope = gelu_parts(matmul(b, wide_ref[:, 4 * DD : 4 * DD + DFF]))
        hidden_ref[rows, :] = after.astype(BF)
        unit_z, rate_z = normalize(middle + matmul(hidden_ref[rows, :], down_ref[...]))
        z = (unit_z * gain_out).astype(BF)
        z_ref[rows, :] = z
        pred = matmul(z, head_ref[...])
        parts = []
        for part in range(PD // LANES):
            band = part * LANES // (PATCH * PATCH)
            mean = stats_ref[band : band + 1, :] / pixels
            var = stats_ref[BANDS + band : BANDS + band + 1, :] / pixels - mean * mean
            lanes = slice(part * LANES, (part + 1) * LANES)
            parts.append((picked_ref[rows, lanes] - mean) * lax.rsqrt(var + EPS))
        normed = jnp.concatenate(parts, 1)
        coarse = exact_product(normed, pool_ref[...])
        err_high = pred[:, :PD] - (normed - exact_product(coarse, spread_ref[...]))
        err_low = pred[:, PD:] - coarse
        flag = column_ref[all_rows, 0:1]
        length = jnp.sqrt(err_high * err_high + 1.0)
        loss_ref[:, :PD] += jnp.sum((length - 1.0) * flag, 0, keepdims=True) * (1.0 / PD)
        loss_ref[:, PD:] += jnp.sum(err_low * err_low * flag, 0, keepdims=True) * (1.0 / LOWD)
        share = flag / flagged
        dpred_ref[rows, :PD] = (err_high / length * (share * (1.0 / PD))).astype(BF)
        dpred_ref[rows, PD:] = (err_low * (share * (2.0 / LOWD))).astype(BF)
        dz = right_t(dpred_ref[rows, :], head_ref[...])
        dend, dgain = normalize_back(unit_z, rate_z, gain_out, dz)
        vec_ref[2:3, :] += dgain
        dbranch_ref[rows, :] = dend.astype(BF)
        dhidden = right_t(dbranch_ref[rows, :], down_ref[...])
        dbefore_ref[rows, :] = (dhidden * slope).astype(BF)
        db = right_t(dbefore_ref[rows, :], wide_ref[:, 4 * DD : 4 * DD + DFF])
        dmiddle, dgain = normalize_back(unit_b, rate_b, gain_two, db)
        vec_ref[1:2, :] += dgain
        dmiddle = dmiddle + dend
        dmiddle_ref[rows, :] = dmiddle
        dattn_ref[rows, :] = dmiddle.astype(BF)
        dmixed = right_t(dattn_ref[rows, :], wide_ref[:, 3 * DD : 4 * DD])
        dmixed_ref[rows, :] = dmixed.astype(BF)
        return 0

    lax.fori_loop(0, 2, follow, 0)

    rows = DD // owners

    def store(block, grad):
        grads_ref[:, block] = grad.astype(BF).reshape(owners, rows, UNIT)

    parts = DFF // DD
    down_grad = left_t(hidden_ref[...], dbranch_ref[...]).astype(BF)
    down_grad = down_grad.reshape(owners, parts, rows, UNIT)
    for part in range(parts):
        grads_ref[:, part] = down_grad[:, part]
    store(
        parts + 3,
        jnp.concatenate([matmul(mixed_t[g], dattn_ref[...]) for g in range(DD // LANES)], 0),
    )
    for n in range(DFF // UNIT):
        store(parts + 4 + n, left_t(b_ref[...], dbefore_ref[:, n * UNIT : (n + 1) * UNIT]))
    for n in range(HEADP // UNIT):
        store(parts + 8 + n, left_t(z_ref[...], dpred_ref[:, n * UNIT : (n + 1) * UNIT]))

    def attend_back_group(g, _):
        lanes = pl.ds(pl.multiple_of(g * LANES, LANES), LANES)
        query, keys, values, dout = [r[:, lanes] for r in (q_ref, k_ref, v_ref, dmixed_ref)]
        keys_t = keys.T
        dkeys = jnp.zeros((TOK_DEV, LANES), F32)
        dvalues = jnp.zeros((TOK_DEV, LANES), F32)
        dquery = []
        for j in range(per):
            scores = right_t(keys, only(query, lane_head, j)) * factor + bias_ref[...]
            probs = jnp.exp(scores - lse_ref[g, j : j + 1, :])
            dvalues = jnp.where(key_head == j, matmul(probs.astype(BF), dout), dvalues)
            dprobs = right_t(values, only(dout, lane_head, j))
            delta = jnp.sum(dprobs * probs, 0, keepdims=True)
            dscores = (probs * (dprobs - delta)).astype(BF)
            dkeys = jnp.where(key_head == j, matmul(dscores, query), dkeys)
            dquery.append(matmul(keys_t[j * size : (j + 1) * size, :], dscores))
        dq_ref[:, lanes] = (jnp.concatenate(dquery, 0) * factor).astype(BF).T
        dk_ref[:, lanes] = (dkeys * factor).astype(BF)
        dv_ref[:, lanes] = dvalues.astype(BF)
        return 0

    lax.fori_loop(0, DD // LANES, attend_back_group, 0)

    store(parts, left_t(a_ref[VIS:, :], dq_ref[...]))
    store(parts + 1, left_t(a_ref[...], dk_ref[...]))
    store(parts + 2, left_t(a_ref[...], dv_ref[...]))

    def start_rows(rows, da):
        unit, rate = normalize(y_ref[rows, :])
        da = da + right_t(dk_ref[rows, :], wide_ref[:, DD : 2 * DD])
        da = da + right_t(dv_ref[rows, :], wide_ref[:, 2 * DD : 3 * DD])
        dh, dgain = normalize_back(unit, rate, gain_one, da)
        vec_ref[0:1, :] += dgain
        return dh

    dy = start_rows(slice(0, VIS), 0.0)
    dy_ref[...] = dy
    vec_ref[3:4, :] += jnp.sum(jnp.where(kept, 0.0, dy), 0, keepdims=True)

    def start_hidden(n, _):
        rows, all_rows = hidden_rows(n)
        dy = start_rows(all_rows, right_t(dq_ref[rows, :], wide_ref[:, :DD]))
        vec_ref[3:4, :] += jnp.sum(dy + dmiddle_ref[rows, :], 0, keepdims=True)
        return 0

    lax.fori_loop(0, 2, start_hidden, 0)
    vec_out[...] = jnp.zeros_like(vec_out)
    for n in range(4):
        vec_out[3 + n // 2 : 4 + n // 2, n % 2 * DD : (n % 2 + 1) * DD] = vec_ref[n : n + 1, :]
    vec_out[5:6, :] = jnp.broadcast_to(jnp.sum(loss_ref[...], 1, keepdims=True), (1, D))


def decoder_step(pos, seen, by_row, by_column, picked, stats, vectors, wide, down):
    owners = lax.axis_size("fsdp")
    scratch = [
        ((TOK_DEV, DD), F32),
        ((TOK_DEV, DD), BF),
        ((HID, DD), BF),
        ((TOK_DEV, DD), BF),
        ((TOK_DEV, DD), BF),
        ((DD // LANES, LANES, HID), BF),
        ((HID, DD), BF),
        ((DD // LANES, LANES * DHEADS // DD, HID), F32),
        ((DD, HEADP), BF),
        ((HID, DD), BF),
        ((HID, DFF), BF),
        ((HID, DD), BF),
        ((HID, HEADP), BF),
        ((HID, DD), BF),
        ((HID, DFF), BF),
        ((HID, DD), BF),
        ((HID, DD), BF),
        ((HID, DD), F32),
        ((HID, DD), BF),
        ((TOK_DEV, DD), BF),
        ((TOK_DEV, DD), BF),
        ((1, HEADP), F32),
        ((TOK_DEV, HID), F32),
        ((PD, LOWP), BF),
        ((LOWP, PD), BF),
        ((8, DD), F32),
    ]
    vmem = pl.BlockSpec(memory_space=pltpu.VMEM)
    grads, dy, vec = pl.pallas_call(
        partial(decoder_kernel, owners),
        out_shape=(
            jax.ShapeDtypeStruct((owners, DFF // DD + 10, DD // owners, UNIT), BF),
            jax.ShapeDtypeStruct((VIS, DD), F32),
            jax.ShapeDtypeStruct((8, D), F32),
        ),
        in_specs=[vmem] * 9,
        out_specs=(vmem,) * 3,
        scratch_shapes=[pltpu.VMEM(*entry) for entry in scratch],
        compiler_params=pltpu.CompilerParams(vmem_limit_bytes=60 * 2**20),
        cost_estimate=pl.CostEstimate(
            flops=40 * 10**9, bytes_accessed=40 * 2**20, transcendentals=2 * 10**7
        ),
    )(
        pos,
        seen,
        by_row,
        by_column,
        picked,
        stats,
        vectors,
        wide,
        down,
    )
    return grads, dy, vec


def block_forward(h, weights, gains, bias, heads, skip):
    wqkv, wout, wup, wdown = weights
    width = h.shape[1]
    normed_a = layer_norm(h, gains[0]).astype(BF)
    query = matmul(normed_a[skip:], wqkv[:, :width]).astype(BF)
    keys = matmul(normed_a, wqkv[:, width : 2 * width]).astype(BF)
    values = matmul(normed_a, wqkv[:, 2 * width :]).astype(BF)
    mixed_t, lse = attend(query.T, keys, values.T, bias, width // heads)
    middle = h[skip:] + left_t(mixed_t, wout)
    normed_b = layer_norm(middle, gains[1]).astype(BF)
    after, slope = gelu_parts(matmul(normed_b, wup))
    hidden = after.astype(BF)
    end = middle + matmul(hidden, wdown)
    return end, (h, normed_a, query, keys, values, mixed_t, lse, middle, normed_b, slope, hidden)


def block_backward(saved, grad, weights, gains, bias, heads, skip):
    wqkv, wout, wup, wdown = weights
    h, normed_a, query, keys, values, mixed_t, lse, middle, normed_b, slope, hidden = saved
    width = h.shape[1]
    dbranch = grad.astype(BF)
    dbefore = (right_t(dbranch, wdown) * slope).astype(BF)
    dmiddle, dgain_two = norm_back(middle, gains[1], right_t(dbefore, wup))
    dmiddle = dmiddle + grad
    dattn = dmiddle.astype(BF)
    dmixed = right_t(dattn, wout).astype(BF)
    dqt, dkeys, dvalues = attend_back(query, keys, values, dmixed, bias, lse, width // heads)
    dquery = dqt.T
    if skip:
        dquery = jnp.pad(dquery, ((skip, 0), (0, 0)))
        dmiddle = jnp.pad(dmiddle, ((skip, 0), (0, 0)))
    dqkv = jnp.concatenate([dquery, dkeys, dvalues], 1)
    dh, dgain_one = norm_back(h, gains[0], right_t(dqkv, wqkv))
    factors = ((normed_a.T, dqkv), (mixed_t, dattn), (normed_b.T, dbefore), (hidden.T, dbranch))
    return (dh + dmiddle, factors, (dgain_one, dgain_two))


def reduce_rows(grad):
    return lax.psum_scatter(grad.astype(BF), "fsdp", scatter_dimension=0, tiled=True)


def enc_split(wide, down):
    return (
        (wide[:, : 3 * D], wide[:, 3 * D : 4 * D], wide[:, 4 * D : 4 * D + FF], down),
        wide[:, 4 * D + FF :],
    )


def advance(weight, mom, avg, grad, rate):
    grad = grad + DECAY * weight
    buf = MOMENTUM * mom + grad
    new = weight - rate * (grad + MOMENTUM * buf)
    return (buf, new, AVERAGE * avg + (1.0 - AVERAGE) * new)


def advance_kernel(rate, *refs):
    grads, weights, moms, avgs, outs = [refs[5 * n : 5 * n + 5] for n in range(4)] + [refs[20:]]

    def update(n):
        weight = weights[n][...]
        grad = grads[n][:, : weight.shape[1]].astype(F32)
        buf, new, avg = advance(weight, moms[n][...], avgs[n][...], grad, rate)
        outs[4 * n][...] = buf
        outs[4 * n + 1][...] = new
        outs[4 * n + 2][...] = avg
        outs[4 * n + 3][...] = new.astype(BF)

    pl.when(pl.program_id(0) == 0)(partial(update, 0))
    for n in range(1, 5):
        update(n)


def advance_all(rate, grads, weights, moms, avgs):
    steps = weights[3].shape[0] // 16

    def spec(n, array):
        if n == 0:
            return pl.BlockSpec(array.shape, lambda i: (0, 0))
        return pl.BlockSpec((array.shape[0] // steps, array.shape[1]), lambda i: (i, 0))

    arrays = [a for group in (grads, weights, moms, avgs) for a in group]
    outs = [(n, jax.ShapeDtypeStruct(w.shape, t)) for n, w in enumerate(weights) for t in (F32, F32, F32, BF)]
    size = sum(w.size for w in weights)
    return pl.pallas_call(
        partial(advance_kernel, rate),
        grid=(steps,),
        out_shape=[out for _, out in outs],
        in_specs=[spec(n % 5, a) for n, a in enumerate(arrays)],
        out_specs=[spec(n, out) for n, out in outs],
        compiler_params=pltpu.CompilerParams(vmem_limit_bytes=58 * 2**20),
        cost_estimate=pl.CostEstimate(flops=12 * size, bytes_accessed=28 * size, transcendentals=0),
    )(*arrays)


def arrange(valid, masked, scene_ids):
    slots = valid.shape[0]
    live = valid > 0
    kinds = jnp.stack([live & (masked == 0), live & (masked > 0), ~live], 1)
    index = jnp.arange(slots, dtype=jnp.int32)
    ranks = matmul((index[None, :] < index[:, None]).astype(BF), kinds.astype(BF)).astype(jnp.int32)
    n_seen, n_hid = [jnp.sum(kinds[:, i].astype(jnp.int32)) for i in range(2)]
    empty = ranks[:, 2]
    to_empty = jnp.where(empty < VIS - n_seen, n_seen + empty, n_seen + n_hid + empty)
    place = jnp.where(
        kinds[:, 0], ranks[:, 0], jnp.where(kinds[:, 1], VIS + ranks[:, 1], to_empty)
    )
    return (place[None, :] == index[:, None]).astype(BF), n_seen, n_hid


def exact_pick(pick, array):
    high = lax.reduce_precision(array, 8, 7)
    rest = array - high
    mid = lax.reduce_precision(rest, 8, 7)
    low = rest - mid
    return (
        matmul(pick, high.astype(BF)) + matmul(pick, mid.astype(BF)) + matmul(pick, low.astype(BF))
    )


def body(
    pixels,
    masked,
    valid,
    scene_ids,
    gsd_index,
    coords,
    embed,
    wide_enc,
    enc_down,
    wide_dec,
    dec_down,
    vectors,
    embed_mom,
    wide_enc_mom,
    enc_down_mom,
    wide_dec_mom,
    dec_down_mom,
    vector_mom,
    embed_avg,
    wide_enc_avg,
    enc_down_avg,
    wide_dec_avg,
    dec_down_avg,
    vector_avg,
):
    slots = pixels.shape[0]
    fast = (lax.axis_size("dp"), lax.axis_size("fsdp")) == (4, 8)
    vector_row = vectors.reshape(1, -1)
    levels = jnp.exp2(0.5 * gsd_index.astype(jnp.float32) - 1.0)
    gains_enc = (vectors[:D], vectors[D : 2 * D])
    gain_enc_out = vectors[2 * D : 3 * D]
    if fast:
        facts = jnp.stack([valid, masked, scene_ids % 2, coords[:, 0], coords[:, 1]])
        facts = jnp.pad(facts, ((0, 3), (0, 0))).astype(F32)
        scale = jnp.pad(jnp.broadcast_to(levels[:, None], (2, LANES)), ((0, 6), (0, 0)))
        w_enc, w_enc_down, w_dec, w_dec_down, picked_hidden, slope, *saved = encoder_forward(
            pixels, facts, scale, vector_row, embed, wide_enc, enc_down, wide_dec, dec_down
        )
        stats, by_row, by_column, pos_dec, bias_enc, *saved = saved
        *factors, h_start, qkv, middle, h_end, seen_out = saved
    else:
        rows_ok = valid.astype(jnp.float32)
        flags = rows_ok * masked.astype(jnp.float32)
        bands = pixels.reshape(slots, BANDS, PATCH * PATCH)
        weighted = bands * rows_ok[:, None, None]
        band_sum = jnp.sum(weighted, axis=(0, 2))
        counts = jnp.stack([jnp.sum(rows_ok), jnp.sum(flags)])
        band_sq = jnp.sum(weighted * bands, axis=(0, 2))
        stats = jnp.concatenate([band_sum, band_sq, counts])
        stats = jnp.broadcast_to(lax.psum(stats, ("dp", "fsdp"))[:, None], (8, LANES))
        pick, n_seen, n_hid = arrange(valid, masked, scene_ids)
        picked_pixels = exact_pick(pick, pixels)
        picked_hidden = picked_pixels[VIS:]
        small = matmul(pick, jnp.concatenate([(scene_ids % 2)[:, None], coords], 1).astype(BF))
        odd, coord = small[:, 0], small[:, 1:]
        scale = jnp.where(odd == 0, levels[0], levels[1])
        index = jnp.arange(slots, dtype=jnp.int32)
        live = jnp.concatenate([index[:VIS] < n_seen, index[:HID] < n_hid])
        allow = live[:, None] & (odd[:, None] == odd[None, :]) | (index[:, None] == index[None, :])
        bias_enc = jnp.where(allow, 0.0, NEGATIVE)[:VIS, :VIS]
        by_row = jnp.pad(jnp.stack([live.astype(F32), odd, odd]), ((0, 5), (0, 0)))
        by_column = by_row.T
        pos_dec = positions(coord, scale, DD)
    count = stats[7, 0]
    if not fast:
        w_embed, w_enc, w_enc_down, w_dec, w_dec_down = [
            lax.all_gather(w.astype(BF), "fsdp", axis=0, tiled=True)
            for w in (embed, wide_enc, enc_down, wide_dec, dec_down)
        ]
        enc_weights, w_link = enc_split(w_enc, w_enc_down)
        mean = jnp.repeat(stats[:3, 0] / (stats[6, 0] * (PATCH * PATCH)), PATCH * PATCH)
        square = jnp.repeat(stats[3:6, 0] / (stats[6, 0] * (PATCH * PATCH)), PATCH * PATCH)
        rate = lax.rsqrt(square - mean * mean + EPS)
        inputs = ((picked_pixels[:VIS] - mean) * rate).astype(BF)
        h_start = matmul(inputs, w_embed) + positions(coord[:VIS], scale[:VIS], D)
        h_end, enc_saved = block_forward(h_start, enc_weights, gains_enc, bias_enc, HEADS, 0)
        encoded = layer_norm(h_end, gain_enc_out).astype(BF)
        seen_out = matmul(encoded, w_link)
    dec_grads, dy_seen, vec = decoder_step(
        pos_dec,
        seen_out,
        by_row,
        by_column,
        picked_hidden,
        stats,
        vector_row,
        w_dec,
        w_dec_down,
    )
    if fast:
        inputs_t, a_t, mixed_t, b_t, hidden_t, z_t = factors
        *enc_parts, dec_wide, dec_tall, vec = encoder_back(
            dy_seen,
            by_column,
            vec,
            vector_row,
            bias_enc,
            qkv,
            dec_grads,
            (h_end, middle, h_start, slope),
            w_enc,
            w_enc_down,
            (z_t, hidden_t, b_t, mixed_t, a_t, inputs_t),
        )
        dec_parts = (dec_wide, dec_tall)
        vector_grad, loss_sum = vec[:5].reshape(-1), vec[5, 0]
    else:
        dseen = (dy_seen * by_column[:VIS, 0:1]).astype(BF)
        dec_vec, local_loss = vec[3:5].reshape(-1), vec[5, 0]
        dh_end, dgain_enc_out = norm_back(h_end, gain_enc_out, right_t(dseen, w_link))
        dh_start, enc_factors, dgains_enc = block_backward(
            enc_saved, dh_end, enc_weights, gains_enc, bias_enc, HEADS, 0
        )
        enc_grads = [matmul(*pair).astype(BF) for pair in enc_factors]
        link_grad = left_t(encoded, dseen).astype(BF)
        enc_parts = lax.psum(
            (
                reduce_rows(left_t(inputs, dh_start.astype(BF))),
                reduce_rows(
                    jnp.concatenate([enc_grads[0], enc_grads[1], enc_grads[2], link_grad], 1)
                ),
                reduce_rows(enc_grads[3]),
            ),
            "dp",
        )
        dec_sum = lax.psum(reduce_rows(dec_grads), "dp")[0]
        rows, parts = dec_sum.shape[1], DFF // DD
        dec_parts = (
            dec_sum[parts:].transpose(1, 0, 2).reshape(rows, -1),
            dec_sum[:parts].reshape(-1, DD),
        )
        vector_grad = jnp.concatenate([*dgains_enc, dgain_enc_out, dec_vec])
        vector_grad, loss_sum = lax.psum((vector_grad, local_loss), ("dp", "fsdp"))
    grads = (*enc_parts, *dec_parts)
    rate = STEP_UNIT * (PD * TOK_DEV * lax.axis_size("dp") * lax.axis_size("fsdp")) ** 0.5
    weights = (embed, wide_enc, enc_down, wide_dec, dec_down)
    moms = (embed_mom, wide_enc_mom, enc_down_mom, wide_dec_mom, dec_down_mom)
    avgs = (embed_avg, wide_enc_avg, enc_down_avg, wide_dec_avg, dec_down_avg)
    outs = advance_all(rate, grads, weights, moms, avgs)
    return (*outs, *advance(vectors, vector_mom, vector_avg, vector_grad, rate), loss_sum, count)


def solution(mesh):
    both, rows = P(("dp", "fsdp")), P("fsdp", None)
    placed = (P(("dp", "fsdp"), None), both, both, both, both, P(("dp", "fsdp"), None))
    states = (rows,) * 5 + (P(),)
    return jax.shard_map(
        body,
        mesh=mesh,
        in_specs=placed + states * 3,
        out_specs=(rows,) * 20 + (P(),) * 5,
        check_vma=False,
    )
```

```python
from functools import partial

import jax
import jax.numpy as jnp
from jax import lax
from jax.experimental import pallas as pl
from jax.experimental.pallas import tpu as pltpu
from jax.sharding import PartitionSpec as P

D = 1024
HEADS = 16
FF = 4096
DD = 512
DHEADS = 16
DFF = 2048
PATCH = 16
BANDS = 3
TOK_DEV = 768
PD = 768
LOWD = 192
VIS = 192
HID = TOK_DEV - VIS

EPS = 1e-06
MOMENTUM = 0.9
DECAY = 0.0001
AVERAGE = 0.9
STEP_UNIT = 0.003
NEGATIVE = -1e30
LANES = 128
BF = jnp.bfloat16
F32 = jnp.float32


def matmul(left, right):
    return jnp.dot(left, right, preferred_element_type=jnp.float32)


def left_t(left, right):
    return lax.dot_general(
        left, right, (((0,), (0,)), ((), ())), preferred_element_type=jnp.float32
    )


def right_t(left, right):
    return lax.dot_general(
        left, right, (((1,), (1,)), ((), ())), preferred_element_type=jnp.float32
    )


def layer_norm(h, gain):
    mean = jnp.mean(h, -1, keepdims=True)
    cent = h - mean
    var = jnp.mean(cent * cent, -1, keepdims=True)
    return cent * lax.rsqrt(var + EPS) * gain


def norm_back(h, gain, grad):
    result, pull = jax.vjp(layer_norm, h, gain)
    return pull(grad)


def gelu_parts(before):
    below = 0.5 * (1.0 + lax.erf(before * 0.5**0.5))
    slope = below + before * jnp.exp(before * before * -0.5) * (0.5 / jnp.pi) ** 0.5
    return before * below, slope


def positions(coord, scale, width):
    quarter = width // 4
    omega = 10000.0 ** (-jnp.arange(quarter, dtype=jnp.float32) / quarter)
    angle_x = coord[:, 0:1] * scale[:, None] * omega[None, :]
    angle_y = coord[:, 1:2] * scale[:, None] * omega[None, :]
    return jnp.concatenate(
        [jnp.sin(angle_x), jnp.cos(angle_x), jnp.sin(angle_y), jnp.cos(angle_y)], -1
    )


def row_loss(pred, normed):
    rows = normed.shape[0]
    coarse = jnp.mean(normed.reshape(rows, BANDS, PATCH // 2, 2, PATCH // 2, 2), axis=(3, 5))
    upper = jnp.repeat(jnp.repeat(coarse, 2, axis=2), 2, axis=3).reshape(rows, PD)
    err_high = pred[:, :PD] - (normed - upper)
    err_low = pred[:, PD:] - coarse.reshape(rows, LOWD)
    return jnp.mean(jnp.sqrt(err_high * err_high + 1.0) - 1.0, -1) + jnp.mean(err_low * err_low, -1)


def attend_kernel(size, qt_ref, k_ref, vt_ref, bias_ref, ot_ref, lse_ref):
    per = LANES // size
    row_head = lax.broadcasted_iota(jnp.int32, qt_ref.shape, 0) // size
    factor = size ** (-0.5)
    for j in range(per):
        query = jnp.where(row_head == j, qt_ref[...].astype(F32), 0.0).astype(BF)
        scores = matmul(k_ref[...], query) * factor + bias_ref[...]
        top = jnp.max(scores, 0, keepdims=True)
        probs = jnp.exp(scores - top)
        total = jnp.sum(probs, 0, keepdims=True)
        probs = (probs * (1.0 / total)).astype(BF)
        rows = slice(j * size, (j + 1) * size)
        ot_ref[rows, :] = matmul(vt_ref[rows, :], probs).astype(BF)
        lse_ref[0, j : j + 1, :] = top + jnp.log(total)


def attend(qt, keys, vt, bias, size):
    width, queries = qt.shape
    rows = keys.shape[0]
    groups, per = width // LANES, LANES // size
    return pl.pallas_call(
        partial(attend_kernel, size),
        grid=(groups,),
        out_shape=(
            jax.ShapeDtypeStruct((width, queries), BF),
            jax.ShapeDtypeStruct((groups, per, queries), F32),
        ),
        in_specs=[
            pl.BlockSpec((LANES, queries), lambda g: (g, 0)),
            pl.BlockSpec((rows, LANES), lambda g: (0, g)),
            pl.BlockSpec((LANES, rows), lambda g: (g, 0)),
            pl.BlockSpec((rows, queries), lambda g: (0, 0)),
        ],
        out_specs=(
            pl.BlockSpec((LANES, queries), lambda g: (g, 0)),
            pl.BlockSpec((1, per, queries), lambda g: (g, 0, 0)),
        ),
        compiler_params=pltpu.CompilerParams(vmem_limit_bytes=40 * 2**20),
        cost_estimate=pl.CostEstimate(
            flops=4 * rows * queries * width * per,
            bytes_accessed=4 * rows * queries,
            transcendentals=rows * queries * width // size,
        ),
    )(qt, keys, vt, bias)


def attend_back_kernel(
    size,
    qt_ref,
    q_ref,
    k_ref,
    kt_ref,
    v_ref,
    do_ref,
    dot_ref,
    bias_ref,
    *rest,
):
    *lse_ref, dqt_ref, dk_ref, dv_ref = rest
    per = LANES // size
    row_head = lax.broadcasted_iota(jnp.int32, qt_ref.shape, 0) // size
    lane_head = lax.broadcasted_iota(jnp.int32, dk_ref.shape, 1) // size
    factor = size ** (-0.5)
    dkeys = jnp.zeros(dk_ref.shape, F32)
    dvalues = jnp.zeros(dv_ref.shape, F32)
    for j in range(per):
        query = jnp.where(row_head == j, qt_ref[...].astype(F32), 0.0).astype(BF)
        dout = jnp.where(row_head == j, dot_ref[...].astype(F32), 0.0).astype(BF)
        scores = matmul(k_ref[...], query) * factor + bias_ref[...]
        if lse_ref:
            probs = jnp.exp(scores - lse_ref[0][0, j : j + 1, :])
        else:
            probs = jnp.exp(scores - jnp.max(scores, 0, keepdims=True))
            probs = probs * (1.0 / jnp.sum(probs, 0, keepdims=True))
        dvalues = jnp.where(lane_head == j, matmul(probs.astype(BF), do_ref[...]), dvalues)
        dprobs = matmul(v_ref[...], dout)
        delta = jnp.sum(dprobs * probs, 0, keepdims=True)
        dscores = (probs * (dprobs - delta)).astype(BF)
        dkeys = jnp.where(lane_head == j, matmul(dscores, q_ref[...]), dkeys)
        rows = slice(j * size, (j + 1) * size)
        dqt_ref[rows, :] = (matmul(kt_ref[rows, :], dscores) * factor).astype(BF)
    dk_ref[...] = (dkeys * factor).astype(BF)
    dv_ref[...] = dvalues.astype(BF)


def attend_back(query, keys, values, dmixed, bias, lse, size):
    queries, width = query.shape
    rows = keys.shape[0]
    groups, per = width // LANES, LANES // size
    tall = lambda n: pl.BlockSpec((n, LANES), lambda g: (0, g))
    flat = lambda n: pl.BlockSpec((LANES, n), lambda g: (g, 0))
    return pl.pallas_call(
        partial(attend_back_kernel, size),
        grid=(groups,),
        out_shape=(
            jax.ShapeDtypeStruct((width, queries), BF),
            jax.ShapeDtypeStruct((rows, width), BF),
            jax.ShapeDtypeStruct((rows, width), BF),
        ),
        in_specs=[
            flat(queries),
            tall(queries),
            tall(rows),
            flat(rows),
            tall(rows),
            tall(queries),
            flat(queries),
            pl.BlockSpec((rows, queries), lambda g: (0, 0)),
        ]
        + [pl.BlockSpec((1, per, queries), lambda g: (g, 0, 0))] * (lse is not None),
        out_specs=(flat(queries), tall(rows), tall(rows)),
        compiler_params=pltpu.CompilerParams(vmem_limit_bytes=48 * 2**20),
        cost_estimate=pl.CostEstimate(
            flops=10 * rows * queries * width * per,
            bytes_accessed=4 * rows * queries,
            transcendentals=rows * queries * width // size,
        ),
    )(query.T, query, keys, keys.T, values, dmixed, dmixed.T, bias, *([] if lse is None else [lse]))


MESH = pl.DeviceIdType.MESH
UNIT = 512
HALF = UNIT // 2
ROWS = 128
HALF_ROWS = ROWS // 2
LAGS = (1, 3, 4, 6, 9)


def put(source, target, send, recv, device):
    return pltpu.make_async_remote_copy(
        src_ref=source,
        dst_ref=target,
        send_sem=send,
        recv_sem=recv,
        device_id=device,
        device_id_type=MESH,
    )


def back_kernel(
    dec_units,
    blocks,
    units,
    spots,
    dy_ref,
    column_ref,
    vec_ref,
    vectors_ref,
    bias_ref,
    qkv_ref,
    ready_ref,
    dec_ref,
    end_ref,
    middle_ref,
    start_ref,
    slope_ref,
    wide_ref,
    down_ref,
    *refs,
):
    n_left = max(b[0] for b in blocks) + 1
    lefts, refs = refs[:n_left], refs[n_left:]
    outs, refs = refs[:5], refs[5:]
    vec_out, refs = refs[0], refs[1:]
    (
        xo,
        xp,
        yo,
        yp,
        do,
        dp,
        a_out,
        a_in,
        b_out,
        b_in,
        sums,
        z_out,
        z_one,
        z_two,
        z_ready,
        v_in,
        v_out,
        wide_buf,
        down_buf,
        slope_buf,
        h_buf,
        dend_ref,
        dmid_ref,
        dbranch_ref,
        dmixed_ref,
        dqkv_ref,
        grad_vec,
        wide_sem,
        down_sem,
        slope_sem,
        h_sem,
        dec_sem,
        left_sem,
        right_sem,
        a_send,
        a_recv,
        b_send,
        b_recv,
        z_send,
        z_recv,
        v_send,
        v_recv,
        store_sem,
    ) = refs
    count, extra = dec_units + len(units), z_ready.shape[0]
    z, f = lax.axis_index("dp"), lax.axis_index("fsdp")
    core, place = f % 2, f // 2
    x, y = place % 2, place // 2
    partner = (z, f + 1 - 2 * core)
    x_side = (z, f + 2 - 4 * x)
    y_side = (z, f + 4 - 8 * y)
    at_x, at_y, at_far = place + 1 - 2 * x, place + 2 - 4 * y, 3 - place
    low = z < 2
    outer = (z == 0) | (z == 3)
    inner = (z == 1) | (z == 2)
    inward = (jnp.where(low, 1, 2), f)
    across = (3 - z, f)
    outward = (jnp.where(low, 0, 3), f)

    ring = wide_buf.shape[0]
    up_chunks, out_chunks, qkv_chunks = FF // UNIT, D // UNIT, 3 * D // UNIT
    chunks = 1 + up_chunks + out_chunks + qkv_chunks

    def wide_copy(w):
        inside = jnp.where(w < 1 + up_chunks, 4 * D + UNIT * (w - 1), 3 * D + UNIT * (w - 1 - up_chunks))
        column = jnp.where(
            w == 0,
            4 * D + FF,
            jnp.where(w < 1 + up_chunks + out_chunks, inside, UNIT * (w - 1 - up_chunks - out_chunks)),
        )
        return pltpu.make_async_copy(
            wide_ref.at[:, pl.ds(pl.multiple_of(column, UNIT), UNIT)],
            wide_buf.at[w % ring],
            wide_sem.at[w % ring],
        )

    def down_copy(j):
        rows = pl.ds(pl.multiple_of(j * UNIT, UNIT), UNIT)
        return pltpu.make_async_copy(down_ref.at[rows], down_buf.at[j % 2], down_sem.at[j % 2])

    def slope_copy(j):
        columns = pl.ds(pl.multiple_of(j * UNIT, UNIT), UNIT)
        return pltpu.make_async_copy(slope_ref.at[:, columns], slope_buf.at[j % 2], slope_sem.at[j % 2])

    def h_copy(source):
        return pltpu.make_async_copy(source, h_buf, h_sem.at[0])

    h_copy(end_ref).start()
    for n in range(ring):
        wide_copy(n).start()
    for n in range(2):
        down_copy(n).start()
        slope_copy(n).start()

    barrier = pltpu.get_barrier_semaphore()
    for device in (partner, x_side, y_side):
        pl.semaphore_signal(barrier, inc=1, device_id=device, device_id_type=MESH)

    @pl.when(outer)
    def _():
        pl.semaphore_signal(barrier, inc=1, device_id=inward, device_id_type=MESH)
        pl.semaphore_wait(barrier, 4)

    @pl.when(inner)
    def _():
        pl.semaphore_signal(barrier, inc=1, device_id=across, device_id_type=MESH)
        pl.semaphore_signal(barrier, inc=1, device_id=outward, device_id_type=MESH)
        pl.semaphore_wait(barrier, 5)

    def swap_dec(source, n):
        return put(source, dp.at[n], dec_sem.at[n, 1], dec_sem.at[n, 2], partner)

    def swap_left(source, b):
        return put(source, xp.at[b], left_sem.at[b, 1], left_sem.at[b, 2], partner)

    def swap_right(r):
        return put(yo.at[r], yp.at[r], right_sem.at[r, 0], right_sem.at[r, 1], partner)

    for n in range(dec_units):
        swap_dec(dec_ref.at[:, 1 - core, n], n).start()
        pltpu.make_async_copy(dec_ref.at[:, core, n], do.at[n], dec_sem.at[n, 0]).start()
    for b, (left, sub) in enumerate(blocks):
        rows = pl.ds(sub * ROWS, ROWS)
        swap_left(lefts[left].at[:, 1 - core, rows], b).start()
        pltpu.make_async_copy(lefts[left].at[:, core, rows], xo.at[b], left_sem.at[b, 0]).start()

    firsts = 1 + out_chunks
    single = next(n for n in range(1, len(units)) if units[n][1] >= firsts)
    starts = [n for n in range(1, len(units)) if units[n][0] != units[n - 1][0]]

    def block_of(e):
        return sum([jnp.where(e >= n, 1, 0) for n in starts], jnp.int32(0))

    def right_of(e):
        early = jnp.where(e == 0, 0, 1 + (e + out_chunks - 1) % out_chunks)
        return jnp.where(e < single, early, e - single + firsts)

    first, second = pl.ds(0, HALF), pl.ds(HALF, HALF)

    def ready_part(n, owners, columns):
        parts = [do[n, o, :, columns].astype(F32) + dp[n, o, :, columns].astype(F32) for o in owners]
        return parts[0] if len(parts) == 1 else jnp.concatenate(parts, 0)

    def formed_part(e, owners, columns):
        b, r = block_of(e), right_of(e)
        mine, other = [jnp.concatenate([ref[b, o] for o in owners], 0) for ref in (xo, xp)]
        return matmul(mine, yo[r, :, columns]) + matmul(other, yp[r, :, columns])

    def on_unit(u, stage):
        @pl.when(u < dec_units)
        def _():
            stage(partial(ready_part, jnp.minimum(u, dec_units - 1)))

        @pl.when(u >= dec_units)
        def _():
            stage(partial(formed_part, jnp.maximum(u - dec_units, 0)))

    def copy_a(u, side):
        slot = u % a_out.shape[0]
        return put(
            a_out.at[slot, side],
            a_in.at[u, side],
            a_send.at[slot, side],
            a_recv.at[u, side],
            (x_side, y_side)[side],
        )

    def copy_b(u, side):
        slot = u % b_out.shape[0]
        return put(
            b_out.at[slot, side],
            b_in.at[u, side],
            b_send.at[slot, side],
            b_recv.at[u, side],
            (y_side, x_side)[side],
        )

    z_slots = z_out.shape[0]

    def copy_in(u):
        return put(z_out.at[u % z_slots], z_one.at[u], z_send.at[u, 0], z_recv.at[u, 0], inward)

    def copy_across(u):
        return put(z_out.at[u % z_slots], z_two.at[u], z_send.at[u, 0], z_recv.at[u, 1], across)

    def copy_out(u):
        return put(z_one.at[u], z_one.at[u], z_send.at[u, 1], z_recv.at[u, 0], outward)

    def ready_in(n):
        u = count + n
        return put(z_ready.at[n], z_one.at[u], z_send.at[u, 0], z_recv.at[u, 0], inward)

    def ready_across(n):
        u = count + n
        return put(z_ready.at[n], z_two.at[u], z_send.at[u, 0], z_recv.at[u, 1], across)

    def copy_v(step, device):
        return put(v_out.at[step], v_in.at[step], v_send.at[step], v_recv.at[step], device)

    gain_one, gain_two, gain_out = [vectors_ref[:, n * D : (n + 1) * D] for n in range(3)]

    def give(r, value):
        yo[r] = value
        swap_right(r).start()

    def columns_at(n):
        return slice(n * UNIT, (n + 1) * UNIT)

    def back_link():
        dseen = jnp.where(column_ref[:VIS, 0:1] > 0, dy_ref[...], 0.0).astype(BF)
        give(0, dseen)
        wide_copy(0).wait()
        h_copy(end_ref).wait()
        unit, rate = normalize(h_buf[...])
        dend, dgain = normalize_back(unit, rate, gain_out, right_t(dseen, wide_buf[0]))
        grad_vec[...] = vec_ref[...]
        grad_vec[2:3, :] = dgain
        dend_ref[...] = dend
        dbranch_ref[...] = dend.astype(BF)
        for n in range(out_chunks):
            give(1 + n, dbranch_ref[:, columns_at(n)])
        wide_copy(ring).start()
        h_copy(middle_ref).start()
        dmid_ref[...] = jnp.zeros_like(dmid_ref)

    def back_hidden(j):
        w = 1 + j
        down_copy(j).wait()
        slope_copy(j).wait()
        wide_copy(w).wait()
        dhidden = right_t(dbranch_ref[...], down_buf[j % 2])
        dbefore = (dhidden * slope_buf[j % 2]).astype(BF)
        give(firsts + j, dbefore)
        dmid_ref[...] += right_t(dbefore, wide_buf[w % ring])
        wide_copy(w + ring).start()

        @pl.when(j + 2 < up_chunks)
        def _():
            down_copy(j + 2).start()
            slope_copy(j + 2).start()

    def back_out():
        h_copy(middle_ref).wait()
        unit, rate = normalize(h_buf[...])
        dmiddle, dgain = normalize_back(unit, rate, gain_two, dmid_ref[...])
        grad_vec[1:2, :] = dgain
        dmiddle = dmiddle + dend_ref[...]
        dend_ref[...] = dmiddle
        dattn = dmiddle.astype(BF)
        dmixed = jnp.zeros((VIS, D), F32)
        for n in range(out_chunks):
            w = 1 + up_chunks + n
            piece = dattn[:, columns_at(n)]
            give(firsts + up_chunks + n, piece)
            wide_copy(w).wait()
            dmixed = dmixed + right_t(piece, wide_buf[w % ring])
            wide_copy(w + ring).start()
        dmixed_ref[...] = dmixed.astype(BF)
        h_copy(start_ref).start()
        dmid_ref[...] = jnp.zeros_like(dmid_ref)

    size = D // HEADS
    lane_head = lax.broadcasted_iota(jnp.int32, (VIS, LANES), 1) // size

    def only(array, j):
        return jnp.where(lane_head == j, array.astype(F32), 0.0).astype(BF)

    def back_attention(g):
        at = [pl.ds(pl.multiple_of(n * D + g * LANES, LANES), LANES) for n in range(3)]
        query, keys, values = [qkv_ref[:, lanes] for lanes in at]
        dout = dmixed_ref[:, at[0]]
        keys_t = keys.T
        factor = size ** (-0.5)
        dkeys, dvalues = jnp.zeros((VIS, LANES), F32), jnp.zeros((VIS, LANES), F32)
        dquery = []
        for j in range(LANES // size):
            scores = right_t(keys, only(query, j)) * factor + bias_ref[...]
            probs = jnp.exp(scores - jnp.max(scores, 0, keepdims=True))
            probs = probs * (1.0 / jnp.sum(probs, 0, keepdims=True))
            dvalues = jnp.where(lane_head == j, matmul(probs.astype(BF), dout), dvalues)
            dprobs = right_t(values, only(dout, j))
            delta = jnp.sum(dprobs * probs, 0, keepdims=True)
            dscores = (probs * (dprobs - delta)).astype(BF)
            dkeys = jnp.where(lane_head == j, matmul(dscores, query), dkeys)
            dquery.append(matmul(keys_t[j * size : (j + 1) * size, :], dscores))
        dqkv_ref[:, at[0]] = (jnp.concatenate(dquery, 0) * factor).astype(BF).T
        dqkv_ref[:, at[1]] = (dkeys * factor).astype(BF)
        dqkv_ref[:, at[2]] = dvalues.astype(BF)

    def give_qkv():
        for c in range(qkv_chunks):
            give(firsts + up_chunks + out_chunks + c, dqkv_ref[:, columns_at(c)])

    def back_qkv(c):
        w = 1 + up_chunks + out_chunks + c
        wide_copy(w).wait()
        piece = dqkv_ref[:, pl.ds(pl.multiple_of(c * UNIT, UNIT), UNIT)]
        dmid_ref[...] += right_t(piece, wide_buf[w % ring])

        @pl.when(w + ring < chunks)
        def _():
            wide_copy(w + ring).start()

    def back_start():
        h_copy(start_ref).wait()
        unit, rate = normalize(h_buf[...])
        dh, dgain = normalize_back(unit, rate, gain_one, dmid_ref[...])
        grad_vec[0:1, :] = dgain
        dh = (dh + dend_ref[...]).astype(BF)
        for n in range(out_chunks):
            give(firsts + up_chunks + out_chunks + qkv_chunks + n, dh[:, columns_at(n)])

    at_hidden = 1
    at_out = at_hidden + up_chunks
    at_attention = at_out + 1
    groups = D // LANES
    at_qkv = at_attention + groups
    at_start = at_qkv + qkv_chunks
    at_vec = at_start + 1

    def step(i, _):
        def stage(lag, also=None):
            u = i - lag
            ok = (u >= 0) & (u < count)
            if also is not None:
                ok = ok & also
            return u, pl.when(ok)

        u0, when = stage(0)

        @when
        def _():
            u = u0

            @pl.when(u < dec_units)
            def _():
                pltpu.make_async_copy(do.at[u], do.at[u], dec_sem.at[u, 0]).wait()
                swap_dec(do.at[u], u).wait()

            @pl.when(u == dec_units)
            def _():
                for b in range(len(blocks)):
                    pltpu.make_async_copy(xo.at[b], xo.at[b], left_sem.at[b, 0]).wait()
                    swap_left(xo.at[b], b).wait()
                for r in range(firsts):
                    swap_right(r).wait()

            @pl.when(u >= dec_units + single)
            def _():
                swap_right(u - dec_units - single + firsts).wait()

            @pl.when(u >= a_out.shape[0])
            def _():
                for side in range(2):
                    copy_a(u - a_out.shape[0], side).wait_send()

            slot = u % a_out.shape[0]

            def send(part):
                for side, (near, columns) in enumerate(((at_x, first), (at_y, second))):
                    both = part((near, at_far), columns).astype(BF)
                    a_out[slot, side] = both.reshape(2, ROWS, HALF)

            on_unit(u, send)
            for side in range(2):
                copy_a(u, side).start()

        u1, when = stage(LAGS[0])

        @when
        def _():
            u = u1
            slot = u % b_out.shape[0]

            @pl.when(u >= b_out.shape[0])
            def _():
                for side in range(2):
                    copy_b(u - b_out.shape[0], side).wait_send()

            for side in range(2):
                copy_a(u, side).wait_recv()

            def send(part):
                for side, (near, columns) in enumerate(((at_y, first), (at_x, second))):
                    total = part((near,), columns) + a_in[u, side, 1].astype(F32)
                    b_out[slot, side] = total.astype(BF)

            on_unit(u, send)
            for side in range(2):
                copy_b(u, side).start()

        u2, when = stage(LAGS[1])

        @when
        def _():
            u = u2
            copy_b(u, 0).wait_recv()
            copy_b(u, 1).wait_recv()

            def keep(part):
                whole = part((place,), slice(None))
                for side, columns in enumerate((slice(0, HALF), slice(HALF, UNIT))):
                    total = whole[:, columns] + a_in[u, side, 0].astype(F32)
                    sums[u % 4, :, columns] = total + b_in[u, side].astype(F32)

            on_unit(u, keep)

            @pl.when(outer)
            def _():
                @pl.when(u >= z_slots)
                def _():
                    copy_in(u - z_slots).wait_send()

                z_out[u % z_slots] = sums[u % 4].astype(BF)
                copy_in(u).start()

        u3, when = stage(LAGS[2], inner)

        @when
        def _():
            u = u3
            copy_in(u).wait_recv()

            @pl.when(u >= z_slots)
            def _():
                copy_across(u - z_slots).wait_send()

            z_out[u % z_slots] = (sums[u % 4] + z_one[u].astype(F32)).astype(BF)
            copy_across(u).start()

        u4, when = stage(LAGS[3], inner)

        @when
        def _():
            u = u4
            copy_across(u).wait_recv()
            z_one[u] = (z_out[u % z_slots].astype(F32) + z_two[u].astype(F32)).astype(BF)
            copy_out(u).start()

        u5, when = stage(LAGS[4], outer)

        @when
        def _():
            copy_out(u5).wait_recv()

        ends = [lag - LAGS[1] for lag in LAGS[2:]]

        @pl.when((i < extra) & outer)
        def _():
            z_ready[i] = ready_ref[i].astype(BF)
            ready_in(i).start()

        @pl.when((i >= ends[0]) & (i < extra + ends[0]) & inner)
        def _():
            n = i - ends[0]
            ready_in(n).wait_recv()
            z_ready[n] = (ready_ref[n] + z_one[count + n].astype(F32)).astype(BF)
            ready_across(n).start()

        @pl.when((i >= ends[1]) & (i < extra + ends[1]) & inner)
        def _():
            n = i - ends[1]
            ready_across(n).wait_recv()
            total = z_ready[n].astype(F32) + z_two[count + n].astype(F32)
            z_one[count + n] = total.astype(BF)
            copy_out(count + n).start()

        @pl.when((i >= ends[2]) & (i < extra + ends[2]) & outer)
        def _():
            copy_out(count + i - ends[2]).wait_recv()

        pl.when(i == 0)(back_link)

        @pl.when((i >= at_hidden) & (i < at_hidden + up_chunks))
        def _():
            back_hidden(i - at_hidden)

        pl.when(i == at_out)(back_out)

        @pl.when((i >= at_attention) & (i < at_attention + groups))
        def _():
            back_attention(i - at_attention)

        pl.when(i == at_qkv)(give_qkv)

        @pl.when((i >= at_qkv) & (i < at_qkv + qkv_chunks))
        def _():
            back_qkv(i - at_qkv)

        pl.when(i == at_start)(back_start)

        for number, device in enumerate((partner, x_side, y_side)):

            @pl.when(i == at_vec + number)
            def _():
                if number == 0:
                    v_out[0] = grad_vec[...]
                else:
                    copy_v(number - 1, (partner, x_side, y_side)[number - 1]).wait_recv()
                    v_out[number] = v_out[number - 1] + v_in[number - 1]
                copy_v(number, device).start()

        @pl.when(i == at_vec + 3)
        def _():
            copy_v(2, y_side).wait_recv()
            v_out[3] = v_out[2] + v_in[2]

            @pl.when(outer)
            def _():
                copy_v(3, inward).start()

        @pl.when((i == at_vec + 4) & inner)
        def _():
            copy_v(3, inward).wait_recv()
            v_out[4] = v_out[3] + v_in[3]
            copy_v(4, across).start()

        @pl.when((i == at_vec + 5) & inner)
        def _():
            copy_v(4, across).wait_recv()
            v_out[5] = v_out[4] + v_in[4]
            copy_v(5, outward).start()
            vec_out[...] = v_out[5]

        @pl.when((i == at_vec + 7) & outer)
        def _():
            copy_v(5, outward).wait_recv()
            vec_out[...] = v_in[5]

        return 0

    lax.fori_loop(0, count + LAGS[4], step, 0)

    stores = []
    for n, (u, start, out, row, rows, column) in enumerate(spots):
        stores.append(
            pltpu.make_async_copy(
                z_one.at[u, pl.ds(start, rows)],
                outs[out].at[pl.ds(row, rows), pl.ds(column, UNIT)],
                store_sem.at[n],
            )
        )
    for store in stores:
        store.start()
    for u in range(count - a_out.shape[0], count):
        for side in range(2):
            copy_a(u, side).wait_send()
    for u in range(count - b_out.shape[0], count):
        for side in range(2):
            copy_b(u, side).wait_send()
    for number, device in enumerate((partner, x_side, y_side)):
        copy_v(number, device).wait_send()
    for store in stores:
        store.wait()

    @pl.when(outer)
    def _():
        copy_v(3, inward).wait_send()
        for u in range(count - z_slots, count):
            copy_in(u).wait_send()
        for n in range(extra):
            ready_in(n).wait_send()

    @pl.when(inner)
    def _():
        copy_v(4, across).wait_send()
        copy_v(5, outward).wait_send()
        for u in range(count - z_slots, count):
            copy_across(u).wait_send()
        for n in range(extra):
            ready_across(n).wait_send()

        def drain(u, _):
            copy_out(u).wait_send()
            return 0

        lax.fori_loop(0, count + extra, drain, 0)


def encoder_back(dy, by_column, vec, vectors, bias, qkv, ready, dec, states, wide, down, lefts):
    owners = lax.axis_size("fsdp")
    own = PD // owners
    dec_units = LATE // 2
    dec = dec.reshape(4, 2, dec_units, ROWS, UNIT)
    half = ROWS // 2
    blocks, units, spots = [], [], []
    def add(left, sub, right, out, row, rows, column, columns):
        blocks.append((left, sub))
        for n in range(columns // UNIT):
            spots.append((dec_units + len(units), 0, out, row, rows, column + n * UNIT))
            units.append((len(blocks) - 1, right + n))

    subs = FF // owners // ROWS
    add(0, 0, 0, 1, 0, ROWS, 4 * D + FF, DD)
    for n in range(subs):
        add(1, n, 1, 2, n * ROWS, ROWS, 0, D)
    right = 1 + D // UNIT
    add(2, 0, right, 1, 0, ROWS, 4 * D, FF)
    right += FF // UNIT
    add(3, 0, right, 1, 0, ROWS, 3 * D, D)
    right += D // UNIT
    add(4, 0, right, 1, 0, ROWS, 0, 3 * D)
    right += 3 * D // UNIT
    add(5, 0, right, 0, 0, own, 0, D)
    right += D // UNIT
    count = dec_units + len(units)
    tall = DFF // DD
    for n in range(EARLY + LATE):
        if tall <= n < tall + LATE:
            unit = (n - tall) // 2
        else:
            unit = count + (n if n < tall else n - LATE) // 2
        place = (4, n * half, half, 0) if n < tall else (3, 0, half, (n - tall) * UNIT)
        spots.append((unit, n % 2 * half, *place))
    full = count + ready.shape[0]
    shapes = ((own, D), (ROWS, 4 * D + FF + DD), (FF // owners, D), (half, 10 * UNIT), (DFF // owners, DD))
    lefts = [a.reshape(4, 2, -1, VIS) for a in lefts]
    slots = 3
    dma = pltpu.SemaphoreType.DMA
    vmem, anywhere = pl.BlockSpec(memory_space=pltpu.VMEM), pl.BlockSpec(memory_space=pl.ANY)
    return pl.pallas_call(
        partial(back_kernel, dec_units, tuple(blocks), tuple(units), tuple(spots)),
        out_shape=tuple(jax.ShapeDtypeStruct(shape, BF) for shape in shapes)
        + (jax.ShapeDtypeStruct(vec.shape, F32),),
        in_specs=[vmem] * 7 + [anywhere] * (7 + len(lefts)),
        out_specs=(anywhere,) * len(shapes) + (vmem,),
        scratch_shapes=[
            pltpu.VMEM((len(blocks), 4, ROWS, VIS), BF),
            pltpu.VMEM((len(blocks), 4, ROWS, VIS), BF),
            pltpu.VMEM((right, VIS, UNIT), BF),
            pltpu.VMEM((right, VIS, UNIT), BF),
            pltpu.VMEM((dec_units, 4, ROWS, UNIT), BF),
            pltpu.VMEM((dec_units, 4, ROWS, UNIT), BF),
            pltpu.VMEM((slots, 2, 2, ROWS, HALF), BF),
            pltpu.VMEM((count, 2, 2, ROWS, HALF), BF),
            pltpu.VMEM((slots, 2, ROWS, HALF), BF),
            pltpu.VMEM((count, 2, ROWS, HALF), BF),
            pltpu.VMEM((4, ROWS, UNIT), F32),
            pltpu.VMEM((6, ROWS, UNIT), BF),
            pltpu.VMEM((full, ROWS, UNIT), BF),
            pltpu.VMEM((full, ROWS, UNIT), BF),
            pltpu.VMEM(ready.shape, BF),
            pltpu.VMEM((6, *vec.shape), F32),
            pltpu.VMEM((6, *vec.shape), F32),
            pltpu.VMEM((3, D, UNIT), BF),
            pltpu.VMEM((2, UNIT, D), BF),
            pltpu.VMEM((2, VIS, UNIT), F32),
            pltpu.VMEM((VIS, D), F32),
            pltpu.VMEM((VIS, D), F32),
            pltpu.VMEM((VIS, D), F32),
            pltpu.VMEM((VIS, D), BF),
            pltpu.VMEM((VIS, D), BF),
            pltpu.VMEM((VIS, 3 * D), BF),
            pltpu.VMEM(vec.shape, F32),
            dma((3,)),
            dma((2,)),
            dma((2,)),
            dma((1,)),
            dma((dec_units, 3)),
            dma((len(blocks), 3)),
            dma((right, 2)),
            dma((slots, 2)),
            dma((count, 2)),
            dma((slots, 2)),
            dma((count, 2)),
            dma((full, 2)),
            dma((full, 2)),
            dma((6,)),
            dma((6,)),
            dma((len(spots),)),
        ],
        compiler_params=pltpu.CompilerParams(
            collective_id=0, has_side_effects=True, vmem_limit_bytes=61 * 2**20
        ),
        cost_estimate=pl.CostEstimate(
            flops=30 * 10**9, bytes_accessed=300 * 2**20, transcendentals=0
        ),
    )(dy, by_column, vec, vectors, bias, qkv, ready, dec, *states, wide, down, *lefts)


def encoder_pieces(shapes):
    (own, width), (rows, _), (tall, _), (dec_rows, dec_width), (dec_tall, _) = shapes
    half = dec_rows // 2
    pieces = [(3, n * half, half, 0, dec_width, n + 1) for n in range(2)]
    pieces += [(0, 0, own, 0, width, 0)]
    pieces += [(1, 0, rows, n * D, D, (1, 2, 0)[n]) for n in range(3)]
    pieces += [(1, 0, rows, 3 * D, D, 1)]
    pieces += [(1, 0, rows, 4 * D + n * D, D, (2, 0, 1, 2)[n]) for n in range(FF // D)]
    pieces += [(2, n * rows, rows, 0, D, (0, 1, 2, 0)[n]) for n in range(tall // rows)]
    pieces += [(1, 0, rows, 4 * D + FF, DD, 0)]
    pieces += [(4, 0, dec_tall, 0, DD, 0)]
    return pieces


def norm_rows(h, gain):
    mean = jnp.mean(h, -1, keepdims=True)
    cent = h - mean
    var = jnp.mean(cent * cent, -1, keepdims=True)
    return (cent * lax.rsqrt(var + EPS) * gain).astype(BF)


def encoder_kernel(
    pixels_ref,
    row_ref,
    column_ref,
    scale_ref,
    omega_ref,
    vectors_ref,
    embed_ref,
    wide_ref,
    down_ref,
    dec_wide_ref,
    dec_down_ref,
    wide_out,
    down_out,
    dec_wide_out,
    dec_down_out,
    picked_out,
    slope_out,
    stats_out,
    by_row,
    by_column,
    pos_out,
    bias_out,
    inputs_t,
    a_t,
    mixed_t,
    b_t,
    hidden_t,
    z_t,
    start_ref,
    qkv_ref,
    middle_ref,
    end_ref,
    seen_ref,
    inputs_ref,
    a_ref,
    mixed_ref,
    b_ref,
    hidden_ref,
    z_ref,
    w_embed,
    w_wide,
    w_down,
    stage_ref,
    pick_ref,
    high_ref,
    mid_ref,
    low_ref,
    picked_ref,
    pos_ref,
    bias_ref,
    dec_stage,
    dec_stage_down,
    dec_own,
    dec_own_down,
    slope_ref,
    hidden_pixels,
    v_in,
    v_out,
    load_sem,
    store_sem,
    send_sem,
    recv_sem,
    v_send,
    v_recv,
    side_sem,
):
    shards = (embed_ref, wide_ref, down_ref, dec_wide_ref, dec_down_ref)
    gathered = (w_embed, w_wide, w_down, dec_wide_out, dec_down_out)
    gain_one, gain_two, gain_out = [vectors_ref[:, n * D : (n + 1) * D] for n in range(3)]
    pieces = encoder_pieces([ref.shape for ref in shards])
    count, base = len(pieces), 2
    stores = []
    z, f = lax.axis_index("dp"), lax.axis_index("fsdp")
    core, place = f % 2, f // 2
    x, y = place % 2, place // 2
    f_x, f_y, f_far = f + 2 - 4 * x, f + 4 - 8 * y, f + 6 - 4 * x - 8 * y
    partner = (z, f + 1 - 2 * core)
    x_side, y_side, z_side = (z, f_x), (z, f_y), (z + 1 - 2 * (z % 2), f)
    outer = (z == 0) | (z == 3)
    inner = (z == 1) | (z == 2)
    across = (3 - z, f)

    barrier = pltpu.get_barrier_semaphore()
    for device in (partner, x_side, y_side, z_side):
        pl.semaphore_signal(barrier, inc=1, device_id=device, device_id_type=MESH)

    @pl.when(outer)
    def _():
        pl.semaphore_wait(barrier, 4)

    @pl.when(inner)
    def _():
        pl.semaphore_signal(barrier, inc=1, device_id=across, device_id_type=MESH)
        pl.semaphore_wait(barrier, 5)

    stages = stage_ref.shape[0]

    def load(t):
        array, row, rows, column, columns, _ = pieces[t]
        return pltpu.make_async_copy(
            shards[array].at[pl.ds(row, rows), pl.ds(column, columns)],
            stage_ref.at[staged[t], pl.ds(0, rows), pl.ds(0, columns)],
            load_sem.at[staged[t]],
        )

    encoder = [t for t, piece in enumerate(pieces) if piece[0] < 3]
    staged = {t: n % stages for n, t in enumerate(encoder)}
    after = dict(zip(encoder, encoder[stages:]))
    dec_loads = [
        pltpu.make_async_copy(dec_wide_ref, dec_stage, side_sem.at[0]),
        pltpu.make_async_copy(dec_down_ref, dec_stage_down, side_sem.at[1]),
    ]
    for copy in dec_loads:
        copy.start()
    for t in encoder[:stages]:
        load(t).start()

    def spot(t, owner, half=None):
        array, row, rows, column, columns, _ = pieces[t]
        if array > 2:
            if half is not None:
                rows //= 2
                row += half * rows
            return gathered[array].at[owner, pl.ds(row, rows)]
        if half is not None:
            columns //= 2
            column += half * columns
        return gathered[array].at[owner, pl.ds(row, rows), pl.ds(column, columns)]

    def move(t, owner, send, recv, device, half=None):
        target = source = spot(t, owner, half)
        array, row, rows = pieces[t][:3]
        if send < 3 and array > 2:
            source = (dec_own, dec_own_down)[array - 3].at[pl.ds(row, rows)]
        return put(source, target, send_sem.at[t, send], recv_sem.at[t, recv], device)

    def own_x(t):
        return move(t, f, 0, 0, x_side)

    def own_y(t):
        return move(t, f, 1, 1, y_side)

    def own_core(t):
        return move(t, f, 2, 4, partner)

    def far_x(t):
        return move(t, f_y, 3, 2, x_side, 0)

    def far_y(t):
        return move(t, f_x, 4, 3, y_side, 1)

    def to_core(t, n):
        return move(t, (f_x, f_y, f_far)[n], 5 + n, 5 + n, partner)

    def to_z(t, n):
        return move(t, (f_x, f_y, f_far)[n], 8 + n, 8 + n, z_side)

    def brings(t, then, other=None):
        kind = pieces[t][5]
        if kind == 0:
            then()
            return
        pl.when(z % 2 == kind - 1)(then)
        if other is not None:
            pl.when(z % 2 != kind - 1)(other)

    def first(t):
        array, row, rows, column, columns, _ = pieces[t]
        if array < 3:
            load(t).wait()
            spot(t, f)[...] = stage_ref[staged[t], :rows, :columns].astype(BF)
            if t in after:
                load(after[t]).start()
        else:
            if row == 0:
                dec_loads[array - 3].wait()
            own = (dec_own, dec_own_down)[array - 3]
            own[row : row + rows, :] = (dec_stage, dec_stage_down)[array - 3][
                row : row + rows, :
            ].astype(BF)
            store = pltpu.make_async_copy(own.at[pl.ds(row, rows)], spot(t, f), store_sem.at[t])
            store.start()
            stores.append(store)
        own_core(t).start()

        def then():
            own_x(t).start()
            own_y(t).start()

        brings(t, then)

    def second(t):
        def then():
            own_x(t).wait_recv()
            far_y(t).start()
            own_y(t).wait_recv()
            far_x(t).start()
            for n in range(2):
                to_core(t, n).start()
                if pieces[t][5]:
                    to_z(t, n).start()

        brings(t, then)

    def third(t):
        def then():
            far_x(t).wait_recv()
            far_y(t).wait_recv()
            to_core(t, 2).start()
            if pieces[t][5]:
                to_z(t, 2).start()

        brings(t, then)

    def taken(t, n):
        def other():
            to_z(t, n).wait_recv()
            to_core(t, n).start()

        brings(t, lambda: None, other)

    def whole(t):
        own_core(t).wait_recv()
        for n in range(3):
            to_core(t, n).wait_recv()

    def drain(t):
        own_core(t).wait_send()
        for n in range(3):
            to_core(t, n).wait_send()

        def then():
            for copy in (own_x(t), own_y(t), far_x(t), far_y(t)):
                copy.wait_send()
            if pieces[t][5]:
                for n in range(3):
                    to_z(t, n).wait_send()

        brings(t, then)

    def copy_v(step, device):
        return put(v_out.at[step], v_in.at[step], v_send.at[step], v_recv.at[step], device)

    sides = (partner, x_side, y_side)

    def statistics(i):
        if i <= 3:
            if i > 0:
                copy_v(i - 1, sides[i - 1]).wait_recv()
                v_out[i] = v_out[i - 1] + v_in[i - 1]
            if i < 3:
                copy_v(i, sides[i]).start()
            else:

                @pl.when(outer)
                def _():
                    copy_v(3, z_side).start()

        if i == 4:

            @pl.when(inner)
            def _():
                copy_v(3, z_side).wait_recv()
                v_out[4] = v_out[3] + v_in[3]
                copy_v(4, across).start()

        if i == 5:

            @pl.when(inner)
            def _():
                copy_v(4, across).wait_recv()
                v_out[5] = v_out[4] + v_in[4]
                copy_v(5, z_side).start()
                stats_out[...] = v_out[5]

            @pl.when(outer)
            def _():
                copy_v(5, z_side).wait_recv()
                stats_out[...] = v_in[5]

    def turn(source, target, start=0, width=D):
        for lane in range(start, start + width, LANES):
            target[lane : lane + LANES, :] = source[:, lane : lane + LANES].T

    def columns_of(t):
        array, row, rows, column, columns, _ = pieces[t]
        weight = gathered[array][:, row : row + rows, column : column + columns]
        return weight.reshape(-1, columns)

    def local_statistics():
        pixels = pixels_ref[...]
        weighted = pixels * column_ref[:, 0:1]
        sums = jnp.sum(weighted, 0, keepdims=True)
        squares = jnp.sum(weighted * pixels, 0, keepdims=True)
        live = row_ref[0:1, :]
        totals = [r[:, n * PATCH**2 : (n + 1) * PATCH**2] for r in (sums, squares) for n in range(BANDS)]
        for n, total in enumerate((*totals, live, live * row_ref[1:2, :])):
            v_out[0, n : n + 1, :] = jnp.broadcast_to(jnp.sum(total, 1, keepdims=True), (1, LANES))

    def arrange_step():
        slots = (TOK_DEV, TOK_DEV)
        down, along = [lax.broadcasted_iota(jnp.int32, slots, n) for n in range(2)]
        live, masked = row_ref[0:1, :], row_ref[1:2, :]
        seen, hid = live * (1.0 - masked), live * masked
        kind = lax.broadcasted_iota(jnp.int32, row_ref.shape, 0)
        kinds = jnp.where(kind == 0, seen, jnp.where(kind == 1, hid, 1.0 - live))
        ranks = matmul(kinds.astype(BF), jnp.where(down < along, 1.0, 0.0).astype(BF))
        n_seen, n_hid = [jnp.sum(r, 1, keepdims=True) for r in (seen, hid)]
        empty = ranks[2:3, :]
        place = jnp.where(empty < VIS - n_seen, n_seen + empty, n_seen + n_hid + empty)
        place = jnp.where(hid > 0, VIS + ranks[1:2, :], place)
        place = jnp.where(seen > 0, ranks[0:1, :], place)
        pick_ref[...] = jnp.where(down == place.astype(jnp.int32), 1.0, 0.0).astype(BF)
        facts = row_ref[...].astype(BF)
        by_row[...] = right_t(facts, pick_ref[...])
        by_column[...] = right_t(pick_ref[...], facts)
        pixels = pixels_ref[...]
        high = pixels.astype(BF)
        rest = pixels - high.astype(F32)
        mid = rest.astype(BF)
        high_ref[...], mid_ref[...] = high, mid
        low_ref[...] = (rest - mid.astype(F32)).astype(BF)

    def pick_rows(rows):
        pick = pick_ref[rows, :]
        return matmul(pick, high_ref[...]) + matmul(pick, mid_ref[...]) + matmul(pick, low_ref[...])

    def pick_step():
        picked_ref[...] = pick_rows(slice(0, VIS))
        same = by_column[:VIS, 2:3] == by_row[2:3, :VIS]
        shape = (VIS, VIS)
        bias_out[...] = mask_bias(by_column[:VIS, 0:1] > 0, same, shape, 0)
        bias_ref[...] = mask_bias(by_row[0:1, :VIS] > 0, same, shape, 0, 1)

    def position_rows(target, rows, width, row):
        quarter = width // 4
        odd = by_column[rows, 2:3] > 0
        scale = jnp.where(odd, scale_ref[1:2, 0:1], scale_ref[0:1, 0:1])
        for n in range(2):
            angle = by_column[rows, 3 + n : 4 + n] * scale * omega_ref[row : row + 1, :quarter]
            target[rows, 2 * n * quarter : (2 * n + 1) * quarter] = jnp.sin(angle)
            target[rows, (2 * n + 1) * quarter : (2 * n + 2) * quarter] = jnp.cos(angle)

    def pixel_store(n):
        return pltpu.make_async_copy(
            hidden_pixels, picked_out.at[pl.ds((n - 1) * VIS, VIS)], side_sem.at[4]
        )

    def hidden_step(n):
        rows = slice(n * VIS, (n + 1) * VIS)
        if n > 0:
            if n > 1:
                pixel_store(n - 1).wait()
            hidden_pixels[...] = pick_rows(rows)
            pixel_store(n).start()
        position_rows(pos_out, rows, DD, 1)

    def embed_step():
        pixels = stats_out[6:7, :] * (PATCH * PATCH)
        for band in range(BANDS):
            mean = stats_out[band : band + 1, :] / pixels
            var = stats_out[BANDS + band : BANDS + band + 1, :] / pixels - mean * mean
            rate = lax.rsqrt(var + EPS)
            for part in range(PATCH * PATCH // LANES):
                lanes = pl.ds(band * PATCH * PATCH + part * LANES, LANES)
                inputs_ref[:, lanes] = ((picked_ref[:, lanes] - mean) * rate).astype(BF)
        start_ref[...] = matmul(inputs_ref[...], columns_of(base)) + pos_ref[...]
        a_ref[...] = norm_rows(start_ref[...], gain_one)
        own = w_embed.shape[1]
        flipped = jnp.concatenate(
            [inputs_ref[:, lane : lane + LANES].T for lane in range(0, PD, LANES)], 0
        )
        inputs_t[...] = jnp.zeros_like(inputs_t)
        for owner in range(w_embed.shape[0]):
            inputs_t[owner, :own, :] = flipped[owner * own : (owner + 1) * own, :]
        turn(a_ref, a_t)

    def qkv_step(n):
        qkv_ref[:, n * D : (n + 1) * D] = matmul(a_ref[...], columns_of(base + 1 + n)).astype(BF)

    def attention_step():
        size = D // HEADS
        lane_head = lax.broadcasted_iota(jnp.int32, (VIS, LANES), 1) // size

        def group(g, _):
            query, keys, values = [
                qkv_ref[:, pl.ds(pl.multiple_of(n * D + g * LANES, LANES), LANES)] for n in range(3)
            ]
            mixed = jnp.zeros((VIS, LANES), F32)
            for j in range(LANES // size):
                one = jnp.where(lane_head == j, query.astype(F32), 0.0).astype(BF)
                scores = right_t(one, keys) * size ** (-0.5) + bias_ref[...]
                probs = jnp.exp(scores - jnp.max(scores, -1, keepdims=True))
                probs = probs * (1.0 / jnp.sum(probs, -1, keepdims=True))
                mixed = jnp.where(lane_head == j, matmul(probs.astype(BF), values), mixed)
            mixed_ref[:, pl.ds(pl.multiple_of(g * LANES, LANES), LANES)] = mixed.astype(BF)
            return 0

        lax.fori_loop(0, D // LANES, group, 0)

    def out_step():
        turn(mixed_ref, mixed_t)
        middle_ref[...] = start_ref[...] + matmul(mixed_ref[...], columns_of(base + 4))
        b_ref[...] = norm_rows(middle_ref[...], gain_two)
        turn(b_ref, b_t)

    def slope_store(n):
        return pltpu.make_async_copy(
            slope_ref.at[n % 2], slope_out.at[:, pl.ds(n * D, D)], side_sem.at[2 + n % 2]
        )

    def up_step(n):
        columns = slice(n * D, (n + 1) * D)
        after, slope = gelu_parts(matmul(b_ref[...], columns_of(base + 5 + n)))
        hidden_ref[:, columns] = after.astype(BF)
        if n > 1:
            slope_store(n - 2).wait()
        slope_ref[n % 2] = slope
        slope_store(n).start()
        turn(hidden_ref, hidden_t, n * D)

    def down_step(n):
        rows, owners = w_wide.shape[1], w_down.shape[0]
        tall = w_down.shape[1]
        parts = [hidden_ref[:, o * tall + n * rows : o * tall + (n + 1) * rows] for o in range(owners)]
        total = matmul(jnp.concatenate(parts, 1), columns_of(base + 9 + n))
        end_ref[...] = (middle_ref[...] if n == 0 else end_ref[...]) + total

    def link_step():
        z_ref[...] = norm_rows(end_ref[...], gain_out)
        turn(z_ref, z_t)
        seen_ref[...] = matmul(z_ref[...], columns_of(base + 13))

    work = [(0, None, arrange_step), (1, None, pick_step)]
    work += [(2, None, partial(position_rows, pos_ref, slice(0, VIS), D, 0))]
    work += [(at, None, partial(hidden_step, n)) for n, at in enumerate((3, 4, 11, 14))]
    work += [(6, base, embed_step), (8, base + 1, partial(qkv_step, 0))]
    work += [(9, base + 2, partial(qkv_step, 1)), (9, base + 3, partial(qkv_step, 2))]
    work += [(9, None, attention_step), (11, base + 4, out_step)]
    work += [(at, base + 5 + n, partial(up_step, n)) for n, at in enumerate((12, 12, 14, 15))]
    work += [(at, base + 9 + n, partial(down_step, n)) for n, at in enumerate((15, 17, 18, 18))]
    work += [(19, base + 13, link_step)]

    first(0)
    local_statistics()
    first(1)
    for i in range(20):
        if i + 2 < count:
            first(i + 2)
        statistics(i)
        if i < count:
            second(i)
        if 0 <= i - 1 < count:
            third(i - 1)
        if 0 <= i - 3 < count:
            taken(i - 3, 0)
            taken(i - 3, 1)
        if 0 <= i - 4 < count:
            taken(i - 4, 2)
        for at, piece, run in work:
            if at != i:
                continue
            if piece is not None:
                whole(piece)
                array, row, rows, column, columns, _ = pieces[piece]
                if array:
                    where = (slice(None), pl.ds(row, rows), pl.ds(column, columns))
                    store = pltpu.make_async_copy(
                        gathered[array].at[where],
                        (None, wide_out, down_out)[array].at[where],
                        store_sem.at[piece],
                    )
                    store.start()
                    stores.append(store)
            run()
    for t, piece in enumerate(pieces):
        if piece[0] > 2:
            whole(t)
    for n in range(2):
        slope_store(FF // D - 2 + n).wait()
    pixel_store(HID // VIS).wait()
    for store in stores:
        store.wait()
    for t in range(count):
        drain(t)
    for step in range(3):
        copy_v(step, sides[step]).wait_send()

    @pl.when(outer)
    def _():
        copy_v(3, z_side).wait_send()

    @pl.when(inner)
    def _():
        copy_v(4, across).wait_send()
        copy_v(5, z_side).wait_send()


def encoder_forward(pixels, facts, scale, vectors, *shards):
    owners = lax.axis_size("fsdp")
    shapes = [w.shape for w in shards]
    count = len(encoder_pieces(shapes))
    omega = [
        10000.0 ** (-jnp.arange(width // 4, dtype=jnp.float32) / (width // 4)) for width in (D, DD)
    ]
    omega = jnp.stack([omega[0], jnp.pad(omega[1], (0, D // 4 - DD // 4))] + [omega[0]] * 6)
    full = [jax.ShapeDtypeStruct((owners, *shape), BF) for shape in shapes[1:]]
    full += [jax.ShapeDtypeStruct((HID, PD), F32), jax.ShapeDtypeStruct((VIS, FF), F32)]
    local = [
        jax.ShapeDtypeStruct((8, LANES), F32),
        jax.ShapeDtypeStruct((8, TOK_DEV), F32),
        jax.ShapeDtypeStruct((TOK_DEV, 8), F32),
        jax.ShapeDtypeStruct((TOK_DEV, DD), F32),
        jax.ShapeDtypeStruct((VIS, VIS), F32),
        jax.ShapeDtypeStruct((owners, ROWS, VIS), BF),
        *[jax.ShapeDtypeStruct((width, VIS), BF) for width in (D, D, D, FF, D)],
        jax.ShapeDtypeStruct((VIS, D), F32),
        jax.ShapeDtypeStruct((VIS, 3 * D), BF),
        jax.ShapeDtypeStruct((VIS, D), F32),
        jax.ShapeDtypeStruct((VIS, D), F32),
        jax.ShapeDtypeStruct((VIS, DD), F32),
    ]
    vmem, anywhere = pl.BlockSpec(memory_space=pltpu.VMEM), pl.BlockSpec(memory_space=pl.ANY)
    dma = pltpu.SemaphoreType.DMA
    wide_full, down_full, dec_wide, dec_down, *rest = pl.pallas_call(
        encoder_kernel,
        out_shape=(*full, *local),
        in_specs=[vmem] * 6 + [anywhere] * len(shards),
        out_specs=(anywhere,) * len(full) + (vmem,) * len(local),
        scratch_shapes=[pltpu.VMEM((VIS, width), BF) for width in (PD, D, D, D, FF, D)]
        + [pltpu.VMEM((owners, *shape), BF) for shape in shapes[:3]]
        + [
            pltpu.VMEM((4, ROWS, D), F32),
            *[pltpu.VMEM((TOK_DEV, PD), BF)] * 4,
            pltpu.VMEM((VIS, PD), F32),
            pltpu.VMEM((VIS, D), F32),
            pltpu.VMEM((VIS, VIS), F32),
            *[pltpu.VMEM(shape, F32) for shape in shapes[3:]],
            *[pltpu.VMEM(shape, BF) for shape in shapes[3:]],
            pltpu.VMEM((2, VIS, D), F32),
            pltpu.VMEM((VIS, PD), F32),
            pltpu.VMEM((6, 8, LANES), F32),
            pltpu.VMEM((6, 8, LANES), F32),
            dma((4,)),
            dma((count,)),
            dma((count, 11)),
            dma((count, 11)),
            dma((6,)),
            dma((6,)),
            dma((5,)),
        ],
        compiler_params=pltpu.CompilerParams(
            collective_id=1, has_side_effects=True, vmem_limit_bytes=60 * 2**20
        ),
        cost_estimate=pl.CostEstimate(
            flops=2 * VIS * 14 * 2**20, bytes_accessed=200 * 2**20, transcendentals=0
        ),
    )(pixels, facts, facts.T, scale, omega, vectors, *shards)
    return (
        wide_full.reshape(D, -1),
        down_full.reshape(FF, D),
        dec_wide.reshape(DD, -1),
        dec_down.reshape(DFF, DD),
        *rest,
    )


LOWP = 256
HEADP = PD + LOWP
BLOCK = HID // 2


def mask_bias(live, same, shape, offset, keys=0):
    key, query = [lax.broadcasted_iota(jnp.int32, shape, (keys + n) % 2) for n in range(2)]
    return jnp.where((live & same) | (key + offset == query), 0.0, NEGATIVE)


def normalize(h):
    cent = h - jnp.mean(h, -1, keepdims=True)
    rate = lax.rsqrt(jnp.mean(cent * cent, -1, keepdims=True) + EPS)
    return cent * rate, rate


def normalize_back(unit, rate, gain, grad):
    scaled = grad * gain
    along = jnp.mean(scaled * unit, -1, keepdims=True)
    dh = rate * (scaled - jnp.mean(scaled, -1, keepdims=True) - unit * along)
    return dh, jnp.sum(grad * unit, 0, keepdims=True)


def exact_product(array, weight):
    high = array.astype(BF)
    rest = array - high.astype(F32)
    mid = rest.astype(BF)
    low = (rest - mid.astype(F32)).astype(BF)
    return matmul(high, weight) + matmul(mid, weight) + matmul(low, weight)


EARLY = DFF // DD + DFF // UNIT + HEADP // UNIT
LATE = 4


def decoder_kernel(
    owners,
    fast,
    pos_ref,
    seen_ref,
    row_ref,
    column_ref,
    picked_ref,
    stats_ref,
    vectors_ref,
    wide_ref,
    down_ref,
    late_ref,
    dy_ref,
    vec_out,
    sums_ref,
    early_ref,
    y_ref,
    a_ref,
    q_ref,
    k_ref,
    v_ref,
    mixed_t,
    mixed_ref,
    lse_ref,
    head_ref,
    b_ref,
    hidden_ref,
    z_ref,
    dpred_ref,
    dbranch_ref,
    dbefore_ref,
    dattn_ref,
    dmixed_ref,
    dmiddle_ref,
    dq_ref,
    dk_ref,
    dv_ref,
    loss_ref,
    bias_ref,
    pool_ref,
    spread_ref,
    vec_ref,
    *links,
):
    if fast:
        (dp, a_out, a_in, b_out, b_in, swap_sem, a_send, a_recv, b_send, b_recv) = links
        ready = EARLY // 2
        z, f = lax.axis_index("dp"), lax.axis_index("fsdp")
        core, place = f % 2, f // 2
        x, y = place % 2, place // 2
        partner = (z, f + 1 - 2 * core)
        x_side, y_side = (z, f + 2 - 4 * x), (z, f + 4 - 8 * y)
        at_x, at_y, at_far = place + 1 - 2 * x, place + 2 - 4 * y, 3 - place
        first, second = pl.ds(0, HALF), pl.ds(HALF, HALF)
        barrier = pltpu.get_barrier_semaphore()
        for device in (partner, x_side, y_side):
            pl.semaphore_signal(barrier, inc=1, device_id=device, device_id_type=MESH)

        def swap(u):
            return put(
                early_ref.at[:, 1 - core, pl.ds(2 * u, 2)],
                dp.at[u],
                swap_sem.at[u, 0],
                swap_sem.at[u, 1],
                partner,
            )

        def share(u, owner, columns):
            own = early_ref[owner, core, pl.ds(2 * u, 2), :, columns].astype(F32)
            both = own + dp[u, owner, :, :, columns].astype(F32)
            return both.reshape(ROWS, HALF)

        def copy_a(u, side):
            return put(
                a_out.at[u, side],
                a_in.at[u, side],
                a_send.at[u, side],
                a_recv.at[u, side],
                (x_side, y_side)[side],
            )

        def copy_b(u, side):
            return put(
                b_out.at[u, side],
                b_in.at[u, side],
                b_send.at[u, side],
                b_recv.at[u, side],
                (y_side, x_side)[side],
            )

        def exchange(c):
            @pl.when(c < ready)
            def _():
                swap(c).wait()
                a_out[c, 0, 0] = share(c, at_x, first).astype(BF)
                a_out[c, 0, 1] = share(c, at_far, first).astype(BF)
                copy_a(c, 0).start()
                a_out[c, 1, 0] = share(c, at_y, second).astype(BF)
                a_out[c, 1, 1] = share(c, at_far, second).astype(BF)
                copy_a(c, 1).start()

            @pl.when((c >= 2) & (c < ready + 2))
            def _():
                u = c - 2
                copy_a(u, 0).wait_recv()
                b_out[u, 0] = (share(u, at_y, first) + a_in[u, 0, 1].astype(F32)).astype(BF)
                copy_b(u, 0).start()
                copy_a(u, 1).wait_recv()
                b_out[u, 1] = (share(u, at_x, second) + a_in[u, 1, 1].astype(F32)).astype(BF)
                copy_b(u, 1).start()

            @pl.when((c >= 4) & (c < ready + 4))
            def _():
                u = c - 4
                for side, columns in enumerate((first, second)):
                    copy_b(u, side).wait_recv()
                    total = share(u, place, columns) + a_in[u, side, 0].astype(F32)
                    sums_ref[u, :, columns] = total + b_in[u, side].astype(F32)

    size = DD // DHEADS
    per = LANES // size
    factor = size ** (-0.5)
    gain_one, gain_two, gain_out, token = [
        vectors_ref[:, 3 * D + n * DD : 3 * D + (n + 1) * DD] for n in range(4)
    ]

    def pooled(shape, pixels):
        pixel, low = [lax.broadcasted_iota(jnp.int32, shape, (pixels + n) % 2) for n in range(2)]
        row, column = (pixel >> 4) & 15, pixel & 15
        return ((pixel >> 8) << 6) + ((row >> 1) << 3) + (column >> 1) == low

    pool_ref[...] = jnp.where(pooled((PD, LOWP), 0), 0.25, 0.0).astype(BF)
    spread_ref[...] = jnp.where(pooled((LOWP, PD), 1), 1.0, 0.0).astype(BF)
    lane_head = lax.broadcasted_iota(jnp.int32, (HID, LANES), 1) // size
    key_head = lax.broadcasted_iota(jnp.int32, (TOK_DEV, LANES), 1) // size
    kept = column_ref[:VIS, 0:1] > 0
    for start in range(0, TOK_DEV, VIS):
        rows = slice(start, start + VIS)
        bias_ref[rows, :] = mask_bias(
            column_ref[rows, 0:1] > 0,
            column_ref[rows, 2:3] == row_ref[2:3, VIS:],
            (VIS, HID),
            start - VIS,
        )
    if not fast:
        sums_ref[...] = jnp.zeros_like(sums_ref)
    vec_ref[...] = jnp.zeros_like(vec_ref)
    loss_ref[...] = jnp.zeros_like(loss_ref)
    head_ref[...] = jnp.zeros_like(head_ref)
    head_ref[:, : PD + LOWD] = wide_ref[:, 4 * DD + DFF :]

    def project(rows, with_query):
        a = (normalize(y_ref[rows, :])[0] * gain_one).astype(BF)
        a_ref[rows, :] = a
        k_ref[rows, :] = matmul(a, wide_ref[:, DD : 2 * DD]).astype(BF)
        v_ref[rows, :] = matmul(a, wide_ref[:, 2 * DD : 3 * DD]).astype(BF)
        return a

    y_ref[:VIS, :] = pos_ref[:VIS, :] + jnp.where(kept, seen_ref[...], token)
    y_ref[VIS:, :] = pos_ref[VIS:, :] + token
    project(slice(0, VIS), False)

    def hidden_rows(n):
        start = pl.multiple_of(n * BLOCK, BLOCK)
        return pl.ds(start, BLOCK), pl.ds(pl.multiple_of(start + VIS, 32), BLOCK)

    def project_hidden(n, _):
        rows, all_rows = hidden_rows(n)
        a = project(all_rows, True)
        q_ref[rows, :] = matmul(a, wide_ref[:, :DD]).astype(BF)
        return 0

    lax.fori_loop(0, 2, project_hidden, 0)

    def only(array, head_of, j):
        return jnp.where(head_of == j, array.astype(F32), 0.0).astype(BF)

    def attend_group(g, _):
        lanes = pl.ds(pl.multiple_of(g * LANES, LANES), LANES)
        keys, query = k_ref[:, lanes], q_ref[:, lanes]
        values_t = v_ref[:, lanes].T
        for j in range(per):
            scores = right_t(keys, only(query, lane_head, j)) * factor + bias_ref[...]
            top = jnp.max(scores, 0, keepdims=True)
            probs = jnp.exp(scores - top)
            total = jnp.sum(probs, 0, keepdims=True)
            probs = (probs * (1.0 / total)).astype(BF)
            rows = slice(j * size, (j + 1) * size)
            mixed_t[g, rows, :] = matmul(values_t[rows, :], probs).astype(BF)
            lse_ref[g, j : j + 1, :] = top + jnp.log(total)
        mixed_ref[:, lanes] = mixed_t[g].T
        return 0

    lax.fori_loop(0, DD // LANES, attend_group, 0)

    pixels = stats_ref[6:7, :] * (PATCH * PATCH)
    flagged = stats_ref[7:8, 0:1]

    def follow(n, _):
        rows, all_rows = hidden_rows(n)
        middle = y_ref[all_rows, :] + matmul(mixed_ref[rows, :], wide_ref[:, 3 * DD : 4 * DD])
        unit_b, rate_b = normalize(middle)
        b = (unit_b * gain_two).astype(BF)
        b_ref[rows, :] = b
        after, slope = gelu_parts(matmul(b, wide_ref[:, 4 * DD : 4 * DD + DFF]))
        hidden_ref[rows, :] = after.astype(BF)
        unit_z, rate_z = normalize(middle + matmul(hidden_ref[rows, :], down_ref[...]))
        z = (unit_z * gain_out).astype(BF)
        z_ref[rows, :] = z
        pred = matmul(z, head_ref[...])
        parts = []
        for part in range(PD // LANES):
            band = part * LANES // (PATCH * PATCH)
            mean = stats_ref[band : band + 1, :] / pixels
            var = stats_ref[BANDS + band : BANDS + band + 1, :] / pixels - mean * mean
            lanes = slice(part * LANES, (part + 1) * LANES)
            parts.append((picked_ref[rows, lanes] - mean) * lax.rsqrt(var + EPS))
        normed = jnp.concatenate(parts, 1)
        coarse = exact_product(normed, pool_ref[...])
        err_high = pred[:, :PD] - (normed - exact_product(coarse, spread_ref[...]))
        err_low = pred[:, PD:] - coarse
        flag = column_ref[all_rows, 0:1]
        length = jnp.sqrt(err_high * err_high + 1.0)
        loss_ref[:, :PD] += jnp.sum((length - 1.0) * flag, 0, keepdims=True) * (1.0 / PD)
        loss_ref[:, PD:] += jnp.sum(err_low * err_low * flag, 0, keepdims=True) * (1.0 / LOWD)
        share = flag / flagged
        dpred_ref[rows, :PD] = (err_high / length * (share * (1.0 / PD))).astype(BF)
        dpred_ref[rows, PD:] = (err_low * (share * (2.0 / LOWD))).astype(BF)
        dz = right_t(dpred_ref[rows, :], head_ref[...])
        dend, dgain = normalize_back(unit_z, rate_z, gain_out, dz)
        vec_ref[2:3, :] += dgain
        dbranch_ref[rows, :] = dend.astype(BF)
        dhidden = right_t(dbranch_ref[rows, :], down_ref[...])
        dbefore_ref[rows, :] = (dhidden * slope).astype(BF)
        db = right_t(dbefore_ref[rows, :], wide_ref[:, 4 * DD : 4 * DD + DFF])
        dmiddle, dgain = normalize_back(unit_b, rate_b, gain_two, db)
        vec_ref[1:2, :] += dgain
        dmiddle = dmiddle + dend
        dmiddle_ref[rows, :] = dmiddle
        dattn_ref[rows, :] = dmiddle.astype(BF)
        dmixed = right_t(dattn_ref[rows, :], wide_ref[:, 3 * DD : 4 * DD])
        dmixed_ref[rows, :] = dmixed.astype(BF)
        return 0

    lax.fori_loop(0, 2, follow, 0)

    rows = DD // owners

    def store(ref, block, grad):
        ref[:, :, block] = grad.astype(BF).reshape(owners // 2, 2, rows, UNIT)

    parts = DFF // DD
    down_grad = left_t(hidden_ref[...], dbranch_ref[...]).astype(BF)
    down_grad = down_grad.reshape(owners // 2, 2, parts, rows, UNIT)
    for part in range(parts):
        early_ref[:, :, part] = down_grad[:, :, part]
    for n in range(DFF // UNIT):
        columns = slice(n * UNIT, (n + 1) * UNIT)
        store(early_ref, parts + n, left_t(b_ref[...], dbefore_ref[:, columns]))
    for n in range(HEADP // UNIT):
        columns = slice(n * UNIT, (n + 1) * UNIT)
        store(early_ref, parts + DFF // UNIT + n, left_t(z_ref[...], dpred_ref[:, columns]))
    if fast:
        pl.semaphore_wait(barrier, 3)
        for u in range(ready):
            swap(u).start()
    store(
        late_ref,
        3,
        jnp.concatenate([matmul(mixed_t[g], dattn_ref[...]) for g in range(DD // LANES)], 0),
    )

    def attend_back_group(g, _):
        lanes = pl.ds(pl.multiple_of(g * LANES, LANES), LANES)
        query, keys, values, dout = [r[:, lanes] for r in (q_ref, k_ref, v_ref, dmixed_ref)]
        keys_t = keys.T
        dkeys = jnp.zeros((TOK_DEV, LANES), F32)
        dvalues = jnp.zeros((TOK_DEV, LANES), F32)
        dquery = []
        for j in range(per):
            if fast and j % 2 == 0:
                exchange(2 * g + j // 2)
            scores = right_t(keys, only(query, lane_head, j)) * factor + bias_ref[...]
            probs = jnp.exp(scores - lse_ref[g, j : j + 1, :])
            dvalues = jnp.where(key_head == j, matmul(probs.astype(BF), dout), dvalues)
            dprobs = right_t(values, only(dout, lane_head, j))
            delta = jnp.sum(dprobs * probs, 0, keepdims=True)
            dscores = (probs * (dprobs - delta)).astype(BF)
            dkeys = jnp.where(key_head == j, matmul(dscores, query), dkeys)
            dquery.append(matmul(keys_t[j * size : (j + 1) * size, :], dscores))
        dq_ref[:, lanes] = (jnp.concatenate(dquery, 0) * factor).astype(BF).T
        dk_ref[:, lanes] = (dkeys * factor).astype(BF)
        dv_ref[:, lanes] = dvalues.astype(BF)
        return 0

    lax.fori_loop(0, DD // LANES, attend_back_group, 0)

    store(late_ref, 0, left_t(a_ref[VIS:, :], dq_ref[...]))
    if fast:
        exchange(2 * (DD // LANES))
    store(late_ref, 1, left_t(a_ref[...], dk_ref[...]))
    store(late_ref, 2, left_t(a_ref[...], dv_ref[...]))

    def start_rows(rows, da):
        unit, rate = normalize(y_ref[rows, :])
        da = da + right_t(dk_ref[rows, :], wide_ref[:, DD : 2 * DD])
        da = da + right_t(dv_ref[rows, :], wide_ref[:, 2 * DD : 3 * DD])
        dh, dgain = normalize_back(unit, rate, gain_one, da)
        vec_ref[0:1, :] += dgain
        return dh

    dy = start_rows(slice(0, VIS), 0.0)
    dy_ref[...] = dy
    vec_ref[3:4, :] += jnp.sum(jnp.where(kept, 0.0, dy), 0, keepdims=True)

    def start_hidden(n, _):
        rows, all_rows = hidden_rows(n)
        dy = start_rows(all_rows, right_t(dq_ref[rows, :], wide_ref[:, :DD]))
        vec_ref[3:4, :] += jnp.sum(dy + dmiddle_ref[rows, :], 0, keepdims=True)
        return 0

    lax.fori_loop(0, 2, start_hidden, 0)
    vec_out[...] = jnp.zeros_like(vec_out)
    for n in range(4):
        vec_out[3 + n // 2 : 4 + n // 2, n % 2 * DD : (n % 2 + 1) * DD] = vec_ref[n : n + 1, :]
    vec_out[5:6, :] = jnp.broadcast_to(jnp.sum(loss_ref[...], 1, keepdims=True), (1, D))
    if fast:
        for u in range(ready):
            for side in range(2):
                copy_a(u, side).wait_send()
                copy_b(u, side).wait_send()


def decoder_step(fast, pos, seen, by_row, by_column, picked, stats, vectors, wide, down):
    owners = lax.axis_size("fsdp")
    scratch = [
        ((TOK_DEV, DD), F32),
        ((TOK_DEV, DD), BF),
        ((HID, DD), BF),
        ((TOK_DEV, DD), BF),
        ((TOK_DEV, DD), BF),
        ((DD // LANES, LANES, HID), BF),
        ((HID, DD), BF),
        ((DD // LANES, LANES * DHEADS // DD, HID), F32),
        ((DD, HEADP), BF),
        ((HID, DD), BF),
        ((HID, DFF), BF),
        ((HID, DD), BF),
        ((HID, HEADP), BF),
        ((HID, DD), BF),
        ((HID, DFF), BF),
        ((HID, DD), BF),
        ((HID, DD), BF),
        ((HID, DD), F32),
        ((HID, DD), BF),
        ((TOK_DEV, DD), BF),
        ((TOK_DEV, DD), BF),
        ((1, HEADP), F32),
        ((TOK_DEV, HID), F32),
        ((PD, LOWP), BF),
        ((LOWP, PD), BF),
        ((8, DD), F32),
    ]
    vmem = pl.BlockSpec(memory_space=pltpu.VMEM)
    early, late = [
        jax.ShapeDtypeStruct((owners // 2, 2, blocks, DD // owners, UNIT), BF)
        for blocks in (EARLY, LATE)
    ]
    ready = EARLY // 2
    dma = pltpu.SemaphoreType.DMA
    scratch = [pltpu.VMEM(*entry) for entry in scratch]
    params = {}
    if fast:
        sums = jax.ShapeDtypeStruct((ready, ROWS, UNIT), F32)
        scratch = [pltpu.VMEM(early.shape, BF)] + scratch
        scratch += [
            pltpu.VMEM((ready, owners // 2, 2, DD // owners, UNIT), BF),
            pltpu.VMEM((ready, 2, 2, ROWS, HALF), BF),
            pltpu.VMEM((ready, 2, 2, ROWS, HALF), BF),
            pltpu.VMEM((ready, 2, ROWS, HALF), BF),
            pltpu.VMEM((ready, 2, ROWS, HALF), BF),
            *[dma((ready, 2))] * 5,
        ]
        params = {"collective_id": 2, "has_side_effects": True}
    else:
        sums = jax.ShapeDtypeStruct((8, LANES), F32)
    outs = (
        late,
        jax.ShapeDtypeStruct((VIS, DD), F32),
        jax.ShapeDtypeStruct((8, D), F32),
        sums,
        *([] if fast else [early]),
    )
    return pl.pallas_call(
        partial(decoder_kernel, owners, fast),
        out_shape=outs,
        in_specs=[vmem] * 9,
        out_specs=(vmem,) * len(outs),
        scratch_shapes=scratch,
        compiler_params=pltpu.CompilerParams(vmem_limit_bytes=60 * 2**20, **params),
        cost_estimate=pl.CostEstimate(
            flops=40 * 10**9, bytes_accessed=40 * 2**20, transcendentals=2 * 10**7
        ),
    )(
        pos,
        seen,
        by_row,
        by_column,
        picked,
        stats,
        vectors,
        wide,
        down,
    )


def block_forward(h, weights, gains, bias, heads, skip):
    wqkv, wout, wup, wdown = weights
    width = h.shape[1]
    normed_a = layer_norm(h, gains[0]).astype(BF)
    query = matmul(normed_a[skip:], wqkv[:, :width]).astype(BF)
    keys = matmul(normed_a, wqkv[:, width : 2 * width]).astype(BF)
    values = matmul(normed_a, wqkv[:, 2 * width :]).astype(BF)
    mixed_t, lse = attend(query.T, keys, values.T, bias, width // heads)
    middle = h[skip:] + left_t(mixed_t, wout)
    normed_b = layer_norm(middle, gains[1]).astype(BF)
    after, slope = gelu_parts(matmul(normed_b, wup))
    hidden = after.astype(BF)
    end = middle + matmul(hidden, wdown)
    return end, (h, normed_a, query, keys, values, mixed_t, lse, middle, normed_b, slope, hidden)


def block_backward(saved, grad, weights, gains, bias, heads, skip):
    wqkv, wout, wup, wdown = weights
    h, normed_a, query, keys, values, mixed_t, lse, middle, normed_b, slope, hidden = saved
    width = h.shape[1]
    dbranch = grad.astype(BF)
    dbefore = (right_t(dbranch, wdown) * slope).astype(BF)
    dmiddle, dgain_two = norm_back(middle, gains[1], right_t(dbefore, wup))
    dmiddle = dmiddle + grad
    dattn = dmiddle.astype(BF)
    dmixed = right_t(dattn, wout).astype(BF)
    dqt, dkeys, dvalues = attend_back(query, keys, values, dmixed, bias, lse, width // heads)
    dquery = dqt.T
    if skip:
        dquery = jnp.pad(dquery, ((skip, 0), (0, 0)))
        dmiddle = jnp.pad(dmiddle, ((skip, 0), (0, 0)))
    dqkv = jnp.concatenate([dquery, dkeys, dvalues], 1)
    dh, dgain_one = norm_back(h, gains[0], right_t(dqkv, wqkv))
    factors = ((normed_a.T, dqkv), (mixed_t, dattn), (normed_b.T, dbefore), (hidden.T, dbranch))
    return (dh + dmiddle, factors, (dgain_one, dgain_two))


def reduce_rows(grad):
    return lax.psum_scatter(grad.astype(BF), "fsdp", scatter_dimension=0, tiled=True)


def enc_split(wide, down):
    return (
        (wide[:, : 3 * D], wide[:, 3 * D : 4 * D], wide[:, 4 * D : 4 * D + FF], down),
        wide[:, 4 * D + FF :],
    )


def advance(weight, mom, avg, grad, rate):
    grad = grad + DECAY * weight
    buf = MOMENTUM * mom + grad
    new = weight - rate * (grad + MOMENTUM * buf)
    return (buf, new, AVERAGE * avg + (1.0 - AVERAGE) * new)


def advance_kernel(rate, *refs):
    grads, weights, moms, avgs, outs = [refs[5 * n : 5 * n + 5] for n in range(4)] + [refs[20:]]

    def update(n):
        weight = weights[n][...]
        grad = grads[n][:, : weight.shape[1]].astype(F32)
        buf, new, avg = advance(weight, moms[n][...], avgs[n][...], grad, rate)
        outs[4 * n][...] = buf
        outs[4 * n + 1][...] = new
        outs[4 * n + 2][...] = avg
        outs[4 * n + 3][...] = new.astype(BF)

    pl.when(pl.program_id(0) == 0)(partial(update, 0))
    for n in range(1, 5):
        update(n)


def advance_all(rate, grads, weights, moms, avgs):
    steps = weights[3].shape[0] // 16

    def spec(n, array):
        if n == 0:
            return pl.BlockSpec(array.shape, lambda i: (0, 0))
        return pl.BlockSpec((array.shape[0] // steps, array.shape[1]), lambda i: (i, 0))

    arrays = [a for group in (grads, weights, moms, avgs) for a in group]
    outs = [(n, jax.ShapeDtypeStruct(w.shape, t)) for n, w in enumerate(weights) for t in (F32, F32, F32, BF)]
    size = sum(w.size for w in weights)
    return pl.pallas_call(
        partial(advance_kernel, rate),
        grid=(steps,),
        out_shape=[out for _, out in outs],
        in_specs=[spec(n % 5, a) for n, a in enumerate(arrays)],
        out_specs=[spec(n, out) for n, out in outs],
        compiler_params=pltpu.CompilerParams(vmem_limit_bytes=58 * 2**20),
        cost_estimate=pl.CostEstimate(flops=12 * size, bytes_accessed=28 * size, transcendentals=0),
    )(*arrays)


def arrange(valid, masked, scene_ids):
    slots = valid.shape[0]
    live = valid > 0
    kinds = jnp.stack([live & (masked == 0), live & (masked > 0), ~live], 1)
    index = jnp.arange(slots, dtype=jnp.int32)
    ranks = matmul((index[None, :] < index[:, None]).astype(BF), kinds.astype(BF)).astype(jnp.int32)
    n_seen, n_hid = [jnp.sum(kinds[:, i].astype(jnp.int32)) for i in range(2)]
    empty = ranks[:, 2]
    to_empty = jnp.where(empty < VIS - n_seen, n_seen + empty, n_seen + n_hid + empty)
    place = jnp.where(
        kinds[:, 0], ranks[:, 0], jnp.where(kinds[:, 1], VIS + ranks[:, 1], to_empty)
    )
    return (place[None, :] == index[:, None]).astype(BF), n_seen, n_hid


def exact_pick(pick, array):
    high = lax.reduce_precision(array, 8, 7)
    rest = array - high
    mid = lax.reduce_precision(rest, 8, 7)
    low = rest - mid
    return (
        matmul(pick, high.astype(BF)) + matmul(pick, mid.astype(BF)) + matmul(pick, low.astype(BF))
    )


def body(
    pixels,
    masked,
    valid,
    scene_ids,
    gsd_index,
    coords,
    embed,
    wide_enc,
    enc_down,
    wide_dec,
    dec_down,
    vectors,
    embed_mom,
    wide_enc_mom,
    enc_down_mom,
    wide_dec_mom,
    dec_down_mom,
    vector_mom,
    embed_avg,
    wide_enc_avg,
    enc_down_avg,
    wide_dec_avg,
    dec_down_avg,
    vector_avg,
):
    slots = pixels.shape[0]
    fast = (lax.axis_size("dp"), lax.axis_size("fsdp")) == (4, 8)
    vector_row = vectors.reshape(1, -1)
    levels = jnp.exp2(0.5 * gsd_index.astype(jnp.float32) - 1.0)
    gains_enc = (vectors[:D], vectors[D : 2 * D])
    gain_enc_out = vectors[2 * D : 3 * D]
    if fast:
        facts = jnp.stack([valid, masked, scene_ids % 2, coords[:, 0], coords[:, 1]])
        facts = jnp.pad(facts, ((0, 3), (0, 0))).astype(F32)
        scale = jnp.pad(jnp.broadcast_to(levels[:, None], (2, LANES)), ((0, 6), (0, 0)))
        w_enc, w_enc_down, w_dec, w_dec_down, picked_hidden, slope, *saved = encoder_forward(
            pixels, facts, scale, vector_row, embed, wide_enc, enc_down, wide_dec, dec_down
        )
        stats, by_row, by_column, pos_dec, bias_enc, *saved = saved
        *factors, h_start, qkv, middle, h_end, seen_out = saved
    else:
        rows_ok = valid.astype(jnp.float32)
        flags = rows_ok * masked.astype(jnp.float32)
        bands = pixels.reshape(slots, BANDS, PATCH * PATCH)
        weighted = bands * rows_ok[:, None, None]
        band_sum = jnp.sum(weighted, axis=(0, 2))
        counts = jnp.stack([jnp.sum(rows_ok), jnp.sum(flags)])
        band_sq = jnp.sum(weighted * bands, axis=(0, 2))
        stats = jnp.concatenate([band_sum, band_sq, counts])
        stats = jnp.broadcast_to(lax.psum(stats, ("dp", "fsdp"))[:, None], (8, LANES))
        pick, n_seen, n_hid = arrange(valid, masked, scene_ids)
        picked_pixels = exact_pick(pick, pixels)
        picked_hidden = picked_pixels[VIS:]
        small = matmul(pick, jnp.concatenate([(scene_ids % 2)[:, None], coords], 1).astype(BF))
        odd, coord = small[:, 0], small[:, 1:]
        scale = jnp.where(odd == 0, levels[0], levels[1])
        index = jnp.arange(slots, dtype=jnp.int32)
        live = jnp.concatenate([index[:VIS] < n_seen, index[:HID] < n_hid])
        allow = live[:, None] & (odd[:, None] == odd[None, :]) | (index[:, None] == index[None, :])
        bias_enc = jnp.where(allow, 0.0, NEGATIVE)[:VIS, :VIS]
        by_row = jnp.pad(jnp.stack([live.astype(F32), odd, odd]), ((0, 5), (0, 0)))
        by_column = by_row.T
        pos_dec = positions(coord, scale, DD)
    count = stats[7, 0]
    if not fast:
        w_embed, w_enc, w_enc_down, w_dec, w_dec_down = [
            lax.all_gather(w.astype(BF), "fsdp", axis=0, tiled=True)
            for w in (embed, wide_enc, enc_down, wide_dec, dec_down)
        ]
        enc_weights, w_link = enc_split(w_enc, w_enc_down)
        mean = jnp.repeat(stats[:3, 0] / (stats[6, 0] * (PATCH * PATCH)), PATCH * PATCH)
        square = jnp.repeat(stats[3:6, 0] / (stats[6, 0] * (PATCH * PATCH)), PATCH * PATCH)
        rate = lax.rsqrt(square - mean * mean + EPS)
        inputs = ((picked_pixels[:VIS] - mean) * rate).astype(BF)
        h_start = matmul(inputs, w_embed) + positions(coord[:VIS], scale[:VIS], D)
        h_end, enc_saved = block_forward(h_start, enc_weights, gains_enc, bias_enc, HEADS, 0)
        encoded = layer_norm(h_end, gain_enc_out).astype(BF)
        seen_out = matmul(encoded, w_link)
    late, dy_seen, vec, ready, *early = decoder_step(
        fast,
        pos_dec,
        seen_out,
        by_row,
        by_column,
        picked_hidden,
        stats,
        vector_row,
        w_dec,
        w_dec_down,
    )
    if fast:
        inputs_t, a_t, mixed_t, b_t, hidden_t, z_t = factors
        *enc_parts, dec_wide, dec_tall, vec = encoder_back(
            dy_seen,
            by_column,
            vec,
            vector_row,
            bias_enc,
            qkv,
            ready,
            late,
            (h_end, middle, h_start, slope),
            w_enc,
            w_enc_down,
            (z_t, hidden_t, b_t, mixed_t, a_t, inputs_t),
        )
        dec_parts = (dec_wide, dec_tall)
        vector_grad, loss_sum = vec[:5].reshape(-1), vec[5, 0]
    else:
        dseen = (dy_seen * by_column[:VIS, 0:1]).astype(BF)
        dec_vec, local_loss = vec[3:5].reshape(-1), vec[5, 0]
        dh_end, dgain_enc_out = norm_back(h_end, gain_enc_out, right_t(dseen, w_link))
        dh_start, enc_factors, dgains_enc = block_backward(
            enc_saved, dh_end, enc_weights, gains_enc, bias_enc, HEADS, 0
        )
        enc_grads = [matmul(*pair).astype(BF) for pair in enc_factors]
        link_grad = left_t(encoded, dseen).astype(BF)
        enc_parts = lax.psum(
            (
                reduce_rows(left_t(inputs, dh_start.astype(BF))),
                reduce_rows(
                    jnp.concatenate([enc_grads[0], enc_grads[1], enc_grads[2], link_grad], 1)
                ),
                reduce_rows(enc_grads[3]),
            ),
            "dp",
        )
        parts = DFF // DD
        early = early[0]
        dec_grads = jnp.concatenate([early[:, :, :parts], late, early[:, :, parts:]], 2)
        dec_grads = dec_grads.reshape(-1, *dec_grads.shape[2:])
        dec_sum = lax.psum(reduce_rows(dec_grads), "dp")[0]
        rows, parts = dec_sum.shape[1], DFF // DD
        dec_parts = (
            dec_sum[parts:].transpose(1, 0, 2).reshape(rows, -1),
            dec_sum[:parts].reshape(-1, DD),
        )
        vector_grad = jnp.concatenate([*dgains_enc, dgain_enc_out, dec_vec])
        vector_grad, loss_sum = lax.psum((vector_grad, local_loss), ("dp", "fsdp"))
    grads = (*enc_parts, *dec_parts)
    rate = STEP_UNIT * (PD * TOK_DEV * lax.axis_size("dp") * lax.axis_size("fsdp")) ** 0.5
    weights = (embed, wide_enc, enc_down, wide_dec, dec_down)
    moms = (embed_mom, wide_enc_mom, enc_down_mom, wide_dec_mom, dec_down_mom)
    avgs = (embed_avg, wide_enc_avg, enc_down_avg, wide_dec_avg, dec_down_avg)
    outs = advance_all(rate, grads, weights, moms, avgs)
    return (*outs, *advance(vectors, vector_mom, vector_avg, vector_grad, rate), loss_sum, count)


def solution(mesh):
    both, rows = P(("dp", "fsdp")), P("fsdp", None)
    placed = (P(("dp", "fsdp"), None), both, both, both, both, P(("dp", "fsdp"), None))
    states = (rows,) * 5 + (P(),)
    return jax.shard_map(
        body,
        mesh=mesh,
        in_specs=placed + states * 3,
        out_specs=(rows,) * 20 + (P(),) * 5,
        check_vma=False,
    )
```

```python
from functools import partial

import jax
import jax.numpy as jnp
from jax import lax
from jax.experimental import pallas as pl
from jax.experimental.pallas import tpu as pltpu
from jax.sharding import PartitionSpec as P

D = 1024
HEADS = 16
FF = 4096
DD = 512
DHEADS = 16
DFF = 2048
PATCH = 16
BANDS = 3
TOK_DEV = 768
PD = 768
LOWD = 192
VIS = 192
HID = TOK_DEV - VIS

EPS = 1e-06
MOMENTUM = 0.9
DECAY = 0.0001
AVERAGE = 0.9
STEP_UNIT = 0.003
NEGATIVE = -1e30
LANES = 128
BF = jnp.bfloat16
F32 = jnp.float32


def matmul(left, right):
    return jnp.dot(left, right, preferred_element_type=jnp.float32)


def left_t(left, right):
    return lax.dot_general(
        left, right, (((0,), (0,)), ((), ())), preferred_element_type=jnp.float32
    )


def right_t(left, right):
    return lax.dot_general(
        left, right, (((1,), (1,)), ((), ())), preferred_element_type=jnp.float32
    )


def layer_norm(h, gain):
    mean = jnp.mean(h, -1, keepdims=True)
    cent = h - mean
    var = jnp.mean(cent * cent, -1, keepdims=True)
    return cent * lax.rsqrt(var + EPS) * gain


def norm_back(h, gain, grad):
    result, pull = jax.vjp(layer_norm, h, gain)
    return pull(grad)


def gelu_parts(before):
    below = 0.5 * (1.0 + lax.erf(before * 0.5**0.5))
    slope = below + before * jnp.exp(before * before * -0.5) * (0.5 / jnp.pi) ** 0.5
    return before * below, slope


def positions(coord, scale, width):
    quarter = width // 4
    omega = 10000.0 ** (-jnp.arange(quarter, dtype=jnp.float32) / quarter)
    angle_x = coord[:, 0:1] * scale[:, None] * omega[None, :]
    angle_y = coord[:, 1:2] * scale[:, None] * omega[None, :]
    return jnp.concatenate(
        [jnp.sin(angle_x), jnp.cos(angle_x), jnp.sin(angle_y), jnp.cos(angle_y)], -1
    )


def row_loss(pred, normed):
    rows = normed.shape[0]
    coarse = jnp.mean(normed.reshape(rows, BANDS, PATCH // 2, 2, PATCH // 2, 2), axis=(3, 5))
    upper = jnp.repeat(jnp.repeat(coarse, 2, axis=2), 2, axis=3).reshape(rows, PD)
    err_high = pred[:, :PD] - (normed - upper)
    err_low = pred[:, PD:] - coarse.reshape(rows, LOWD)
    return jnp.mean(jnp.sqrt(err_high * err_high + 1.0) - 1.0, -1) + jnp.mean(err_low * err_low, -1)


def attend_kernel(size, qt_ref, k_ref, vt_ref, bias_ref, ot_ref, lse_ref):
    per = LANES // size
    row_head = lax.broadcasted_iota(jnp.int32, qt_ref.shape, 0) // size
    factor = size ** (-0.5)
    for j in range(per):
        query = jnp.where(row_head == j, qt_ref[...].astype(F32), 0.0).astype(BF)
        scores = matmul(k_ref[...], query) * factor + bias_ref[...]
        top = jnp.max(scores, 0, keepdims=True)
        probs = jnp.exp(scores - top)
        total = jnp.sum(probs, 0, keepdims=True)
        probs = (probs * (1.0 / total)).astype(BF)
        rows = slice(j * size, (j + 1) * size)
        ot_ref[rows, :] = matmul(vt_ref[rows, :], probs).astype(BF)
        lse_ref[0, j : j + 1, :] = top + jnp.log(total)


def attend(qt, keys, vt, bias, size):
    width, queries = qt.shape
    rows = keys.shape[0]
    groups, per = width // LANES, LANES // size
    return pl.pallas_call(
        partial(attend_kernel, size),
        grid=(groups,),
        out_shape=(
            jax.ShapeDtypeStruct((width, queries), BF),
            jax.ShapeDtypeStruct((groups, per, queries), F32),
        ),
        in_specs=[
            pl.BlockSpec((LANES, queries), lambda g: (g, 0)),
            pl.BlockSpec((rows, LANES), lambda g: (0, g)),
            pl.BlockSpec((LANES, rows), lambda g: (g, 0)),
            pl.BlockSpec((rows, queries), lambda g: (0, 0)),
        ],
        out_specs=(
            pl.BlockSpec((LANES, queries), lambda g: (g, 0)),
            pl.BlockSpec((1, per, queries), lambda g: (g, 0, 0)),
        ),
        compiler_params=pltpu.CompilerParams(vmem_limit_bytes=40 * 2**20),
        cost_estimate=pl.CostEstimate(
            flops=4 * rows * queries * width * per,
            bytes_accessed=4 * rows * queries,
            transcendentals=rows * queries * width // size,
        ),
    )(qt, keys, vt, bias)


def attend_back_kernel(
    size,
    qt_ref,
    q_ref,
    k_ref,
    kt_ref,
    v_ref,
    do_ref,
    dot_ref,
    bias_ref,
    *rest,
):
    *lse_ref, dqt_ref, dk_ref, dv_ref = rest
    per = LANES // size
    row_head = lax.broadcasted_iota(jnp.int32, qt_ref.shape, 0) // size
    lane_head = lax.broadcasted_iota(jnp.int32, dk_ref.shape, 1) // size
    factor = size ** (-0.5)
    dkeys = jnp.zeros(dk_ref.shape, F32)
    dvalues = jnp.zeros(dv_ref.shape, F32)
    for j in range(per):
        query = jnp.where(row_head == j, qt_ref[...].astype(F32), 0.0).astype(BF)
        dout = jnp.where(row_head == j, dot_ref[...].astype(F32), 0.0).astype(BF)
        scores = matmul(k_ref[...], query) * factor + bias_ref[...]
        if lse_ref:
            probs = jnp.exp(scores - lse_ref[0][0, j : j + 1, :])
        else:
            probs = jnp.exp(scores - jnp.max(scores, 0, keepdims=True))
            probs = probs * (1.0 / jnp.sum(probs, 0, keepdims=True))
        dvalues = jnp.where(lane_head == j, matmul(probs.astype(BF), do_ref[...]), dvalues)
        dprobs = matmul(v_ref[...], dout)
        delta = jnp.sum(dprobs * probs, 0, keepdims=True)
        dscores = (probs * (dprobs - delta)).astype(BF)
        dkeys = jnp.where(lane_head == j, matmul(dscores, q_ref[...]), dkeys)
        rows = slice(j * size, (j + 1) * size)
        dqt_ref[rows, :] = (matmul(kt_ref[rows, :], dscores) * factor).astype(BF)
    dk_ref[...] = (dkeys * factor).astype(BF)
    dv_ref[...] = dvalues.astype(BF)


def attend_back(query, keys, values, dmixed, bias, lse, size):
    queries, width = query.shape
    rows = keys.shape[0]
    groups, per = width // LANES, LANES // size
    tall = lambda n: pl.BlockSpec((n, LANES), lambda g: (0, g))
    flat = lambda n: pl.BlockSpec((LANES, n), lambda g: (g, 0))
    return pl.pallas_call(
        partial(attend_back_kernel, size),
        grid=(groups,),
        out_shape=(
            jax.ShapeDtypeStruct((width, queries), BF),
            jax.ShapeDtypeStruct((rows, width), BF),
            jax.ShapeDtypeStruct((rows, width), BF),
        ),
        in_specs=[
            flat(queries),
            tall(queries),
            tall(rows),
            flat(rows),
            tall(rows),
            tall(queries),
            flat(queries),
            pl.BlockSpec((rows, queries), lambda g: (0, 0)),
        ]
        + [pl.BlockSpec((1, per, queries), lambda g: (g, 0, 0))] * (lse is not None),
        out_specs=(flat(queries), tall(rows), tall(rows)),
        compiler_params=pltpu.CompilerParams(vmem_limit_bytes=48 * 2**20),
        cost_estimate=pl.CostEstimate(
            flops=10 * rows * queries * width * per,
            bytes_accessed=4 * rows * queries,
            transcendentals=rows * queries * width // size,
        ),
    )(query.T, query, keys, keys.T, values, dmixed, dmixed.T, bias, *([] if lse is None else [lse]))


MESH = pl.DeviceIdType.MESH
UNIT = 512
HALF = UNIT // 2
ROWS = 128
HALF_ROWS = ROWS // 2
LAGS = (1, 3, 4, 6, 9)


def put(source, target, send, recv, device):
    return pltpu.make_async_remote_copy(
        src_ref=source,
        dst_ref=target,
        send_sem=send,
        recv_sem=recv,
        device_id=device,
        device_id_type=MESH,
    )


def back_kernel(
    dec_units,
    blocks,
    units,
    spots,
    dy_ref,
    column_ref,
    vec_ref,
    vectors_ref,
    bias_ref,
    qkv_ref,
    ready_ref,
    dec_ref,
    end_ref,
    middle_ref,
    start_ref,
    slope_ref,
    wide_ref,
    down_ref,
    *refs,
):
    n_left = max(b[0] for b in blocks) + 1
    lefts, refs = refs[:n_left], refs[n_left:]
    outs, refs = refs[:5], refs[5:]
    vec_out, refs = refs[0], refs[1:]
    (
        xo,
        xp,
        yo,
        yp,
        do,
        dp,
        a_out,
        a_in,
        b_out,
        b_in,
        sums,
        z_out,
        z_one,
        z_two,
        z_ready,
        v_in,
        v_out,
        wide_buf,
        down_buf,
        slope_buf,
        h_buf,
        dend_ref,
        dmid_ref,
        dbranch_ref,
        dmixed_ref,
        dqkv_ref,
        grad_vec,
        wide_sem,
        down_sem,
        slope_sem,
        h_sem,
        dec_sem,
        left_sem,
        right_sem,
        a_send,
        a_recv,
        b_send,
        b_recv,
        z_send,
        z_recv,
        v_send,
        v_recv,
        store_sem,
    ) = refs
    count, extra = dec_units + len(units), z_ready.shape[0]
    z, f = lax.axis_index("dp"), lax.axis_index("fsdp")
    core, place = f % 2, f // 2
    x, y = place % 2, place // 2
    partner = (z, f + 1 - 2 * core)
    x_side = (z, f + 2 - 4 * x)
    y_side = (z, f + 4 - 8 * y)
    at_x, at_y, at_far = place + 1 - 2 * x, place + 2 - 4 * y, 3 - place
    low = z < 2
    outer = (z == 0) | (z == 3)
    inner = (z == 1) | (z == 2)
    inward = (jnp.where(low, 1, 2), f)
    across = (3 - z, f)
    outward = (jnp.where(low, 0, 3), f)

    ring = wide_buf.shape[0]
    up_chunks, out_chunks, qkv_chunks = FF // UNIT, D // UNIT, 3 * D // UNIT
    chunks = 1 + up_chunks + out_chunks + qkv_chunks

    def wide_copy(w):
        inside = jnp.where(w < 1 + up_chunks, 4 * D + UNIT * (w - 1), 3 * D + UNIT * (w - 1 - up_chunks))
        column = jnp.where(
            w == 0,
            4 * D + FF,
            jnp.where(w < 1 + up_chunks + out_chunks, inside, UNIT * (w - 1 - up_chunks - out_chunks)),
        )
        return pltpu.make_async_copy(
            wide_ref.at[:, pl.ds(pl.multiple_of(column, UNIT), UNIT)],
            wide_buf.at[w % ring],
            wide_sem.at[w % ring],
        )

    def down_copy(j):
        rows = pl.ds(pl.multiple_of(j * UNIT, UNIT), UNIT)
        return pltpu.make_async_copy(down_ref.at[rows], down_buf.at[j % 2], down_sem.at[j % 2])

    def slope_copy(j):
        columns = pl.ds(pl.multiple_of(j * UNIT, UNIT), UNIT)
        return pltpu.make_async_copy(slope_ref.at[:, columns], slope_buf.at[j % 2], slope_sem.at[j % 2])

    def h_copy(source):
        return pltpu.make_async_copy(source, h_buf, h_sem.at[0])

    h_copy(end_ref).start()
    for n in range(ring):
        wide_copy(n).start()
    for n in range(2):
        down_copy(n).start()
        slope_copy(n).start()

    barrier = pltpu.get_barrier_semaphore()
    for device in (partner, x_side, y_side):
        pl.semaphore_signal(barrier, inc=1, device_id=device, device_id_type=MESH)

    @pl.when(outer)
    def _():
        pl.semaphore_signal(barrier, inc=1, device_id=inward, device_id_type=MESH)
        pl.semaphore_wait(barrier, 4)

    @pl.when(inner)
    def _():
        pl.semaphore_signal(barrier, inc=1, device_id=across, device_id_type=MESH)
        pl.semaphore_signal(barrier, inc=1, device_id=outward, device_id_type=MESH)
        pl.semaphore_wait(barrier, 5)

    def swap_dec(source, n):
        return put(source, dp.at[n], dec_sem.at[n, 1], dec_sem.at[n, 2], partner)

    def swap_left(source, b):
        return put(source, xp.at[b], left_sem.at[b, 1], left_sem.at[b, 2], partner)

    def swap_right(r):
        return put(yo.at[r], yp.at[r], right_sem.at[r, 0], right_sem.at[r, 1], partner)

    for n in range(dec_units):
        swap_dec(dec_ref.at[:, 1 - core, n], n).start()
        pltpu.make_async_copy(dec_ref.at[:, core, n], do.at[n], dec_sem.at[n, 0]).start()
    for b, (left, sub) in enumerate(blocks):
        rows = pl.ds(sub * ROWS, ROWS)
        swap_left(lefts[left].at[:, 1 - core, rows], b).start()
        pltpu.make_async_copy(lefts[left].at[:, core, rows], xo.at[b], left_sem.at[b, 0]).start()

    firsts = 1 + out_chunks
    single = next(n for n in range(1, len(units)) if units[n][1] >= firsts)
    starts = [n for n in range(1, len(units)) if units[n][0] != units[n - 1][0]]

    def block_of(e):
        return sum([jnp.where(e >= n, 1, 0) for n in starts], jnp.int32(0))

    def right_of(e):
        early = jnp.where(e == 0, 0, 1 + (e + out_chunks - 1) % out_chunks)
        return jnp.where(e < single, early, e - single + firsts)

    first, second = pl.ds(0, HALF), pl.ds(HALF, HALF)

    def ready_part(n, owners, columns):
        parts = [do[n, o, :, columns].astype(F32) + dp[n, o, :, columns].astype(F32) for o in owners]
        return parts[0] if len(parts) == 1 else jnp.concatenate(parts, 0)

    def formed_part(e, owners, columns):
        b, r = block_of(e), right_of(e)
        mine, other = [jnp.concatenate([ref[b, o] for o in owners], 0) for ref in (xo, xp)]
        return matmul(mine, yo[r, :, columns]) + matmul(other, yp[r, :, columns])

    def on_unit(u, stage):
        @pl.when(u < dec_units)
        def _():
            stage(partial(ready_part, jnp.minimum(u, dec_units - 1)))

        @pl.when(u >= dec_units)
        def _():
            stage(partial(formed_part, jnp.maximum(u - dec_units, 0)))

    def copy_a(u, side):
        slot = u % a_out.shape[0]
        return put(
            a_out.at[slot, side],
            a_in.at[u, side],
            a_send.at[slot, side],
            a_recv.at[u, side],
            (x_side, y_side)[side],
        )

    def copy_b(u, side):
        slot = u % b_out.shape[0]
        return put(
            b_out.at[slot, side],
            b_in.at[u, side],
            b_send.at[slot, side],
            b_recv.at[u, side],
            (y_side, x_side)[side],
        )

    z_slots = z_out.shape[0]

    def copy_in(u):
        return put(z_out.at[u % z_slots], z_one.at[u], z_send.at[u, 0], z_recv.at[u, 0], inward)

    def copy_across(u):
        return put(z_out.at[u % z_slots], z_two.at[u], z_send.at[u, 0], z_recv.at[u, 1], across)

    def copy_out(u):
        return put(z_one.at[u], z_one.at[u], z_send.at[u, 1], z_recv.at[u, 0], outward)

    def ready_in(n):
        u = count + n
        return put(z_ready.at[n], z_one.at[u], z_send.at[u, 0], z_recv.at[u, 0], inward)

    def ready_across(n):
        u = count + n
        return put(z_ready.at[n], z_two.at[u], z_send.at[u, 0], z_recv.at[u, 1], across)

    def copy_v(step, device):
        return put(v_out.at[step], v_in.at[step], v_send.at[step], v_recv.at[step], device)

    gain_one, gain_two, gain_out = [vectors_ref[:, n * D : (n + 1) * D] for n in range(3)]

    def give(r, value):
        yo[r] = value
        swap_right(r).start()

    def columns_at(n):
        return slice(n * UNIT, (n + 1) * UNIT)

    def back_link():
        dseen = jnp.where(column_ref[:VIS, 0:1] > 0, dy_ref[...], 0.0).astype(BF)
        give(0, dseen)
        wide_copy(0).wait()
        h_copy(end_ref).wait()
        unit, rate = normalize(h_buf[...])
        dend, dgain = normalize_back(unit, rate, gain_out, right_t(dseen, wide_buf[0]))
        grad_vec[...] = vec_ref[...]
        grad_vec[2:3, :] = dgain
        dend_ref[...] = dend
        dbranch_ref[...] = dend.astype(BF)
        for n in range(out_chunks):
            give(1 + n, dbranch_ref[:, columns_at(n)])
        wide_copy(ring).start()
        h_copy(middle_ref).start()
        dmid_ref[...] = jnp.zeros_like(dmid_ref)

    def back_hidden(j):
        w = 1 + j
        down_copy(j).wait()
        slope_copy(j).wait()
        wide_copy(w).wait()
        dhidden = right_t(dbranch_ref[...], down_buf[j % 2])
        dbefore = (dhidden * slope_buf[j % 2]).astype(BF)
        give(firsts + j, dbefore)
        dmid_ref[...] += right_t(dbefore, wide_buf[w % ring])
        wide_copy(w + ring).start()

        @pl.when(j + 2 < up_chunks)
        def _():
            down_copy(j + 2).start()
            slope_copy(j + 2).start()

    def back_out():
        h_copy(middle_ref).wait()
        unit, rate = normalize(h_buf[...])
        dmiddle, dgain = normalize_back(unit, rate, gain_two, dmid_ref[...])
        grad_vec[1:2, :] = dgain
        dmiddle = dmiddle + dend_ref[...]
        dend_ref[...] = dmiddle
        dattn = dmiddle.astype(BF)
        dmixed = jnp.zeros((VIS, D), F32)
        for n in range(out_chunks):
            w = 1 + up_chunks + n
            piece = dattn[:, columns_at(n)]
            give(firsts + up_chunks + n, piece)
            wide_copy(w).wait()
            dmixed = dmixed + right_t(piece, wide_buf[w % ring])
            wide_copy(w + ring).start()
        dmixed_ref[...] = dmixed.astype(BF)
        h_copy(start_ref).start()
        dmid_ref[...] = jnp.zeros_like(dmid_ref)

    size = D // HEADS
    lane_head = lax.broadcasted_iota(jnp.int32, (VIS, LANES), 1) // size

    def only(array, j):
        return jnp.where(lane_head == j, array.astype(F32), 0.0).astype(BF)

    def back_attention(g):
        at = [pl.ds(pl.multiple_of(n * D + g * LANES, LANES), LANES) for n in range(3)]
        query, keys, values = [qkv_ref[:, lanes] for lanes in at]
        dout = dmixed_ref[:, at[0]]
        keys_t = keys.T
        factor = size ** (-0.5)
        dkeys, dvalues = jnp.zeros((VIS, LANES), F32), jnp.zeros((VIS, LANES), F32)
        dquery = []
        for j in range(LANES // size):
            scores = right_t(keys, only(query, j)) * factor + bias_ref[...]
            probs = jnp.exp(scores - jnp.max(scores, 0, keepdims=True))
            probs = probs * (1.0 / jnp.sum(probs, 0, keepdims=True))
            dvalues = jnp.where(lane_head == j, matmul(probs.astype(BF), dout), dvalues)
            dprobs = right_t(values, only(dout, j))
            delta = jnp.sum(dprobs * probs, 0, keepdims=True)
            dscores = (probs * (dprobs - delta)).astype(BF)
            dkeys = jnp.where(lane_head == j, matmul(dscores, query), dkeys)
            dquery.append(matmul(keys_t[j * size : (j + 1) * size, :], dscores))
        dqkv_ref[:, at[0]] = (jnp.concatenate(dquery, 0) * factor).astype(BF).T
        dqkv_ref[:, at[1]] = (dkeys * factor).astype(BF)
        dqkv_ref[:, at[2]] = dvalues.astype(BF)

    def give_qkv():
        for c in range(qkv_chunks):
            give(firsts + up_chunks + out_chunks + c, dqkv_ref[:, columns_at(c)])

    def back_qkv(c):
        w = 1 + up_chunks + out_chunks + c
        wide_copy(w).wait()
        piece = dqkv_ref[:, pl.ds(pl.multiple_of(c * UNIT, UNIT), UNIT)]
        dmid_ref[...] += right_t(piece, wide_buf[w % ring])

        @pl.when(w + ring < chunks)
        def _():
            wide_copy(w + ring).start()

    def back_start():
        h_copy(start_ref).wait()
        unit, rate = normalize(h_buf[...])
        dh, dgain = normalize_back(unit, rate, gain_one, dmid_ref[...])
        grad_vec[0:1, :] = dgain
        dh = (dh + dend_ref[...]).astype(BF)
        for n in range(out_chunks):
            give(firsts + up_chunks + out_chunks + qkv_chunks + n, dh[:, columns_at(n)])

    at_hidden = 1
    at_out = at_hidden + up_chunks
    at_attention = at_out + 1
    groups = D // LANES
    at_qkv = at_attention + groups
    at_start = at_qkv + qkv_chunks
    at_vec = at_start + 1

    def step(i, _):
        def stage(lag, also=None):
            u = i - lag
            ok = (u >= 0) & (u < count)
            if also is not None:
                ok = ok & also
            return u, pl.when(ok)

        u0, when = stage(0)

        @when
        def _():
            u = u0

            @pl.when(u < dec_units)
            def _():
                pltpu.make_async_copy(do.at[u], do.at[u], dec_sem.at[u, 0]).wait()
                swap_dec(do.at[u], u).wait()

            @pl.when(u == dec_units)
            def _():
                for b in range(len(blocks)):
                    pltpu.make_async_copy(xo.at[b], xo.at[b], left_sem.at[b, 0]).wait()
                    swap_left(xo.at[b], b).wait()
                for r in range(firsts):
                    swap_right(r).wait()

            @pl.when(u >= dec_units + single)
            def _():
                swap_right(u - dec_units - single + firsts).wait()

            @pl.when(u >= a_out.shape[0])
            def _():
                for side in range(2):
                    copy_a(u - a_out.shape[0], side).wait_send()

            slot = u % a_out.shape[0]

            def send(part):
                for side, (near, columns) in enumerate(((at_x, first), (at_y, second))):
                    both = part((near, at_far), columns).astype(BF)
                    a_out[slot, side] = both.reshape(2, ROWS, HALF)

            on_unit(u, send)
            for side in range(2):
                copy_a(u, side).start()

        u1, when = stage(LAGS[0])

        @when
        def _():
            u = u1
            slot = u % b_out.shape[0]

            @pl.when(u >= b_out.shape[0])
            def _():
                for side in range(2):
                    copy_b(u - b_out.shape[0], side).wait_send()

            for side in range(2):
                copy_a(u, side).wait_recv()

            def send(part):
                for side, (near, columns) in enumerate(((at_y, first), (at_x, second))):
                    total = part((near,), columns) + a_in[u, side, 1].astype(F32)
                    b_out[slot, side] = total.astype(BF)

            on_unit(u, send)
            for side in range(2):
                copy_b(u, side).start()

        u2, when = stage(LAGS[1])

        @when
        def _():
            u = u2
            copy_b(u, 0).wait_recv()
            copy_b(u, 1).wait_recv()

            def keep(part):
                whole = part((place,), slice(None))
                for side, columns in enumerate((slice(0, HALF), slice(HALF, UNIT))):
                    total = whole[:, columns] + a_in[u, side, 0].astype(F32)
                    sums[u % 4, :, columns] = total + b_in[u, side].astype(F32)

            on_unit(u, keep)

            @pl.when(outer)
            def _():
                @pl.when(u >= z_slots)
                def _():
                    copy_in(u - z_slots).wait_send()

                z_out[u % z_slots] = sums[u % 4].astype(BF)
                copy_in(u).start()

        u3, when = stage(LAGS[2], inner)

        @when
        def _():
            u = u3
            copy_in(u).wait_recv()

            @pl.when(u >= z_slots)
            def _():
                copy_across(u - z_slots).wait_send()

            z_out[u % z_slots] = (sums[u % 4] + z_one[u].astype(F32)).astype(BF)
            copy_across(u).start()

        u4, when = stage(LAGS[3], inner)

        @when
        def _():
            u = u4
            copy_across(u).wait_recv()
            z_one[u] = (z_out[u % z_slots].astype(F32) + z_two[u].astype(F32)).astype(BF)
            copy_out(u).start()

        u5, when = stage(LAGS[4], outer)

        @when
        def _():
            copy_out(u5).wait_recv()

        ends = [lag - LAGS[1] for lag in LAGS[2:]]

        @pl.when((i < extra) & outer)
        def _():
            z_ready[i] = ready_ref[i].astype(BF)
            ready_in(i).start()

        @pl.when((i >= ends[0]) & (i < extra + ends[0]) & inner)
        def _():
            n = i - ends[0]
            ready_in(n).wait_recv()
            z_ready[n] = (ready_ref[n] + z_one[count + n].astype(F32)).astype(BF)
            ready_across(n).start()

        @pl.when((i >= ends[1]) & (i < extra + ends[1]) & inner)
        def _():
            n = i - ends[1]
            ready_across(n).wait_recv()
            total = z_ready[n].astype(F32) + z_two[count + n].astype(F32)
            z_one[count + n] = total.astype(BF)
            copy_out(count + n).start()

        @pl.when((i >= ends[2]) & (i < extra + ends[2]) & outer)
        def _():
            copy_out(count + i - ends[2]).wait_recv()

        pl.when(i == 0)(back_link)

        @pl.when((i >= at_hidden) & (i < at_hidden + up_chunks))
        def _():
            back_hidden(i - at_hidden)

        pl.when(i == at_out)(back_out)

        @pl.when((i >= at_attention) & (i < at_attention + groups))
        def _():
            back_attention(i - at_attention)

        pl.when(i == at_qkv)(give_qkv)

        @pl.when((i >= at_qkv) & (i < at_qkv + qkv_chunks))
        def _():
            back_qkv(i - at_qkv)

        pl.when(i == at_start)(back_start)

        for number, device in enumerate((partner, x_side, y_side)):

            @pl.when(i == at_vec + number)
            def _():
                if number == 0:
                    v_out[0] = grad_vec[...]
                else:
                    copy_v(number - 1, (partner, x_side, y_side)[number - 1]).wait_recv()
                    v_out[number] = v_out[number - 1] + v_in[number - 1]
                copy_v(number, device).start()

        @pl.when(i == at_vec + 3)
        def _():
            copy_v(2, y_side).wait_recv()
            v_out[3] = v_out[2] + v_in[2]

            @pl.when(outer)
            def _():
                copy_v(3, inward).start()

        @pl.when((i == at_vec + 4) & inner)
        def _():
            copy_v(3, inward).wait_recv()
            v_out[4] = v_out[3] + v_in[3]
            copy_v(4, across).start()

        @pl.when((i == at_vec + 5) & inner)
        def _():
            copy_v(4, across).wait_recv()
            v_out[5] = v_out[4] + v_in[4]
            copy_v(5, outward).start()
            vec_out[...] = v_out[5]

        @pl.when((i == at_vec + 7) & outer)
        def _():
            copy_v(5, outward).wait_recv()
            vec_out[...] = v_in[5]

        return 0

    lax.fori_loop(0, count + LAGS[4], step, 0)

    stores = []
    for n, (u, start, out, row, rows, column) in enumerate(spots):
        stores.append(
            pltpu.make_async_copy(
                z_one.at[u, pl.ds(start, rows)],
                outs[out].at[pl.ds(row, rows), pl.ds(column, UNIT)],
                store_sem.at[n],
            )
        )
    for store in stores:
        store.start()
    for u in range(count - a_out.shape[0], count):
        for side in range(2):
            copy_a(u, side).wait_send()
    for u in range(count - b_out.shape[0], count):
        for side in range(2):
            copy_b(u, side).wait_send()
    for number, device in enumerate((partner, x_side, y_side)):
        copy_v(number, device).wait_send()
    for store in stores:
        store.wait()

    @pl.when(outer)
    def _():
        copy_v(3, inward).wait_send()
        for u in range(count - z_slots, count):
            copy_in(u).wait_send()
        for n in range(extra):
            ready_in(n).wait_send()

    @pl.when(inner)
    def _():
        copy_v(4, across).wait_send()
        copy_v(5, outward).wait_send()
        for u in range(count - z_slots, count):
            copy_across(u).wait_send()
        for n in range(extra):
            ready_across(n).wait_send()

        def drain(u, _):
            copy_out(u).wait_send()
            return 0

        lax.fori_loop(0, count + extra, drain, 0)


def encoder_back(dy, by_column, vec, vectors, bias, qkv, ready, dec, states, wide, down, lefts):
    owners = lax.axis_size("fsdp")
    own = PD // owners
    dec_units = LATE // 2
    dec = dec.reshape(4, 2, dec_units, ROWS, UNIT)
    half = ROWS // 2
    blocks, units, spots = [], [], []
    def add(left, sub, right, out, row, rows, column, columns):
        blocks.append((left, sub))
        for n in range(columns // UNIT):
            spots.append((dec_units + len(units), 0, out, row, rows, column + n * UNIT))
            units.append((len(blocks) - 1, right + n))

    subs = FF // owners // ROWS
    add(0, 0, 0, 1, 0, ROWS, 4 * D + FF, DD)
    for n in range(subs):
        add(1, n, 1, 2, n * ROWS, ROWS, 0, D)
    right = 1 + D // UNIT
    add(2, 0, right, 1, 0, ROWS, 4 * D, FF)
    right += FF // UNIT
    add(3, 0, right, 1, 0, ROWS, 3 * D, D)
    right += D // UNIT
    add(4, 0, right, 1, 0, ROWS, 0, 3 * D)
    right += 3 * D // UNIT
    add(5, 0, right, 0, 0, own, 0, D)
    right += D // UNIT
    count = dec_units + len(units)
    tall = DFF // DD
    for n in range(EARLY + LATE):
        if tall <= n < tall + LATE:
            unit = (n - tall) // 2
        else:
            unit = count + (n if n < tall else n - LATE) // 2
        place = (4, n * half, half, 0) if n < tall else (3, 0, half, (n - tall) * UNIT)
        spots.append((unit, n % 2 * half, *place))
    full = count + ready.shape[0]
    shapes = ((own, D), (ROWS, 4 * D + FF + DD), (FF // owners, D), (half, 10 * UNIT), (DFF // owners, DD))
    lefts = [a.reshape(4, 2, -1, VIS) for a in lefts]
    slots = 3
    dma = pltpu.SemaphoreType.DMA
    vmem, anywhere = pl.BlockSpec(memory_space=pltpu.VMEM), pl.BlockSpec(memory_space=pl.ANY)
    return pl.pallas_call(
        partial(back_kernel, dec_units, tuple(blocks), tuple(units), tuple(spots)),
        out_shape=tuple(jax.ShapeDtypeStruct(shape, BF) for shape in shapes)
        + (jax.ShapeDtypeStruct(vec.shape, F32),),
        in_specs=[vmem] * 7 + [anywhere] * (7 + len(lefts)),
        out_specs=(anywhere,) * len(shapes) + (vmem,),
        scratch_shapes=[
            pltpu.VMEM((len(blocks), 4, ROWS, VIS), BF),
            pltpu.VMEM((len(blocks), 4, ROWS, VIS), BF),
            pltpu.VMEM((right, VIS, UNIT), BF),
            pltpu.VMEM((right, VIS, UNIT), BF),
            pltpu.VMEM((dec_units, 4, ROWS, UNIT), BF),
            pltpu.VMEM((dec_units, 4, ROWS, UNIT), BF),
            pltpu.VMEM((slots, 2, 2, ROWS, HALF), BF),
            pltpu.VMEM((count, 2, 2, ROWS, HALF), BF),
            pltpu.VMEM((slots, 2, ROWS, HALF), BF),
            pltpu.VMEM((count, 2, ROWS, HALF), BF),
            pltpu.VMEM((4, ROWS, UNIT), F32),
            pltpu.VMEM((6, ROWS, UNIT), BF),
            pltpu.VMEM((full, ROWS, UNIT), BF),
            pltpu.VMEM((full, ROWS, UNIT), BF),
            pltpu.VMEM(ready.shape, BF),
            pltpu.VMEM((6, *vec.shape), F32),
            pltpu.VMEM((6, *vec.shape), F32),
            pltpu.VMEM((3, D, UNIT), BF),
            pltpu.VMEM((2, UNIT, D), BF),
            pltpu.VMEM((2, VIS, UNIT), F32),
            pltpu.VMEM((VIS, D), F32),
            pltpu.VMEM((VIS, D), F32),
            pltpu.VMEM((VIS, D), F32),
            pltpu.VMEM((VIS, D), BF),
            pltpu.VMEM((VIS, D), BF),
            pltpu.VMEM((VIS, 3 * D), BF),
            pltpu.VMEM(vec.shape, F32),
            dma((3,)),
            dma((2,)),
            dma((2,)),
            dma((1,)),
            dma((dec_units, 3)),
            dma((len(blocks), 3)),
            dma((right, 2)),
            dma((slots, 2)),
            dma((count, 2)),
            dma((slots, 2)),
            dma((count, 2)),
            dma((full, 2)),
            dma((full, 2)),
            dma((6,)),
            dma((6,)),
            dma((len(spots),)),
        ],
        compiler_params=pltpu.CompilerParams(
            collective_id=0, has_side_effects=True, vmem_limit_bytes=61 * 2**20
        ),
        cost_estimate=pl.CostEstimate(
            flops=30 * 10**9, bytes_accessed=300 * 2**20, transcendentals=0
        ),
    )(dy, by_column, vec, vectors, bias, qkv, ready, dec, *states, wide, down, *lefts)


def encoder_pieces(shapes):
    (own, width), (rows, _), (tall, _), (dec_rows, dec_width), (dec_tall, _) = shapes
    half = dec_rows // 2
    named = {"embed": (0, 0, own, 0, width, 0), "out": (1, 0, rows, 3 * D, D, 1)}
    named["link"] = (1, 0, rows, 4 * D + FF, DD, 0)
    named["tall"] = (4, 0, dec_tall, 0, DD, 0)
    for n in range(3):
        named["qkv", n] = (1, 0, rows, n * D, D, (1, 2, 0)[n])
    for n in range(FF // D):
        named["up", n] = (1, 0, rows, 4 * D + n * D, D, (2, 0, 1, 2)[n])
    for n in range(tall // rows):
        named["down", n] = (2, n * rows, rows, 0, D, (0, 1, 2, 0)[n])
    for n in range(2):
        named["wide", n] = (3, n * half, half, 0, dec_width, n + 1)
    order = [("qkv", 0), ("qkv", 1), "out", ("up", 0), "embed", ("qkv", 2), ("up", 2), ("up", 3)]
    order += [("up", 1), ("down", 1), ("down", 2), ("down", 0), ("wide", 0), ("wide", 1)]
    order += [("down", 3), "link", "tall"]
    return [named[name] for name in order], {name: t for t, name in enumerate(order)}


def norm_rows(h, gain):
    mean = jnp.mean(h, -1, keepdims=True)
    cent = h - mean
    var = jnp.mean(cent * cent, -1, keepdims=True)
    return (cent * lax.rsqrt(var + EPS) * gain).astype(BF)


def encoder_kernel(
    pixels_ref,
    row_ref,
    column_ref,
    scale_ref,
    omega_ref,
    vectors_ref,
    embed_ref,
    wide_ref,
    down_ref,
    dec_wide_ref,
    dec_down_ref,
    wide_out,
    down_out,
    dec_wide_out,
    dec_down_out,
    picked_out,
    slope_out,
    stats_out,
    by_row,
    by_column,
    pos_out,
    bias_out,
    inputs_t,
    a_t,
    mixed_t,
    b_t,
    hidden_t,
    z_t,
    start_ref,
    qkv_ref,
    middle_ref,
    end_ref,
    seen_ref,
    inputs_ref,
    a_ref,
    mixed_ref,
    b_ref,
    hidden_ref,
    z_ref,
    w_embed,
    w_wide,
    w_down,
    stage_ref,
    pick_ref,
    high_ref,
    mid_ref,
    low_ref,
    picked_ref,
    pos_ref,
    bias_ref,
    dec_stage,
    dec_stage_down,
    dec_own,
    dec_own_down,
    slope_ref,
    hidden_pixels,
    v_in,
    v_out,
    load_sem,
    store_sem,
    send_sem,
    recv_sem,
    v_send,
    v_recv,
    side_sem,
):
    shards = (embed_ref, wide_ref, down_ref, dec_wide_ref, dec_down_ref)
    gathered = (w_embed, w_wide, w_down, dec_wide_out, dec_down_out)
    gain_one, gain_two, gain_out = [vectors_ref[:, n * D : (n + 1) * D] for n in range(3)]
    pieces, at = encoder_pieces([ref.shape for ref in shards])
    count = len(pieces)
    stores = []
    z, f = lax.axis_index("dp"), lax.axis_index("fsdp")
    core, place = f % 2, f // 2
    x, y = place % 2, place // 2
    f_x, f_y, f_far = f + 2 - 4 * x, f + 4 - 8 * y, f + 6 - 4 * x - 8 * y
    partner = (z, f + 1 - 2 * core)
    x_side, y_side, z_side = (z, f_x), (z, f_y), (z + 1 - 2 * (z % 2), f)
    outer = (z == 0) | (z == 3)
    inner = (z == 1) | (z == 2)
    across = (3 - z, f)

    barrier = pltpu.get_barrier_semaphore()
    for device in (partner, x_side, y_side, z_side):
        pl.semaphore_signal(barrier, inc=1, device_id=device, device_id_type=MESH)

    @pl.when(outer)
    def _():
        pl.semaphore_wait(barrier, 4)

    @pl.when(inner)
    def _():
        pl.semaphore_signal(barrier, inc=1, device_id=across, device_id_type=MESH)
        pl.semaphore_wait(barrier, 5)

    stages = stage_ref.shape[0]

    def load(t):
        array, row, rows, column, columns, _ = pieces[t]
        return pltpu.make_async_copy(
            shards[array].at[pl.ds(row, rows), pl.ds(column, columns)],
            stage_ref.at[staged[t], pl.ds(0, rows), pl.ds(0, columns)],
            load_sem.at[staged[t]],
        )

    encoder = [t for t, piece in enumerate(pieces) if piece[0] < 3]
    staged = {t: n % stages for n, t in enumerate(encoder)}
    after = dict(zip(encoder, encoder[stages:]))
    dec_loads = [
        pltpu.make_async_copy(dec_wide_ref, dec_stage, side_sem.at[0]),
        pltpu.make_async_copy(dec_down_ref, dec_stage_down, side_sem.at[1]),
    ]
    for copy in dec_loads:
        copy.start()
    for t in encoder[:stages]:
        load(t).start()

    def spot(t, owner, half=None):
        array, row, rows, column, columns, _ = pieces[t]
        if array > 2:
            if half is not None:
                rows //= 2
                row += half * rows
            return gathered[array].at[owner, pl.ds(row, rows)]
        if half is not None:
            columns //= 2
            column += half * columns
        return gathered[array].at[owner, pl.ds(row, rows), pl.ds(column, columns)]

    def move(t, owner, send, recv, device, half=None):
        target = source = spot(t, owner, half)
        array, row, rows = pieces[t][:3]
        if send < 3 and array > 2:
            source = (dec_own, dec_own_down)[array - 3].at[pl.ds(row, rows)]
        return put(source, target, send_sem.at[t, send], recv_sem.at[t, recv], device)

    def own_x(t):
        return move(t, f, 0, 0, x_side)

    def own_y(t):
        return move(t, f, 1, 1, y_side)

    def own_core(t):
        return move(t, f, 2, 4, partner)

    def far_x(t):
        return move(t, f_y, 3, 2, x_side, 0)

    def far_y(t):
        return move(t, f_x, 4, 3, y_side, 1)

    def to_core(t, n):
        return move(t, (f_x, f_y, f_far)[n], 5 + n, 5 + n, partner)

    def to_z(t, n):
        return move(t, (f_x, f_y, f_far)[n], 8 + n, 8 + n, z_side)

    def brings(t, then, other=None):
        kind = pieces[t][5]
        if kind == 0:
            then()
            return
        pl.when(z % 2 == kind - 1)(then)
        if other is not None:
            pl.when(z % 2 != kind - 1)(other)

    def first(t):
        array, row, rows, column, columns, _ = pieces[t]
        if array < 3:
            load(t).wait()
            spot(t, f)[...] = stage_ref[staged[t], :rows, :columns].astype(BF)
            if t in after:
                load(after[t]).start()
        else:
            if row == 0:
                dec_loads[array - 3].wait()
            own = (dec_own, dec_own_down)[array - 3]
            own[row : row + rows, :] = (dec_stage, dec_stage_down)[array - 3][
                row : row + rows, :
            ].astype(BF)
            store = pltpu.make_async_copy(own.at[pl.ds(row, rows)], spot(t, f), store_sem.at[t])
            store.start()
            stores.append(store)
        own_core(t).start()

        def then():
            own_x(t).start()
            own_y(t).start()

        brings(t, then)

    def second(t):
        def then():
            own_x(t).wait_recv()
            far_y(t).start()
            own_y(t).wait_recv()
            far_x(t).start()
            for n in range(2):
                to_core(t, n).start()
                if pieces[t][5]:
                    to_z(t, n).start()

        brings(t, then)

    def third(t):
        def then():
            far_x(t).wait_recv()
            far_y(t).wait_recv()
            to_core(t, 2).start()
            if pieces[t][5]:
                to_z(t, 2).start()

        brings(t, then)

    def taken(t, n):
        def other():
            to_z(t, n).wait_recv()
            to_core(t, n).start()

        brings(t, lambda: None, other)

    def whole(t):
        own_core(t).wait_recv()
        for n in range(3):
            to_core(t, n).wait_recv()

    def drain(t):
        own_core(t).wait_send()
        for n in range(3):
            to_core(t, n).wait_send()

        def then():
            for copy in (own_x(t), own_y(t), far_x(t), far_y(t)):
                copy.wait_send()
            if pieces[t][5]:
                for n in range(3):
                    to_z(t, n).wait_send()

        brings(t, then)

    def copy_v(step, device):
        return put(v_out.at[step], v_in.at[step], v_send.at[step], v_recv.at[step], device)

    sides = (partner, x_side, y_side)

    def statistics(i):
        if i <= 3:
            if i > 0:
                copy_v(i - 1, sides[i - 1]).wait_recv()
                v_out[i] = v_out[i - 1] + v_in[i - 1]
            if i < 3:
                copy_v(i, sides[i]).start()
            else:

                @pl.when(outer)
                def _():
                    copy_v(3, z_side).start()

        if i == 4:

            @pl.when(inner)
            def _():
                copy_v(3, z_side).wait_recv()
                v_out[4] = v_out[3] + v_in[3]
                copy_v(4, across).start()

        if i == 5:

            @pl.when(inner)
            def _():
                copy_v(4, across).wait_recv()
                v_out[5] = v_out[4] + v_in[4]
                copy_v(5, z_side).start()
                stats_out[...] = v_out[5]

            @pl.when(outer)
            def _():
                copy_v(5, z_side).wait_recv()
                stats_out[...] = v_in[5]

    def turn(source, target, start=0, width=D):
        for lane in range(start, start + width, LANES):
            target[lane : lane + LANES, :] = source[:, lane : lane + LANES].T

    def columns_of(t):
        array, row, rows, column, columns, _ = pieces[t]
        weight = gathered[array][:, row : row + rows, column : column + columns]
        return weight.reshape(-1, columns)

    def local_statistics():
        pixels = pixels_ref[...]
        weighted = pixels * column_ref[:, 0:1]
        sums = jnp.sum(weighted, 0, keepdims=True)
        squares = jnp.sum(weighted * pixels, 0, keepdims=True)
        live = row_ref[0:1, :]
        totals = [r[:, n * PATCH**2 : (n + 1) * PATCH**2] for r in (sums, squares) for n in range(BANDS)]
        for n, total in enumerate((*totals, live, live * row_ref[1:2, :])):
            v_out[0, n : n + 1, :] = jnp.broadcast_to(jnp.sum(total, 1, keepdims=True), (1, LANES))

    def arrange_step():
        slots = (TOK_DEV, TOK_DEV)
        down, along = [lax.broadcasted_iota(jnp.int32, slots, n) for n in range(2)]
        live, masked = row_ref[0:1, :], row_ref[1:2, :]
        seen, hid = live * (1.0 - masked), live * masked
        kind = lax.broadcasted_iota(jnp.int32, row_ref.shape, 0)
        kinds = jnp.where(kind == 0, seen, jnp.where(kind == 1, hid, 1.0 - live))
        ranks = matmul(kinds.astype(BF), jnp.where(down < along, 1.0, 0.0).astype(BF))
        n_seen, n_hid = [jnp.sum(r, 1, keepdims=True) for r in (seen, hid)]
        empty = ranks[2:3, :]
        place = jnp.where(empty < VIS - n_seen, n_seen + empty, n_seen + n_hid + empty)
        place = jnp.where(hid > 0, VIS + ranks[1:2, :], place)
        place = jnp.where(seen > 0, ranks[0:1, :], place)
        pick_ref[...] = jnp.where(down == place.astype(jnp.int32), 1.0, 0.0).astype(BF)
        facts = row_ref[...].astype(BF)
        by_row[...] = right_t(facts, pick_ref[...])
        by_column[...] = right_t(pick_ref[...], facts)
        pixels = pixels_ref[...]
        high = pixels.astype(BF)
        rest = pixels - high.astype(F32)
        mid = rest.astype(BF)
        high_ref[...], mid_ref[...] = high, mid
        low_ref[...] = (rest - mid.astype(F32)).astype(BF)

    def pick_rows(rows):
        pick = pick_ref[rows, :]
        return matmul(pick, high_ref[...]) + matmul(pick, mid_ref[...]) + matmul(pick, low_ref[...])

    def pick_step():
        picked_ref[...] = pick_rows(slice(0, VIS))
        same = by_column[:VIS, 2:3] == by_row[2:3, :VIS]
        shape = (VIS, VIS)
        bias_out[...] = mask_bias(by_column[:VIS, 0:1] > 0, same, shape, 0)
        bias_ref[...] = mask_bias(by_row[0:1, :VIS] > 0, same, shape, 0, 1)

    def position_rows(target, rows, width, row):
        quarter = width // 4
        odd = by_column[rows, 2:3] > 0
        scale = jnp.where(odd, scale_ref[1:2, 0:1], scale_ref[0:1, 0:1])
        for n in range(2):
            angle = by_column[rows, 3 + n : 4 + n] * scale * omega_ref[row : row + 1, :quarter]
            target[rows, 2 * n * quarter : (2 * n + 1) * quarter] = jnp.sin(angle)
            target[rows, (2 * n + 1) * quarter : (2 * n + 2) * quarter] = jnp.cos(angle)

    def pixel_store(n):
        return pltpu.make_async_copy(
            hidden_pixels, picked_out.at[pl.ds((n - 1) * VIS, VIS)], side_sem.at[4]
        )

    def hidden_step(n):
        rows = slice(n * VIS, (n + 1) * VIS)
        if n > 0:
            if n > 1:
                pixel_store(n - 1).wait()
            hidden_pixels[...] = pick_rows(rows)
            pixel_store(n).start()
        position_rows(pos_out, rows, DD, 1)

    def embed_step():
        pixels = stats_out[6:7, :] * (PATCH * PATCH)
        for band in range(BANDS):
            mean = stats_out[band : band + 1, :] / pixels
            var = stats_out[BANDS + band : BANDS + band + 1, :] / pixels - mean * mean
            rate = lax.rsqrt(var + EPS)
            for part in range(PATCH * PATCH // LANES):
                lanes = pl.ds(band * PATCH * PATCH + part * LANES, LANES)
                inputs_ref[:, lanes] = ((picked_ref[:, lanes] - mean) * rate).astype(BF)
        start_ref[...] = matmul(inputs_ref[...], columns_of(at["embed"])) + pos_ref[...]
        a_ref[...] = norm_rows(start_ref[...], gain_one)
        own = w_embed.shape[1]
        flipped = jnp.concatenate(
            [inputs_ref[:, lane : lane + LANES].T for lane in range(0, PD, LANES)], 0
        )
        inputs_t[...] = jnp.zeros_like(inputs_t)
        for owner in range(w_embed.shape[0]):
            inputs_t[owner, :own, :] = flipped[owner * own : (owner + 1) * own, :]
        turn(a_ref, a_t)

    def qkv_step(n):
        qkv_ref[:, n * D : (n + 1) * D] = matmul(a_ref[...], columns_of(at["qkv", n])).astype(BF)

    def attention_step():
        size = D // HEADS
        lane_head = lax.broadcasted_iota(jnp.int32, (VIS, LANES), 1) // size

        def group(g, _):
            query, keys, values = [
                qkv_ref[:, pl.ds(pl.multiple_of(n * D + g * LANES, LANES), LANES)] for n in range(3)
            ]
            mixed = jnp.zeros((VIS, LANES), F32)
            for j in range(LANES // size):
                one = jnp.where(lane_head == j, query.astype(F32), 0.0).astype(BF)
                scores = right_t(one, keys) * size ** (-0.5) + bias_ref[...]
                probs = jnp.exp(scores - jnp.max(scores, -1, keepdims=True))
                probs = probs * (1.0 / jnp.sum(probs, -1, keepdims=True))
                mixed = jnp.where(lane_head == j, matmul(probs.astype(BF), values), mixed)
            mixed_ref[:, pl.ds(pl.multiple_of(g * LANES, LANES), LANES)] = mixed.astype(BF)
            return 0

        lax.fori_loop(0, D // LANES, group, 0)

    def out_step():
        turn(mixed_ref, mixed_t)
        middle_ref[...] = start_ref[...] + matmul(mixed_ref[...], columns_of(at["out"]))
        b_ref[...] = norm_rows(middle_ref[...], gain_two)
        turn(b_ref, b_t)

    def slope_store(n):
        return pltpu.make_async_copy(
            slope_ref.at[n % 2], slope_out.at[:, pl.ds(n * D, D)], side_sem.at[2 + n % 2]
        )

    def up_step(n):
        columns = slice(n * D, (n + 1) * D)
        after, slope = gelu_parts(matmul(b_ref[...], columns_of(at["up", n])))
        hidden_ref[:, columns] = after.astype(BF)
        if n > 1:
            slope_store(n - 2).wait()
        slope_ref[n % 2] = slope
        slope_store(n).start()
        turn(hidden_ref, hidden_t, n * D)

    def down_step(n):
        rows, owners = w_wide.shape[1], w_down.shape[0]
        tall = w_down.shape[1]
        parts = [hidden_ref[:, o * tall + n * rows : o * tall + (n + 1) * rows] for o in range(owners)]
        total = matmul(jnp.concatenate(parts, 1), columns_of(at["down", n]))
        end_ref[...] = (middle_ref[...] if n == 0 else end_ref[...]) + total

    def link_step():
        z_ref[...] = norm_rows(end_ref[...], gain_out)
        turn(z_ref, z_t)
        seen_ref[...] = matmul(z_ref[...], columns_of(at["link"]))

    work = [(0, None, arrange_step), (1, None, pick_step)]
    work += [(2, None, partial(position_rows, pos_ref, slice(0, VIS), D, 0))]
    work += [(when, None, partial(hidden_step, n)) for n, when in enumerate((3, 4, 11, 14))]
    work += [(6, "embed", embed_step)]
    work += [(when, ("qkv", n), partial(qkv_step, n)) for n, when in enumerate((6, 7, 7))]
    work += [(8, None, attention_step), (8, "out", out_step)]
    work += [(when, ("up", n), partial(up_step, n)) for n, when in enumerate((9, 10, 12, 13))]
    work += [(when, ("down", n), partial(down_step, n)) for n, when in enumerate((13, 14, 16, 16))]
    work += [(17, "link", link_step)]

    first(0)
    local_statistics()
    first(1)
    for i in range(19):
        if i + 2 < count:
            first(i + 2)
        statistics(i)
        if i < count:
            second(i)
        if 0 <= i - 1 < count:
            third(i - 1)
        if 0 <= i - 4 < count:
            taken(i - 4, 0)
            taken(i - 4, 1)
        if 0 <= i - 5 < count:
            taken(i - 5, 2)
        for when, piece, run in work:
            if when != i:
                continue
            if piece is not None:
                piece = at[piece]
                whole(piece)
                array, row, rows, column, columns, _ = pieces[piece]
                if array:
                    where = (slice(None), pl.ds(row, rows), pl.ds(column, columns))
                    store = pltpu.make_async_copy(
                        gathered[array].at[where],
                        (None, wide_out, down_out)[array].at[where],
                        store_sem.at[piece],
                    )
                    store.start()
                    stores.append(store)
            run()
    for t, piece in enumerate(pieces):
        if piece[0] > 2:
            whole(t)
    for n in range(2):
        slope_store(FF // D - 2 + n).wait()
    pixel_store(HID // VIS).wait()
    for store in stores:
        store.wait()
    for t in range(count):
        drain(t)
    for step in range(3):
        copy_v(step, sides[step]).wait_send()

    @pl.when(outer)
    def _():
        copy_v(3, z_side).wait_send()

    @pl.when(inner)
    def _():
        copy_v(4, across).wait_send()
        copy_v(5, z_side).wait_send()


def encoder_forward(pixels, facts, scale, vectors, *shards):
    owners = lax.axis_size("fsdp")
    shapes = [w.shape for w in shards]
    count = len(encoder_pieces(shapes)[0])
    omega = [
        10000.0 ** (-jnp.arange(width // 4, dtype=jnp.float32) / (width // 4)) for width in (D, DD)
    ]
    omega = jnp.stack([omega[0], jnp.pad(omega[1], (0, D // 4 - DD // 4))] + [omega[0]] * 6)
    full = [jax.ShapeDtypeStruct((owners, *shape), BF) for shape in shapes[1:]]
    full += [jax.ShapeDtypeStruct((HID, PD), F32), jax.ShapeDtypeStruct((VIS, FF), F32)]
    local = [
        jax.ShapeDtypeStruct((8, LANES), F32),
        jax.ShapeDtypeStruct((8, TOK_DEV), F32),
        jax.ShapeDtypeStruct((TOK_DEV, 8), F32),
        jax.ShapeDtypeStruct((TOK_DEV, DD), F32),
        jax.ShapeDtypeStruct((VIS, VIS), F32),
        jax.ShapeDtypeStruct((owners, ROWS, VIS), BF),
        *[jax.ShapeDtypeStruct((width, VIS), BF) for width in (D, D, D, FF, D)],
        jax.ShapeDtypeStruct((VIS, D), F32),
        jax.ShapeDtypeStruct((VIS, 3 * D), BF),
        jax.ShapeDtypeStruct((VIS, D), F32),
        jax.ShapeDtypeStruct((VIS, D), F32),
        jax.ShapeDtypeStruct((VIS, DD), F32),
    ]
    vmem, anywhere = pl.BlockSpec(memory_space=pltpu.VMEM), pl.BlockSpec(memory_space=pl.ANY)
    dma = pltpu.SemaphoreType.DMA
    wide_full, down_full, dec_wide, dec_down, *rest = pl.pallas_call(
        encoder_kernel,
        out_shape=(*full, *local),
        in_specs=[vmem] * 6 + [anywhere] * len(shards),
        out_specs=(anywhere,) * len(full) + (vmem,) * len(local),
        scratch_shapes=[pltpu.VMEM((VIS, width), BF) for width in (PD, D, D, D, FF, D)]
        + [pltpu.VMEM((owners, *shape), BF) for shape in shapes[:3]]
        + [
            pltpu.VMEM((4, ROWS, D), F32),
            *[pltpu.VMEM((TOK_DEV, PD), BF)] * 4,
            pltpu.VMEM((VIS, PD), F32),
            pltpu.VMEM((VIS, D), F32),
            pltpu.VMEM((VIS, VIS), F32),
            *[pltpu.VMEM(shape, F32) for shape in shapes[3:]],
            *[pltpu.VMEM(shape, BF) for shape in shapes[3:]],
            pltpu.VMEM((2, VIS, D), F32),
            pltpu.VMEM((VIS, PD), F32),
            pltpu.VMEM((6, 8, LANES), F32),
            pltpu.VMEM((6, 8, LANES), F32),
            dma((4,)),
            dma((count,)),
            dma((count, 11)),
            dma((count, 11)),
            dma((6,)),
            dma((6,)),
            dma((5,)),
        ],
        compiler_params=pltpu.CompilerParams(
            collective_id=1, has_side_effects=True, vmem_limit_bytes=60 * 2**20
        ),
        cost_estimate=pl.CostEstimate(
            flops=2 * VIS * 14 * 2**20, bytes_accessed=200 * 2**20, transcendentals=0
        ),
    )(pixels, facts, facts.T, scale, omega, vectors, *shards)
    return (
        wide_full.reshape(D, -1),
        down_full.reshape(FF, D),
        dec_wide.reshape(DD, -1),
        dec_down.reshape(DFF, DD),
        *rest,
    )


LOWP = 256
HEADP = PD + LOWP
BLOCK = HID // 2


def mask_bias(live, same, shape, offset, keys=0):
    key, query = [lax.broadcasted_iota(jnp.int32, shape, (keys + n) % 2) for n in range(2)]
    return jnp.where((live & same) | (key + offset == query), 0.0, NEGATIVE)


def normalize(h):
    cent = h - jnp.mean(h, -1, keepdims=True)
    rate = lax.rsqrt(jnp.mean(cent * cent, -1, keepdims=True) + EPS)
    return cent * rate, rate


def normalize_back(unit, rate, gain, grad):
    scaled = grad * gain
    along = jnp.mean(scaled * unit, -1, keepdims=True)
    dh = rate * (scaled - jnp.mean(scaled, -1, keepdims=True) - unit * along)
    return dh, jnp.sum(grad * unit, 0, keepdims=True)


def exact_product(array, weight):
    high = array.astype(BF)
    rest = array - high.astype(F32)
    mid = rest.astype(BF)
    low = (rest - mid.astype(F32)).astype(BF)
    return matmul(high, weight) + matmul(mid, weight) + matmul(low, weight)


EARLY = DFF // DD + DFF // UNIT + HEADP // UNIT
LATE = 4


def decoder_kernel(
    owners,
    fast,
    pos_ref,
    seen_ref,
    row_ref,
    column_ref,
    picked_ref,
    stats_ref,
    vectors_ref,
    wide_ref,
    down_ref,
    late_ref,
    dy_ref,
    vec_out,
    sums_ref,
    early_ref,
    y_ref,
    a_ref,
    q_ref,
    k_ref,
    v_ref,
    mixed_t,
    mixed_ref,
    lse_ref,
    head_ref,
    b_ref,
    hidden_ref,
    z_ref,
    dpred_ref,
    dbranch_ref,
    dbefore_ref,
    dattn_ref,
    dmixed_ref,
    dmiddle_ref,
    dq_ref,
    dk_ref,
    dv_ref,
    loss_ref,
    bias_ref,
    pool_ref,
    spread_ref,
    vec_ref,
    *links,
):
    if fast:
        (dp, a_out, a_in, b_out, b_in, swap_sem, a_send, a_recv, b_send, b_recv) = links
        ready = EARLY // 2
        z, f = lax.axis_index("dp"), lax.axis_index("fsdp")
        core, place = f % 2, f // 2
        x, y = place % 2, place // 2
        partner = (z, f + 1 - 2 * core)
        x_side, y_side = (z, f + 2 - 4 * x), (z, f + 4 - 8 * y)
        at_x, at_y, at_far = place + 1 - 2 * x, place + 2 - 4 * y, 3 - place
        first, second = pl.ds(0, HALF), pl.ds(HALF, HALF)
        barrier = pltpu.get_barrier_semaphore()
        for device in (partner, x_side, y_side):
            pl.semaphore_signal(barrier, inc=1, device_id=device, device_id_type=MESH)

        def swap(u):
            return put(
                early_ref.at[:, 1 - core, pl.ds(2 * u, 2)],
                dp.at[u],
                swap_sem.at[u, 0],
                swap_sem.at[u, 1],
                partner,
            )

        def share(u, owner, columns):
            own = early_ref[owner, core, pl.ds(2 * u, 2), :, columns].astype(F32)
            both = own + dp[u, owner, :, :, columns].astype(F32)
            return both.reshape(ROWS, HALF)

        def copy_a(u, side):
            return put(
                a_out.at[u, side],
                a_in.at[u, side],
                a_send.at[u, side],
                a_recv.at[u, side],
                (x_side, y_side)[side],
            )

        def copy_b(u, side):
            return put(
                b_out.at[u, side],
                b_in.at[u, side],
                b_send.at[u, side],
                b_recv.at[u, side],
                (y_side, x_side)[side],
            )

        def exchange(c):
            @pl.when(c < ready)
            def _():
                swap(c).wait()
                a_out[c, 0, 0] = share(c, at_x, first).astype(BF)
                a_out[c, 0, 1] = share(c, at_far, first).astype(BF)
                copy_a(c, 0).start()
                a_out[c, 1, 0] = share(c, at_y, second).astype(BF)
                a_out[c, 1, 1] = share(c, at_far, second).astype(BF)
                copy_a(c, 1).start()

            @pl.when((c >= 2) & (c < ready + 2))
            def _():
                u = c - 2
                copy_a(u, 0).wait_recv()
                b_out[u, 0] = (share(u, at_y, first) + a_in[u, 0, 1].astype(F32)).astype(BF)
                copy_b(u, 0).start()
                copy_a(u, 1).wait_recv()
                b_out[u, 1] = (share(u, at_x, second) + a_in[u, 1, 1].astype(F32)).astype(BF)
                copy_b(u, 1).start()

            @pl.when((c >= 4) & (c < ready + 4))
            def _():
                u = c - 4
                for side, columns in enumerate((first, second)):
                    copy_b(u, side).wait_recv()
                    total = share(u, place, columns) + a_in[u, side, 0].astype(F32)
                    sums_ref[u, :, columns] = total + b_in[u, side].astype(F32)

    size = DD // DHEADS
    per = LANES // size
    factor = size ** (-0.5)
    gain_one, gain_two, gain_out, token = [
        vectors_ref[:, 3 * D + n * DD : 3 * D + (n + 1) * DD] for n in range(4)
    ]

    def pooled(shape, pixels):
        pixel, low = [lax.broadcasted_iota(jnp.int32, shape, (pixels + n) % 2) for n in range(2)]
        row, column = (pixel >> 4) & 15, pixel & 15
        return ((pixel >> 8) << 6) + ((row >> 1) << 3) + (column >> 1) == low

    pool_ref[...] = jnp.where(pooled((PD, LOWP), 0), 0.25, 0.0).astype(BF)
    spread_ref[...] = jnp.where(pooled((LOWP, PD), 1), 1.0, 0.0).astype(BF)
    lane_head = lax.broadcasted_iota(jnp.int32, (HID, LANES), 1) // size
    key_head = lax.broadcasted_iota(jnp.int32, (TOK_DEV, LANES), 1) // size
    kept = column_ref[:VIS, 0:1] > 0
    for start in range(0, TOK_DEV, VIS):
        rows = slice(start, start + VIS)
        bias_ref[rows, :] = mask_bias(
            column_ref[rows, 0:1] > 0,
            column_ref[rows, 2:3] == row_ref[2:3, VIS:],
            (VIS, HID),
            start - VIS,
        )
    if not fast:
        sums_ref[...] = jnp.zeros_like(sums_ref)
    vec_ref[...] = jnp.zeros_like(vec_ref)
    loss_ref[...] = jnp.zeros_like(loss_ref)
    head_ref[...] = jnp.zeros_like(head_ref)
    head_ref[:, : PD + LOWD] = wide_ref[:, 4 * DD + DFF :]

    def project(rows, with_query):
        a = (normalize(y_ref[rows, :])[0] * gain_one).astype(BF)
        a_ref[rows, :] = a
        k_ref[rows, :] = matmul(a, wide_ref[:, DD : 2 * DD]).astype(BF)
        v_ref[rows, :] = matmul(a, wide_ref[:, 2 * DD : 3 * DD]).astype(BF)
        return a

    y_ref[:VIS, :] = pos_ref[:VIS, :] + jnp.where(kept, seen_ref[...], token)
    y_ref[VIS:, :] = pos_ref[VIS:, :] + token
    project(slice(0, VIS), False)

    def hidden_rows(n):
        start = pl.multiple_of(n * BLOCK, BLOCK)
        return pl.ds(start, BLOCK), pl.ds(pl.multiple_of(start + VIS, 32), BLOCK)

    def project_hidden(n, _):
        rows, all_rows = hidden_rows(n)
        a = project(all_rows, True)
        q_ref[rows, :] = matmul(a, wide_ref[:, :DD]).astype(BF)
        return 0

    lax.fori_loop(0, 2, project_hidden, 0)

    def only(array, head_of, j):
        return jnp.where(head_of == j, array.astype(F32), 0.0).astype(BF)

    def attend_group(g, _):
        lanes = pl.ds(pl.multiple_of(g * LANES, LANES), LANES)
        keys, query = k_ref[:, lanes], q_ref[:, lanes]
        values_t = v_ref[:, lanes].T
        for j in range(per):
            scores = right_t(keys, only(query, lane_head, j)) * factor + bias_ref[...]
            top = jnp.max(scores, 0, keepdims=True)
            probs = jnp.exp(scores - top)
            total = jnp.sum(probs, 0, keepdims=True)
            probs = (probs * (1.0 / total)).astype(BF)
            rows = slice(j * size, (j + 1) * size)
            mixed_t[g, rows, :] = matmul(values_t[rows, :], probs).astype(BF)
            lse_ref[g, j : j + 1, :] = top + jnp.log(total)
        mixed_ref[:, lanes] = mixed_t[g].T
        return 0

    lax.fori_loop(0, DD // LANES, attend_group, 0)

    pixels = stats_ref[6:7, :] * (PATCH * PATCH)
    flagged = stats_ref[7:8, 0:1]

    def follow(n, _):
        rows, all_rows = hidden_rows(n)
        middle = y_ref[all_rows, :] + matmul(mixed_ref[rows, :], wide_ref[:, 3 * DD : 4 * DD])
        unit_b, rate_b = normalize(middle)
        b = (unit_b * gain_two).astype(BF)
        b_ref[rows, :] = b
        after, slope = gelu_parts(matmul(b, wide_ref[:, 4 * DD : 4 * DD + DFF]))
        hidden_ref[rows, :] = after.astype(BF)
        unit_z, rate_z = normalize(middle + matmul(hidden_ref[rows, :], down_ref[...]))
        z = (unit_z * gain_out).astype(BF)
        z_ref[rows, :] = z
        pred = matmul(z, head_ref[...])
        parts = []
        for part in range(PD // LANES):
            band = part * LANES // (PATCH * PATCH)
            mean = stats_ref[band : band + 1, :] / pixels
            var = stats_ref[BANDS + band : BANDS + band + 1, :] / pixels - mean * mean
            lanes = slice(part * LANES, (part + 1) * LANES)
            parts.append((picked_ref[rows, lanes] - mean) * lax.rsqrt(var + EPS))
        normed = jnp.concatenate(parts, 1)
        coarse = exact_product(normed, pool_ref[...])
        err_high = pred[:, :PD] - (normed - exact_product(coarse, spread_ref[...]))
        err_low = pred[:, PD:] - coarse
        flag = column_ref[all_rows, 0:1]
        length = jnp.sqrt(err_high * err_high + 1.0)
        loss_ref[:, :PD] += jnp.sum((length - 1.0) * flag, 0, keepdims=True) * (1.0 / PD)
        loss_ref[:, PD:] += jnp.sum(err_low * err_low * flag, 0, keepdims=True) * (1.0 / LOWD)
        share = flag / flagged
        dpred_ref[rows, :PD] = (err_high / length * (share * (1.0 / PD))).astype(BF)
        dpred_ref[rows, PD:] = (err_low * (share * (2.0 / LOWD))).astype(BF)
        dz = right_t(dpred_ref[rows, :], head_ref[...])
        dend, dgain = normalize_back(unit_z, rate_z, gain_out, dz)
        vec_ref[2:3, :] += dgain
        dbranch_ref[rows, :] = dend.astype(BF)
        dhidden = right_t(dbranch_ref[rows, :], down_ref[...])
        dbefore_ref[rows, :] = (dhidden * slope).astype(BF)
        db = right_t(dbefore_ref[rows, :], wide_ref[:, 4 * DD : 4 * DD + DFF])
        dmiddle, dgain = normalize_back(unit_b, rate_b, gain_two, db)
        vec_ref[1:2, :] += dgain
        dmiddle = dmiddle + dend
        dmiddle_ref[rows, :] = dmiddle
        dattn_ref[rows, :] = dmiddle.astype(BF)
        dmixed = right_t(dattn_ref[rows, :], wide_ref[:, 3 * DD : 4 * DD])
        dmixed_ref[rows, :] = dmixed.astype(BF)
        return 0

    lax.fori_loop(0, 2, follow, 0)

    rows = DD // owners

    def store(ref, block, grad):
        ref[:, :, block] = grad.astype(BF).reshape(owners // 2, 2, rows, UNIT)

    parts = DFF // DD
    down_grad = left_t(hidden_ref[...], dbranch_ref[...]).astype(BF)
    down_grad = down_grad.reshape(owners // 2, 2, parts, rows, UNIT)
    for part in range(parts):
        early_ref[:, :, part] = down_grad[:, :, part]
    for n in range(DFF // UNIT):
        columns = slice(n * UNIT, (n + 1) * UNIT)
        store(early_ref, parts + n, left_t(b_ref[...], dbefore_ref[:, columns]))
    for n in range(HEADP // UNIT):
        columns = slice(n * UNIT, (n + 1) * UNIT)
        store(early_ref, parts + DFF // UNIT + n, left_t(z_ref[...], dpred_ref[:, columns]))
    if fast:
        pl.semaphore_wait(barrier, 3)
        for u in range(ready):
            swap(u).start()
    store(
        late_ref,
        3,
        jnp.concatenate([matmul(mixed_t[g], dattn_ref[...]) for g in range(DD // LANES)], 0),
    )

    def attend_back_group(g, _):
        lanes = pl.ds(pl.multiple_of(g * LANES, LANES), LANES)
        query, keys, values, dout = [r[:, lanes] for r in (q_ref, k_ref, v_ref, dmixed_ref)]
        keys_t = keys.T
        dkeys = jnp.zeros((TOK_DEV, LANES), F32)
        dvalues = jnp.zeros((TOK_DEV, LANES), F32)
        dquery = []
        for j in range(per):
            if fast and j % 2 == 0:
                exchange(2 * g + j // 2)
            scores = right_t(keys, only(query, lane_head, j)) * factor + bias_ref[...]
            probs = jnp.exp(scores - lse_ref[g, j : j + 1, :])
            dvalues = jnp.where(key_head == j, matmul(probs.astype(BF), dout), dvalues)
            dprobs = right_t(values, only(dout, lane_head, j))
            delta = jnp.sum(dprobs * probs, 0, keepdims=True)
            dscores = (probs * (dprobs - delta)).astype(BF)
            dkeys = jnp.where(key_head == j, matmul(dscores, query), dkeys)
            dquery.append(matmul(keys_t[j * size : (j + 1) * size, :], dscores))
        dq_ref[:, lanes] = (jnp.concatenate(dquery, 0) * factor).astype(BF).T
        dk_ref[:, lanes] = (dkeys * factor).astype(BF)
        dv_ref[:, lanes] = dvalues.astype(BF)
        return 0

    lax.fori_loop(0, DD // LANES, attend_back_group, 0)

    store(late_ref, 0, left_t(a_ref[VIS:, :], dq_ref[...]))
    if fast:
        exchange(2 * (DD // LANES))
    store(late_ref, 1, left_t(a_ref[...], dk_ref[...]))
    store(late_ref, 2, left_t(a_ref[...], dv_ref[...]))

    def start_rows(rows, da):
        unit, rate = normalize(y_ref[rows, :])
        da = da + right_t(dk_ref[rows, :], wide_ref[:, DD : 2 * DD])
        da = da + right_t(dv_ref[rows, :], wide_ref[:, 2 * DD : 3 * DD])
        dh, dgain = normalize_back(unit, rate, gain_one, da)
        vec_ref[0:1, :] += dgain
        return dh

    dy = start_rows(slice(0, VIS), 0.0)
    dy_ref[...] = dy
    vec_ref[3:4, :] += jnp.sum(jnp.where(kept, 0.0, dy), 0, keepdims=True)

    def start_hidden(n, _):
        rows, all_rows = hidden_rows(n)
        dy = start_rows(all_rows, right_t(dq_ref[rows, :], wide_ref[:, :DD]))
        vec_ref[3:4, :] += jnp.sum(dy + dmiddle_ref[rows, :], 0, keepdims=True)
        return 0

    lax.fori_loop(0, 2, start_hidden, 0)
    vec_out[...] = jnp.zeros_like(vec_out)
    for n in range(4):
        vec_out[3 + n // 2 : 4 + n // 2, n % 2 * DD : (n % 2 + 1) * DD] = vec_ref[n : n + 1, :]
    vec_out[5:6, :] = jnp.broadcast_to(jnp.sum(loss_ref[...], 1, keepdims=True), (1, D))
    if fast:
        for u in range(ready):
            for side in range(2):
                copy_a(u, side).wait_send()
                copy_b(u, side).wait_send()


def decoder_step(fast, pos, seen, by_row, by_column, picked, stats, vectors, wide, down):
    owners = lax.axis_size("fsdp")
    scratch = [
        ((TOK_DEV, DD), F32),
        ((TOK_DEV, DD), BF),
        ((HID, DD), BF),
        ((TOK_DEV, DD), BF),
        ((TOK_DEV, DD), BF),
        ((DD // LANES, LANES, HID), BF),
        ((HID, DD), BF),
        ((DD // LANES, LANES * DHEADS // DD, HID), F32),
        ((DD, HEADP), BF),
        ((HID, DD), BF),
        ((HID, DFF), BF),
        ((HID, DD), BF),
        ((HID, HEADP), BF),
        ((HID, DD), BF),
        ((HID, DFF), BF),
        ((HID, DD), BF),
        ((HID, DD), BF),
        ((HID, DD), F32),
        ((HID, DD), BF),
        ((TOK_DEV, DD), BF),
        ((TOK_DEV, DD), BF),
        ((1, HEADP), F32),
        ((TOK_DEV, HID), F32),
        ((PD, LOWP), BF),
        ((LOWP, PD), BF),
        ((8, DD), F32),
    ]
    vmem = pl.BlockSpec(memory_space=pltpu.VMEM)
    early, late = [
        jax.ShapeDtypeStruct((owners // 2, 2, blocks, DD // owners, UNIT), BF)
        for blocks in (EARLY, LATE)
    ]
    ready = EARLY // 2
    dma = pltpu.SemaphoreType.DMA
    scratch = [pltpu.VMEM(*entry) for entry in scratch]
    params = {}
    if fast:
        sums = jax.ShapeDtypeStruct((ready, ROWS, UNIT), F32)
        scratch = [pltpu.VMEM(early.shape, BF)] + scratch
        scratch += [
            pltpu.VMEM((ready, owners // 2, 2, DD // owners, UNIT), BF),
            pltpu.VMEM((ready, 2, 2, ROWS, HALF), BF),
            pltpu.VMEM((ready, 2, 2, ROWS, HALF), BF),
            pltpu.VMEM((ready, 2, ROWS, HALF), BF),
            pltpu.VMEM((ready, 2, ROWS, HALF), BF),
            *[dma((ready, 2))] * 5,
        ]
        params = {"collective_id": 2, "has_side_effects": True}
    else:
        sums = jax.ShapeDtypeStruct((8, LANES), F32)
    outs = (
        late,
        jax.ShapeDtypeStruct((VIS, DD), F32),
        jax.ShapeDtypeStruct((8, D), F32),
        sums,
        *([] if fast else [early]),
    )
    return pl.pallas_call(
        partial(decoder_kernel, owners, fast),
        out_shape=outs,
        in_specs=[vmem] * 9,
        out_specs=(vmem,) * len(outs),
        scratch_shapes=scratch,
        compiler_params=pltpu.CompilerParams(vmem_limit_bytes=60 * 2**20, **params),
        cost_estimate=pl.CostEstimate(
            flops=40 * 10**9, bytes_accessed=40 * 2**20, transcendentals=2 * 10**7
        ),
    )(
        pos,
        seen,
        by_row,
        by_column,
        picked,
        stats,
        vectors,
        wide,
        down,
    )


def block_forward(h, weights, gains, bias, heads, skip):
    wqkv, wout, wup, wdown = weights
    width = h.shape[1]
    normed_a = layer_norm(h, gains[0]).astype(BF)
    query = matmul(normed_a[skip:], wqkv[:, :width]).astype(BF)
    keys = matmul(normed_a, wqkv[:, width : 2 * width]).astype(BF)
    values = matmul(normed_a, wqkv[:, 2 * width :]).astype(BF)
    mixed_t, lse = attend(query.T, keys, values.T, bias, width // heads)
    middle = h[skip:] + left_t(mixed_t, wout)
    normed_b = layer_norm(middle, gains[1]).astype(BF)
    after, slope = gelu_parts(matmul(normed_b, wup))
    hidden = after.astype(BF)
    end = middle + matmul(hidden, wdown)
    return end, (h, normed_a, query, keys, values, mixed_t, lse, middle, normed_b, slope, hidden)


def block_backward(saved, grad, weights, gains, bias, heads, skip):
    wqkv, wout, wup, wdown = weights
    h, normed_a, query, keys, values, mixed_t, lse, middle, normed_b, slope, hidden = saved
    width = h.shape[1]
    dbranch = grad.astype(BF)
    dbefore = (right_t(dbranch, wdown) * slope).astype(BF)
    dmiddle, dgain_two = norm_back(middle, gains[1], right_t(dbefore, wup))
    dmiddle = dmiddle + grad
    dattn = dmiddle.astype(BF)
    dmixed = right_t(dattn, wout).astype(BF)
    dqt, dkeys, dvalues = attend_back(query, keys, values, dmixed, bias, lse, width // heads)
    dquery = dqt.T
    if skip:
        dquery = jnp.pad(dquery, ((skip, 0), (0, 0)))
        dmiddle = jnp.pad(dmiddle, ((skip, 0), (0, 0)))
    dqkv = jnp.concatenate([dquery, dkeys, dvalues], 1)
    dh, dgain_one = norm_back(h, gains[0], right_t(dqkv, wqkv))
    factors = ((normed_a.T, dqkv), (mixed_t, dattn), (normed_b.T, dbefore), (hidden.T, dbranch))
    return (dh + dmiddle, factors, (dgain_one, dgain_two))


def reduce_rows(grad):
    return lax.psum_scatter(grad.astype(F32), "fsdp", scatter_dimension=0, tiled=True)


def enc_split(wide, down):
    return (
        (wide[:, : 3 * D], wide[:, 3 * D : 4 * D], wide[:, 4 * D : 4 * D + FF], down),
        wide[:, 4 * D + FF :],
    )


def advance(weight, mom, avg, grad, rate):
    grad = grad + DECAY * weight
    buf = MOMENTUM * mom + grad
    new = weight - rate * (grad + MOMENTUM * buf)
    return (buf, new, AVERAGE * avg + (1.0 - AVERAGE) * new)


def advance_kernel(rate, *refs):
    grads, weights, moms, avgs, outs = [refs[5 * n : 5 * n + 5] for n in range(4)] + [refs[20:]]

    def update(n):
        weight = weights[n][...]
        grad = grads[n][:, : weight.shape[1]].astype(F32)
        buf, new, avg = advance(weight, moms[n][...], avgs[n][...], grad, rate)
        outs[4 * n][...] = buf
        outs[4 * n + 1][...] = new
        outs[4 * n + 2][...] = avg
        outs[4 * n + 3][...] = new.astype(BF)

    pl.when(pl.program_id(0) == 0)(partial(update, 0))
    for n in range(1, 5):
        update(n)


def advance_all(rate, grads, weights, moms, avgs):
    steps = weights[3].shape[0] // 16

    def spec(n, array):
        if n == 0:
            return pl.BlockSpec(array.shape, lambda i: (0, 0))
        return pl.BlockSpec((array.shape[0] // steps, array.shape[1]), lambda i: (i, 0))

    arrays = [a for group in (grads, weights, moms, avgs) for a in group]
    outs = [(n, jax.ShapeDtypeStruct(w.shape, t)) for n, w in enumerate(weights) for t in (F32, F32, F32, BF)]
    size = sum(w.size for w in weights)
    return pl.pallas_call(
        partial(advance_kernel, rate),
        grid=(steps,),
        out_shape=[out for _, out in outs],
        in_specs=[spec(n % 5, a) for n, a in enumerate(arrays)],
        out_specs=[spec(n, out) for n, out in outs],
        compiler_params=pltpu.CompilerParams(vmem_limit_bytes=58 * 2**20),
        cost_estimate=pl.CostEstimate(flops=12 * size, bytes_accessed=28 * size, transcendentals=0),
    )(*arrays)


def arrange(valid, masked, scene_ids):
    slots = valid.shape[0]
    live = valid > 0
    kinds = jnp.stack([live & (masked == 0), live & (masked > 0), ~live], 1)
    index = jnp.arange(slots, dtype=jnp.int32)
    ranks = matmul((index[None, :] < index[:, None]).astype(BF), kinds.astype(BF)).astype(jnp.int32)
    n_seen, n_hid = [jnp.sum(kinds[:, i].astype(jnp.int32)) for i in range(2)]
    empty = ranks[:, 2]
    to_empty = jnp.where(empty < VIS - n_seen, n_seen + empty, n_seen + n_hid + empty)
    place = jnp.where(
        kinds[:, 0], ranks[:, 0], jnp.where(kinds[:, 1], VIS + ranks[:, 1], to_empty)
    )
    return (place[None, :] == index[:, None]).astype(BF), n_seen, n_hid


def exact_pick(pick, array):
    high = lax.reduce_precision(array, 8, 7)
    rest = array - high
    mid = lax.reduce_precision(rest, 8, 7)
    low = rest - mid
    return (
        matmul(pick, high.astype(BF)) + matmul(pick, mid.astype(BF)) + matmul(pick, low.astype(BF))
    )


def body(
    pixels,
    masked,
    valid,
    scene_ids,
    gsd_index,
    coords,
    embed,
    wide_enc,
    enc_down,
    wide_dec,
    dec_down,
    vectors,
    embed_mom,
    wide_enc_mom,
    enc_down_mom,
    wide_dec_mom,
    dec_down_mom,
    vector_mom,
    embed_avg,
    wide_enc_avg,
    enc_down_avg,
    wide_dec_avg,
    dec_down_avg,
    vector_avg,
):
    slots = pixels.shape[0]
    fast = (lax.axis_size("dp"), lax.axis_size("fsdp")) == (4, 8)
    vector_row = vectors.reshape(1, -1)
    levels = jnp.exp2(0.5 * gsd_index.astype(jnp.float32) - 1.0)
    gains_enc = (vectors[:D], vectors[D : 2 * D])
    gain_enc_out = vectors[2 * D : 3 * D]
    if fast:
        facts = jnp.stack([valid, masked, scene_ids % 2, coords[:, 0], coords[:, 1]])
        facts = jnp.pad(facts, ((0, 3), (0, 0))).astype(F32)
        scale = jnp.pad(jnp.broadcast_to(levels[:, None], (2, LANES)), ((0, 6), (0, 0)))
        w_enc, w_enc_down, w_dec, w_dec_down, picked_hidden, slope, *saved = encoder_forward(
            pixels, facts, scale, vector_row, embed, wide_enc, enc_down, wide_dec, dec_down
        )
        stats, by_row, by_column, pos_dec, bias_enc, *saved = saved
        *factors, h_start, qkv, middle, h_end, seen_out = saved
    else:
        rows_ok = valid.astype(jnp.float32)
        flags = rows_ok * masked.astype(jnp.float32)
        bands = pixels.reshape(slots, BANDS, PATCH * PATCH)
        weighted = bands * rows_ok[:, None, None]
        band_sum = jnp.sum(weighted, axis=(0, 2))
        counts = jnp.stack([jnp.sum(rows_ok), jnp.sum(flags)])
        band_sq = jnp.sum(weighted * bands, axis=(0, 2))
        stats = jnp.concatenate([band_sum, band_sq, counts])
        stats = jnp.broadcast_to(lax.psum(stats, ("dp", "fsdp"))[:, None], (8, LANES))
        pick, n_seen, n_hid = arrange(valid, masked, scene_ids)
        picked_pixels = exact_pick(pick, pixels)
        picked_hidden = picked_pixels[VIS:]
        small = matmul(pick, jnp.concatenate([(scene_ids % 2)[:, None], coords], 1).astype(BF))
        odd, coord = small[:, 0], small[:, 1:]
        scale = jnp.where(odd == 0, levels[0], levels[1])
        index = jnp.arange(slots, dtype=jnp.int32)
        live = jnp.concatenate([index[:VIS] < n_seen, index[:HID] < n_hid])
        allow = live[:, None] & (odd[:, None] == odd[None, :]) | (index[:, None] == index[None, :])
        bias_enc = jnp.where(allow, 0.0, NEGATIVE)[:VIS, :VIS]
        by_row = jnp.pad(jnp.stack([live.astype(F32), odd, odd]), ((0, 5), (0, 0)))
        by_column = by_row.T
        pos_dec = positions(coord, scale, DD)
    count = stats[7, 0]
    if not fast:
        w_embed, w_enc, w_enc_down, w_dec, w_dec_down = [
            lax.all_gather(w.astype(BF), "fsdp", axis=0, tiled=True)
            for w in (embed, wide_enc, enc_down, wide_dec, dec_down)
        ]
        enc_weights, w_link = enc_split(w_enc, w_enc_down)
        mean = jnp.repeat(stats[:3, 0] / (stats[6, 0] * (PATCH * PATCH)), PATCH * PATCH)
        square = jnp.repeat(stats[3:6, 0] / (stats[6, 0] * (PATCH * PATCH)), PATCH * PATCH)
        rate = lax.rsqrt(square - mean * mean + EPS)
        inputs = ((picked_pixels[:VIS] - mean) * rate).astype(BF)
        h_start = matmul(inputs, w_embed) + positions(coord[:VIS], scale[:VIS], D)
        h_end, enc_saved = block_forward(h_start, enc_weights, gains_enc, bias_enc, HEADS, 0)
        encoded = layer_norm(h_end, gain_enc_out).astype(BF)
        seen_out = matmul(encoded, w_link)
    late, dy_seen, vec, ready, *early = decoder_step(
        fast,
        pos_dec,
        seen_out,
        by_row,
        by_column,
        picked_hidden,
        stats,
        vector_row,
        w_dec,
        w_dec_down,
    )
    if fast:
        inputs_t, a_t, mixed_t, b_t, hidden_t, z_t = factors
        *enc_parts, dec_wide, dec_tall, vec = encoder_back(
            dy_seen,
            by_column,
            vec,
            vector_row,
            bias_enc,
            qkv,
            ready,
            late,
            (h_end, middle, h_start, slope),
            w_enc,
            w_enc_down,
            (z_t, hidden_t, b_t, mixed_t, a_t, inputs_t),
        )
        dec_parts = (dec_wide, dec_tall)
        vector_grad, loss_sum = vec[:5].reshape(-1), vec[5, 0]
    else:
        dseen = (dy_seen * by_column[:VIS, 0:1]).astype(BF)
        dec_vec, local_loss = vec[3:5].reshape(-1), vec[5, 0]
        dh_end, dgain_enc_out = norm_back(h_end, gain_enc_out, right_t(dseen, w_link))
        dh_start, enc_factors, dgains_enc = block_backward(
            enc_saved, dh_end, enc_weights, gains_enc, bias_enc, HEADS, 0
        )
        enc_grads = [matmul(*pair) for pair in enc_factors]
        link_grad = left_t(encoded, dseen)
        enc_parts = lax.psum(
            (
                reduce_rows(left_t(inputs, dh_start.astype(BF))),
                reduce_rows(
                    jnp.concatenate([enc_grads[0], enc_grads[1], enc_grads[2], link_grad], 1)
                ),
                reduce_rows(enc_grads[3]),
            ),
            "dp",
        )
        parts = DFF // DD
        early = early[0]
        dec_grads = jnp.concatenate([early[:, :, :parts], late, early[:, :, parts:]], 2)
        dec_grads = dec_grads.reshape(-1, *dec_grads.shape[2:])
        dec_sum = lax.psum(reduce_rows(dec_grads), "dp")[0]
        rows, parts = dec_sum.shape[1], DFF // DD
        dec_parts = (
            dec_sum[parts:].transpose(1, 0, 2).reshape(rows, -1),
            dec_sum[:parts].reshape(-1, DD),
        )
        vector_grad = jnp.concatenate([*dgains_enc, dgain_enc_out, dec_vec])
        vector_grad, loss_sum = lax.psum((vector_grad, local_loss), ("dp", "fsdp"))
    grads = (*enc_parts, *dec_parts)
    rate = STEP_UNIT * (PD * TOK_DEV * lax.axis_size("dp") * lax.axis_size("fsdp")) ** 0.5
    weights = (embed, wide_enc, enc_down, wide_dec, dec_down)
    moms = (embed_mom, wide_enc_mom, enc_down_mom, wide_dec_mom, dec_down_mom)
    avgs = (embed_avg, wide_enc_avg, enc_down_avg, wide_dec_avg, dec_down_avg)
    outs = advance_all(rate, grads, weights, moms, avgs)
    return (*outs, *advance(vectors, vector_mom, vector_avg, vector_grad, rate), loss_sum, count)


def solution(mesh):
    both, rows = P(("dp", "fsdp")), P("fsdp", None)
    placed = (P(("dp", "fsdp"), None), both, both, both, both, P(("dp", "fsdp"), None))
    states = (rows,) * 5 + (P(),)
    return jax.shard_map(
        body,
        mesh=mesh,
        in_specs=placed + states * 3,
        out_specs=(rows,) * 20 + (P(),) * 5,
        check_vma=False,
    )
```

```python
from functools import partial

import jax
import jax.numpy as jnp
import numpy as np
from jax import lax
from jax.experimental import pallas as pl
from jax.experimental.pallas import tpu as pltpu
from jax.sharding import PartitionSpec as P

D = 1024
HEADS = 16
FF = 4096
DD = 512
DHEADS = 16
DFF = 2048
PATCH = 16
BANDS = 3
TOK_DEV = 768
PD = 768
LOWD = 192
VIS = 192
HID = TOK_DEV - VIS

EPS = 1e-06
MOMENTUM = 0.9
DECAY = 0.0001
AVERAGE = 0.9
STEP_UNIT = 0.003
NEGATIVE = -1e30
LANES = 128
BF = jnp.bfloat16
F32 = jnp.float32


def matmul(left, right):
    return jnp.dot(left, right, preferred_element_type=jnp.float32)


def left_t(left, right):
    return lax.dot_general(
        left, right, (((0,), (0,)), ((), ())), preferred_element_type=jnp.float32
    )


def right_t(left, right):
    return lax.dot_general(
        left, right, (((1,), (1,)), ((), ())), preferred_element_type=jnp.float32
    )


def layer_norm(h, gain):
    mean = jnp.mean(h, -1, keepdims=True)
    cent = h - mean
    var = jnp.mean(cent * cent, -1, keepdims=True)
    return cent * lax.rsqrt(var + EPS) * gain


def norm_back(h, gain, grad):
    result, pull = jax.vjp(layer_norm, h, gain)
    return pull(grad)


def gelu_parts(before):
    below = 0.5 * (1.0 + lax.erf(before * 0.5**0.5))
    slope = below + before * jnp.exp(before * before * -0.5) * (0.5 / jnp.pi) ** 0.5
    return before * below, slope


def positions(coord, scale, width):
    quarter = width // 4
    omega = 10000.0 ** (-jnp.arange(quarter, dtype=jnp.float32) / quarter)
    angle_x = coord[:, 0:1] * scale[:, None] * omega[None, :]
    angle_y = coord[:, 1:2] * scale[:, None] * omega[None, :]
    return jnp.concatenate(
        [jnp.sin(angle_x), jnp.cos(angle_x), jnp.sin(angle_y), jnp.cos(angle_y)], -1
    )


def row_loss(pred, normed):
    rows = normed.shape[0]
    coarse = jnp.mean(normed.reshape(rows, BANDS, PATCH // 2, 2, PATCH // 2, 2), axis=(3, 5))
    upper = jnp.repeat(jnp.repeat(coarse, 2, axis=2), 2, axis=3).reshape(rows, PD)
    err_high = pred[:, :PD] - (normed - upper)
    err_low = pred[:, PD:] - coarse.reshape(rows, LOWD)
    return jnp.mean(jnp.sqrt(err_high * err_high + 1.0) - 1.0, -1) + jnp.mean(err_low * err_low, -1)


def attend_kernel(size, qt_ref, k_ref, vt_ref, bias_ref, ot_ref, lse_ref):
    per = LANES // size
    row_head = lax.broadcasted_iota(jnp.int32, qt_ref.shape, 0) // size
    factor = size ** (-0.5)
    for j in range(per):
        query = jnp.where(row_head == j, qt_ref[...].astype(F32), 0.0).astype(BF)
        scores = matmul(k_ref[...], query) * factor + bias_ref[...]
        top = jnp.max(scores, 0, keepdims=True)
        probs = jnp.exp(scores - top)
        total = jnp.sum(probs, 0, keepdims=True)
        probs = (probs * (1.0 / total)).astype(BF)
        rows = slice(j * size, (j + 1) * size)
        ot_ref[rows, :] = matmul(vt_ref[rows, :], probs).astype(BF)
        lse_ref[0, j : j + 1, :] = top + jnp.log(total)


def attend(qt, keys, vt, bias, size):
    width, queries = qt.shape
    rows = keys.shape[0]
    groups, per = width // LANES, LANES // size
    return pl.pallas_call(
        partial(attend_kernel, size),
        grid=(groups,),
        out_shape=(
            jax.ShapeDtypeStruct((width, queries), BF),
            jax.ShapeDtypeStruct((groups, per, queries), F32),
        ),
        in_specs=[
            pl.BlockSpec((LANES, queries), lambda g: (g, 0)),
            pl.BlockSpec((rows, LANES), lambda g: (0, g)),
            pl.BlockSpec((LANES, rows), lambda g: (g, 0)),
            pl.BlockSpec((rows, queries), lambda g: (0, 0)),
        ],
        out_specs=(
            pl.BlockSpec((LANES, queries), lambda g: (g, 0)),
            pl.BlockSpec((1, per, queries), lambda g: (g, 0, 0)),
        ),
        compiler_params=pltpu.CompilerParams(vmem_limit_bytes=40 * 2**20),
        cost_estimate=pl.CostEstimate(
            flops=4 * rows * queries * width * per,
            bytes_accessed=4 * rows * queries,
            transcendentals=rows * queries * width // size,
        ),
    )(qt, keys, vt, bias)


def attend_back_kernel(
    size,
    qt_ref,
    q_ref,
    k_ref,
    kt_ref,
    v_ref,
    do_ref,
    dot_ref,
    bias_ref,
    *rest,
):
    *lse_ref, dqt_ref, dk_ref, dv_ref = rest
    per = LANES // size
    row_head = lax.broadcasted_iota(jnp.int32, qt_ref.shape, 0) // size
    lane_head = lax.broadcasted_iota(jnp.int32, dk_ref.shape, 1) // size
    factor = size ** (-0.5)
    dkeys = jnp.zeros(dk_ref.shape, F32)
    dvalues = jnp.zeros(dv_ref.shape, F32)
    for j in range(per):
        query = jnp.where(row_head == j, qt_ref[...].astype(F32), 0.0).astype(BF)
        dout = jnp.where(row_head == j, dot_ref[...].astype(F32), 0.0).astype(BF)
        scores = matmul(k_ref[...], query) * factor + bias_ref[...]
        if lse_ref:
            probs = jnp.exp(scores - lse_ref[0][0, j : j + 1, :])
        else:
            probs = jnp.exp(scores - jnp.max(scores, 0, keepdims=True))
            probs = probs * (1.0 / jnp.sum(probs, 0, keepdims=True))
        dvalues = jnp.where(lane_head == j, matmul(probs.astype(BF), do_ref[...]), dvalues)
        dprobs = matmul(v_ref[...], dout)
        delta = jnp.sum(dprobs * probs, 0, keepdims=True)
        dscores = (probs * (dprobs - delta)).astype(BF)
        dkeys = jnp.where(lane_head == j, matmul(dscores, q_ref[...]), dkeys)
        rows = slice(j * size, (j + 1) * size)
        dqt_ref[rows, :] = (matmul(kt_ref[rows, :], dscores) * factor).astype(BF)
    dk_ref[...] = (dkeys * factor).astype(BF)
    dv_ref[...] = dvalues.astype(BF)


def attend_back(query, keys, values, dmixed, bias, lse, size):
    queries, width = query.shape
    rows = keys.shape[0]
    groups, per = width // LANES, LANES // size
    tall = lambda n: pl.BlockSpec((n, LANES), lambda g: (0, g))
    flat = lambda n: pl.BlockSpec((LANES, n), lambda g: (g, 0))
    return pl.pallas_call(
        partial(attend_back_kernel, size),
        grid=(groups,),
        out_shape=(
            jax.ShapeDtypeStruct((width, queries), BF),
            jax.ShapeDtypeStruct((rows, width), BF),
            jax.ShapeDtypeStruct((rows, width), BF),
        ),
        in_specs=[
            flat(queries),
            tall(queries),
            tall(rows),
            flat(rows),
            tall(rows),
            tall(queries),
            flat(queries),
            pl.BlockSpec((rows, queries), lambda g: (0, 0)),
        ]
        + [pl.BlockSpec((1, per, queries), lambda g: (g, 0, 0))] * (lse is not None),
        out_specs=(flat(queries), tall(rows), tall(rows)),
        compiler_params=pltpu.CompilerParams(vmem_limit_bytes=48 * 2**20),
        cost_estimate=pl.CostEstimate(
            flops=10 * rows * queries * width * per,
            bytes_accessed=4 * rows * queries,
            transcendentals=rows * queries * width // size,
        ),
    )(query.T, query, keys, keys.T, values, dmixed, dmixed.T, bias, *([] if lse is None else [lse]))


MESH = pl.DeviceIdType.MESH
UNIT = 512
HALF = UNIT // 2
ROWS = 128
HALF_ROWS = ROWS // 2
LAGS = (1, 3, 4, 6, 9)


def put(source, target, send, recv, device):
    return pltpu.make_async_remote_copy(
        src_ref=source,
        dst_ref=target,
        send_sem=send,
        recv_sem=recv,
        device_id=device,
        device_id_type=MESH,
    )


def back_kernel(
    dec_units,
    blocks,
    units,
    spots,
    dy_ref,
    column_ref,
    vec_ref,
    vectors_ref,
    bias_ref,
    qkv_ref,
    ready_ref,
    dec_ref,
    end_ref,
    middle_ref,
    start_ref,
    slope_ref,
    wide_ref,
    down_ref,
    *refs,
):
    n_left = max(b[0] for b in blocks) + 1
    lefts, refs = refs[:n_left], refs[n_left:]
    outs, refs = refs[:5], refs[5:]
    vec_out, refs = refs[0], refs[1:]
    (
        xo,
        xp,
        yo,
        yp,
        do,
        dp,
        a_out,
        a_in,
        b_out,
        b_in,
        sums,
        z_out,
        z_one,
        z_two,
        z_ready,
        v_in,
        v_out,
        wide_buf,
        down_buf,
        slope_buf,
        h_buf,
        dend_ref,
        dmid_ref,
        dbranch_ref,
        dmixed_ref,
        dqkv_ref,
        grad_vec,
        wide_sem,
        down_sem,
        slope_sem,
        h_sem,
        dec_sem,
        left_sem,
        right_sem,
        a_send,
        a_recv,
        b_send,
        b_recv,
        z_send,
        z_recv,
        v_send,
        v_recv,
        store_sem,
    ) = refs
    count, extra = dec_units + len(units), z_ready.shape[0]
    z, f = lax.axis_index("dp"), lax.axis_index("fsdp")
    core, place = f % 2, f // 2
    x, y = place % 2, place // 2
    partner = (z, f + 1 - 2 * core)
    x_side = (z, f + 2 - 4 * x)
    y_side = (z, f + 4 - 8 * y)
    at_x, at_y, at_far = place + 1 - 2 * x, place + 2 - 4 * y, 3 - place
    low = z < 2
    outer = (z == 0) | (z == 3)
    inner = (z == 1) | (z == 2)
    inward = (jnp.where(low, 1, 2), f)
    across = (3 - z, f)
    outward = (jnp.where(low, 0, 3), f)

    ring = wide_buf.shape[0]
    up_chunks, out_chunks, qkv_chunks = FF // UNIT, D // UNIT, 3 * D // UNIT
    chunks = 1 + up_chunks + out_chunks + qkv_chunks

    def wide_copy(w):
        inside = jnp.where(w < 1 + up_chunks, 4 * D + UNIT * (w - 1), 3 * D + UNIT * (w - 1 - up_chunks))
        column = jnp.where(
            w == 0,
            4 * D + FF,
            jnp.where(w < 1 + up_chunks + out_chunks, inside, UNIT * (w - 1 - up_chunks - out_chunks)),
        )
        return pltpu.make_async_copy(
            wide_ref.at[:, pl.ds(pl.multiple_of(column, UNIT), UNIT)],
            wide_buf.at[w % ring],
            wide_sem.at[w % ring],
        )

    def down_copy(j):
        rows = pl.ds(pl.multiple_of(j * UNIT, UNIT), UNIT)
        return pltpu.make_async_copy(down_ref.at[rows], down_buf.at[j % 2], down_sem.at[j % 2])

    def slope_copy(j):
        columns = pl.ds(pl.multiple_of(j * UNIT, UNIT), UNIT)
        return pltpu.make_async_copy(slope_ref.at[:, columns], slope_buf.at[j % 2], slope_sem.at[j % 2])

    def h_copy(source):
        return pltpu.make_async_copy(source, h_buf, h_sem.at[0])

    h_copy(end_ref).start()
    for n in range(ring):
        wide_copy(n).start()
    for n in range(2):
        down_copy(n).start()
        slope_copy(n).start()

    barrier = pltpu.get_barrier_semaphore()
    for device in (partner, x_side, y_side):
        pl.semaphore_signal(barrier, inc=1, device_id=device, device_id_type=MESH)

    @pl.when(outer)
    def _():
        pl.semaphore_signal(barrier, inc=1, device_id=inward, device_id_type=MESH)
        pl.semaphore_wait(barrier, 4)

    @pl.when(inner)
    def _():
        pl.semaphore_signal(barrier, inc=1, device_id=across, device_id_type=MESH)
        pl.semaphore_signal(barrier, inc=1, device_id=outward, device_id_type=MESH)
        pl.semaphore_wait(barrier, 5)

    def swap_dec(source, n):
        return put(source, dp.at[n], dec_sem.at[n, 1], dec_sem.at[n, 2], partner)

    def swap_left(source, b):
        return put(source, xp.at[b], left_sem.at[b, 1], left_sem.at[b, 2], partner)

    def swap_right(r):
        return put(yo.at[r], yp.at[r], right_sem.at[r, 0], right_sem.at[r, 1], partner)

    for n in range(dec_units):
        swap_dec(dec_ref.at[:, 1 - core, n], n).start()
        pltpu.make_async_copy(dec_ref.at[:, core, n], do.at[n], dec_sem.at[n, 0]).start()
    for b, (left, sub) in enumerate(blocks):
        rows = pl.ds(sub * ROWS, ROWS)
        swap_left(lefts[left].at[:, 1 - core, rows], b).start()
        pltpu.make_async_copy(lefts[left].at[:, core, rows], xo.at[b], left_sem.at[b, 0]).start()

    firsts = 1 + out_chunks
    single = next(n for n in range(1, len(units)) if units[n][1] >= firsts)
    starts = [n for n in range(1, len(units)) if units[n][0] != units[n - 1][0]]

    def block_of(e):
        return sum([jnp.where(e >= n, 1, 0) for n in starts], jnp.int32(0))

    def right_of(e):
        early = jnp.where(e == 0, 0, 1 + (e + out_chunks - 1) % out_chunks)
        return jnp.where(e < single, early, e - single + firsts)

    first, second = pl.ds(0, HALF), pl.ds(HALF, HALF)

    def ready_part(n, owners, columns):
        parts = [do[n, o, :, columns].astype(F32) + dp[n, o, :, columns].astype(F32) for o in owners]
        return parts[0] if len(parts) == 1 else jnp.concatenate(parts, 0)

    def formed_part(e, owners, columns):
        b, r = block_of(e), right_of(e)
        mine, other = [jnp.concatenate([ref[b, o] for o in owners], 0) for ref in (xo, xp)]
        return matmul(mine, yo[r, :, columns]) + matmul(other, yp[r, :, columns])

    def on_unit(u, stage):
        @pl.when(u < dec_units)
        def _():
            stage(partial(ready_part, jnp.minimum(u, dec_units - 1)))

        @pl.when(u >= dec_units)
        def _():
            stage(partial(formed_part, jnp.maximum(u - dec_units, 0)))

    def copy_a(u, side):
        slot = u % a_out.shape[0]
        return put(
            a_out.at[slot, side],
            a_in.at[u, side],
            a_send.at[slot, side],
            a_recv.at[u, side],
            (x_side, y_side)[side],
        )

    def copy_b(u, side):
        slot = u % b_out.shape[0]
        return put(
            b_out.at[slot, side],
            b_in.at[u, side],
            b_send.at[slot, side],
            b_recv.at[u, side],
            (y_side, x_side)[side],
        )

    z_slots = z_out.shape[0]

    def copy_in(u):
        return put(z_out.at[u % z_slots], z_one.at[u], z_send.at[u, 0], z_recv.at[u, 0], inward)

    def copy_across(u):
        return put(z_out.at[u % z_slots], z_two.at[u], z_send.at[u, 0], z_recv.at[u, 1], across)

    def copy_out(u):
        return put(z_one.at[u], z_one.at[u], z_send.at[u, 1], z_recv.at[u, 0], outward)

    def ready_in(n):
        u = count + n
        return put(z_ready.at[n], z_one.at[u], z_send.at[u, 0], z_recv.at[u, 0], inward)

    def ready_across(n):
        u = count + n
        return put(z_ready.at[n], z_two.at[u], z_send.at[u, 0], z_recv.at[u, 1], across)

    def copy_v(step, device):
        return put(v_out.at[step], v_in.at[step], v_send.at[step], v_recv.at[step], device)

    gain_one, gain_two, gain_out = [vectors_ref[:, n * D : (n + 1) * D] for n in range(3)]

    def give(r, value):
        yo[r] = value
        swap_right(r).start()

    def columns_at(n):
        return slice(n * UNIT, (n + 1) * UNIT)

    def back_link():
        dseen = jnp.where(column_ref[:VIS, 0:1] > 0, dy_ref[...], 0.0).astype(BF)
        give(0, dseen)
        wide_copy(0).wait()
        h_copy(end_ref).wait()
        unit, rate = normalize(h_buf[...])
        dend, dgain = normalize_back(unit, rate, gain_out, right_t(dseen, wide_buf[0]))
        grad_vec[...] = vec_ref[...]
        grad_vec[2:3, :] = dgain
        dend_ref[...] = dend
        dbranch_ref[...] = dend.astype(BF)
        for n in range(out_chunks):
            give(1 + n, dbranch_ref[:, columns_at(n)])
        wide_copy(ring).start()
        h_copy(middle_ref).start()
        dmid_ref[...] = jnp.zeros_like(dmid_ref)

    def back_hidden(j):
        w = 1 + j
        down_copy(j).wait()
        slope_copy(j).wait()
        wide_copy(w).wait()
        dhidden = right_t(dbranch_ref[...], down_buf[j % 2])
        dbefore = (dhidden * slope_buf[j % 2]).astype(BF)
        give(firsts + j, dbefore)
        dmid_ref[...] += right_t(dbefore, wide_buf[w % ring])
        wide_copy(w + ring).start()

        @pl.when(j + 2 < up_chunks)
        def _():
            down_copy(j + 2).start()
            slope_copy(j + 2).start()

    def back_out():
        h_copy(middle_ref).wait()
        unit, rate = normalize(h_buf[...])
        dmiddle, dgain = normalize_back(unit, rate, gain_two, dmid_ref[...])
        grad_vec[1:2, :] = dgain
        dmiddle = dmiddle + dend_ref[...]
        dend_ref[...] = dmiddle
        dattn = dmiddle.astype(BF)
        dmixed = jnp.zeros((VIS, D), F32)
        for n in range(out_chunks):
            w = 1 + up_chunks + n
            piece = dattn[:, columns_at(n)]
            give(firsts + up_chunks + n, piece)
            wide_copy(w).wait()
            dmixed = dmixed + right_t(piece, wide_buf[w % ring])
            wide_copy(w + ring).start()
        dmixed_ref[...] = dmixed.astype(BF)
        h_copy(start_ref).start()
        dmid_ref[...] = jnp.zeros_like(dmid_ref)

    size = D // HEADS
    lane_head = lax.broadcasted_iota(jnp.int32, (VIS, LANES), 1) // size

    def only(array, j):
        return jnp.where(lane_head == j, array.astype(F32), 0.0).astype(BF)

    def back_attention(g):
        at = [pl.ds(pl.multiple_of(n * D + g * LANES, LANES), LANES) for n in range(3)]
        query, keys, values = [qkv_ref[:, lanes] for lanes in at]
        dout = dmixed_ref[:, at[0]]
        keys_t = keys.T
        factor = size ** (-0.5)
        dkeys, dvalues = jnp.zeros((VIS, LANES), F32), jnp.zeros((VIS, LANES), F32)
        dquery = []
        for j in range(LANES // size):
            scores = right_t(keys, only(query, j)) * factor + bias_ref[...]
            probs = jnp.exp(scores - jnp.max(scores, 0, keepdims=True))
            probs = probs * (1.0 / jnp.sum(probs, 0, keepdims=True))
            dvalues = jnp.where(lane_head == j, matmul(probs.astype(BF), dout), dvalues)
            dprobs = right_t(values, only(dout, j))
            delta = jnp.sum(dprobs * probs, 0, keepdims=True)
            dscores = (probs * (dprobs - delta)).astype(BF)
            dkeys = jnp.where(lane_head == j, matmul(dscores, query), dkeys)
            dquery.append(matmul(keys_t[j * size : (j + 1) * size, :], dscores))
        dqkv_ref[:, at[0]] = (jnp.concatenate(dquery, 0) * factor).astype(BF).T
        dqkv_ref[:, at[1]] = (dkeys * factor).astype(BF)
        dqkv_ref[:, at[2]] = dvalues.astype(BF)

    def give_qkv():
        for c in range(qkv_chunks):
            give(firsts + up_chunks + out_chunks + c, dqkv_ref[:, columns_at(c)])

    def back_qkv(c):
        w = 1 + up_chunks + out_chunks + c
        wide_copy(w).wait()
        piece = dqkv_ref[:, pl.ds(pl.multiple_of(c * UNIT, UNIT), UNIT)]
        dmid_ref[...] += right_t(piece, wide_buf[w % ring])

        @pl.when(w + ring < chunks)
        def _():
            wide_copy(w + ring).start()

    def back_start():
        h_copy(start_ref).wait()
        unit, rate = normalize(h_buf[...])
        dh, dgain = normalize_back(unit, rate, gain_one, dmid_ref[...])
        grad_vec[0:1, :] = dgain
        dh = (dh + dend_ref[...]).astype(BF)
        for n in range(out_chunks):
            give(firsts + up_chunks + out_chunks + qkv_chunks + n, dh[:, columns_at(n)])

    at_hidden = 1
    at_out = at_hidden + up_chunks
    at_attention = at_out + 1
    groups = D // LANES
    at_qkv = at_attention + groups
    at_start = at_qkv + qkv_chunks
    at_vec = at_start + 1

    def step(i, _):
        def stage(lag, also=None):
            u = i - lag
            ok = (u >= 0) & (u < count)
            if also is not None:
                ok = ok & also
            return u, pl.when(ok)

        u0, when = stage(0)

        @when
        def _():
            u = u0

            @pl.when(u < dec_units)
            def _():
                pltpu.make_async_copy(do.at[u], do.at[u], dec_sem.at[u, 0]).wait()
                swap_dec(do.at[u], u).wait()

            @pl.when(u == dec_units)
            def _():
                for b in range(len(blocks)):
                    pltpu.make_async_copy(xo.at[b], xo.at[b], left_sem.at[b, 0]).wait()
                    swap_left(xo.at[b], b).wait()
                for r in range(firsts):
                    swap_right(r).wait()

            @pl.when(u >= dec_units + single)
            def _():
                swap_right(u - dec_units - single + firsts).wait()

            @pl.when(u >= a_out.shape[0])
            def _():
                for side in range(2):
                    copy_a(u - a_out.shape[0], side).wait_send()

            slot = u % a_out.shape[0]

            def send(part):
                for side, (near, columns) in enumerate(((at_x, first), (at_y, second))):
                    both = part((near, at_far), columns).astype(BF)
                    a_out[slot, side] = both.reshape(2, ROWS, HALF)

            on_unit(u, send)
            for side in range(2):
                copy_a(u, side).start()

        u1, when = stage(LAGS[0])

        @when
        def _():
            u = u1
            slot = u % b_out.shape[0]

            @pl.when(u >= b_out.shape[0])
            def _():
                for side in range(2):
                    copy_b(u - b_out.shape[0], side).wait_send()

            for side in range(2):
                copy_a(u, side).wait_recv()

            def send(part):
                for side, (near, columns) in enumerate(((at_y, first), (at_x, second))):
                    total = part((near,), columns) + a_in[u, side, 1].astype(F32)
                    b_out[slot, side] = total.astype(BF)

            on_unit(u, send)
            for side in range(2):
                copy_b(u, side).start()

        u2, when = stage(LAGS[1])

        @when
        def _():
            u = u2
            copy_b(u, 0).wait_recv()
            copy_b(u, 1).wait_recv()

            def keep(part):
                whole = part((place,), slice(None))
                for side, columns in enumerate((slice(0, HALF), slice(HALF, UNIT))):
                    total = whole[:, columns] + a_in[u, side, 0].astype(F32)
                    sums[u % 4, :, columns] = total + b_in[u, side].astype(F32)

            on_unit(u, keep)

            @pl.when(outer)
            def _():
                @pl.when(u >= z_slots)
                def _():
                    copy_in(u - z_slots).wait_send()

                z_out[u % z_slots] = sums[u % 4].astype(BF)
                copy_in(u).start()

        u3, when = stage(LAGS[2], inner)

        @when
        def _():
            u = u3
            copy_in(u).wait_recv()

            @pl.when(u >= z_slots)
            def _():
                copy_across(u - z_slots).wait_send()

            z_out[u % z_slots] = (sums[u % 4] + z_one[u].astype(F32)).astype(BF)
            copy_across(u).start()

        u4, when = stage(LAGS[3], inner)

        @when
        def _():
            u = u4
            copy_across(u).wait_recv()
            z_one[u] = (z_out[u % z_slots].astype(F32) + z_two[u].astype(F32)).astype(BF)
            copy_out(u).start()

        u5, when = stage(LAGS[4], outer)

        @when
        def _():
            copy_out(u5).wait_recv()

        ends = [lag - LAGS[1] for lag in LAGS[2:]]

        @pl.when((i < extra) & outer)
        def _():
            z_ready[i] = ready_ref[i].astype(BF)
            ready_in(i).start()

        @pl.when((i >= ends[0]) & (i < extra + ends[0]) & inner)
        def _():
            n = i - ends[0]
            ready_in(n).wait_recv()
            z_ready[n] = (ready_ref[n] + z_one[count + n].astype(F32)).astype(BF)
            ready_across(n).start()

        @pl.when((i >= ends[1]) & (i < extra + ends[1]) & inner)
        def _():
            n = i - ends[1]
            ready_across(n).wait_recv()
            total = z_ready[n].astype(F32) + z_two[count + n].astype(F32)
            z_one[count + n] = total.astype(BF)
            copy_out(count + n).start()

        @pl.when((i >= ends[2]) & (i < extra + ends[2]) & outer)
        def _():
            copy_out(count + i - ends[2]).wait_recv()

        pl.when(i == 0)(back_link)

        @pl.when((i >= at_hidden) & (i < at_hidden + up_chunks))
        def _():
            back_hidden(i - at_hidden)

        pl.when(i == at_out)(back_out)

        @pl.when((i >= at_attention) & (i < at_attention + groups))
        def _():
            back_attention(i - at_attention)

        pl.when(i == at_qkv)(give_qkv)

        @pl.when((i >= at_qkv) & (i < at_qkv + qkv_chunks))
        def _():
            back_qkv(i - at_qkv)

        pl.when(i == at_start)(back_start)

        for number, device in enumerate((partner, x_side, y_side)):

            @pl.when(i == at_vec + number)
            def _():
                if number == 0:
                    v_out[0] = grad_vec[...]
                else:
                    copy_v(number - 1, (partner, x_side, y_side)[number - 1]).wait_recv()
                    v_out[number] = v_out[number - 1] + v_in[number - 1]
                copy_v(number, device).start()

        @pl.when(i == at_vec + 3)
        def _():
            copy_v(2, y_side).wait_recv()
            v_out[3] = v_out[2] + v_in[2]

            @pl.when(outer)
            def _():
                copy_v(3, inward).start()

        @pl.when((i == at_vec + 4) & inner)
        def _():
            copy_v(3, inward).wait_recv()
            v_out[4] = v_out[3] + v_in[3]
            copy_v(4, across).start()

        @pl.when((i == at_vec + 5) & inner)
        def _():
            copy_v(4, across).wait_recv()
            v_out[5] = v_out[4] + v_in[4]
            copy_v(5, outward).start()
            vec_out[...] = v_out[5]

        @pl.when((i == at_vec + 7) & outer)
        def _():
            copy_v(5, outward).wait_recv()
            vec_out[...] = v_in[5]

        return 0

    lax.fori_loop(0, count + LAGS[4], step, 0)

    stores = []
    for n, (u, start, out, row, rows, column) in enumerate(spots):
        stores.append(
            pltpu.make_async_copy(
                z_one.at[u, pl.ds(start, rows)],
                outs[out].at[pl.ds(row, rows), pl.ds(column, UNIT)],
                store_sem.at[n],
            )
        )
    for store in stores:
        store.start()
    for u in range(count - a_out.shape[0], count):
        for side in range(2):
            copy_a(u, side).wait_send()
    for u in range(count - b_out.shape[0], count):
        for side in range(2):
            copy_b(u, side).wait_send()
    for number, device in enumerate((partner, x_side, y_side)):
        copy_v(number, device).wait_send()
    for store in stores:
        store.wait()

    @pl.when(outer)
    def _():
        copy_v(3, inward).wait_send()
        for u in range(count - z_slots, count):
            copy_in(u).wait_send()
        for n in range(extra):
            ready_in(n).wait_send()

    @pl.when(inner)
    def _():
        copy_v(4, across).wait_send()
        copy_v(5, outward).wait_send()
        for u in range(count - z_slots, count):
            copy_across(u).wait_send()
        for n in range(extra):
            ready_across(n).wait_send()

        def drain(u, _):
            copy_out(u).wait_send()
            return 0

        lax.fori_loop(0, count + extra, drain, 0)


def encoder_back(dy, by_column, vec, vectors, bias, qkv, ready, dec, states, wide, down, lefts):
    owners = lax.axis_size("fsdp")
    own = PD // owners
    dec_units = LATE // 2
    dec = dec.reshape(4, 2, dec_units, ROWS, UNIT)
    half = ROWS // 2
    blocks, units, spots = [], [], []
    def add(left, sub, right, out, row, rows, column, columns):
        blocks.append((left, sub))
        for n in range(columns // UNIT):
            spots.append((dec_units + len(units), 0, out, row, rows, column + n * UNIT))
            units.append((len(blocks) - 1, right + n))

    subs = FF // owners // ROWS
    add(0, 0, 0, 1, 0, ROWS, 4 * D + FF, DD)
    for n in range(subs):
        add(1, n, 1, 2, n * ROWS, ROWS, 0, D)
    right = 1 + D // UNIT
    add(2, 0, right, 1, 0, ROWS, 4 * D, FF)
    right += FF // UNIT
    add(3, 0, right, 1, 0, ROWS, 3 * D, D)
    right += D // UNIT
    add(4, 0, right, 1, 0, ROWS, 0, 3 * D)
    right += 3 * D // UNIT
    add(5, 0, right, 0, 0, own, 0, D)
    right += D // UNIT
    count = dec_units + len(units)
    tall = DFF // DD
    for n in range(EARLY + LATE):
        if tall <= n < tall + LATE:
            unit = (n - tall) // 2
        else:
            unit = count + (n if n < tall else n - LATE) // 2
        place = (4, n * half, half, 0) if n < tall else (3, 0, half, (n - tall) * UNIT)
        spots.append((unit, n % 2 * half, *place))
    full = count + ready.shape[0]
    shapes = ((own, D), (ROWS, 4 * D + FF + DD), (FF // owners, D), (half, 10 * UNIT), (DFF // owners, DD))
    lefts = [a.reshape(4, 2, -1, VIS) for a in lefts]
    slots = 3
    dma = pltpu.SemaphoreType.DMA
    vmem, anywhere = pl.BlockSpec(memory_space=pltpu.VMEM), pl.BlockSpec(memory_space=pl.ANY)
    return pl.pallas_call(
        partial(back_kernel, dec_units, tuple(blocks), tuple(units), tuple(spots)),
        out_shape=tuple(jax.ShapeDtypeStruct(shape, BF) for shape in shapes)
        + (jax.ShapeDtypeStruct(vec.shape, F32),),
        in_specs=[vmem] * 7 + [anywhere] * (7 + len(lefts)),
        out_specs=(anywhere,) * len(shapes) + (vmem,),
        scratch_shapes=[
            pltpu.VMEM((len(blocks), 4, ROWS, VIS), BF),
            pltpu.VMEM((len(blocks), 4, ROWS, VIS), BF),
            pltpu.VMEM((right, VIS, UNIT), BF),
            pltpu.VMEM((right, VIS, UNIT), BF),
            pltpu.VMEM((dec_units, 4, ROWS, UNIT), BF),
            pltpu.VMEM((dec_units, 4, ROWS, UNIT), BF),
            pltpu.VMEM((slots, 2, 2, ROWS, HALF), BF),
            pltpu.VMEM((count, 2, 2, ROWS, HALF), BF),
            pltpu.VMEM((slots, 2, ROWS, HALF), BF),
            pltpu.VMEM((count, 2, ROWS, HALF), BF),
            pltpu.VMEM((4, ROWS, UNIT), F32),
            pltpu.VMEM((6, ROWS, UNIT), BF),
            pltpu.VMEM((full, ROWS, UNIT), BF),
            pltpu.VMEM((full, ROWS, UNIT), BF),
            pltpu.VMEM(ready.shape, BF),
            pltpu.VMEM((6, *vec.shape), F32),
            pltpu.VMEM((6, *vec.shape), F32),
            pltpu.VMEM((3, D, UNIT), BF),
            pltpu.VMEM((2, UNIT, D), BF),
            pltpu.VMEM((2, VIS, UNIT), F32),
            pltpu.VMEM((VIS, D), F32),
            pltpu.VMEM((VIS, D), F32),
            pltpu.VMEM((VIS, D), F32),
            pltpu.VMEM((VIS, D), BF),
            pltpu.VMEM((VIS, D), BF),
            pltpu.VMEM((VIS, 3 * D), BF),
            pltpu.VMEM(vec.shape, F32),
            dma((3,)),
            dma((2,)),
            dma((2,)),
            dma((1,)),
            dma((dec_units, 3)),
            dma((len(blocks), 3)),
            dma((right, 2)),
            dma((slots, 2)),
            dma((count, 2)),
            dma((slots, 2)),
            dma((count, 2)),
            dma((full, 2)),
            dma((full, 2)),
            dma((6,)),
            dma((6,)),
            dma((len(spots),)),
        ],
        compiler_params=pltpu.CompilerParams(
            collective_id=0, has_side_effects=True, vmem_limit_bytes=61 * 2**20
        ),
        cost_estimate=pl.CostEstimate(
            flops=30 * 10**9, bytes_accessed=300 * 2**20, transcendentals=0
        ),
    )(dy, by_column, vec, vectors, bias, qkv, ready, dec, *states, wide, down, *lefts)


def encoder_pieces(shapes):
    (own, width), (rows, _), (tall, _), (dec_rows, dec_width), (dec_tall, _) = shapes
    half = dec_rows // 2
    named = {"embed": (0, 0, own, 0, width, 0), "out": (1, 0, rows, 3 * D, D, 1)}
    named["link"] = (1, 0, rows, 4 * D + FF, DD, 0)
    named["tall"] = (4, 0, dec_tall, 0, DD, 0)
    for n in range(3):
        named["qkv", n] = (1, 0, rows, n * D, D, (1, 2, 0)[n])
    for n in range(FF // D):
        named["up", n] = (1, 0, rows, 4 * D + n * D, D, (2, 0, 1, 2)[n])
    for n in range(tall // rows):
        named["down", n] = (2, n * rows, rows, 0, D, (0, 1, 2, 0)[n])
    for n in range(2):
        named["wide", n] = (3, n * half, half, 0, dec_width, n + 1)
    order = [("qkv", 0), ("qkv", 1), "out", ("up", 0), "embed", ("qkv", 2), ("up", 2), ("up", 3)]
    order += [("up", 1), ("down", 1), ("down", 2), ("down", 0), ("wide", 0), ("wide", 1)]
    order += [("down", 3), "link", "tall"]
    return [named[name] for name in order], {name: t for t, name in enumerate(order)}


def norm_rows(h, gain):
    mean = jnp.mean(h, -1, keepdims=True)
    cent = h - mean
    var = jnp.mean(cent * cent, -1, keepdims=True)
    return (cent * lax.rsqrt(var + EPS) * gain).astype(BF)


def encoder_kernel(
    pixels_ref,
    row_ref,
    column_ref,
    scale_ref,
    omega_ref,
    vectors_ref,
    embed_ref,
    wide_ref,
    down_ref,
    dec_wide_ref,
    dec_down_ref,
    wide_out,
    down_out,
    dec_wide_out,
    dec_down_out,
    picked_out,
    slope_out,
    stats_out,
    by_row,
    by_column,
    pos_out,
    bias_out,
    inputs_t,
    a_t,
    mixed_t,
    b_t,
    hidden_t,
    z_t,
    start_ref,
    qkv_ref,
    middle_ref,
    end_ref,
    seen_ref,
    inputs_ref,
    a_ref,
    mixed_ref,
    b_ref,
    hidden_ref,
    z_ref,
    w_embed,
    w_wide,
    w_down,
    stage_ref,
    pick_ref,
    high_ref,
    mid_ref,
    low_ref,
    picked_ref,
    pos_ref,
    bias_ref,
    dec_stage,
    dec_stage_down,
    dec_own,
    dec_own_down,
    slope_ref,
    hidden_pixels,
    v_in,
    v_out,
    load_sem,
    store_sem,
    send_sem,
    recv_sem,
    v_send,
    v_recv,
    side_sem,
):
    shards = (embed_ref, wide_ref, down_ref, dec_wide_ref, dec_down_ref)
    gathered = (w_embed, w_wide, w_down, dec_wide_out, dec_down_out)
    gain_one, gain_two, gain_out = [vectors_ref[:, n * D : (n + 1) * D] for n in range(3)]
    pieces, at = encoder_pieces([ref.shape for ref in shards])
    count = len(pieces)
    stores = []
    z, f = lax.axis_index("dp"), lax.axis_index("fsdp")
    core, place = f % 2, f // 2
    x, y = place % 2, place // 2
    f_x, f_y, f_far = f + 2 - 4 * x, f + 4 - 8 * y, f + 6 - 4 * x - 8 * y
    partner = (z, f + 1 - 2 * core)
    x_side, y_side, z_side = (z, f_x), (z, f_y), (z + 1 - 2 * (z % 2), f)
    outer = (z == 0) | (z == 3)
    inner = (z == 1) | (z == 2)
    across = (3 - z, f)

    barrier = pltpu.get_barrier_semaphore()
    for device in (partner, x_side, y_side, z_side):
        pl.semaphore_signal(barrier, inc=1, device_id=device, device_id_type=MESH)

    @pl.when(outer)
    def _():
        pl.semaphore_wait(barrier, 4)

    @pl.when(inner)
    def _():
        pl.semaphore_signal(barrier, inc=1, device_id=across, device_id_type=MESH)
        pl.semaphore_wait(barrier, 5)

    stages = stage_ref.shape[0]

    def load(t):
        array, row, rows, column, columns, _ = pieces[t]
        return pltpu.make_async_copy(
            shards[array].at[pl.ds(row, rows), pl.ds(column, columns)],
            stage_ref.at[staged[t], pl.ds(0, rows), pl.ds(0, columns)],
            load_sem.at[staged[t]],
        )

    encoder = [t for t, piece in enumerate(pieces) if piece[0] < 3]
    staged = {t: n % stages for n, t in enumerate(encoder)}
    after = dict(zip(encoder, encoder[stages:]))
    dec_loads = [
        pltpu.make_async_copy(dec_wide_ref, dec_stage, side_sem.at[0]),
        pltpu.make_async_copy(dec_down_ref, dec_stage_down, side_sem.at[1]),
    ]
    for copy in dec_loads:
        copy.start()
    for t in encoder[:stages]:
        load(t).start()

    def spot(t, owner, half=None):
        array, row, rows, column, columns, _ = pieces[t]
        if array > 2:
            if half is not None:
                rows //= 2
                row += half * rows
            return gathered[array].at[owner, pl.ds(row, rows)]
        if half is not None:
            columns //= 2
            column += half * columns
        return gathered[array].at[owner, pl.ds(row, rows), pl.ds(column, columns)]

    def move(t, owner, send, recv, device, half=None):
        target = source = spot(t, owner, half)
        array, row, rows = pieces[t][:3]
        if send < 3 and array > 2:
            source = (dec_own, dec_own_down)[array - 3].at[pl.ds(row, rows)]
        return put(source, target, send_sem.at[t, send], recv_sem.at[t, recv], device)

    def own_x(t):
        return move(t, f, 0, 0, x_side)

    def own_y(t):
        return move(t, f, 1, 1, y_side)

    def own_core(t):
        return move(t, f, 2, 4, partner)

    def far_x(t):
        return move(t, f_y, 3, 2, x_side, 0)

    def far_y(t):
        return move(t, f_x, 4, 3, y_side, 1)

    def to_core(t, n):
        return move(t, (f_x, f_y, f_far)[n], 5 + n, 5 + n, partner)

    def to_z(t, n):
        return move(t, (f_x, f_y, f_far)[n], 8 + n, 8 + n, z_side)

    def brings(t, then, other=None):
        kind = pieces[t][5]
        if kind == 0:
            then()
            return
        pl.when(z % 2 == kind - 1)(then)
        if other is not None:
            pl.when(z % 2 != kind - 1)(other)

    def first(t):
        array, row, rows, column, columns, _ = pieces[t]
        if array < 3:
            load(t).wait()
            spot(t, f)[...] = stage_ref[staged[t], :rows, :columns].astype(BF)
            if t in after:
                load(after[t]).start()
        else:
            if row == 0:
                dec_loads[array - 3].wait()
            own = (dec_own, dec_own_down)[array - 3]
            own[row : row + rows, :] = (dec_stage, dec_stage_down)[array - 3][
                row : row + rows, :
            ].astype(BF)
            store = pltpu.make_async_copy(own.at[pl.ds(row, rows)], spot(t, f), store_sem.at[t])
            store.start()
            stores.append(store)
        own_core(t).start()

        def then():
            own_x(t).start()
            own_y(t).start()

        brings(t, then)

    def second(t):
        def then():
            own_x(t).wait_recv()
            far_y(t).start()
            own_y(t).wait_recv()
            far_x(t).start()
            for n in range(2):
                to_core(t, n).start()
                if pieces[t][5]:
                    to_z(t, n).start()

        brings(t, then)

    def third(t):
        def then():
            far_x(t).wait_recv()
            far_y(t).wait_recv()
            to_core(t, 2).start()
            if pieces[t][5]:
                to_z(t, 2).start()

        brings(t, then)

    def taken(t, n):
        def other():
            to_z(t, n).wait_recv()
            to_core(t, n).start()

        brings(t, lambda: None, other)

    def whole(t):
        own_core(t).wait_recv()
        for n in range(3):
            to_core(t, n).wait_recv()

    def drain(t):
        own_core(t).wait_send()
        for n in range(3):
            to_core(t, n).wait_send()

        def then():
            for copy in (own_x(t), own_y(t), far_x(t), far_y(t)):
                copy.wait_send()
            if pieces[t][5]:
                for n in range(3):
                    to_z(t, n).wait_send()

        brings(t, then)

    def copy_v(step, device):
        return put(v_out.at[step], v_in.at[step], v_send.at[step], v_recv.at[step], device)

    sides = (partner, x_side, y_side)

    def statistics(i):
        if i <= 3:
            if i > 0:
                copy_v(i - 1, sides[i - 1]).wait_recv()
                v_out[i] = v_out[i - 1] + v_in[i - 1]
            if i < 3:
                copy_v(i, sides[i]).start()
            else:

                @pl.when(outer)
                def _():
                    copy_v(3, z_side).start()

        if i == 4:

            @pl.when(inner)
            def _():
                copy_v(3, z_side).wait_recv()
                v_out[4] = v_out[3] + v_in[3]
                copy_v(4, across).start()

        if i == 5:

            @pl.when(inner)
            def _():
                copy_v(4, across).wait_recv()
                v_out[5] = v_out[4] + v_in[4]
                copy_v(5, z_side).start()
                stats_out[...] = v_out[5]

            @pl.when(outer)
            def _():
                copy_v(5, z_side).wait_recv()
                stats_out[...] = v_in[5]

    def turn(source, target, start=0, width=D):
        for lane in range(start, start + width, LANES):
            target[lane : lane + LANES, :] = source[:, lane : lane + LANES].T

    def columns_of(t):
        array, row, rows, column, columns, _ = pieces[t]
        weight = gathered[array][:, row : row + rows, column : column + columns]
        return weight.reshape(-1, columns)

    def local_statistics():
        pixels = pixels_ref[...]
        weighted = pixels * column_ref[:, 0:1]
        sums = jnp.sum(weighted, 0, keepdims=True)
        squares = jnp.sum(weighted * pixels, 0, keepdims=True)
        live = row_ref[0:1, :]
        totals = [r[:, n * PATCH**2 : (n + 1) * PATCH**2] for r in (sums, squares) for n in range(BANDS)]
        for n, total in enumerate((*totals, live, live * row_ref[1:2, :])):
            v_out[0, n : n + 1, :] = jnp.broadcast_to(jnp.sum(total, 1, keepdims=True), (1, LANES))

    def arrange_step():
        slots = (TOK_DEV, TOK_DEV)
        down, along = [lax.broadcasted_iota(jnp.int32, slots, n) for n in range(2)]
        live, masked = row_ref[0:1, :], row_ref[1:2, :]
        seen, hid = live * (1.0 - masked), live * masked
        kind = lax.broadcasted_iota(jnp.int32, row_ref.shape, 0)
        kinds = jnp.where(kind == 0, seen, jnp.where(kind == 1, hid, 1.0 - live))
        ranks = matmul(kinds.astype(BF), jnp.where(down < along, 1.0, 0.0).astype(BF))
        n_seen, n_hid = [jnp.sum(r, 1, keepdims=True) for r in (seen, hid)]
        empty = ranks[2:3, :]
        place = jnp.where(empty < VIS - n_seen, n_seen + empty, n_seen + n_hid + empty)
        place = jnp.where(hid > 0, VIS + ranks[1:2, :], place)
        place = jnp.where(seen > 0, ranks[0:1, :], place)
        pick_ref[...] = jnp.where(down == place.astype(jnp.int32), 1.0, 0.0).astype(BF)
        facts = row_ref[...].astype(BF)
        by_row[...] = right_t(facts, pick_ref[...])
        by_column[...] = right_t(pick_ref[...], facts)
        pixels = pixels_ref[...]
        high = pixels.astype(BF)
        rest = pixels - high.astype(F32)
        mid = rest.astype(BF)
        high_ref[...], mid_ref[...] = high, mid
        low_ref[...] = (rest - mid.astype(F32)).astype(BF)

    def pick_rows(rows):
        pick = pick_ref[rows, :]
        return matmul(pick, high_ref[...]) + matmul(pick, mid_ref[...]) + matmul(pick, low_ref[...])

    def pick_step():
        picked_ref[...] = pick_rows(slice(0, VIS))
        same = by_column[:VIS, 2:3] == by_row[2:3, :VIS]
        shape = (VIS, VIS)
        bias_out[...] = mask_bias(by_column[:VIS, 0:1] > 0, same, shape, 0)
        bias_ref[...] = mask_bias(by_row[0:1, :VIS] > 0, same, shape, 0, 1)

    def position_rows(target, rows, width, row):
        quarter = width // 4
        odd = by_column[rows, 2:3] > 0
        scale = jnp.where(odd, scale_ref[1:2, 0:1], scale_ref[0:1, 0:1])
        for n in range(2):
            angle = by_column[rows, 3 + n : 4 + n] * scale * omega_ref[row : row + 1, :quarter]
            target[rows, 2 * n * quarter : (2 * n + 1) * quarter] = jnp.sin(angle)
            target[rows, (2 * n + 1) * quarter : (2 * n + 2) * quarter] = jnp.cos(angle)

    def pixel_store(n):
        return pltpu.make_async_copy(
            hidden_pixels, picked_out.at[pl.ds((n - 1) * VIS, VIS)], side_sem.at[4]
        )

    def hidden_step(n):
        rows = slice(n * VIS, (n + 1) * VIS)
        if n > 0:
            if n > 1:
                pixel_store(n - 1).wait()
            hidden_pixels[...] = pick_rows(rows)
            pixel_store(n).start()
        position_rows(pos_out, rows, DD, 1)

    def embed_step():
        pixels = stats_out[6:7, :] * (PATCH * PATCH)
        for band in range(BANDS):
            mean = stats_out[band : band + 1, :] / pixels
            var = stats_out[BANDS + band : BANDS + band + 1, :] / pixels - mean * mean
            rate = lax.rsqrt(var + EPS)
            for part in range(PATCH * PATCH // LANES):
                lanes = pl.ds(band * PATCH * PATCH + part * LANES, LANES)
                inputs_ref[:, lanes] = ((picked_ref[:, lanes] - mean) * rate).astype(BF)
        start_ref[...] = matmul(inputs_ref[...], columns_of(at["embed"])) + pos_ref[...]
        a_ref[...] = norm_rows(start_ref[...], gain_one)
        own = w_embed.shape[1]
        flipped = jnp.concatenate(
            [inputs_ref[:, lane : lane + LANES].T for lane in range(0, PD, LANES)], 0
        )
        inputs_t[...] = jnp.zeros_like(inputs_t)
        for owner in range(w_embed.shape[0]):
            inputs_t[owner, :own, :] = flipped[owner * own : (owner + 1) * own, :]
        turn(a_ref, a_t)

    def qkv_step(n):
        qkv_ref[:, n * D : (n + 1) * D] = matmul(a_ref[...], columns_of(at["qkv", n])).astype(BF)

    def attention_step():
        size = D // HEADS
        lane_head = lax.broadcasted_iota(jnp.int32, (VIS, LANES), 1) // size

        def group(g, _):
            query, keys, values = [
                qkv_ref[:, pl.ds(pl.multiple_of(n * D + g * LANES, LANES), LANES)] for n in range(3)
            ]
            mixed = jnp.zeros((VIS, LANES), F32)
            for j in range(LANES // size):
                one = jnp.where(lane_head == j, query.astype(F32), 0.0).astype(BF)
                scores = right_t(one, keys) * size ** (-0.5) + bias_ref[...]
                probs = jnp.exp(scores - jnp.max(scores, -1, keepdims=True))
                probs = probs * (1.0 / jnp.sum(probs, -1, keepdims=True))
                mixed = jnp.where(lane_head == j, matmul(probs.astype(BF), values), mixed)
            mixed_ref[:, pl.ds(pl.multiple_of(g * LANES, LANES), LANES)] = mixed.astype(BF)
            return 0

        lax.fori_loop(0, D // LANES, group, 0)

    def out_step():
        turn(mixed_ref, mixed_t)
        middle_ref[...] = start_ref[...] + matmul(mixed_ref[...], columns_of(at["out"]))
        b_ref[...] = norm_rows(middle_ref[...], gain_two)
        turn(b_ref, b_t)

    def slope_store(n):
        return pltpu.make_async_copy(
            slope_ref.at[n % 2], slope_out.at[:, pl.ds(n * D, D)], side_sem.at[2 + n % 2]
        )

    def up_step(n):
        columns = slice(n * D, (n + 1) * D)
        after, slope = gelu_parts(matmul(b_ref[...], columns_of(at["up", n])))
        hidden_ref[:, columns] = after.astype(BF)
        if n > 1:
            slope_store(n - 2).wait()
        slope_ref[n % 2] = slope
        slope_store(n).start()
        turn(hidden_ref, hidden_t, n * D)

    def down_step(n):
        rows, owners = w_wide.shape[1], w_down.shape[0]
        tall = w_down.shape[1]
        parts = [hidden_ref[:, o * tall + n * rows : o * tall + (n + 1) * rows] for o in range(owners)]
        total = matmul(jnp.concatenate(parts, 1), columns_of(at["down", n]))
        end_ref[...] = (middle_ref[...] if n == 0 else end_ref[...]) + total

    def link_step():
        z_ref[...] = norm_rows(end_ref[...], gain_out)
        turn(z_ref, z_t)
        seen_ref[...] = matmul(z_ref[...], columns_of(at["link"]))

    work = [(0, None, arrange_step), (1, None, pick_step)]
    work += [(2, None, partial(position_rows, pos_ref, slice(0, VIS), D, 0))]
    work += [(when, None, partial(hidden_step, n)) for n, when in enumerate((3, 4, 11, 14))]
    work += [(6, "embed", embed_step)]
    work += [(when, ("qkv", n), partial(qkv_step, n)) for n, when in enumerate((6, 7, 7))]
    work += [(8, None, attention_step), (8, "out", out_step)]
    work += [(when, ("up", n), partial(up_step, n)) for n, when in enumerate((9, 10, 12, 13))]
    work += [(when, ("down", n), partial(down_step, n)) for n, when in enumerate((13, 14, 16, 16))]
    work += [(17, "link", link_step)]

    first(0)
    local_statistics()
    first(1)
    for i in range(19):
        if i + 2 < count:
            first(i + 2)
        statistics(i)
        if i < count:
            second(i)
        if 0 <= i - 1 < count:
            third(i - 1)
        if 0 <= i - 4 < count:
            taken(i - 4, 0)
            taken(i - 4, 1)
        if 0 <= i - 5 < count:
            taken(i - 5, 2)
        for when, piece, run in work:
            if when != i:
                continue
            if piece is not None:
                piece = at[piece]
                whole(piece)
                array, row, rows, column, columns, _ = pieces[piece]
                if array:
                    where = (slice(None), pl.ds(row, rows), pl.ds(column, columns))
                    store = pltpu.make_async_copy(
                        gathered[array].at[where],
                        (None, wide_out, down_out)[array].at[where],
                        store_sem.at[piece],
                    )
                    store.start()
                    stores.append(store)
            run()
    for t, piece in enumerate(pieces):
        if piece[0] > 2:
            whole(t)
    for n in range(2):
        slope_store(FF // D - 2 + n).wait()
    pixel_store(HID // VIS).wait()
    for store in stores:
        store.wait()
    for t in range(count):
        drain(t)
    for step in range(3):
        copy_v(step, sides[step]).wait_send()

    @pl.when(outer)
    def _():
        copy_v(3, z_side).wait_send()

    @pl.when(inner)
    def _():
        copy_v(4, across).wait_send()
        copy_v(5, z_side).wait_send()


def encoder_forward(pixels, facts, scale, vectors, *shards):
    owners = lax.axis_size("fsdp")
    shapes = [w.shape for w in shards]
    count = len(encoder_pieces(shapes)[0])
    omega = np.zeros((8, D // 4), np.float32)
    for row, width in enumerate((D, DD)):
        omega[row, : width // 4] = 10000.0 ** (-np.arange(width // 4) / (width // 4))
    omega = jnp.asarray(omega)
    full = [jax.ShapeDtypeStruct((owners, *shape), BF) for shape in shapes[1:]]
    full += [jax.ShapeDtypeStruct((HID, PD), F32), jax.ShapeDtypeStruct((VIS, FF), F32)]
    local = [
        jax.ShapeDtypeStruct((8, LANES), F32),
        jax.ShapeDtypeStruct((8, TOK_DEV), F32),
        jax.ShapeDtypeStruct((TOK_DEV, 8), F32),
        jax.ShapeDtypeStruct((TOK_DEV, DD), F32),
        jax.ShapeDtypeStruct((VIS, VIS), F32),
        jax.ShapeDtypeStruct((owners, ROWS, VIS), BF),
        *[jax.ShapeDtypeStruct((width, VIS), BF) for width in (D, D, D, FF, D)],
        jax.ShapeDtypeStruct((VIS, D), F32),
        jax.ShapeDtypeStruct((VIS, 3 * D), BF),
        jax.ShapeDtypeStruct((VIS, D), F32),
        jax.ShapeDtypeStruct((VIS, D), F32),
        jax.ShapeDtypeStruct((VIS, DD), F32),
    ]
    vmem, anywhere = pl.BlockSpec(memory_space=pltpu.VMEM), pl.BlockSpec(memory_space=pl.ANY)
    dma = pltpu.SemaphoreType.DMA
    wide_full, down_full, dec_wide, dec_down, *rest = pl.pallas_call(
        encoder_kernel,
        out_shape=(*full, *local),
        in_specs=[vmem] * 6 + [anywhere] * len(shards),
        out_specs=(anywhere,) * len(full) + (vmem,) * len(local),
        scratch_shapes=[pltpu.VMEM((VIS, width), BF) for width in (PD, D, D, D, FF, D)]
        + [pltpu.VMEM((owners, *shape), BF) for shape in shapes[:3]]
        + [
            pltpu.VMEM((4, ROWS, D), F32),
            *[pltpu.VMEM((TOK_DEV, PD), BF)] * 4,
            pltpu.VMEM((VIS, PD), F32),
            pltpu.VMEM((VIS, D), F32),
            pltpu.VMEM((VIS, VIS), F32),
            *[pltpu.VMEM(shape, F32) for shape in shapes[3:]],
            *[pltpu.VMEM(shape, BF) for shape in shapes[3:]],
            pltpu.VMEM((2, VIS, D), F32),
            pltpu.VMEM((VIS, PD), F32),
            pltpu.VMEM((6, 8, LANES), F32),
            pltpu.VMEM((6, 8, LANES), F32),
            dma((4,)),
            dma((count,)),
            dma((count, 11)),
            dma((count, 11)),
            dma((6,)),
            dma((6,)),
            dma((5,)),
        ],
        compiler_params=pltpu.CompilerParams(
            collective_id=1, has_side_effects=True, vmem_limit_bytes=60 * 2**20
        ),
        cost_estimate=pl.CostEstimate(
            flops=2 * VIS * 14 * 2**20, bytes_accessed=200 * 2**20, transcendentals=0
        ),
    )(pixels, facts, facts.T, scale, omega, vectors, *shards)
    return (
        wide_full.reshape(D, -1),
        down_full.reshape(FF, D),
        dec_wide.reshape(DD, -1),
        dec_down.reshape(DFF, DD),
        *rest,
    )


LOWP = 256
HEADP = PD + LOWP
BLOCK = HID // 2


def mask_bias(live, same, shape, offset, keys=0):
    key, query = [lax.broadcasted_iota(jnp.int32, shape, (keys + n) % 2) for n in range(2)]
    return jnp.where((live & same) | (key + offset == query), 0.0, NEGATIVE)


def normalize(h):
    cent = h - jnp.mean(h, -1, keepdims=True)
    rate = lax.rsqrt(jnp.mean(cent * cent, -1, keepdims=True) + EPS)
    return cent * rate, rate


def normalize_back(unit, rate, gain, grad):
    scaled = grad * gain
    along = jnp.mean(scaled * unit, -1, keepdims=True)
    dh = rate * (scaled - jnp.mean(scaled, -1, keepdims=True) - unit * along)
    return dh, jnp.sum(grad * unit, 0, keepdims=True)


def exact_product(array, weight):
    high = array.astype(BF)
    rest = array - high.astype(F32)
    mid = rest.astype(BF)
    low = (rest - mid.astype(F32)).astype(BF)
    return matmul(high, weight) + matmul(mid, weight) + matmul(low, weight)


EARLY = DFF // DD + DFF // UNIT + HEADP // UNIT
LATE = 4


def decoder_kernel(
    owners,
    fast,
    pos_ref,
    seen_ref,
    row_ref,
    column_ref,
    picked_ref,
    stats_ref,
    vectors_ref,
    wide_ref,
    down_ref,
    late_ref,
    dy_ref,
    vec_out,
    sums_ref,
    early_ref,
    y_ref,
    a_ref,
    q_ref,
    k_ref,
    v_ref,
    mixed_t,
    mixed_ref,
    lse_ref,
    head_ref,
    b_ref,
    hidden_ref,
    z_ref,
    dpred_ref,
    dbranch_ref,
    dbefore_ref,
    dattn_ref,
    dmixed_ref,
    dmiddle_ref,
    dq_ref,
    dk_ref,
    dv_ref,
    loss_ref,
    bias_ref,
    pool_ref,
    spread_ref,
    vec_ref,
    *links,
):
    if fast:
        (dp, a_out, a_in, b_out, b_in, swap_sem, a_send, a_recv, b_send, b_recv) = links
        ready = EARLY // 2
        z, f = lax.axis_index("dp"), lax.axis_index("fsdp")
        core, place = f % 2, f // 2
        x, y = place % 2, place // 2
        partner = (z, f + 1 - 2 * core)
        x_side, y_side = (z, f + 2 - 4 * x), (z, f + 4 - 8 * y)
        at_x, at_y, at_far = place + 1 - 2 * x, place + 2 - 4 * y, 3 - place
        first, second = pl.ds(0, HALF), pl.ds(HALF, HALF)
        barrier = pltpu.get_barrier_semaphore()
        for device in (partner, x_side, y_side):
            pl.semaphore_signal(barrier, inc=1, device_id=device, device_id_type=MESH)

        def swap(u):
            return put(
                early_ref.at[:, 1 - core, pl.ds(2 * u, 2)],
                dp.at[u],
                swap_sem.at[u, 0],
                swap_sem.at[u, 1],
                partner,
            )

        def share(u, owner, columns):
            own = early_ref[owner, core, pl.ds(2 * u, 2), :, columns].astype(F32)
            both = own + dp[u, owner, :, :, columns].astype(F32)
            return both.reshape(ROWS, HALF)

        def copy_a(u, side):
            return put(
                a_out.at[u, side],
                a_in.at[u, side],
                a_send.at[u, side],
                a_recv.at[u, side],
                (x_side, y_side)[side],
            )

        def copy_b(u, side):
            return put(
                b_out.at[u, side],
                b_in.at[u, side],
                b_send.at[u, side],
                b_recv.at[u, side],
                (y_side, x_side)[side],
            )

        def exchange(c):
            @pl.when(c < ready)
            def _():
                swap(c).wait()
                a_out[c, 0, 0] = share(c, at_x, first).astype(BF)
                a_out[c, 0, 1] = share(c, at_far, first).astype(BF)
                copy_a(c, 0).start()
                a_out[c, 1, 0] = share(c, at_y, second).astype(BF)
                a_out[c, 1, 1] = share(c, at_far, second).astype(BF)
                copy_a(c, 1).start()

            @pl.when((c >= 2) & (c < ready + 2))
            def _():
                u = c - 2
                copy_a(u, 0).wait_recv()
                b_out[u, 0] = (share(u, at_y, first) + a_in[u, 0, 1].astype(F32)).astype(BF)
                copy_b(u, 0).start()
                copy_a(u, 1).wait_recv()
                b_out[u, 1] = (share(u, at_x, second) + a_in[u, 1, 1].astype(F32)).astype(BF)
                copy_b(u, 1).start()

            @pl.when((c >= 4) & (c < ready + 4))
            def _():
                u = c - 4
                for side, columns in enumerate((first, second)):
                    copy_b(u, side).wait_recv()
                    total = share(u, place, columns) + a_in[u, side, 0].astype(F32)
                    sums_ref[u, :, columns] = total + b_in[u, side].astype(F32)

    size = DD // DHEADS
    per = LANES // size
    factor = size ** (-0.5)
    gain_one, gain_two, gain_out, token = [
        vectors_ref[:, 3 * D + n * DD : 3 * D + (n + 1) * DD] for n in range(4)
    ]

    def pooled(shape, pixels):
        pixel, low = [lax.broadcasted_iota(jnp.int32, shape, (pixels + n) % 2) for n in range(2)]
        row, column = (pixel >> 4) & 15, pixel & 15
        return ((pixel >> 8) << 6) + ((row >> 1) << 3) + (column >> 1) == low

    pool_ref[...] = jnp.where(pooled((PD, LOWP), 0), 0.25, 0.0).astype(BF)
    spread_ref[...] = jnp.where(pooled((LOWP, PD), 1), 1.0, 0.0).astype(BF)
    lane_head = lax.broadcasted_iota(jnp.int32, (HID, LANES), 1) // size
    key_head = lax.broadcasted_iota(jnp.int32, (TOK_DEV, LANES), 1) // size
    kept = column_ref[:VIS, 0:1] > 0
    for start in range(0, TOK_DEV, VIS):
        rows = slice(start, start + VIS)
        bias_ref[rows, :] = mask_bias(
            column_ref[rows, 0:1] > 0,
            column_ref[rows, 2:3] == row_ref[2:3, VIS:],
            (VIS, HID),
            start - VIS,
        )
    if not fast:
        sums_ref[...] = jnp.zeros_like(sums_ref)
    vec_ref[...] = jnp.zeros_like(vec_ref)
    loss_ref[...] = jnp.zeros_like(loss_ref)
    head_ref[...] = jnp.zeros_like(head_ref)
    head_ref[:, : PD + LOWD] = wide_ref[:, 4 * DD + DFF :]

    def project(rows, with_query):
        a = (normalize(y_ref[rows, :])[0] * gain_one).astype(BF)
        a_ref[rows, :] = a
        k_ref[rows, :] = matmul(a, wide_ref[:, DD : 2 * DD]).astype(BF)
        v_ref[rows, :] = matmul(a, wide_ref[:, 2 * DD : 3 * DD]).astype(BF)
        return a

    y_ref[:VIS, :] = pos_ref[:VIS, :] + jnp.where(kept, seen_ref[...], token)
    y_ref[VIS:, :] = pos_ref[VIS:, :] + token
    project(slice(0, VIS), False)

    def hidden_rows(n):
        start = pl.multiple_of(n * BLOCK, BLOCK)
        return pl.ds(start, BLOCK), pl.ds(pl.multiple_of(start + VIS, 32), BLOCK)

    def project_hidden(n, _):
        rows, all_rows = hidden_rows(n)
        a = project(all_rows, True)
        q_ref[rows, :] = matmul(a, wide_ref[:, :DD]).astype(BF)
        return 0

    lax.fori_loop(0, 2, project_hidden, 0)

    def only(array, head_of, j):
        return jnp.where(head_of == j, array.astype(F32), 0.0).astype(BF)

    def attend_group(g, _):
        lanes = pl.ds(pl.multiple_of(g * LANES, LANES), LANES)
        keys, query = k_ref[:, lanes], q_ref[:, lanes]
        values_t = v_ref[:, lanes].T
        for j in range(per):
            scores = right_t(keys, only(query, lane_head, j)) * factor + bias_ref[...]
            top = jnp.max(scores, 0, keepdims=True)
            probs = jnp.exp(scores - top)
            total = jnp.sum(probs, 0, keepdims=True)
            probs = (probs * (1.0 / total)).astype(BF)
            rows = slice(j * size, (j + 1) * size)
            mixed_t[g, rows, :] = matmul(values_t[rows, :], probs).astype(BF)
            lse_ref[g, j : j + 1, :] = top + jnp.log(total)
        mixed_ref[:, lanes] = mixed_t[g].T
        return 0

    lax.fori_loop(0, DD // LANES, attend_group, 0)

    pixels = stats_ref[6:7, :] * (PATCH * PATCH)
    flagged = stats_ref[7:8, 0:1]

    def follow(n, _):
        rows, all_rows = hidden_rows(n)
        middle = y_ref[all_rows, :] + matmul(mixed_ref[rows, :], wide_ref[:, 3 * DD : 4 * DD])
        unit_b, rate_b = normalize(middle)
        b = (unit_b * gain_two).astype(BF)
        b_ref[rows, :] = b
        after, slope = gelu_parts(matmul(b, wide_ref[:, 4 * DD : 4 * DD + DFF]))
        hidden_ref[rows, :] = after.astype(BF)
        unit_z, rate_z = normalize(middle + matmul(hidden_ref[rows, :], down_ref[...]))
        z = (unit_z * gain_out).astype(BF)
        z_ref[rows, :] = z
        pred = matmul(z, head_ref[...])
        parts = []
        for part in range(PD // LANES):
            band = part * LANES // (PATCH * PATCH)
            mean = stats_ref[band : band + 1, :] / pixels
            var = stats_ref[BANDS + band : BANDS + band + 1, :] / pixels - mean * mean
            lanes = slice(part * LANES, (part + 1) * LANES)
            parts.append((picked_ref[rows, lanes] - mean) * lax.rsqrt(var + EPS))
        normed = jnp.concatenate(parts, 1)
        coarse = exact_product(normed, pool_ref[...])
        err_high = pred[:, :PD] - (normed - exact_product(coarse, spread_ref[...]))
        err_low = pred[:, PD:] - coarse
        flag = column_ref[all_rows, 0:1]
        length = jnp.sqrt(err_high * err_high + 1.0)
        loss_ref[:, :PD] += jnp.sum((length - 1.0) * flag, 0, keepdims=True) * (1.0 / PD)
        loss_ref[:, PD:] += jnp.sum(err_low * err_low * flag, 0, keepdims=True) * (1.0 / LOWD)
        share = flag / flagged
        dpred_ref[rows, :PD] = (err_high / length * (share * (1.0 / PD))).astype(BF)
        dpred_ref[rows, PD:] = (err_low * (share * (2.0 / LOWD))).astype(BF)
        dz = right_t(dpred_ref[rows, :], head_ref[...])
        dend, dgain = normalize_back(unit_z, rate_z, gain_out, dz)
        vec_ref[2:3, :] += dgain
        dbranch_ref[rows, :] = dend.astype(BF)
        dhidden = right_t(dbranch_ref[rows, :], down_ref[...])
        dbefore_ref[rows, :] = (dhidden * slope).astype(BF)
        db = right_t(dbefore_ref[rows, :], wide_ref[:, 4 * DD : 4 * DD + DFF])
        dmiddle, dgain = normalize_back(unit_b, rate_b, gain_two, db)
        vec_ref[1:2, :] += dgain
        dmiddle = dmiddle + dend
        dmiddle_ref[rows, :] = dmiddle
        dattn_ref[rows, :] = dmiddle.astype(BF)
        dmixed = right_t(dattn_ref[rows, :], wide_ref[:, 3 * DD : 4 * DD])
        dmixed_ref[rows, :] = dmixed.astype(BF)
        return 0

    lax.fori_loop(0, 2, follow, 0)

    rows = DD // owners

    def store(ref, block, grad):
        ref[:, :, block] = grad.astype(BF).reshape(owners // 2, 2, rows, UNIT)

    parts = DFF // DD
    down_grad = left_t(hidden_ref[...], dbranch_ref[...]).astype(BF)
    down_grad = down_grad.reshape(owners // 2, 2, parts, rows, UNIT)
    for part in range(parts):
        early_ref[:, :, part] = down_grad[:, :, part]
    for n in range(DFF // UNIT):
        columns = slice(n * UNIT, (n + 1) * UNIT)
        store(early_ref, parts + n, left_t(b_ref[...], dbefore_ref[:, columns]))
    for n in range(HEADP // UNIT):
        columns = slice(n * UNIT, (n + 1) * UNIT)
        store(early_ref, parts + DFF // UNIT + n, left_t(z_ref[...], dpred_ref[:, columns]))
    if fast:
        pl.semaphore_wait(barrier, 3)
        for u in range(ready):
            swap(u).start()
    store(
        late_ref,
        3,
        jnp.concatenate([matmul(mixed_t[g], dattn_ref[...]) for g in range(DD // LANES)], 0),
    )

    def attend_back_group(g, _):
        lanes = pl.ds(pl.multiple_of(g * LANES, LANES), LANES)
        query, keys, values, dout = [r[:, lanes] for r in (q_ref, k_ref, v_ref, dmixed_ref)]
        keys_t = keys.T
        dkeys = jnp.zeros((TOK_DEV, LANES), F32)
        dvalues = jnp.zeros((TOK_DEV, LANES), F32)
        dquery = []
        for j in range(per):
            if fast and j % 2 == 0:
                exchange(2 * g + j // 2)
            scores = right_t(keys, only(query, lane_head, j)) * factor + bias_ref[...]
            probs = jnp.exp(scores - lse_ref[g, j : j + 1, :])
            dvalues = jnp.where(key_head == j, matmul(probs.astype(BF), dout), dvalues)
            dprobs = right_t(values, only(dout, lane_head, j))
            delta = jnp.sum(dprobs * probs, 0, keepdims=True)
            dscores = (probs * (dprobs - delta)).astype(BF)
            dkeys = jnp.where(key_head == j, matmul(dscores, query), dkeys)
            dquery.append(matmul(keys_t[j * size : (j + 1) * size, :], dscores))
        dq_ref[:, lanes] = (jnp.concatenate(dquery, 0) * factor).astype(BF).T
        dk_ref[:, lanes] = (dkeys * factor).astype(BF)
        dv_ref[:, lanes] = dvalues.astype(BF)
        return 0

    lax.fori_loop(0, DD // LANES, attend_back_group, 0)

    store(late_ref, 0, left_t(a_ref[VIS:, :], dq_ref[...]))
    if fast:
        exchange(2 * (DD // LANES))
    store(late_ref, 1, left_t(a_ref[...], dk_ref[...]))
    store(late_ref, 2, left_t(a_ref[...], dv_ref[...]))

    def start_rows(rows, da):
        unit, rate = normalize(y_ref[rows, :])
        da = da + right_t(dk_ref[rows, :], wide_ref[:, DD : 2 * DD])
        da = da + right_t(dv_ref[rows, :], wide_ref[:, 2 * DD : 3 * DD])
        dh, dgain = normalize_back(unit, rate, gain_one, da)
        vec_ref[0:1, :] += dgain
        return dh

    dy = start_rows(slice(0, VIS), 0.0)
    dy_ref[...] = dy
    vec_ref[3:4, :] += jnp.sum(jnp.where(kept, 0.0, dy), 0, keepdims=True)

    def start_hidden(n, _):
        rows, all_rows = hidden_rows(n)
        dy = start_rows(all_rows, right_t(dq_ref[rows, :], wide_ref[:, :DD]))
        vec_ref[3:4, :] += jnp.sum(dy + dmiddle_ref[rows, :], 0, keepdims=True)
        return 0

    lax.fori_loop(0, 2, start_hidden, 0)
    vec_out[...] = jnp.zeros_like(vec_out)
    for n in range(4):
        vec_out[3 + n // 2 : 4 + n // 2, n % 2 * DD : (n % 2 + 1) * DD] = vec_ref[n : n + 1, :]
    vec_out[5:6, :] = jnp.broadcast_to(jnp.sum(loss_ref[...], 1, keepdims=True), (1, D))
    if fast:
        for u in range(ready):
            for side in range(2):
                copy_a(u, side).wait_send()
                copy_b(u, side).wait_send()


def decoder_step(fast, pos, seen, by_row, by_column, picked, stats, vectors, wide, down):
    owners = lax.axis_size("fsdp")
    scratch = [
        ((TOK_DEV, DD), F32),
        ((TOK_DEV, DD), BF),
        ((HID, DD), BF),
        ((TOK_DEV, DD), BF),
        ((TOK_DEV, DD), BF),
        ((DD // LANES, LANES, HID), BF),
        ((HID, DD), BF),
        ((DD // LANES, LANES * DHEADS // DD, HID), F32),
        ((DD, HEADP), BF),
        ((HID, DD), BF),
        ((HID, DFF), BF),
        ((HID, DD), BF),
        ((HID, HEADP), BF),
        ((HID, DD), BF),
        ((HID, DFF), BF),
        ((HID, DD), BF),
        ((HID, DD), BF),
        ((HID, DD), F32),
        ((HID, DD), BF),
        ((TOK_DEV, DD), BF),
        ((TOK_DEV, DD), BF),
        ((1, HEADP), F32),
        ((TOK_DEV, HID), F32),
        ((PD, LOWP), BF),
        ((LOWP, PD), BF),
        ((8, DD), F32),
    ]
    vmem = pl.BlockSpec(memory_space=pltpu.VMEM)
    early, late = [
        jax.ShapeDtypeStruct((owners // 2, 2, blocks, DD // owners, UNIT), BF)
        for blocks in (EARLY, LATE)
    ]
    ready = EARLY // 2
    dma = pltpu.SemaphoreType.DMA
    scratch = [pltpu.VMEM(*entry) for entry in scratch]
    params = {}
    if fast:
        sums = jax.ShapeDtypeStruct((ready, ROWS, UNIT), F32)
        scratch = [pltpu.VMEM(early.shape, BF)] + scratch
        scratch += [
            pltpu.VMEM((ready, owners // 2, 2, DD // owners, UNIT), BF),
            pltpu.VMEM((ready, 2, 2, ROWS, HALF), BF),
            pltpu.VMEM((ready, 2, 2, ROWS, HALF), BF),
            pltpu.VMEM((ready, 2, ROWS, HALF), BF),
            pltpu.VMEM((ready, 2, ROWS, HALF), BF),
            *[dma((ready, 2))] * 5,
        ]
        params = {"collective_id": 2, "has_side_effects": True}
    else:
        sums = jax.ShapeDtypeStruct((8, LANES), F32)
    outs = (
        late,
        jax.ShapeDtypeStruct((VIS, DD), F32),
        jax.ShapeDtypeStruct((8, D), F32),
        sums,
        *([] if fast else [early]),
    )
    return pl.pallas_call(
        partial(decoder_kernel, owners, fast),
        out_shape=outs,
        in_specs=[vmem] * 9,
        out_specs=(vmem,) * len(outs),
        scratch_shapes=scratch,
        compiler_params=pltpu.CompilerParams(vmem_limit_bytes=60 * 2**20, **params),
        cost_estimate=pl.CostEstimate(
            flops=40 * 10**9, bytes_accessed=40 * 2**20, transcendentals=2 * 10**7
        ),
    )(
        pos,
        seen,
        by_row,
        by_column,
        picked,
        stats,
        vectors,
        wide,
        down,
    )


def block_forward(h, weights, gains, bias, heads, skip):
    wqkv, wout, wup, wdown = weights
    width = h.shape[1]
    normed_a = layer_norm(h, gains[0]).astype(BF)
    query = matmul(normed_a[skip:], wqkv[:, :width]).astype(BF)
    keys = matmul(normed_a, wqkv[:, width : 2 * width]).astype(BF)
    values = matmul(normed_a, wqkv[:, 2 * width :]).astype(BF)
    mixed_t, lse = attend(query.T, keys, values.T, bias, width // heads)
    middle = h[skip:] + left_t(mixed_t, wout)
    normed_b = layer_norm(middle, gains[1]).astype(BF)
    after, slope = gelu_parts(matmul(normed_b, wup))
    hidden = after.astype(BF)
    end = middle + matmul(hidden, wdown)
    return end, (h, normed_a, query, keys, values, mixed_t, lse, middle, normed_b, slope, hidden)


def block_backward(saved, grad, weights, gains, bias, heads, skip):
    wqkv, wout, wup, wdown = weights
    h, normed_a, query, keys, values, mixed_t, lse, middle, normed_b, slope, hidden = saved
    width = h.shape[1]
    dbranch = grad.astype(BF)
    dbefore = (right_t(dbranch, wdown) * slope).astype(BF)
    dmiddle, dgain_two = norm_back(middle, gains[1], right_t(dbefore, wup))
    dmiddle = dmiddle + grad
    dattn = dmiddle.astype(BF)
    dmixed = right_t(dattn, wout).astype(BF)
    dqt, dkeys, dvalues = attend_back(query, keys, values, dmixed, bias, lse, width // heads)
    dquery = dqt.T
    if skip:
        dquery = jnp.pad(dquery, ((skip, 0), (0, 0)))
        dmiddle = jnp.pad(dmiddle, ((skip, 0), (0, 0)))
    dqkv = jnp.concatenate([dquery, dkeys, dvalues], 1)
    dh, dgain_one = norm_back(h, gains[0], right_t(dqkv, wqkv))
    factors = ((normed_a.T, dqkv), (mixed_t, dattn), (normed_b.T, dbefore), (hidden.T, dbranch))
    return (dh + dmiddle, factors, (dgain_one, dgain_two))


def reduce_rows(grad):
    return lax.psum_scatter(grad.astype(F32), "fsdp", scatter_dimension=0, tiled=True)


def enc_split(wide, down):
    return (
        (wide[:, : 3 * D], wide[:, 3 * D : 4 * D], wide[:, 4 * D : 4 * D + FF], down),
        wide[:, 4 * D + FF :],
    )


def advance(weight, mom, avg, grad, rate):
    grad = grad + DECAY * weight
    buf = MOMENTUM * mom + grad
    new = weight - rate * (grad + MOMENTUM * buf)
    return (buf, new, AVERAGE * avg + (1.0 - AVERAGE) * new)


def advance_kernel(rate, *refs):
    grads, weights, moms, avgs, outs = [refs[5 * n : 5 * n + 5] for n in range(4)] + [refs[20:]]

    def update(n):
        weight = weights[n][...]
        grad = grads[n][:, : weight.shape[1]].astype(F32)
        buf, new, avg = advance(weight, moms[n][...], avgs[n][...], grad, rate)
        outs[4 * n][...] = buf
        outs[4 * n + 1][...] = new
        outs[4 * n + 2][...] = avg
        outs[4 * n + 3][...] = new.astype(BF)

    pl.when(pl.program_id(0) == 0)(partial(update, 0))
    for n in range(1, 5):
        update(n)


def advance_all(rate, grads, weights, moms, avgs):
    steps = weights[3].shape[0] // 16

    def spec(n, array):
        if n == 0:
            return pl.BlockSpec(array.shape, lambda i: (0, 0))
        return pl.BlockSpec((array.shape[0] // steps, array.shape[1]), lambda i: (i, 0))

    arrays = [a for group in (grads, weights, moms, avgs) for a in group]
    outs = [(n, jax.ShapeDtypeStruct(w.shape, t)) for n, w in enumerate(weights) for t in (F32, F32, F32, BF)]
    size = sum(w.size for w in weights)
    return pl.pallas_call(
        partial(advance_kernel, rate),
        grid=(steps,),
        out_shape=[out for _, out in outs],
        in_specs=[spec(n % 5, a) for n, a in enumerate(arrays)],
        out_specs=[spec(n, out) for n, out in outs],
        compiler_params=pltpu.CompilerParams(vmem_limit_bytes=58 * 2**20),
        cost_estimate=pl.CostEstimate(flops=12 * size, bytes_accessed=28 * size, transcendentals=0),
    )(*arrays)


def arrange(valid, masked, scene_ids):
    slots = valid.shape[0]
    live = valid > 0
    kinds = jnp.stack([live & (masked == 0), live & (masked > 0), ~live], 1)
    index = jnp.arange(slots, dtype=jnp.int32)
    ranks = matmul((index[None, :] < index[:, None]).astype(BF), kinds.astype(BF)).astype(jnp.int32)
    n_seen, n_hid = [jnp.sum(kinds[:, i].astype(jnp.int32)) for i in range(2)]
    empty = ranks[:, 2]
    to_empty = jnp.where(empty < VIS - n_seen, n_seen + empty, n_seen + n_hid + empty)
    place = jnp.where(
        kinds[:, 0], ranks[:, 0], jnp.where(kinds[:, 1], VIS + ranks[:, 1], to_empty)
    )
    return (place[None, :] == index[:, None]).astype(BF), n_seen, n_hid


def exact_pick(pick, array):
    high = lax.reduce_precision(array, 8, 7)
    rest = array - high
    mid = lax.reduce_precision(rest, 8, 7)
    low = rest - mid
    return (
        matmul(pick, high.astype(BF)) + matmul(pick, mid.astype(BF)) + matmul(pick, low.astype(BF))
    )


def body(
    pixels,
    masked,
    valid,
    scene_ids,
    gsd_index,
    coords,
    embed,
    wide_enc,
    enc_down,
    wide_dec,
    dec_down,
    vectors,
    embed_mom,
    wide_enc_mom,
    enc_down_mom,
    wide_dec_mom,
    dec_down_mom,
    vector_mom,
    embed_avg,
    wide_enc_avg,
    enc_down_avg,
    wide_dec_avg,
    dec_down_avg,
    vector_avg,
):
    slots = pixels.shape[0]
    fast = (lax.axis_size("dp"), lax.axis_size("fsdp")) == (4, 8)
    vector_row = vectors.reshape(1, -1)
    levels = jnp.exp2(0.5 * gsd_index.astype(jnp.float32) - 1.0)
    gains_enc = (vectors[:D], vectors[D : 2 * D])
    gain_enc_out = vectors[2 * D : 3 * D]
    if fast:
        facts = jnp.stack([valid, masked, scene_ids & 1, coords[:, 0], coords[:, 1]])
        facts = jnp.pad(facts, ((0, 3), (0, 0))).astype(F32)
        scale = jnp.pad(jnp.broadcast_to(levels[:, None], (2, LANES)), ((0, 6), (0, 0)))
        w_enc, w_enc_down, w_dec, w_dec_down, picked_hidden, slope, *saved = encoder_forward(
            pixels, facts, scale, vector_row, embed, wide_enc, enc_down, wide_dec, dec_down
        )
        stats, by_row, by_column, pos_dec, bias_enc, *saved = saved
        *factors, h_start, qkv, middle, h_end, seen_out = saved
    else:
        rows_ok = valid.astype(jnp.float32)
        flags = rows_ok * masked.astype(jnp.float32)
        bands = pixels.reshape(slots, BANDS, PATCH * PATCH)
        weighted = bands * rows_ok[:, None, None]
        band_sum = jnp.sum(weighted, axis=(0, 2))
        counts = jnp.stack([jnp.sum(rows_ok), jnp.sum(flags)])
        band_sq = jnp.sum(weighted * bands, axis=(0, 2))
        stats = jnp.concatenate([band_sum, band_sq, counts])
        stats = jnp.broadcast_to(lax.psum(stats, ("dp", "fsdp"))[:, None], (8, LANES))
        pick, n_seen, n_hid = arrange(valid, masked, scene_ids)
        picked_pixels = exact_pick(pick, pixels)
        picked_hidden = picked_pixels[VIS:]
        small = matmul(pick, jnp.concatenate([(scene_ids % 2)[:, None], coords], 1).astype(BF))
        odd, coord = small[:, 0], small[:, 1:]
        scale = jnp.where(odd == 0, levels[0], levels[1])
        index = jnp.arange(slots, dtype=jnp.int32)
        live = jnp.concatenate([index[:VIS] < n_seen, index[:HID] < n_hid])
        allow = live[:, None] & (odd[:, None] == odd[None, :]) | (index[:, None] == index[None, :])
        bias_enc = jnp.where(allow, 0.0, NEGATIVE)[:VIS, :VIS]
        by_row = jnp.pad(jnp.stack([live.astype(F32), odd, odd]), ((0, 5), (0, 0)))
        by_column = by_row.T
        pos_dec = positions(coord, scale, DD)
    count = stats[7, 0]
    if not fast:
        w_embed, w_enc, w_enc_down, w_dec, w_dec_down = [
            lax.all_gather(w.astype(BF), "fsdp", axis=0, tiled=True)
            for w in (embed, wide_enc, enc_down, wide_dec, dec_down)
        ]
        enc_weights, w_link = enc_split(w_enc, w_enc_down)
        mean = jnp.repeat(stats[:3, 0] / (stats[6, 0] * (PATCH * PATCH)), PATCH * PATCH)
        square = jnp.repeat(stats[3:6, 0] / (stats[6, 0] * (PATCH * PATCH)), PATCH * PATCH)
        rate = lax.rsqrt(square - mean * mean + EPS)
        inputs = ((picked_pixels[:VIS] - mean) * rate).astype(BF)
        h_start = matmul(inputs, w_embed) + positions(coord[:VIS], scale[:VIS], D)
        h_end, enc_saved = block_forward(h_start, enc_weights, gains_enc, bias_enc, HEADS, 0)
        encoded = layer_norm(h_end, gain_enc_out).astype(BF)
        seen_out = matmul(encoded, w_link)
    late, dy_seen, vec, ready, *early = decoder_step(
        fast,
        pos_dec,
        seen_out,
        by_row,
        by_column,
        picked_hidden,
        stats,
        vector_row,
        w_dec,
        w_dec_down,
    )
    if fast:
        inputs_t, a_t, mixed_t, b_t, hidden_t, z_t = factors
        *enc_parts, dec_wide, dec_tall, vec = encoder_back(
            dy_seen,
            by_column,
            vec,
            vector_row,
            bias_enc,
            qkv,
            ready,
            late,
            (h_end, middle, h_start, slope),
            w_enc,
            w_enc_down,
            (z_t, hidden_t, b_t, mixed_t, a_t, inputs_t),
        )
        dec_parts = (dec_wide, dec_tall)
        vector_grad, loss_sum = vec[:5].reshape(-1), vec[5, 0]
    else:
        dseen = (dy_seen * by_column[:VIS, 0:1]).astype(BF)
        dec_vec, local_loss = vec[3:5].reshape(-1), vec[5, 0]
        dh_end, dgain_enc_out = norm_back(h_end, gain_enc_out, right_t(dseen, w_link))
        dh_start, enc_factors, dgains_enc = block_backward(
            enc_saved, dh_end, enc_weights, gains_enc, bias_enc, HEADS, 0
        )
        enc_grads = [matmul(*pair) for pair in enc_factors]
        link_grad = left_t(encoded, dseen)
        enc_parts = lax.psum(
            (
                reduce_rows(left_t(inputs, dh_start.astype(BF))),
                reduce_rows(
                    jnp.concatenate([enc_grads[0], enc_grads[1], enc_grads[2], link_grad], 1)
                ),
                reduce_rows(enc_grads[3]),
            ),
            "dp",
        )
        parts = DFF // DD
        early = early[0]
        dec_grads = jnp.concatenate([early[:, :, :parts], late, early[:, :, parts:]], 2)
        dec_grads = dec_grads.reshape(-1, *dec_grads.shape[2:])
        dec_sum = lax.psum(reduce_rows(dec_grads), "dp")[0]
        rows, parts = dec_sum.shape[1], DFF // DD
        dec_parts = (
            dec_sum[parts:].transpose(1, 0, 2).reshape(rows, -1),
            dec_sum[:parts].reshape(-1, DD),
        )
        vector_grad = jnp.concatenate([*dgains_enc, dgain_enc_out, dec_vec])
        vector_grad, loss_sum = lax.psum((vector_grad, local_loss), ("dp", "fsdp"))
    grads = (*enc_parts, *dec_parts)
    rate = STEP_UNIT * (PD * TOK_DEV * lax.axis_size("dp") * lax.axis_size("fsdp")) ** 0.5
    weights = (embed, wide_enc, enc_down, wide_dec, dec_down)
    moms = (embed_mom, wide_enc_mom, enc_down_mom, wide_dec_mom, dec_down_mom)
    avgs = (embed_avg, wide_enc_avg, enc_down_avg, wide_dec_avg, dec_down_avg)
    outs = advance_all(rate, grads, weights, moms, avgs)
    return (*outs, *advance(vectors, vector_mom, vector_avg, vector_grad, rate), loss_sum, count)


def solution(mesh):
    both, rows = P(("dp", "fsdp")), P("fsdp", None)
    placed = (P(("dp", "fsdp"), None), both, both, both, both, P(("dp", "fsdp"), None))
    states = (rows,) * 5 + (P(),)
    return jax.shard_map(
        body,
        mesh=mesh,
        in_specs=placed + states * 3,
        out_specs=(rows,) * 20 + (P(),) * 5,
        check_vma=False,
    )
```
